32 devices in a mesh: groups: 2 (over x), ty: 16 (over z, y, core).
Axes of the slice: x: 2, y: 2, z: 4, core: 2. Of those that a mesh axis runs over, the one named last changes fastest.
Arguments:
- spectrum: float32 [2, 4096, 8192], P(None, ('groups', 'ty')), parts along dimension 1, may hold values from -6 to 6
- pupil: bfloat16 [1024, 1024], replicated, may hold values from 0.19921875 to 1
- measured: bfloat16 [32, 256, 1024], P(('groups', 'ty')), parts along dimension 0, may hold values from 0.29882812 to 3
- centre_rows: int32 [32], P('groups'), parts along dimension 0, may hold values from 512 to 1536
- centre_cols: int32 [32], P('groups'), parts along dimension 0, may hold values from 512 to 7680
Outputs:
- updated: float32 [2, 4096, 8192], P(None, ('groups', 'ty')), parts along dimension 1
The draws below stay inside these ranges and needn't reach their ends.
There are 2 independent parts, one for each index of `groups`. The reference program is written for one: setup_inputs(seed, part) draws one part's arguments, and reference() takes and returns one part's arrays. A program takes and returns all parts, laid end to end along the dimension named above; an argument that names none is the same for every part. Nothing has to cross between parts.
Inputs may be any that keep to these rules, and one draw needn't show every extreme that they name: `centre_rows`: each pupil crop lies inside the slab's rows. `centre_cols`: each pupil crop lies inside the slab's columns.
All inputs are finite; a program needn't handle non-finite values.
Results may differ from the reference program's by a relative error of at most 0.00063.
Values may be sent and summed in bfloat16 or wider, within the bound.
No kernel may reach another device: no remote copies, remote signals or barrier semaphores. Data moves between devices by JAX's collectives and lax.ppermute only.
A program may use at most 128 MiB of HBM per device.

```python
import math
import jax
import jax.numpy as jnp
from jax import lax

PS = 1024
NC = 8192
IMG_ROWS = 256
NR = 2048
K = 16


def plant(drawn, rng, smallest, high):
    longest = drawn.shape.index(max(drawn.shape))
    spots = []
    for shift in (0, 1):
        where = [jax.random.randint(jax.random.fold_in(rng, axis), (), 0, length) for axis, length in enumerate(drawn.shape)]
        where[longest] = (where[longest] + shift) % drawn.shape[longest]
        spots.append(tuple(where))
    return drawn.at[spots[0]].set(smallest).at[spots[1]].set(high)


def levels(stream_key, shape, pieces, smallest, largest):
    level, own = 1.0, jax.random.fold_in(stream_key, 6)
    for dim, parts in pieces:
        draws = jnp.exp(jax.random.uniform(jax.random.fold_in(own, dim), (parts,), jnp.float32, smallest / len(pieces), largest / len(pieces)))
        level = level * jnp.repeat(draws, shape[dim] // parts).reshape([-1 if axis == dim else 1 for axis in range(len(shape))])
    return level


def normal_values(stream_key, dims, deviation, reach, cuts=(), kind=jnp.bfloat16):
    level = levels(stream_key, dims, cuts, -0.22, 0.18) if cuts else 1.0
    array = jax.random.normal(stream_key, dims, jnp.float32) * deviation * level
    return jnp.minimum(jnp.maximum(array, -reach), reach).astype(kind)


def setup_inputs(seed: int = 0, part: int = 0) -> dict:
    key_list = jax.random.split(jax.random.key(seed), 6)
    part_keys = jax.random.split(jax.random.fold_in(key_list[5], part), 6)
    spectrum = normal_values(part_keys[0], (2, NR, NC), 1.0, 6.0, ((1, 16),), jnp.float32)
    pupil = jnp.clip(jnp.exp(jax.random.uniform(key_list[1], (PS, PS), jnp.float32, math.log(0.19921875), math.log(1.0))), 0.19921875, 1.0).astype(jnp.bfloat16)
    measured = jnp.clip(jnp.exp(math.log(3.0) - 2.306499 * jax.random.uniform(part_keys[2], (K, IMG_ROWS, PS), jnp.float32) ** levels(part_keys[2], (K, IMG_ROWS, PS), ((0, 16),), -0.2, 0.2)), 0.29882812, 3.0).astype(jnp.bfloat16)
    centre_rows = plant(jax.random.randint(part_keys[3], (K,), PS // 2, NR - PS // 2 + 1), jax.random.fold_in(part_keys[3], 1), PS // 2, (NR - PS // 2 + 1) - 1).astype(jnp.int32)
    centre_cols = plant(jax.random.randint(part_keys[4], (K,), PS // 2, NC - PS // 2 + 1), jax.random.fold_in(part_keys[4], 1), PS // 2, (NC - PS // 2 + 1) - 1).astype(jnp.int32)
    return dict(spectrum=spectrum, pupil=pupil, measured=measured, centre_rows=centre_rows, centre_cols=centre_cols)


step_size = 0.5

def fourier_tables(crop_width):
    counter = jnp.arange(crop_width, dtype=jnp.int32)
    product = counter[:, None] * counter[None, :] % crop_width
    angle = product.astype(jnp.float32) * (2.0 * math.pi / crop_width)
    factor = 1.0 / math.sqrt(crop_width)
    return ((jnp.cos(angle) * factor).astype(jnp.bfloat16), (jnp.sin(angle) * factor).astype(jnp.bfloat16))

def pupil_weight(pupil):
    crop_width = pupil.shape[0]
    counter = jnp.arange(crop_width, dtype=jnp.int32)
    centred = 2 * counter - crop_width + 1
    inside = centred[:, None] * centred[:, None] + centred[None, :] * centred[None, :] <= crop_width * crop_width
    return jnp.where(inside, pupil.astype(jnp.float32), jnp.float32(0.0))

def product_pair(left_real, left_imag, right_real, right_imag):
    real_part = jnp.dot(left_real, right_real, preferred_element_type=jnp.float32) - jnp.dot(left_imag, right_imag, preferred_element_type=jnp.float32)
    imag_part = jnp.dot(left_real, right_imag, preferred_element_type=jnp.float32) + jnp.dot(left_imag, right_real, preferred_element_type=jnp.float32)
    return (real_part, imag_part)

def image_gradient(crop, image, weight, cos_table, sin_table):
    crop_width = weight.shape[0]
    band_rows = image.shape[0]
    band_start = (crop_width - band_rows) // 2
    band_cos = cos_table[band_start:band_start + band_rows]
    band_sin = sin_table[band_start:band_start + band_rows]
    pupiled = (weight[None] * crop.astype(jnp.float32)).astype(jnp.bfloat16)
    mid_real, mid_imag = product_pair(band_cos, band_sin, pupiled[0], pupiled[1])
    mid_real = mid_real.astype(jnp.bfloat16)
    mid_imag = mid_imag.astype(jnp.bfloat16)
    field_real, field_imag = product_pair(mid_real, mid_imag, cos_table, sin_table)
    magnitude = jnp.sqrt(field_real * field_real + field_imag * field_imag)
    keeping = 1.0 - image.astype(jnp.float32) / jnp.maximum(magnitude, 1.0)
    resid_real = (field_real * keeping).astype(jnp.bfloat16)
    resid_imag = (field_imag * keeping).astype(jnp.bfloat16)
    back_real, back_imag = product_pair(resid_real, resid_imag, cos_table, -sin_table)
    back_real = back_real.astype(jnp.bfloat16)
    back_imag = back_imag.astype(jnp.bfloat16)
    grad_real, grad_imag = product_pair(band_cos.T, -band_sin.T, back_real, back_imag)
    return jnp.stack([grad_real * weight, grad_imag * weight])

def reference(spectrum, pupil, measured, centre_rows, centre_cols):
    crop_width = pupil.shape[0]
    spec_low = spectrum.astype(jnp.bfloat16)
    weight = pupil_weight(pupil)
    cos_table, sin_table = fourier_tables(crop_width)

    def visit(summed, inputs):
        row_centre, col_centre, image = inputs
        corner = (jnp.int32(0), (row_centre - crop_width // 2).astype(jnp.int32), (col_centre - crop_width // 2).astype(jnp.int32))
        crop = lax.dynamic_slice(spec_low, corner, (2, crop_width, crop_width))
        gradient = image_gradient(crop, image, weight, cos_table, sin_table)
        current = lax.dynamic_slice(summed, corner, (2, crop_width, crop_width))
        return (lax.dynamic_update_slice(summed, current + gradient, corner), None)
    summed, unused = lax.scan(visit, jnp.zeros(spectrum.shape, jnp.float32), (centre_rows, centre_cols, measured))
    return spectrum - step_size * summed
```

```python
import functools
import math

import jax
import jax.numpy as jnp
import numpy as np
from jax import lax
from jax.experimental import pallas as pl
from jax.experimental.pallas import tpu as pltpu
from jax.sharding import PartitionSpec as P

step_size = 0.5
lane = 128
sublane = 8
vmem_bytes = 56 * 1024 * 1024


def fourier_tables(crop_width):
    counter = np.arange(crop_width, dtype=np.int64)
    angle = (counter[:, None] * counter[None, :] % crop_width) * (2.0 * math.pi / crop_width)
    factor = 1.0 / math.sqrt(crop_width)
    cos_table = (np.cos(angle) * factor).astype(np.float32).astype(jnp.bfloat16)
    sin_table = (np.sin(angle) * factor).astype(np.float32).astype(jnp.bfloat16)
    return cos_table, sin_table


def pupil_weight(pupil):
    crop_width = pupil.shape[0]
    counter = jnp.arange(crop_width, dtype=jnp.int32)
    centred = 2 * counter - crop_width + 1
    inside = (
        centred[:, None] * centred[:, None] + centred[None, :] * centred[None, :]
        <= crop_width * crop_width
    )
    return jnp.where(inside, pupil.astype(jnp.float32), jnp.float32(0.0))


def shifted_rows(window_ref, residual, tile_rows):
    window = window_ref.shape[0]
    return pltpu.roll(window_ref[...], (window - residual) % window, 0)[:tile_rows]


def band_rows_matrix(bt_ref, residual, tile_rows):
    rows = shifted_rows(bt_ref, residual, tile_rows)
    band = rows.shape[1] // 2
    turned = jnp.concatenate([-rows[:, band:], rows[:, :band]], axis=1)
    return jnp.concatenate([rows, turned], axis=0).astype(jnp.bfloat16)


def forward_kernel(info_ref, spec_ref, weight_ref, bt_ref, out_ref, *, tile_rows, crop_width, band):
    step = pl.program_id(0)
    residual = info_ref[1, step]
    col_shift = info_ref[3, step]
    active = info_ref[4, step]
    width = spec_ref.shape[2]

    @pl.when(active == 0)
    def _():
        out_ref[...] = jnp.zeros_like(out_ref)

    @pl.when(active != 0)
    def _():
        weight = shifted_rows(weight_ref, residual, tile_rows)
        parts = []
        for part in range(2):
            low = spec_ref[part].astype(jnp.bfloat16).astype(jnp.float32)
            low = pltpu.roll(low, (width - col_shift) % width, 1)[:, :crop_width]
            parts.append((weight * low).astype(jnp.bfloat16))
        pupiled = jnp.concatenate(parts, axis=0)
        left = band_rows_matrix(bt_ref, residual, tile_rows)
        mid = lax.dot_general(
            left, pupiled, (((0,), (0,)), ((), ())), preferred_element_type=jnp.float32
        )
        out_ref[0] = mid.astype(jnp.bfloat16).reshape(2, band, crop_width)


def backward_kernel(
    info_ref, spec_ref, back_ref, weight_ref, bt_ref, out_ref, *, tile_rows, crop_width, band, width
):
    step = pl.program_id(0)
    residual = info_ref[1, step]
    col_start = info_ref[2, step]
    col_shift = info_ref[3, step]
    active = info_ref[4, step]

    @pl.when(step == 0)
    def _():
        out_ref[...] = spec_ref[...]

    @pl.when(active != 0)
    def _():
        weight = shifted_rows(weight_ref, residual, tile_rows)
        left = band_rows_matrix(bt_ref, residual, tile_rows)
        back = back_ref[0].reshape(2 * band, crop_width)
        grad = jnp.dot(left, back, preferred_element_type=jnp.float32)
        columns = pl.ds(pl.multiple_of(col_start, lane), width)
        pad = jnp.zeros((tile_rows, width - crop_width), jnp.float32)
        for part in range(2):
            piece = grad[part * tile_rows : (part + 1) * tile_rows] * weight * step_size
            piece = pltpu.roll(jnp.concatenate([piece, pad], axis=1), col_shift, 1)
            out_ref[part, :, columns] = out_ref[part, :, columns] - piece


def middle_kernel(mid_ref, image_ref, cos_ref, sin_ref, out_ref, real_ref, imag_ref):
    step = pl.program_id(0)
    hr, hi = mid_ref[0], mid_ref[1]
    cos, sin = cos_ref[...], sin_ref[...]
    dot = functools.partial(jnp.dot, preferred_element_type=jnp.float32)
    field_real = dot(hr, cos) - dot(hi, sin)
    field_imag = dot(hr, sin) + dot(hi, cos)
    magnitude = jnp.sqrt(field_real * field_real + field_imag * field_imag)
    keeping = 1.0 - image_ref[0].astype(jnp.float32) / jnp.maximum(magnitude, 1.0)
    qr = (field_real * keeping).astype(jnp.bfloat16)
    qi = (field_imag * keeping).astype(jnp.bfloat16)

    def turned(left, table):
        return lax.dot_general(
            left, table, (((1,), (1,)), ((), ())), preferred_element_type=jnp.float32
        )

    back_real = turned(qr, cos) + turned(qi, sin)
    back_imag = turned(qi, cos) - turned(qr, sin)

    @pl.when(step == 0)
    def _():
        real_ref[...] = back_real
        imag_ref[...] = back_imag

    @pl.when(step != 0)
    def _():
        real_ref[...] += back_real
        imag_ref[...] += back_imag

    @pl.when(step == pl.num_programs(0) - 1)
    def _():
        out_ref[0] = real_ref[...].astype(jnp.bfloat16)
        out_ref[1] = imag_ref[...].astype(jnp.bfloat16)


def params():
    return pltpu.CompilerParams(vmem_limit_bytes=vmem_bytes)


def forward(info, spectrum, weight, bt):
    _, tile_rows, slab_columns = spectrum.shape
    crop_width = weight.shape[1]
    band = bt.shape[1] // 2
    width = crop_width + lane
    count = info.shape[1]
    window = tile_rows + sublane
    return pl.pallas_call(
        functools.partial(forward_kernel, tile_rows=tile_rows, crop_width=crop_width, band=band),
        grid_spec=pltpu.PrefetchScalarGridSpec(
            num_scalar_prefetch=1,
            grid=(count,),
            in_specs=[
                pl.BlockSpec(
                    (pl.Element(2), pl.Element(tile_rows), pl.Element(width)),
                    lambda i, info: (0, 0, pl.multiple_of(info[2, i], lane)),
                ),
                pl.BlockSpec(
                    (pl.Element(window), pl.Element(crop_width)),
                    lambda i, info: (pl.multiple_of(info[0, i], sublane), 0),
                ),
                pl.BlockSpec(
                    (pl.Element(window), pl.Element(2 * band)),
                    lambda i, info: (pl.multiple_of(info[0, i], sublane), 0),
                ),
            ],
            out_specs=pl.BlockSpec((1, 2, band, crop_width), lambda i, info: (i, 0, 0, 0)),
        ),
        out_shape=jax.ShapeDtypeStruct((count, 2, band, crop_width), jnp.bfloat16),
        compiler_params=params(),
        name="forward",
    )(info, spectrum, weight, bt)


def backward(info, spectrum, back, weight, bt):
    _, tile_rows, slab_columns = spectrum.shape
    crop_width = weight.shape[1]
    band = bt.shape[1] // 2
    width = crop_width + lane
    count = info.shape[1]
    window = tile_rows + sublane
    whole = pl.BlockSpec(
        spectrum.shape, lambda i, info: (0, 0, 0), pipeline_mode=pl.Buffered(1)
    )
    return pl.pallas_call(
        functools.partial(
            backward_kernel, tile_rows=tile_rows, crop_width=crop_width, band=band, width=width
        ),
        grid_spec=pltpu.PrefetchScalarGridSpec(
            num_scalar_prefetch=1,
            grid=(count,),
            in_specs=[
                whole,
                pl.BlockSpec((1, 2, band, crop_width), lambda i, info: (i, 0, 0, 0)),
                pl.BlockSpec(
                    (pl.Element(window), pl.Element(crop_width)),
                    lambda i, info: (pl.multiple_of(info[0, i], sublane), 0),
                ),
                pl.BlockSpec(
                    (pl.Element(window), pl.Element(2 * band)),
                    lambda i, info: (pl.multiple_of(info[0, i], sublane), 0),
                ),
            ],
            out_specs=pl.BlockSpec(spectrum.shape, lambda i, info: (0, 0, 0)),
        ),
        out_shape=jax.ShapeDtypeStruct(spectrum.shape, jnp.float32),
        compiler_params=params(),
        name="backward",
    )(info, spectrum, back, weight, bt)


def middle(mid, image, cos_table, sin_table):
    _, band, crop_width = mid.shape
    block = min(256, crop_width)
    table = pl.BlockSpec((crop_width, block), lambda j: (0, j))
    return pl.pallas_call(
        middle_kernel,
        grid=(crop_width // block,),
        in_specs=[
            pl.BlockSpec((2, band, crop_width), lambda j: (0, 0, 0)),
            pl.BlockSpec((1, band, block), lambda j: (0, 0, j)),
            table,
            table,
        ],
        out_specs=pl.BlockSpec((2, band, crop_width), lambda j: (0, 0, 0)),
        out_shape=jax.ShapeDtypeStruct((2, band, crop_width), jnp.bfloat16),
        scratch_shapes=[pltpu.VMEM((band, crop_width), jnp.float32)] * 2,
        compiler_params=params(),
        name="middle",
    )(mid, image, cos_table, sin_table)


def image_info(position, tile_rows, slab_columns, crop_width, centre_rows, centre_cols):
    tops = centre_rows - crop_width // 2
    lefts = centre_cols - crop_width // 2
    begin = position * tile_rows - tops + tile_rows
    active = (begin > 0) & (begin < crop_width + tile_rows)
    begin = jnp.clip(begin, 0, crop_width + tile_rows)
    aligned = begin // sublane * sublane
    col_start = jnp.minimum(lefts // lane * lane, slab_columns - crop_width - lane)
    return jnp.stack(
        [aligned, begin - aligned, col_start, lefts - col_start, active.astype(jnp.int32)]
    ).astype(jnp.int32)


def per_device(spectrum, pupil, measured, centre_rows, centre_cols):
    position = lax.axis_index("ty")
    _, tile_rows, slab_columns = spectrum.shape
    crop_width = pupil.shape[0]
    band = measured.shape[1]
    band_start = (crop_width - band) // 2
    cos_table, sin_table = fourier_tables(crop_width)
    pads = ((tile_rows, tile_rows + sublane), (0, 0))
    band_table = np.concatenate(
        [
            cos_table[:, band_start : band_start + band],
            sin_table[:, band_start : band_start + band],
        ],
        axis=1,
    ).astype(np.float32)
    bt = jnp.asarray(np.pad(band_table, pads))
    weight = jnp.pad(pupil_weight(pupil), pads)
    info = image_info(position, tile_rows, slab_columns, crop_width, centre_rows, centre_cols)
    partial = forward(info, spectrum, weight, bt)
    mid = lax.psum_scatter(partial, "ty", scatter_dimension=0, tiled=True)[0]
    back = middle(mid, measured, jnp.asarray(cos_table), jnp.asarray(sin_table))
    gathered = lax.all_gather(back, "ty")
    return backward(info, spectrum, gathered, weight, bt)


def solution(mesh):
    return jax.shard_map(
        per_device,
        mesh=mesh,
        in_specs=(
            P(None, ("groups", "ty"), None),
            P(),
            P(("groups", "ty"), None, None),
            P("groups"),
            P("groups"),
        ),
        out_specs=P(None, ("groups", "ty"), None),
        check_vma=False,
    )
```

```python
import functools
import math

import jax
import jax.numpy as jnp
import numpy as np
from jax import lax
from jax.experimental import pallas as pl
from jax.experimental.pallas import tpu as pltpu
from jax.sharding import PartitionSpec as P

step_size = 0.5
lane = 128
row_tile = 16
vmem_bytes = 56 * 1024 * 1024


def fourier_tables(crop_width):
    counter = np.arange(crop_width, dtype=np.int64)
    angle = (counter[:, None] * counter[None, :] % crop_width) * (2.0 * math.pi / crop_width)
    factor = 1.0 / math.sqrt(crop_width)
    cos_table = (np.cos(angle) * factor).astype(np.float32).astype(jnp.bfloat16)
    sin_table = (np.sin(angle) * factor).astype(np.float32).astype(jnp.bfloat16)
    return cos_table, sin_table


def tile_weight(pupil_ref, first_row, shift, tile_rows):
    window, crop_width = pupil_ref.shape
    rows = pltpu.roll(pupil_ref[...].astype(jnp.float32), (2 * window - shift) % window, 0)
    shape = (tile_rows, crop_width)
    row = 2 * (first_row + lax.broadcasted_iota(jnp.int32, shape, 0)) - crop_width + 1
    column = 2 * lax.broadcasted_iota(jnp.int32, shape, 1) - crop_width + 1
    inside = row * row + column * column <= crop_width * crop_width
    return jnp.where(inside, rows[:tile_rows], 0.0)


def tile_band(band_ref, shift, tile_rows):
    window, both = band_ref.shape
    rows = pltpu.roll(band_ref[...].astype(jnp.float32), (2 * window - shift) % window, 0)
    rows = rows[:tile_rows]
    turned = jnp.concatenate([-rows[:, both // 2 :], rows[:, : both // 2]], axis=1)
    return jnp.concatenate([rows, turned], axis=0).astype(jnp.bfloat16)


class Windows:
    def __init__(self, tile_rows, slab_columns, crop_width):
        self.tile_rows = tile_rows
        self.crop_width = crop_width
        self.rows = tile_rows + row_tile
        self.columns = crop_width + lane
        self.last_row = crop_width - self.rows
        self.last_column = slab_columns - self.columns

    def row(self, first_row):
        start = jnp.clip(first_row, 0, self.last_row) // row_tile * row_tile
        return pl.multiple_of(start, row_tile)

    def column(self, left):
        start = jnp.minimum(left // lane * lane, self.last_column)
        return pl.multiple_of(start, lane)

    def active(self, first_row):
        return (first_row > -self.tile_rows) & (first_row < self.crop_width)


def forward_kernel(meta_ref, spec_ref, pupil_ref, band_ref, out_ref, *, base, win):
    slot = base + pl.program_id(0)
    first_row, left = meta_ref[0, slot], meta_ref[1, slot]
    active = win.active(first_row)
    tile_rows, crop_width = win.tile_rows, win.crop_width

    @pl.when(jnp.logical_not(active))
    def _():
        out_ref[...] = jnp.zeros_like(out_ref)

    @pl.when(active)
    def _():
        row_shift = first_row - win.row(first_row)
        col_shift = left - win.column(left)
        weight = tile_weight(pupil_ref, first_row, row_shift, tile_rows)
        parts = []
        for part in range(2):
            low = spec_ref[part].astype(jnp.bfloat16).astype(jnp.float32)
            low = pltpu.roll(low, (win.columns - col_shift) % win.columns, 1)[:, :crop_width]
            parts.append((weight * low).astype(jnp.bfloat16))
        pupiled = jnp.concatenate(parts, axis=0)
        table = tile_band(band_ref, row_shift, tile_rows)
        mid = lax.dot_general(
            table, pupiled, (((0,), (0,)), ((), ())), preferred_element_type=jnp.float32
        )
        out_ref[...] = mid.astype(jnp.bfloat16).reshape(out_ref.shape)


def backward_kernel(meta_ref, spec_ref, pupil_ref, band_ref, *refs, slots, win):
    back_refs = refs[: len(slots)]
    out_ref, held, sems = refs[len(slots) :]
    step = pl.program_id(0)
    count = len(slots)
    tile_rows, crop_width = win.tile_rows, win.crop_width

    def fetch(index, buffer):
        for number, back_ref in enumerate(back_refs):

            @pl.when(index == number)
            def _():
                pltpu.make_async_copy(back_ref, held.at[buffer], sems.at[buffer]).start()

    @pl.when(step == 0)
    def _():
        fetch(0, 0)
        out_ref[...] = spec_ref[...]

    @pl.when(step + 1 < count)
    def _():
        fetch(step + 1, (step + 1) % 2)

    buffer = step % 2
    pltpu.make_async_copy(back_refs[0], held.at[buffer], sems.at[buffer]).wait()
    slot = pick(slots, step)
    first_row, left = meta_ref[0, slot], meta_ref[1, slot]

    @pl.when(win.active(first_row))
    def _():
        row_shift = first_row - win.row(first_row)
        col_start = win.column(left)
        weight = tile_weight(pupil_ref, first_row, row_shift, tile_rows) * step_size
        table = tile_band(band_ref, row_shift, tile_rows)
        back = held[buffer].reshape(table.shape[1], crop_width)
        grad = jnp.dot(table, back, preferred_element_type=jnp.float32)
        columns = pl.ds(col_start, win.columns)
        pad = jnp.zeros((tile_rows, win.columns - crop_width), jnp.float32)
        for part in range(2):
            piece = grad[part * tile_rows : (part + 1) * tile_rows] * weight
            piece = pltpu.roll(jnp.concatenate([piece, pad], axis=1), left - col_start, 1)
            out_ref[part, :, columns] = out_ref[part, :, columns] - piece


def pick(values, index):
    result = jnp.int32(values[0])
    for number, value in enumerate(values[1:], 1):
        result = jnp.where(index == number, jnp.int32(value), result)
    return result


def middle_kernel(own_ref, up_ref, down_ref, image_ref, cos_ref, sin_ref, out_ref, mid_ref, sum_ref):
    step = pl.program_id(0)
    _, band, crop_width = own_ref.shape

    @pl.when(step == 0)
    def _():
        total = own_ref[...].astype(jnp.float32) + up_ref[...].astype(jnp.float32)
        total = total + down_ref[...].astype(jnp.float32)
        mid_ref[...] = total.astype(jnp.bfloat16).reshape(2 * band, crop_width)
        sum_ref[...] = jnp.zeros_like(sum_ref)

    dot = functools.partial(jnp.dot, preferred_element_type=jnp.float32)
    mid = mid_ref[...]
    by_cos, by_sin = dot(mid, cos_ref[...]), dot(mid, sin_ref[...])
    field_real = by_cos[:band] - by_sin[band:]
    field_imag = by_sin[:band] + by_cos[band:]
    magnitude = jnp.sqrt(field_real * field_real + field_imag * field_imag)
    keeping = 1.0 - image_ref[0].astype(jnp.float32) / jnp.maximum(magnitude, 1.0)
    resid = jnp.concatenate([field_real * keeping, field_imag * keeping], axis=0)
    resid = resid.astype(jnp.bfloat16)

    def turned(table):
        return lax.dot_general(
            resid, table, (((1,), (1,)), ((), ())), preferred_element_type=jnp.float32
        )

    by_cos, by_sin = turned(cos_ref[...]), turned(sin_ref[...])
    sum_ref[0] += by_cos[:band] + by_sin[band:]
    sum_ref[1] += by_cos[band:] - by_sin[:band]

    @pl.when(step == pl.num_programs(0) - 1)
    def _():
        out_ref[...] = sum_ref[...].astype(jnp.bfloat16)


def params():
    return pltpu.CompilerParams(vmem_limit_bytes=vmem_bytes)


def cost(count, win, band, moved):
    flops = 16 * count * win.tile_rows * band * win.crop_width
    return pl.CostEstimate(flops=flops, bytes_accessed=moved, transcendentals=0)


def forward(meta, spectrum, pupil, band_table, base, count):
    _, tile_rows, slab_columns = spectrum.shape
    crop_width = pupil.shape[1]
    band = band_table.shape[1] // 2
    win = Windows(tile_rows, slab_columns, crop_width)

    def row(i, meta):
        return (win.row(meta[0, base + i]), 0)

    return pl.pallas_call(
        functools.partial(forward_kernel, base=base, win=win),
        grid_spec=pltpu.PrefetchScalarGridSpec(
            num_scalar_prefetch=1,
            grid=(count,),
            in_specs=[
                pl.BlockSpec(
                    (pl.Element(2), pl.Element(tile_rows), pl.Element(win.columns)),
                    lambda i, meta: (0, 0, win.column(meta[1, base + i])),
                ),
                pl.BlockSpec((pl.Element(win.rows), pl.Element(crop_width)), row),
                pl.BlockSpec((pl.Element(win.rows), pl.Element(2 * band)), row),
            ],
            out_specs=pl.BlockSpec((1, 2, band, crop_width), lambda i, meta: (i, 0, 0, 0)),
        ),
        out_shape=jax.ShapeDtypeStruct((count, 2, band, crop_width), jnp.bfloat16),
        compiler_params=params(),
        cost_estimate=cost(count, win, band, count * 3000000),
        name="forward",
    )(meta, spectrum, pupil, band_table)


def backward(meta, spectrum, pupil, band_table, slots, backs):
    _, tile_rows, slab_columns = spectrum.shape
    crop_width = pupil.shape[1]
    band = band_table.shape[1] // 2
    win = Windows(tile_rows, slab_columns, crop_width)
    count = len(slots)

    def row(i, meta):
        return (win.row(meta[0, pick(slots, i)]), 0)

    return pl.pallas_call(
        functools.partial(backward_kernel, slots=slots, win=win),
        grid_spec=pltpu.PrefetchScalarGridSpec(
            num_scalar_prefetch=1,
            grid=(count,),
            in_specs=[
                pl.BlockSpec(
                    spectrum.shape, lambda i, meta: (0, 0, 0), pipeline_mode=pl.Buffered(1)
                ),
                pl.BlockSpec((pl.Element(win.rows), pl.Element(crop_width)), row),
                pl.BlockSpec((pl.Element(win.rows), pl.Element(2 * band)), row),
            ]
            + [pl.BlockSpec(memory_space=pl.ANY)] * count,
            out_specs=pl.BlockSpec(spectrum.shape, lambda i, meta: (0, 0, 0)),
            scratch_shapes=[
                pltpu.VMEM((2, 2, band, crop_width), jnp.bfloat16),
                pltpu.SemaphoreType.DMA((2,)),
            ],
        ),
        out_shape=jax.ShapeDtypeStruct(spectrum.shape, jnp.float32),
        compiler_params=params(),
        cost_estimate=cost(count, win, band, count * 3000000 + 16 * 1024 * 1024),
        name="backward",
    )(meta, spectrum, pupil, band_table, *backs)


def middle(own, up, down, image, cos_table, sin_table):
    _, band, crop_width = own.shape
    block = min(256, crop_width)
    table = pl.BlockSpec((crop_width, block), lambda j: (0, j))
    whole = pl.BlockSpec((2, band, crop_width), lambda j: (0, 0, 0))
    return pl.pallas_call(
        middle_kernel,
        grid=(crop_width // block,),
        in_specs=[
            whole,
            whole,
            whole,
            pl.BlockSpec((1, band, block), lambda j: (0, 0, j)),
            table,
            table,
        ],
        out_specs=whole,
        out_shape=jax.ShapeDtypeStruct((2, band, crop_width), jnp.bfloat16),
        scratch_shapes=[
            pltpu.VMEM((2 * band, crop_width), jnp.bfloat16),
            pltpu.VMEM((2, band, crop_width), jnp.float32),
        ],
        compiler_params=params(),
        name="middle",
    )(own, up, down, image, cos_table, sin_table)


def total(*terms):
    return sum(term.astype(jnp.float32) for term in terms).astype(jnp.bfloat16)


def far_first(planes):
    rows = []
    for z in range(planes):
        upward = 2 * z < planes
        rows.append(
            sorted(range(planes), key=lambda q: (-abs(q - z), (q < z) if upward else (q > z)))
        )
    return rows


def chosen(plane, options):
    groups = []
    for z, value in options.items():
        for entry in groups:
            if entry[0] is value:
                entry[1].append(z)
                break
        else:
            groups.append((value, [z]))
    result = groups[0][0]
    for value, members in groups[1:]:
        here = functools.reduce(jnp.logical_or, [plane == z for z in members])
        result = jnp.where(here, value, result)
    return result


def per_device(spectrum, pupil, measured, centre_rows, centre_cols):
    count = lax.axis_size("ty")
    planes = count // 4
    position = lax.axis_index("ty")
    plane, corner = position // 4, position % 4
    _, tile_rows, slab_columns = spectrum.shape
    crop_width = pupil.shape[0]
    band = measured.shape[1]
    band_start = (crop_width - band) // 2
    cos_table, sin_table = fourier_tables(crop_width)
    chosen_rows = slice(band_start, band_start + band)
    band_table = jnp.asarray(
        np.concatenate([cos_table[:, chosen_rows], sin_table[:, chosen_rows]], axis=1)
    )
    cos_table, sin_table = jnp.asarray(cos_table), jnp.asarray(sin_table)

    order = far_first(planes)
    flips = jnp.asarray([3, 1, 2, 0], jnp.int32)
    my_order = lax.dynamic_index_in_dim(jnp.asarray(order, jnp.int32), plane, keepdims=False)
    ids = (my_order[:, None] * 4 + (corner ^ flips)[None, :]).reshape(-1)
    match = ids[:, None] == jnp.arange(count, dtype=jnp.int32)[None, :]
    half = crop_width // 2
    tops = jnp.sum(jnp.where(match, centre_rows[None, :], 0), axis=1) - half
    lefts = jnp.sum(jnp.where(match, centre_cols[None, :], 0), axis=1) - half
    meta = jnp.stack([position * tile_rows - tops, lefts]).astype(jnp.int32)

    def sibling(value):
        return lax.ppermute(value, "ty", [(i, i ^ 1) for i in range(count)])

    def across(value):
        return lax.ppermute(value, "ty", [(i, i ^ 2) for i in range(count)])

    def along(value, sources, by):
        pairs = [(4 * z + i, 4 * (z + by) + i) for z in sources for i in range(4)]
        return lax.ppermute(value, "ty", pairs)

    def partial(base, number):
        return forward(meta, spectrum, pupil, band_table, base, number)

    summed = []
    received = []
    up = down = None
    up_total = down_total = None

    def z_step(s):
        nonlocal up, down
        sources = [z for z in range(planes - 1) if z < s]
        value = chosen(plane, {z: summed[order[z].index(planes - s + z)] for z in sources})
        up = along(total(value, up) if up is not None else value, sources, 1)
        sources = [z for z in range(1, planes) if planes - 1 - z < s]
        value = chosen(plane, {z: summed[order[z].index(s - planes + z)] for z in sources})
        down = along(total(value, down) if down is not None else value, sources, -1)

    for j in range(planes):
        if j == 0:
            theirs = [partial(0, 1)[0], partial(1, 1)[0]]
            mine = [partial(2, 1)[0], partial(3, 1)[0]]
            came = [sibling(theirs[0]), sibling(theirs[1])]
        else:
            theirs = partial(4 * j, 2)
            mine = partial(4 * j + 2, 2)
            came = sibling(theirs)
        outgoing = total(mine[0], came[0])
        if j >= 2:
            outgoing, received[j - 2] = lax.optimization_barrier((outgoing, received[j - 2]))
        received.append(across(outgoing))
        if j >= 1:
            z_step(j)
        summed.append(total(mine[1], came[1], received[j]))
    band_back = middle(summed[-1], up, down, measured, cos_table, sin_table)

    near = [list(reversed(row)) for row in order]
    from_below, from_above = [band_back], [band_back]
    column = [band_back]
    other = [across(band_back)]
    result = spectrum
    for s in range(1, planes):
        from_below.append(along(from_below[-1], range(s - 1, planes - 1), 1))
        from_above.append(along(from_above[-1], range(1, planes - s + 1), -1))
        options = {}
        for z in range(planes):
            q = near[z][s]
            options[z] = from_below[z - q] if q < z else from_above[q - z]
        value = chosen(plane, options)
        column.append(value)
        other.append(across(value))

    def slot(j, kind):
        return 4 * (planes - 1 - j) + kind

    slots, backs = [], []
    for j in range(planes):
        slots += [slot(j, 3), slot(j, 1)]
        backs += [column[j], sibling(column[j])]
        if j < planes - 1:
            slots += [slot(j, 2), slot(j, 0)]
            backs += [other[j], sibling(other[j])]
    result = backward(meta, result, pupil, band_table, slots, backs)
    slots = [slot(planes - 1, 2), slot(planes - 1, 0)]
    backs = [other[-1], sibling(other[-1])]
    return backward(meta, result, pupil, band_table, slots, backs)


def solution(mesh):
    return jax.shard_map(
        per_device,
        mesh=mesh,
        in_specs=(
            P(None, ("groups", "ty"), None),
            P(),
            P(("groups", "ty"), None, None),
            P("groups"),
            P("groups"),
        ),
        out_specs=P(None, ("groups", "ty"), None),
        check_vma=False,
    )
```

```python
import functools
import math

import jax
import jax.numpy as jnp
import numpy as np
from jax import lax
from jax.experimental import pallas as pl
from jax.experimental.pallas import tpu as pltpu
from jax.sharding import PartitionSpec as P

step_size = 0.5
lane = 128
row_tile = 16
vmem_bytes = 56 * 1024 * 1024


def fourier_tables(crop_width):
    counter = np.arange(crop_width, dtype=np.int64)
    angle = (counter[:, None] * counter[None, :] % crop_width) * (2.0 * math.pi / crop_width)
    factor = 1.0 / math.sqrt(crop_width)
    cos_table = (np.cos(angle) * factor).astype(np.float32).astype(jnp.bfloat16)
    sin_table = (np.sin(angle) * factor).astype(np.float32).astype(jnp.bfloat16)
    return cos_table, sin_table


def tile_weight(pupil_ref, first_row, shift, tile_rows):
    window, crop_width = pupil_ref.shape
    rows = pltpu.roll(pupil_ref[...].astype(jnp.float32), (2 * window - shift) % window, 0)
    shape = (tile_rows, crop_width)
    row = 2 * (first_row + lax.broadcasted_iota(jnp.int32, shape, 0)) - crop_width + 1
    column = 2 * lax.broadcasted_iota(jnp.int32, shape, 1) - crop_width + 1
    inside = row * row + column * column <= crop_width * crop_width
    return jnp.where(inside, rows[:tile_rows], 0.0)


def tile_band(band_ref, shift, tile_rows):
    window, both = band_ref.shape
    rows = pltpu.roll(band_ref[...].astype(jnp.float32), (2 * window - shift) % window, 0)
    rows = rows[:tile_rows]
    turned = jnp.concatenate([-rows[:, both // 2 :], rows[:, : both // 2]], axis=1)
    return jnp.concatenate([rows, turned], axis=0).astype(jnp.bfloat16)


class Windows:
    def __init__(self, tile_rows, slab_columns, crop_width):
        self.tile_rows = tile_rows
        self.crop_width = crop_width
        self.rows = tile_rows + row_tile
        self.columns = crop_width + lane
        self.last_row = crop_width - self.rows
        self.last_column = slab_columns - self.columns

    def row(self, first_row):
        start = jnp.clip(first_row, 0, self.last_row) // row_tile * row_tile
        return pl.multiple_of(start, row_tile)

    def column(self, left):
        start = jnp.minimum(left // lane * lane, self.last_column)
        return pl.multiple_of(start, lane)

    def active(self, first_row):
        return (first_row > -self.tile_rows) & (first_row < self.crop_width)


def forward_kernel(meta_ref, spec_ref, pupil_ref, band_ref, *refs, base, win, adding):
    came_ref, out_refs = (refs[0], refs[1:]) if adding else (None, refs)
    step = pl.program_id(0)
    slot = base + step
    first_row, left = meta_ref[0, slot], meta_ref[1, slot]
    active = win.active(first_row)
    tile_rows, crop_width = win.tile_rows, win.crop_width
    shape = out_refs[0].shape

    def store(value):
        if not adding:
            out_refs[0][...] = value.reshape(shape)
            return
        for number, out_ref in enumerate(out_refs):

            @pl.when(step == number)
            def _():
                out_ref[...] = value.reshape(shape)

    @pl.when(jnp.logical_not(active))
    def _():
        store(came_ref[...] if adding else jnp.zeros(shape, jnp.bfloat16))

    @pl.when(active)
    def _():
        row_shift = first_row - win.row(first_row)
        col_shift = left - win.column(left)
        weight = tile_weight(pupil_ref, first_row, row_shift, tile_rows)
        parts = []
        for part in range(2):
            low = spec_ref[part].astype(jnp.bfloat16).astype(jnp.float32)
            low = pltpu.roll(low, (win.columns - col_shift) % win.columns, 1)[:, :crop_width]
            parts.append((weight * low).astype(jnp.bfloat16))
        pupiled = jnp.concatenate(parts, axis=0)
        table = tile_band(band_ref, row_shift, tile_rows)
        mid = lax.dot_general(
            table, pupiled, (((0,), (0,)), ((), ())), preferred_element_type=jnp.float32
        )
        if adding:
            mid = mid + came_ref[...].reshape(mid.shape).astype(jnp.float32)
        store(mid.astype(jnp.bfloat16))


def backward_kernel(meta_ref, spec_ref, pupil_ref, band_ref, *refs, slots, win):
    back_refs = refs[: len(slots)]
    out_ref, held, sems = refs[len(slots) :]
    step = pl.program_id(0)
    count = len(slots)
    tile_rows, crop_width = win.tile_rows, win.crop_width

    def fetch(index, buffer):
        for number, back_ref in enumerate(back_refs):

            @pl.when(index == number)
            def _():
                pltpu.make_async_copy(back_ref, held.at[buffer], sems.at[buffer]).start()

    @pl.when(step == 0)
    def _():
        fetch(0, 0)
        out_ref[...] = spec_ref[...]

    @pl.when(step + 1 < count)
    def _():
        fetch(step + 1, (step + 1) % 2)

    buffer = step % 2
    pltpu.make_async_copy(back_refs[0], held.at[buffer], sems.at[buffer]).wait()
    slot = pick(slots, step)
    first_row, left = meta_ref[0, slot], meta_ref[1, slot]

    @pl.when(win.active(first_row))
    def _():
        row_shift = first_row - win.row(first_row)
        col_start = win.column(left)
        weight = tile_weight(pupil_ref, first_row, row_shift, tile_rows) * step_size
        table = tile_band(band_ref, row_shift, tile_rows)
        back = held[buffer].reshape(table.shape[1], crop_width)
        grad = jnp.dot(table, back, preferred_element_type=jnp.float32)
        columns = pl.ds(col_start, win.columns)
        pad = jnp.zeros((tile_rows, win.columns - crop_width), jnp.float32)
        for part in range(2):
            piece = grad[part * tile_rows : (part + 1) * tile_rows] * weight
            piece = pltpu.roll(jnp.concatenate([piece, pad], axis=1), left - col_start, 1)
            out_ref[part, :, columns] = out_ref[part, :, columns] - piece


def pick(values, index):
    result = jnp.int32(values[0])
    for number, value in enumerate(values[1:], 1):
        result = jnp.where(index == number, jnp.int32(value), result)
    return result


def middle_kernel(
    own_ref, up_ref, down_ref, image_ref, cos_ref, sin_ref, out_ref, mid_ref, resid_ref
):
    step = pl.program_id(0)
    _, band, crop_width = own_ref.shape
    block = cos_ref.shape[1]
    blocks = crop_width // block

    @pl.when(step == 0)
    def _():
        total = own_ref[...].astype(jnp.float32) + up_ref[...].astype(jnp.float32)
        total = total + down_ref[...].astype(jnp.float32)
        mid_ref[...] = total.astype(jnp.bfloat16).reshape(2 * band, crop_width)

    def products(left):
        dot = functools.partial(jnp.dot, preferred_element_type=jnp.float32)
        return dot(left, cos_ref[...]), dot(left, sin_ref[...])

    @pl.when(step < blocks)
    def _():
        by_cos, by_sin = products(mid_ref[...])
        field_real = by_cos[:band] - by_sin[band:]
        field_imag = by_sin[:band] + by_cos[band:]
        magnitude = jnp.sqrt(field_real * field_real + field_imag * field_imag)
        keeping = 1.0 - image_ref[0].astype(jnp.float32) / jnp.maximum(magnitude, 1.0)
        resid = jnp.concatenate([field_real * keeping, field_imag * keeping], axis=0)
        columns = pl.ds(pl.multiple_of(step * block, block), block)
        resid_ref[:, columns] = resid.astype(jnp.bfloat16)

    @pl.when(step >= blocks)
    def _():
        by_cos, by_sin = products(resid_ref[...])
        out_ref[0] = (by_cos[:band] + by_sin[band:]).astype(jnp.bfloat16)
        out_ref[1] = (by_cos[band:] - by_sin[:band]).astype(jnp.bfloat16)


def params():
    return pltpu.CompilerParams(vmem_limit_bytes=vmem_bytes)


def cost(count, win, band, moved):
    flops = 16 * count * win.tile_rows * band * win.crop_width
    return pl.CostEstimate(flops=flops, bytes_accessed=moved, transcendentals=0)


def forward(meta, spectrum, pupil, band_table, base, count, came=None):
    _, tile_rows, slab_columns = spectrum.shape
    crop_width = pupil.shape[1]
    band = band_table.shape[1] // 2
    win = Windows(tile_rows, slab_columns, crop_width)
    adding = came is not None

    def row(i, meta):
        return (win.row(meta[0, base + i]), 0)

    stacked = pl.BlockSpec((1, 2, band, crop_width), lambda i, meta: (i, 0, 0, 0))
    single = pl.BlockSpec((2, band, crop_width), lambda i, meta: (0, 0, 0))
    if adding:
        out_specs = [single] * count
        out_shape = [jax.ShapeDtypeStruct((2, band, crop_width), jnp.bfloat16)] * count
    else:
        out_specs = stacked
        out_shape = jax.ShapeDtypeStruct((count, 2, band, crop_width), jnp.bfloat16)
    return pl.pallas_call(
        functools.partial(forward_kernel, base=base, win=win, adding=adding),
        grid_spec=pltpu.PrefetchScalarGridSpec(
            num_scalar_prefetch=1,
            grid=(count,),
            in_specs=[
                pl.BlockSpec(
                    (pl.Element(2), pl.Element(tile_rows), pl.Element(win.columns)),
                    lambda i, meta: (0, 0, win.column(meta[1, base + i])),
                ),
                pl.BlockSpec((pl.Element(win.rows), pl.Element(crop_width)), row),
                pl.BlockSpec((pl.Element(win.rows), pl.Element(2 * band)), row),
            ]
            + [stacked] * adding,
            out_specs=out_specs,
        ),
        out_shape=out_shape,
        compiler_params=params(),
        cost_estimate=cost(count, win, band, count * 3000000),
        name="forward",
    )(meta, spectrum, pupil, band_table, *([came] if adding else []))


def backward(meta, spectrum, pupil, band_table, slots, backs):
    _, tile_rows, slab_columns = spectrum.shape
    crop_width = pupil.shape[1]
    band = band_table.shape[1] // 2
    win = Windows(tile_rows, slab_columns, crop_width)
    count = len(slots)

    def row(i, meta):
        return (win.row(meta[0, pick(slots, i)]), 0)

    return pl.pallas_call(
        functools.partial(backward_kernel, slots=slots, win=win),
        grid_spec=pltpu.PrefetchScalarGridSpec(
            num_scalar_prefetch=1,
            grid=(count,),
            in_specs=[
                pl.BlockSpec(
                    spectrum.shape, lambda i, meta: (0, 0, 0), pipeline_mode=pl.Buffered(1)
                ),
                pl.BlockSpec((pl.Element(win.rows), pl.Element(crop_width)), row),
                pl.BlockSpec((pl.Element(win.rows), pl.Element(2 * band)), row),
            ]
            + [pl.BlockSpec(memory_space=pl.ANY)] * count,
            out_specs=pl.BlockSpec(spectrum.shape, lambda i, meta: (0, 0, 0)),
            scratch_shapes=[
                pltpu.VMEM((2, 2, band, crop_width), jnp.bfloat16),
                pltpu.SemaphoreType.DMA((2,)),
            ],
        ),
        out_shape=jax.ShapeDtypeStruct(spectrum.shape, jnp.float32),
        compiler_params=params(),
        cost_estimate=cost(count, win, band, count * 3000000 + 16 * 1024 * 1024),
        name="backward",
    )(meta, spectrum, pupil, band_table, *backs)


def middle(own, up, down, image, cos_table, sin_table):
    _, band, crop_width = own.shape
    block = min(256, crop_width)
    blocks = crop_width // block
    table = pl.BlockSpec((crop_width, block), lambda j: (0, j % blocks))
    whole = pl.BlockSpec((2, band, crop_width), lambda j: (0, 0, 0))
    return pl.pallas_call(
        middle_kernel,
        grid=(2 * blocks,),
        in_specs=[
            whole,
            whole,
            whole,
            pl.BlockSpec((1, band, block), lambda j: (0, 0, jnp.minimum(j, blocks - 1))),
            table,
            table,
        ],
        out_specs=pl.BlockSpec((2, band, block), lambda j: (0, 0, jnp.maximum(j - blocks, 0))),
        out_shape=jax.ShapeDtypeStruct((2, band, crop_width), jnp.bfloat16),
        scratch_shapes=[pltpu.VMEM((2 * band, crop_width), jnp.bfloat16)] * 2,
        compiler_params=params(),
        cost_estimate=pl.CostEstimate(
            flops=16 * band * crop_width * crop_width,
            bytes_accessed=14 * band * crop_width * 2 + 8 * crop_width * crop_width,
            transcendentals=0,
        ),
        name="middle",
    )(own, up, down, image, cos_table, sin_table)


def total(*terms):
    return sum(term.astype(jnp.float32) for term in terms).astype(jnp.bfloat16)


def far_first(planes):
    rows = []
    for z in range(planes):
        upward = 2 * z < planes
        rows.append(
            sorted(range(planes), key=lambda q: (-abs(q - z), (q < z) if upward else (q > z)))
        )
    return rows


def chosen(plane, options):
    groups = []
    for z, value in options.items():
        for entry in groups:
            if entry[0] is value:
                entry[1].append(z)
                break
        else:
            groups.append((value, [z]))
    result = groups[0][0]
    for value, members in groups[1:]:
        here = functools.reduce(jnp.logical_or, [plane == z for z in members])
        result = jnp.where(here, value, result)
    return result


def per_device(spectrum, pupil, measured, centre_rows, centre_cols):
    count = lax.axis_size("ty")
    planes = count // 4
    position = lax.axis_index("ty")
    plane = position // 4
    _, tile_rows, slab_columns = spectrum.shape
    crop_width = pupil.shape[0]
    band = measured.shape[1]
    band_start = (crop_width - band) // 2
    cos_table, sin_table = fourier_tables(crop_width)
    chosen_rows = slice(band_start, band_start + band)
    band_table = jnp.asarray(
        np.concatenate([cos_table[:, chosen_rows], sin_table[:, chosen_rows]], axis=1)
    )
    cos_table, sin_table = jnp.asarray(cos_table), jnp.asarray(sin_table)

    order = far_first(planes)
    first = [(0, 2)]
    second = [(0, 0), (1, 2), (1, 0)]
    others = [(j, y) for j in range(2, planes) for y in (2, 0)]
    groups = [first, second, others]
    slots = {}
    for core in (1, 0):
        for group in groups:
            for j, y in group:
                slots[j, y + core] = len(slots)
    ids = [
        [order[i // 4][j] * 4 + (i % 4 ^ flip) for (j, flip) in slots] for i in range(count)
    ]
    my_ids = lax.dynamic_index_in_dim(jnp.asarray(ids, jnp.int32), position, keepdims=False)
    match = my_ids[:, None] == jnp.arange(count, dtype=jnp.int32)[None, :]
    half = crop_width // 2
    tops = jnp.sum(jnp.where(match, centre_rows[None, :], 0), axis=1) - half
    lefts = jnp.sum(jnp.where(match, centre_cols[None, :], 0), axis=1) - half
    meta = jnp.stack([position * tile_rows - tops, lefts]).astype(jnp.int32)

    def sibling(value):
        return lax.ppermute(value, "ty", [(i, i ^ 1) for i in range(count)])

    def across(value):
        return lax.ppermute(value, "ty", [(i, i ^ 2) for i in range(count)])

    def along(value, sources, by):
        pairs = [(4 * z + i, 4 * (z + by) + i) for z in sources for i in range(4)]
        return lax.ppermute(value, "ty", pairs)

    def theirs(group, after):
        known = meta if after is None else lax.optimization_barrier((meta, after))[0]
        j, y = group[0]
        return forward(known, spectrum, pupil, band_table, slots[j, y + 1], len(group))

    def mine(group, came, after):
        known = meta if after is None else lax.optimization_barrier((meta, after))[0]
        j, y = group[0]
        return forward(known, spectrum, pupil, band_table, slots[j, y], len(group), came)

    sent = theirs(first, None)
    came_first = sibling(sent)
    sent = theirs(second, sent)
    came_second = sibling(sent)
    (leaving,) = mine(first, came_first, sent)
    received = {0: across(leaving)}
    kept = {}
    sent = theirs(others, leaving)
    came_others = sibling(sent)
    made = mine(second, came_second, sent)
    kept[0], leaving, kept[1] = made
    received[1] = across(leaving)
    made = mine(others, came_others, made[0])
    for (j, y), value in zip(others, made):
        if y:
            received[j] = across(value)
        else:
            kept[j] = value

    up = down = None
    summed = []
    for s in range(1, planes + 1):
        summed.append(total(kept[s - 1], received[s - 1]))
        if s == planes:
            break
        sources = [z for z in range(planes - 1) if z < s]
        value = chosen(plane, {z: summed[order[z].index(planes - s + z)] for z in sources})
        going_up = value if up is None else total(value, up)
        sources_down = [z for z in range(1, planes) if planes - 1 - z < s]
        value = chosen(plane, {z: summed[order[z].index(s - planes + z)] for z in sources_down})
        going_down = value if down is None else total(value, down)
        up, down = along(going_up, sources, 1), along(going_down, sources_down, -1)
    band_back = middle(summed[-1], up, down, measured, cos_table, sin_table)

    near = [list(reversed(row)) for row in order]
    result = spectrum
    from_below, from_above = [band_back], [band_back]
    waiting = []
    value, turned = band_back, None
    for s in range(planes):
        j = planes - 1 - s
        new_slots, arrived = [slots[j, 0]], [value]
        started = [across(value), sibling(value)]
        next_slots = [slots[j, 2], slots[j, 1]]
        if turned is not None:
            started.append(sibling(turned))
            next_slots.append(slots[j + 1, 3])
        if s < planes - 1:
            started.append(along(from_below[-1], range(s, planes - 1), 1))
            started.append(along(from_above[-1], range(1, planes - s), -1))
        waiting.append((slots[j, 0], value))
        if s > 0:
            result = backward(
                meta, result, pupil, band_table, [k for k, _ in waiting], [v for _, v in waiting]
            )
            waiting = []
        started = list(lax.optimization_barrier(tuple([result] + started)))
        result, started = started[0], started[1:]
        waiting += list(zip(next_slots, started))
        turned = started[0]
        if s < planes - 1:
            from_below.append(started[-2])
            from_above.append(started[-1])
            options = {}
            for z in range(planes):
                q = near[z][s + 1]
                options[z] = from_below[z - q] if q < z else from_above[q - z]
            value = chosen(plane, options)
    waiting.append((slots[0, 3], sibling(turned)))
    return backward(
        meta, result, pupil, band_table, [k for k, _ in waiting], [v for _, v in waiting]
    )


def solution(mesh):
    return jax.shard_map(
        per_device,
        mesh=mesh,
        in_specs=(
            P(None, ("groups", "ty"), None),
            P(),
            P(("groups", "ty"), None, None),
            P("groups"),
            P("groups"),
        ),
        out_specs=P(None, ("groups", "ty"), None),
        check_vma=False,
    )
```

```python
import functools
import math

import jax
import jax.numpy as jnp
import numpy as np
from jax import lax
from jax.experimental import pallas as pl
from jax.experimental.pallas import tpu as pltpu
from jax.sharding import PartitionSpec as P

step_size = 0.5
lane = 128
row_tile = 16
vmem_bytes = 64 * 1024 * 1024 - 512 * 1024


def fourier_tables(crop_width):
    counter = np.arange(crop_width, dtype=np.int64)
    angle = (counter[:, None] * counter[None, :] % crop_width) * (2.0 * math.pi / crop_width)
    factor = 1.0 / math.sqrt(crop_width)
    cos_table = (np.cos(angle) * factor).astype(np.float32).astype(jnp.bfloat16)
    sin_table = (np.sin(angle) * factor).astype(np.float32).astype(jnp.bfloat16)
    return cos_table, sin_table


def tile_weight(pupil_ref, first_row, shift, tile_rows):
    window, crop_width = pupil_ref.shape
    rows = pltpu.roll(pupil_ref[...].astype(jnp.float32), (2 * window - shift) % window, 0)
    shape = (tile_rows, crop_width)
    row = 2 * (first_row + lax.broadcasted_iota(jnp.int32, shape, 0)) - crop_width + 1
    column = 2 * lax.broadcasted_iota(jnp.int32, shape, 1) - crop_width + 1
    inside = row * row + column * column <= crop_width * crop_width
    return jnp.where(inside, rows[:tile_rows], 0.0)


def tile_band(band_ref, shift, tile_rows):
    window, both = band_ref.shape
    rows = pltpu.roll(band_ref[...].astype(jnp.float32), (2 * window - shift) % window, 0)
    rows = rows[:tile_rows]
    turned = jnp.concatenate([-rows[:, both // 2 :], rows[:, : both // 2]], axis=1)
    return jnp.concatenate([rows, turned], axis=0).astype(jnp.bfloat16)


class Windows:
    def __init__(self, tile_rows, slab_columns, crop_width):
        self.tile_rows = tile_rows
        self.crop_width = crop_width
        self.rows = tile_rows + row_tile
        self.columns = crop_width + lane
        self.last_row = crop_width - self.rows
        self.last_column = slab_columns - self.columns

    def row(self, first_row):
        start = jnp.clip(first_row, 0, self.last_row) // row_tile * row_tile
        return pl.multiple_of(start, row_tile)

    def column(self, left):
        start = jnp.minimum(left // lane * lane, self.last_column)
        return pl.multiple_of(start, lane)

    def active(self, first_row):
        return (first_row > -self.tile_rows) & (first_row < self.crop_width)


def forward_kernel(meta_ref, spec_ref, pupil_ref, band_ref, *refs, base, win, adding):
    came_ref, out_refs = (refs[0], refs[1:]) if adding else (None, refs)
    step = pl.program_id(0)
    slot = base + step
    first_row, left = meta_ref[0, slot], meta_ref[1, slot]
    active = win.active(first_row)
    tile_rows, crop_width = win.tile_rows, win.crop_width
    shape = out_refs[0].shape

    def store(value):
        if not adding:
            out_refs[0][...] = value.reshape(shape)
            return
        for number, out_ref in enumerate(out_refs):

            @pl.when(step == number)
            def _():
                out_ref[...] = value.reshape(shape)

    @pl.when(jnp.logical_not(active))
    def _():
        store(came_ref[...] if adding else jnp.zeros(shape, jnp.bfloat16))

    @pl.when(active)
    def _():
        row_shift = first_row - win.row(first_row)
        col_shift = left - win.column(left)
        weight = tile_weight(pupil_ref, first_row, row_shift, tile_rows)
        parts = []
        for part in range(2):
            low = spec_ref[part].astype(jnp.bfloat16).astype(jnp.float32)
            low = pltpu.roll(low, (win.columns - col_shift) % win.columns, 1)[:, :crop_width]
            parts.append((weight * low).astype(jnp.bfloat16))
        pupiled = jnp.concatenate(parts, axis=0)
        table = tile_band(band_ref, row_shift, tile_rows)
        mid = lax.dot_general(
            table, pupiled, (((0,), (0,)), ((), ())), preferred_element_type=jnp.float32
        )
        if adding:
            mid = mid + came_ref[...].reshape(mid.shape).astype(jnp.float32)
        store(mid.astype(jnp.bfloat16))


def backward_kernel(meta_ref, spec_ref, pupil_ref, band_ref, *refs, slots, win):
    back_refs, (out_ref, held, sems) = refs[:-3], refs[-3:]
    stacked = len(back_refs) < len(slots)
    step = pl.program_id(0)
    count = len(slots)
    tile_rows, crop_width = win.tile_rows, win.crop_width

    def fetch(index, buffer):
        for number, back_ref in enumerate([] if stacked else back_refs):

            @pl.when(index == number)
            def _():
                pltpu.make_async_copy(back_ref, held.at[buffer], sems.at[buffer]).start()

        if stacked:
            source = back_refs[0].at[index]
            pltpu.make_async_copy(source, held.at[buffer], sems.at[buffer]).start()

    @pl.when(step == 0)
    def _():
        fetch(0, 0)
        out_ref[...] = spec_ref[...]

    @pl.when(step + 1 < count)
    def _():
        fetch(step + 1, (step + 1) % 2)

    buffer = step % 2
    sample = back_refs[0].at[0] if stacked else back_refs[0]
    pltpu.make_async_copy(sample, held.at[buffer], sems.at[buffer]).wait()
    slot = pick(slots, step)
    first_row, left = meta_ref[0, slot], meta_ref[1, slot]

    @pl.when(win.active(first_row))
    def _():
        row_shift = first_row - win.row(first_row)
        col_start = win.column(left)
        weight = tile_weight(pupil_ref, first_row, row_shift, tile_rows) * step_size
        table = tile_band(band_ref, row_shift, tile_rows)
        back = held[buffer].reshape(table.shape[1], crop_width)
        grad = jnp.dot(table, back, preferred_element_type=jnp.float32)
        columns = pl.ds(col_start, win.columns)
        pad = jnp.zeros((tile_rows, win.columns - crop_width), jnp.float32)
        for part in range(2):
            piece = grad[part * tile_rows : (part + 1) * tile_rows] * weight
            piece = pltpu.roll(jnp.concatenate([piece, pad], axis=1), left - col_start, 1)
            out_ref[part, :, columns] = out_ref[part, :, columns] - piece


def pick(values, index):
    if list(values) == list(range(len(values))):
        return index
    result = jnp.int32(values[0])
    for number, value in enumerate(values[1:], 1):
        result = jnp.where(index == number, jnp.int32(value), result)
    return result


def middle_kernel(*refs, terms):
    term_refs, (image_ref, cos_ref, sin_ref, out_ref, mid_ref, resid_ref) = refs[:terms], refs[terms:]
    step = pl.program_id(0)
    _, band, crop_width = term_refs[0].shape
    block = cos_ref.shape[1]
    blocks = crop_width // block

    @pl.when(step == 0)
    def _():
        total = sum(ref[...].astype(jnp.float32) for ref in term_refs)
        mid_ref[...] = total.astype(jnp.bfloat16).reshape(2 * band, crop_width)

    def products(left):
        dot = functools.partial(jnp.dot, preferred_element_type=jnp.float32)
        return dot(left, cos_ref[...]), dot(left, sin_ref[...])

    @pl.when(step < blocks)
    def _():
        by_cos, by_sin = products(mid_ref[...])
        field_real = by_cos[:band] - by_sin[band:]
        field_imag = by_sin[:band] + by_cos[band:]
        power = field_real * field_real + field_imag * field_imag
        keeping = 1.0 - image_ref[0].astype(jnp.float32) * lax.rsqrt(jnp.maximum(power, 1.0))
        resid = jnp.concatenate([field_real * keeping, field_imag * keeping], axis=0)
        columns = pl.ds(pl.multiple_of(step * block, block), block)
        resid_ref[:, columns] = resid.astype(jnp.bfloat16)

    @pl.when(step >= blocks)
    def _():
        by_cos, by_sin = products(resid_ref[...])
        out_ref[0] = (by_cos[:band] + by_sin[band:]).astype(jnp.bfloat16)
        out_ref[1] = (by_cos[band:] - by_sin[:band]).astype(jnp.bfloat16)


def params():
    return pltpu.CompilerParams(vmem_limit_bytes=vmem_bytes)


def cost(count, win, band, moved):
    flops = 16 * count * win.tile_rows * band * win.crop_width
    return pl.CostEstimate(flops=flops, bytes_accessed=moved, transcendentals=0)


def forward(meta, spectrum, pupil, band_table, base, count, came=None):
    _, tile_rows, slab_columns = spectrum.shape
    crop_width = pupil.shape[1]
    band = band_table.shape[1] // 2
    win = Windows(tile_rows, slab_columns, crop_width)
    adding = came is not None

    def row(i, meta):
        return (win.row(meta[0, base + i]), 0)

    stacked = pl.BlockSpec((1, 2, band, crop_width), lambda i, meta: (i, 0, 0, 0))
    single = pl.BlockSpec((2, band, crop_width), lambda i, meta: (0, 0, 0))
    if adding:
        out_specs = [single] * count
        out_shape = [jax.ShapeDtypeStruct((2, band, crop_width), jnp.bfloat16)] * count
    else:
        out_specs = stacked
        out_shape = jax.ShapeDtypeStruct((count, 2, band, crop_width), jnp.bfloat16)
    return pl.pallas_call(
        functools.partial(forward_kernel, base=base, win=win, adding=adding),
        grid_spec=pltpu.PrefetchScalarGridSpec(
            num_scalar_prefetch=1,
            grid=(count,),
            in_specs=[
                pl.BlockSpec(
                    (pl.Element(2), pl.Element(tile_rows), pl.Element(win.columns)),
                    lambda i, meta: (0, 0, win.column(meta[1, base + i])),
                ),
                pl.BlockSpec((pl.Element(win.rows), pl.Element(crop_width)), row),
                pl.BlockSpec((pl.Element(win.rows), pl.Element(2 * band)), row),
            ]
            + [stacked] * adding,
            out_specs=out_specs,
        ),
        out_shape=out_shape,
        compiler_params=params(),
        cost_estimate=cost(count, win, band, count * 3000000),
        name="forward",
    )(meta, spectrum, pupil, band_table, *([came] if adding else []))


def backward(meta, spectrum, pupil, band_table, slots, backs):
    _, tile_rows, slab_columns = spectrum.shape
    crop_width = pupil.shape[1]
    band = band_table.shape[1] // 2
    win = Windows(tile_rows, slab_columns, crop_width)
    count = len(slots)

    def row(i, meta):
        return (win.row(meta[0, pick(slots, i)]), 0)

    return pl.pallas_call(
        functools.partial(backward_kernel, slots=slots, win=win),
        grid_spec=pltpu.PrefetchScalarGridSpec(
            num_scalar_prefetch=1,
            grid=(count,),
            in_specs=[
                pl.BlockSpec(
                    spectrum.shape, lambda i, meta: (0, 0, 0), pipeline_mode=pl.Buffered(1)
                ),
                pl.BlockSpec((pl.Element(win.rows), pl.Element(crop_width)), row),
                pl.BlockSpec((pl.Element(win.rows), pl.Element(2 * band)), row),
            ]
            + [pl.BlockSpec(memory_space=pl.ANY)] * len(backs),
            out_specs=pl.BlockSpec(spectrum.shape, lambda i, meta: (0, 0, 0)),
            scratch_shapes=[
                pltpu.VMEM((2, 2, band, crop_width), jnp.bfloat16),
                pltpu.SemaphoreType.DMA((2,)),
            ],
        ),
        out_shape=jax.ShapeDtypeStruct(spectrum.shape, jnp.float32),
        compiler_params=params(),
        cost_estimate=cost(count, win, band, count * 3000000 + 16 * 1024 * 1024),
        name="backward",
    )(meta, spectrum, pupil, band_table, *backs)


def middle(terms, image, cos_table, sin_table):
    _, band, crop_width = terms[0].shape
    block = min(256, crop_width)
    blocks = crop_width // block
    table = pl.BlockSpec((crop_width, block), lambda j: (0, j % blocks))
    whole = pl.BlockSpec((2, band, crop_width), lambda j: (0, 0, 0))
    return pl.pallas_call(
        functools.partial(middle_kernel, terms=len(terms)),
        grid=(2 * blocks,),
        in_specs=[whole] * len(terms)
        + [
            pl.BlockSpec((1, band, block), lambda j: (0, 0, jnp.minimum(j, blocks - 1))),
            table,
            table,
        ],
        out_specs=pl.BlockSpec((2, band, block), lambda j: (0, 0, jnp.maximum(j - blocks, 0))),
        out_shape=jax.ShapeDtypeStruct((2, band, crop_width), jnp.bfloat16),
        scratch_shapes=[pltpu.VMEM((2 * band, crop_width), jnp.bfloat16)] * 2,
        compiler_params=params(),
        cost_estimate=pl.CostEstimate(
            flops=16 * band * crop_width * crop_width,
            bytes_accessed=14 * band * crop_width * 2 + 8 * crop_width * crop_width,
            transcendentals=0,
        ),
        name="middle",
    )(*terms, image, cos_table, sin_table)


def total(*terms):
    return sum(term.astype(jnp.float32) for term in terms).astype(jnp.bfloat16)


def per_device(spectrum, pupil, measured, centre_rows, centre_cols):
    count = lax.axis_size("ty")
    planes = count // 4
    position = lax.axis_index("ty")
    plane = position // 4
    _, tile_rows, slab_columns = spectrum.shape
    crop_width = pupil.shape[0]
    band = measured.shape[1]
    band_start = (crop_width - band) // 2
    cos_table, sin_table = fourier_tables(crop_width)
    chosen_rows = slice(band_start, band_start + band)
    band_table = jnp.asarray(
        np.concatenate([cos_table[:, chosen_rows], sin_table[:, chosen_rows]], axis=1)
    )
    cos_table, sin_table = jnp.asarray(cos_table), jnp.asarray(sin_table)

    half = crop_width // 2

    def image_meta(ids):
        match = ids[:, None] == jnp.arange(count, dtype=jnp.int32)[None, :]
        tops = jnp.sum(jnp.where(match, centre_rows[None, :], 0), axis=1) - half
        lefts = jnp.sum(jnp.where(match, centre_cols[None, :], 0), axis=1) - half
        return jnp.stack([position * tile_rows - tops, lefts]).astype(jnp.int32)

    if planes != 4:
        meta = image_meta(jnp.arange(count, dtype=jnp.int32))
        partial = forward(meta, spectrum, pupil, band_table, 0, count)
        mid = lax.psum_scatter(partial, "ty", scatter_dimension=0, tiled=True)[0]
        back = lax.all_gather(middle([mid], measured, cos_table, sin_table), "ty")
        return backward(meta, spectrum, pupil, band_table, list(range(count)), [back])

    first = [(3, 2)]
    second = [(3, 0), (2, 2), (2, 0)]
    others = [(1, 2), (1, 0), (0, 2), (0, 0)]
    slots = {}
    for core in (1, 0):
        for j, y in first + second + others:
            slots[j, y + core] = len(slots)
    ids = [[((i // 4) ^ j) * 4 + (i % 4 ^ flip) for (j, flip) in slots] for i in range(count)]
    my_ids = lax.dynamic_index_in_dim(jnp.asarray(ids, jnp.int32), position, keepdims=False)
    meta = image_meta(my_ids)

    def sibling(value):
        return lax.ppermute(value, "ty", [(i, i ^ 1) for i in range(count)])

    def across(value):
        return lax.ppermute(value, "ty", [(i, i ^ 2) for i in range(count)])

    def along(value, plane_pairs):
        pairs = [(4 * a + i, 4 * b + i) for a, b in plane_pairs for i in range(4)]
        return lax.ppermute(value, "ty", pairs)

    swap_one = [(0, 1), (1, 0), (2, 3), (3, 2)]
    swap_two = [(0, 2), (1, 3), (2, 0), (3, 1)]
    swap_middle = [(1, 2), (2, 1)]

    def after(value, *earlier):
        return lax.optimization_barrier((value,) + earlier)[0]

    def theirs(group, known):
        j, y = group[0]
        return forward(known, spectrum, pupil, band_table, slots[j, y + 1], len(group))

    def mine(group, known, came=None):
        j, y = group[0]
        return forward(known, spectrum, pupil, band_table, slots[j, y], len(group), came)

    sent = theirs(first, meta)
    came_first = sibling(sent[0])
    known = after(meta, sent)
    own = mine(first, known)
    received = {3: across(total(own[0], came_first))}
    known = after(meta, own)
    sent = theirs(second, known)
    came_second = sibling(sent)
    known = after(meta, sent)
    sent = theirs(others, known)
    came_others = sibling(sent)
    known = after(meta, sent)
    kept = {}
    kept[3], leaving, kept[2] = mine(second, known, came_second)
    received[2] = across(leaving)
    known = after(meta, leaving)
    leaving_1, kept[1], leaving_0, kept[0] = mine(others, known, came_others)
    received[1] = across(leaving_1)
    received[0] = across(leaving_0)

    far = total(kept[3], received[3])
    far_from_end = along(far, [(0, 1), (3, 2)])
    far_from_middle = along(far, swap_middle)
    kept[2] = after(kept[2], leaving_1)
    two = along(total(kept[2], received[2], far_from_end), swap_two)
    one = along(total(kept[1], received[1]), swap_one)
    terms = [kept[0], received[0], one, far_from_middle, two]
    back = middle(terms, measured, cos_table, sin_table)

    def apply(result, pieces):
        names, values = zip(*pieces)
        return backward(
            meta, result, pupil, band_table, [slots[name] for name in names], list(values)
        )

    from_two = along(back, swap_two)
    from_one = along(back, swap_one)
    other = across(back)
    twin = sibling(back)
    from_one, other, twin = lax.optimization_barrier((from_one, other, twin))
    other_one = across(from_one)
    result = apply(
        spectrum, [((0, 0), back), ((0, 1), twin), ((1, 0), from_one), ((0, 2), other)]
    )
    from_one, other = lax.optimization_barrier((from_one, other, result))[:2]
    twin_one, twin_other = sibling(from_one), sibling(other)

    from_two, other_one, twin_one, twin_other, result, back = lax.optimization_barrier(
        (from_two, other_one, twin_one, twin_other, result, back)
    )
    from_end = along(from_two, [(1, 0), (2, 3)])
    from_middle = along(back, swap_middle)
    other_two = across(from_two)
    result = apply(
        result,
        [((1, 1), twin_one), ((0, 3), twin_other), ((2, 0), from_two), ((1, 2), other_one)],
    )
    from_two, other_one = lax.optimization_barrier((from_two, other_one, result))[:2]
    twin_two, twin_other = sibling(from_two), sibling(other_one)

    from_end, from_middle, other_two, twin_two, twin_other, result = lax.optimization_barrier(
        (from_end, from_middle, other_two, twin_two, twin_other, result)
    )
    from_three = jnp.where((plane == 0) | (plane == 3), from_end, from_middle)
    other_three = across(from_three)
    result = apply(
        result,
        [((2, 1), twin_two), ((1, 3), twin_other), ((3, 0), from_three), ((2, 2), other_two)],
    )
    from_three, other_two = lax.optimization_barrier((from_three, other_two, result))[:2]
    twin_three, twin_other = sibling(from_three), sibling(other_two)
    twin_last = sibling(other_three)
    return apply(
        result,
        [((3, 1), twin_three), ((2, 3), twin_other), ((3, 2), other_three), ((3, 3), twin_last)],
    )


def solution(mesh):
    return jax.shard_map(
        per_device,
        mesh=mesh,
        in_specs=(
            P(None, ("groups", "ty"), None),
            P(),
            P(("groups", "ty"), None, None),
            P("groups"),
            P("groups"),
        ),
        out_specs=P(None, ("groups", "ty"), None),
        check_vma=False,
    )
```

```python
import functools
import math

import jax
import jax.numpy as jnp
import numpy as np
from jax import lax
from jax.experimental import pallas as pl
from jax.experimental.pallas import tpu as pltpu
from jax.sharding import PartitionSpec as P

step_size = 0.5
lane = 128
row_tile = 16
vmem_bytes = 64 * 1024 * 1024 - 512 * 1024


def fourier_tables(crop_width):
    counter = np.arange(crop_width, dtype=np.int64)
    angle = (counter[:, None] * counter[None, :] % crop_width) * (2.0 * math.pi / crop_width)
    factor = 1.0 / math.sqrt(crop_width)
    cos_table = (np.cos(angle) * factor).astype(np.float32).astype(jnp.bfloat16)
    sin_table = (np.sin(angle) * factor).astype(np.float32).astype(jnp.bfloat16)
    return cos_table, sin_table


def tile_weight(pupil_ref, first_row, shift, tile_rows):
    window, crop_width = pupil_ref.shape
    rows = pltpu.roll(pupil_ref[...].astype(jnp.float32), (2 * window - shift) % window, 0)
    shape = (tile_rows, crop_width)
    row = 2 * (first_row + lax.broadcasted_iota(jnp.int32, shape, 0)) - crop_width + 1
    column = 2 * lax.broadcasted_iota(jnp.int32, shape, 1) - crop_width + 1
    inside = row * row + column * column <= crop_width * crop_width
    return jnp.where(inside, rows[:tile_rows], 0.0)


def tile_band(band_ref, shift, tile_rows):
    window, both = band_ref.shape
    rows = pltpu.roll(band_ref[...].astype(jnp.float32), (2 * window - shift) % window, 0)
    rows = rows[:tile_rows]
    turned = jnp.concatenate([-rows[:, both // 2 :], rows[:, : both // 2]], axis=1)
    return jnp.concatenate([rows, turned], axis=0).astype(jnp.bfloat16)


class Windows:
    def __init__(self, tile_rows, slab_columns, crop_width):
        self.tile_rows = tile_rows
        self.crop_width = crop_width
        self.rows = tile_rows + row_tile
        self.columns = crop_width + lane
        self.last_row = crop_width - self.rows
        self.last_column = slab_columns - self.columns

    def row(self, first_row):
        start = jnp.clip(first_row, 0, self.last_row) // row_tile * row_tile
        return pl.multiple_of(start, row_tile)

    def column(self, left):
        start = jnp.minimum(left // lane * lane, self.last_column)
        return pl.multiple_of(start, lane)

    def active(self, first_row):
        return (first_row > -self.tile_rows) & (first_row < self.crop_width)


def forward_kernel(meta_ref, *refs, base, win, halves):
    tiles, out_refs = refs[: 4 * halves], refs[4 * halves :]
    step = pl.program_id(0)
    slot = base + step
    left = meta_ref[halves, slot]
    first_rows = [meta_ref[half, slot] for half in range(halves)]
    active = functools.reduce(jnp.logical_or, [win.active(row) for row in first_rows])
    tile_rows, crop_width = win.tile_rows, win.crop_width
    shape = out_refs[0].shape

    def store(value):
        if len(out_refs) == 1:
            out_refs[0][...] = value.reshape(shape)
            return
        for number, out_ref in enumerate(out_refs):

            @pl.when(step == number)
            def _():
                out_ref[...] = value.reshape(shape)

    @pl.when(jnp.logical_not(active))
    def _():
        store(jnp.zeros(shape, jnp.bfloat16))

    @pl.when(active)
    def _():
        col_shift = left - win.column(left)
        parts, tables = [], []
        for half, first_row in enumerate(first_rows):
            real_ref, imag_ref, pupil_ref, band_ref = tiles[4 * half : 4 * half + 4]
            row_shift = first_row - win.row(first_row)
            weight = tile_weight(pupil_ref, first_row, row_shift, tile_rows)
            for part_ref in (real_ref, imag_ref):
                low = part_ref[...].astype(jnp.float32)
                low = pltpu.roll(low, (win.columns - col_shift) % win.columns, 1)
                parts.append((weight * low[:, :crop_width]).astype(jnp.bfloat16))
            tables.append(tile_band(band_ref, row_shift, tile_rows))
        mid = lax.dot_general(
            jnp.concatenate(tables, axis=0),
            jnp.concatenate(parts, axis=0),
            (((0,), (0,)), ((), ())),
            preferred_element_type=jnp.float32,
        )
        store(mid.astype(jnp.bfloat16))


def backward_kernel(meta_ref, spec_ref, pupil_ref, band_ref, *refs, slots, win):
    back_refs, (out_ref, held, sems) = refs[:-3], refs[-3:]
    stacked = len(back_refs) < len(slots)
    step = pl.program_id(0)
    count = len(slots)
    tile_rows, crop_width = win.tile_rows, win.crop_width

    def fetch(index, buffer):
        for number, back_ref in enumerate([] if stacked else back_refs):

            @pl.when(index == number)
            def _():
                pltpu.make_async_copy(back_ref, held.at[buffer], sems.at[buffer]).start()

        if stacked:
            source = back_refs[0].at[index]
            pltpu.make_async_copy(source, held.at[buffer], sems.at[buffer]).start()

    @pl.when(step == 0)
    def _():
        fetch(0, 0)
        out_ref[...] = spec_ref[...]

    @pl.when(step + 1 < count)
    def _():
        fetch(step + 1, (step + 1) % 2)

    buffer = step % 2
    sample = back_refs[0].at[0] if stacked else back_refs[0]
    pltpu.make_async_copy(sample, held.at[buffer], sems.at[buffer]).wait()
    slot = pick(slots, step)
    first_row, left = meta_ref[0, slot], meta_ref[meta_ref.shape[0] - 1, slot]

    @pl.when(win.active(first_row))
    def _():
        row_shift = first_row - win.row(first_row)
        col_start = win.column(left)
        weight = tile_weight(pupil_ref, first_row, row_shift, tile_rows) * step_size
        table = tile_band(band_ref, row_shift, tile_rows)
        back = held[buffer].reshape(table.shape[1], crop_width)
        grad = jnp.dot(table, back, preferred_element_type=jnp.float32)
        columns = pl.ds(col_start, win.columns)
        pad = jnp.zeros((tile_rows, win.columns - crop_width), jnp.float32)
        for part in range(2):
            piece = grad[part * tile_rows : (part + 1) * tile_rows] * weight
            piece = pltpu.roll(jnp.concatenate([piece, pad], axis=1), left - col_start, 1)
            out_ref[part, :, columns] = out_ref[part, :, columns] - piece


def pick(values, index):
    if list(values) == list(range(len(values))):
        return index
    result = jnp.int32(values[0])
    for number, value in enumerate(values[1:], 1):
        result = jnp.where(index == number, jnp.int32(value), result)
    return result


def middle_kernel(*refs, terms):
    term_refs, (image_ref, cos_ref, sin_ref, out_ref, mid_ref, resid_ref) = refs[:terms], refs[terms:]
    step = pl.program_id(0)
    _, band, crop_width = term_refs[0].shape
    block = cos_ref.shape[1]
    blocks = crop_width // block

    @pl.when(step == 0)
    def _():
        total = sum(ref[...].astype(jnp.float32) for ref in term_refs)
        mid_ref[...] = total.astype(jnp.bfloat16).reshape(2 * band, crop_width)

    def products(left):
        dot = functools.partial(jnp.dot, preferred_element_type=jnp.float32)
        return dot(left, cos_ref[...]), dot(left, sin_ref[...])

    @pl.when(step < blocks)
    def _():
        by_cos, by_sin = products(mid_ref[...])
        field_real = by_cos[:band] - by_sin[band:]
        field_imag = by_sin[:band] + by_cos[band:]
        power = field_real * field_real + field_imag * field_imag
        keeping = 1.0 - image_ref[0].astype(jnp.float32) * lax.rsqrt(jnp.maximum(power, 1.0))
        resid = jnp.concatenate([field_real * keeping, field_imag * keeping], axis=0)
        columns = pl.ds(pl.multiple_of(step * block, block), block)
        resid_ref[:, columns] = resid.astype(jnp.bfloat16)

    @pl.when(step >= blocks)
    def _():
        by_cos, by_sin = products(resid_ref[...])
        out_ref[0] = (by_cos[:band] + by_sin[band:]).astype(jnp.bfloat16)
        out_ref[1] = (by_cos[band:] - by_sin[:band]).astype(jnp.bfloat16)


def params():
    return pltpu.CompilerParams(vmem_limit_bytes=vmem_bytes)


def light():
    return pl.CostEstimate(flops=1024, bytes_accessed=1024, transcendentals=0)


def forward(meta, lows, pupil, band_table, base, count, stacked=False):
    tile_rows, slab_columns = lows[0][0].shape
    crop_width = pupil.shape[1]
    band = band_table.shape[1] // 2
    win = Windows(tile_rows, slab_columns, crop_width)
    halves = len(lows)

    def tile(i, meta):
        return (0, win.column(meta[halves, base + i]))

    in_specs, operands = [], []
    for half, (real, imag) in enumerate(lows):

        def row(i, meta, half=half):
            return (win.row(meta[half, base + i]), 0)

        part = pl.BlockSpec((pl.Element(tile_rows), pl.Element(win.columns)), tile)
        in_specs += [part, part]
        in_specs.append(pl.BlockSpec((pl.Element(win.rows), pl.Element(crop_width)), row))
        in_specs.append(pl.BlockSpec((pl.Element(win.rows), pl.Element(2 * band)), row))
        operands += [real, imag, pupil, band_table]
    if stacked:
        out_specs = pl.BlockSpec((1, 2, band, crop_width), lambda i, meta: (i, 0, 0, 0))
        out_shape = jax.ShapeDtypeStruct((count, 2, band, crop_width), jnp.bfloat16)
    else:
        single = pl.BlockSpec((2, band, crop_width), lambda i, meta: (0, 0, 0))
        out_specs = [single] * count
        out_shape = [jax.ShapeDtypeStruct((2, band, crop_width), jnp.bfloat16)] * count
    return pl.pallas_call(
        functools.partial(forward_kernel, base=base, win=win, halves=halves),
        grid_spec=pltpu.PrefetchScalarGridSpec(
            num_scalar_prefetch=1, grid=(count,), in_specs=in_specs, out_specs=out_specs
        ),
        out_shape=out_shape,
        compiler_params=params(),
        cost_estimate=light(),
        name="forward",
    )(meta, *operands)


def backward(meta, spectrum, pupil, band_table, slots, backs):
    _, tile_rows, slab_columns = spectrum.shape
    crop_width = pupil.shape[1]
    band = band_table.shape[1] // 2
    win = Windows(tile_rows, slab_columns, crop_width)
    count = len(slots)

    def row(i, meta):
        return (win.row(meta[0, pick(slots, i)]), 0)

    return pl.pallas_call(
        functools.partial(backward_kernel, slots=slots, win=win),
        grid_spec=pltpu.PrefetchScalarGridSpec(
            num_scalar_prefetch=1,
            grid=(count,),
            in_specs=[
                pl.BlockSpec(
                    spectrum.shape, lambda i, meta: (0, 0, 0), pipeline_mode=pl.Buffered(1)
                ),
                pl.BlockSpec((pl.Element(win.rows), pl.Element(crop_width)), row),
                pl.BlockSpec((pl.Element(win.rows), pl.Element(2 * band)), row),
            ]
            + [pl.BlockSpec(memory_space=pl.ANY)] * len(backs),
            out_specs=pl.BlockSpec(spectrum.shape, lambda i, meta: (0, 0, 0)),
            scratch_shapes=[
                pltpu.VMEM((2, 2, band, crop_width), jnp.bfloat16),
                pltpu.SemaphoreType.DMA((2,)),
            ],
        ),
        out_shape=jax.ShapeDtypeStruct(spectrum.shape, jnp.float32),
        compiler_params=params(),
        cost_estimate=light(),
        name="backward",
    )(meta, spectrum, pupil, band_table, *backs)


def middle(terms, image, cos_table, sin_table):
    _, band, crop_width = terms[0].shape
    block = min(256, crop_width)
    blocks = crop_width // block
    table = pl.BlockSpec((crop_width, block), lambda j: (0, j % blocks))
    whole = pl.BlockSpec((2, band, crop_width), lambda j: (0, 0, 0))
    return pl.pallas_call(
        functools.partial(middle_kernel, terms=len(terms)),
        grid=(2 * blocks,),
        in_specs=[whole] * len(terms)
        + [
            pl.BlockSpec((1, band, block), lambda j: (0, 0, jnp.minimum(j, blocks - 1))),
            table,
            table,
        ],
        out_specs=pl.BlockSpec((2, band, block), lambda j: (0, 0, jnp.maximum(j - blocks, 0))),
        out_shape=jax.ShapeDtypeStruct((2, band, crop_width), jnp.bfloat16),
        scratch_shapes=[pltpu.VMEM((2 * band, crop_width), jnp.bfloat16)] * 2,
        compiler_params=params(),
        cost_estimate=pl.CostEstimate(
            flops=16 * band * crop_width * crop_width,
            bytes_accessed=14 * band * crop_width * 2 + 8 * crop_width * crop_width,
            transcendentals=0,
        ),
        name="middle",
    )(*terms, image, cos_table, sin_table)


def total(*terms):
    return sum(term.astype(jnp.float32) for term in terms).astype(jnp.bfloat16)


def per_device(spectrum, pupil, measured, centre_rows, centre_cols):
    count = lax.axis_size("ty")
    planes = count // 4
    position = lax.axis_index("ty")
    plane = position // 4
    _, tile_rows, slab_columns = spectrum.shape
    crop_width = pupil.shape[0]
    band = measured.shape[1]
    band_start = (crop_width - band) // 2
    cos_table, sin_table = fourier_tables(crop_width)
    chosen_rows = slice(band_start, band_start + band)
    band_table = jnp.asarray(
        np.concatenate([cos_table[:, chosen_rows], sin_table[:, chosen_rows]], axis=1)
    )
    cos_table, sin_table = jnp.asarray(cos_table), jnp.asarray(sin_table)

    half = crop_width // 2

    lows = [[spectrum[part].astype(jnp.bfloat16) for part in range(2)]]

    def image_meta(ids, positions):
        match = ids[:, None] == jnp.arange(count, dtype=jnp.int32)[None, :]
        tops = jnp.sum(jnp.where(match, centre_rows[None, :], 0), axis=1) - half
        lefts = jnp.sum(jnp.where(match, centre_cols[None, :], 0), axis=1) - half
        rows = [place * tile_rows - tops for place in positions]
        return jnp.stack(rows + [lefts]).astype(jnp.int32)

    if planes != 4:
        meta = image_meta(jnp.arange(count, dtype=jnp.int32), [position])
        partial = forward(meta, lows, pupil, band_table, 0, count, stacked=True)
        mid = lax.psum_scatter(partial, "ty", scatter_dimension=0, tiled=True)[0]
        back = lax.all_gather(middle([mid], measured, cos_table, sin_table), "ty")
        return backward(meta, spectrum, pupil, band_table, list(range(count)), [back])

    own_core = [(3, 2), (3, 0), (2, 2), (2, 0), (1, 2), (1, 0), (0, 2), (0, 0)]
    slots = {}
    for core in (0, 1):
        for j, y in own_core:
            slots[j, y + core] = len(slots)
    ids = [[((i // 4) ^ j) * 4 + (i % 4 ^ flip) for (j, flip) in slots] for i in range(count)]
    my_ids = lax.dynamic_index_in_dim(jnp.asarray(ids, jnp.int32), position, keepdims=False)
    meta = image_meta(my_ids, [position, position ^ 1])

    def sibling(value):
        return lax.ppermute(value, "ty", [(i, i ^ 1) for i in range(count)])

    def across(value):
        return lax.ppermute(value, "ty", [(i, i ^ 2) for i in range(count)])

    def along(value, plane_pairs):
        pairs = [(4 * a + i, 4 * b + i) for a, b in plane_pairs for i in range(4)]
        return lax.ppermute(value, "ty", pairs)

    swap_one = [(0, 1), (1, 0), (2, 3), (3, 2)]
    swap_two = [(0, 2), (1, 3), (2, 0), (3, 1)]
    swap_middle = [(1, 2), (2, 1)]

    def after(value, *earlier):
        return lax.optimization_barrier((value,) + earlier)[0]

    together = lax.optimization_barrier

    lows.append([sibling(low) for low in lows[0]])
    (leaving_3,) = forward(meta, lows, pupil, band_table, 0, 1)
    far_other = across(leaving_3)
    kept_3, leaving_2, kept_2, leaving_1, kept_1, leaving_0, kept_0 = forward(
        after(meta, leaving_3), lows, pupil, band_table, 1, 7
    )
    far_other, leaving_2, kept_3, leaving_1 = together(
        (far_other, leaving_2, kept_3, leaving_1)
    )
    two_other = across(leaving_2)
    far = total(kept_3, far_other)
    far_from_end = along(far, [(0, 1), (3, 2)])
    far_from_middle = along(far, swap_middle)
    two_other, far_from_end, leaving_1 = together((two_other, far_from_end, leaving_1))
    one_other = across(leaving_1)
    two = along(total(kept_2, two_other, far_from_end), swap_two)
    one_other, far_from_middle, leaving_0 = together((one_other, far_from_middle, leaving_0))
    zero_other = across(leaving_0)
    one = along(total(kept_1, one_other), swap_one)
    terms = [kept_0, zero_other, one, far_from_middle, two]
    back = middle(terms, measured, cos_table, sin_table)

    def apply(result, pieces):
        names, values = zip(*pieces)
        return backward(
            meta, result, pupil, band_table, [slots[name] for name in names], list(values)
        )

    from_two = along(back, swap_two)
    from_one = along(back, swap_one)
    other = across(back)
    twin = sibling(back)
    from_one, other, twin, back = together((from_one, other, twin, back))

    other_one = across(from_one)
    twin_one, twin_other = sibling(from_one), sibling(other)
    result = apply(
        spectrum, [((0, 0), back), ((0, 1), twin), ((1, 0), from_one), ((0, 2), other)]
    )
    from_two, other_one, twin_one, twin_other, result, back = together(
        (from_two, other_one, twin_one, twin_other, result, back)
    )

    from_end = along(from_two, [(1, 0), (2, 3)])
    from_middle = along(back, swap_middle)
    other_two = across(from_two)
    twin_two, twin_other_one = sibling(from_two), sibling(other_one)
    result = apply(
        result,
        [((1, 1), twin_one), ((0, 3), twin_other), ((2, 0), from_two), ((1, 2), other_one)],
    )
    from_end, from_middle, other_two, twin_two, twin_other_one, result = together(
        (from_end, from_middle, other_two, twin_two, twin_other_one, result)
    )

    from_three = jnp.where((plane == 0) | (plane == 3), from_end, from_middle)
    other_three = across(from_three)
    twin_three, twin_other_two = sibling(from_three), sibling(other_two)
    result = apply(
        result,
        [((2, 1), twin_two), ((1, 3), twin_other_one), ((3, 0), from_three), ((2, 2), other_two)],
    )
    other_three, twin_three, twin_other_two, result = together(
        (other_three, twin_three, twin_other_two, result)
    )
    twin_last = sibling(other_three)
    return apply(
        result,
        [
            ((3, 1), twin_three),
            ((2, 3), twin_other_two),
            ((3, 2), other_three),
            ((3, 3), twin_last),
        ],
    )


def solution(mesh):
    return jax.shard_map(
        per_device,
        mesh=mesh,
        in_specs=(
            P(None, ("groups", "ty"), None),
            P(),
            P(("groups", "ty"), None, None),
            P("groups"),
            P("groups"),
        ),
        out_specs=P(None, ("groups", "ty"), None),
        check_vma=False,
    )
```

```python
import functools
import math

import jax
import jax.numpy as jnp
import numpy as np
from jax import lax
from jax.experimental import pallas as pl
from jax.experimental.pallas import tpu as pltpu
from jax.sharding import PartitionSpec as P

step_size = 0.5
lane = 128
row_tile = 16
vmem_bytes = 32 * 1024 * 1024


def fourier_tables(crop_width):
    counter = np.arange(crop_width, dtype=np.int64)
    angle = (counter[:, None] * counter[None, :] % crop_width) * (2.0 * math.pi / crop_width)
    factor = 1.0 / math.sqrt(crop_width)
    cos_table = (np.cos(angle) * factor).astype(np.float32).astype(jnp.bfloat16)
    sin_table = (np.sin(angle) * factor).astype(np.float32).astype(jnp.bfloat16)
    return cos_table, sin_table


def tile_weight(pupil_ref, first_row, win):
    start = win.row(first_row)
    rows = pupil_ref[pl.ds(start, win.rows), :].astype(jnp.float32)
    rows = pltpu.roll(rows, (2 * win.rows + start - first_row) % win.rows, 0)
    shape = (win.tile_rows, win.crop_width)
    row = 2 * (first_row + lax.broadcasted_iota(jnp.int32, shape, 0)) - win.crop_width + 1
    column = 2 * lax.broadcasted_iota(jnp.int32, shape, 1) - win.crop_width + 1
    inside = row * row + column * column <= win.crop_width * win.crop_width
    return jnp.where(inside, rows[: win.tile_rows], 0.0)


def tile_band(band_ref, first_row, win):
    start = win.row(first_row)
    rows = band_ref[pl.ds(start, win.rows), :].astype(jnp.float32)
    rows = pltpu.roll(rows, (2 * win.rows + start - first_row) % win.rows, 0)[: win.tile_rows]
    band = rows.shape[1] // 2
    turned = jnp.concatenate([-rows[:, band:], rows[:, :band]], axis=1)
    return jnp.concatenate([rows, turned], axis=0).astype(jnp.bfloat16)


class Windows:
    def __init__(self, tile_rows, slab_columns, crop_width):
        self.tile_rows = tile_rows
        self.crop_width = crop_width
        self.rows = tile_rows + row_tile
        self.columns = crop_width + lane
        self.last_row = crop_width - self.rows
        self.last_column = slab_columns - self.columns

    def row(self, first_row):
        start = jnp.clip(first_row, 0, self.last_row) // row_tile * row_tile
        return pl.multiple_of(start, row_tile)

    def column(self, left):
        start = jnp.minimum(left // lane * lane, self.last_column)
        return pl.multiple_of(start, lane)

    def active(self, first_row):
        return (first_row > -self.tile_rows) & (first_row < self.crop_width)


def image_band(meta_ref, slot, lows, pupil_ref, band_ref, win, store):
    halves = len(lows)
    left = meta_ref[halves, slot]
    first_rows = [meta_ref[half, slot] for half in range(halves)]
    active = functools.reduce(jnp.logical_or, [win.active(row) for row in first_rows])
    band = band_ref.shape[1] // 2
    shape = (2, band, win.crop_width)

    @pl.when(jnp.logical_not(active))
    def _():
        store(jnp.zeros(shape, jnp.bfloat16))

    @pl.when(active)
    def _():
        col_start = win.column(left)
        shift = (win.columns - (left - col_start)) % win.columns
        parts, tables = [], []
        for first_row, low_refs in zip(first_rows, lows):
            weight = tile_weight(pupil_ref, first_row, win)
            for low_ref in low_refs:
                low = low_ref[:, pl.ds(col_start, win.columns)].astype(jnp.float32)
                low = pltpu.roll(low, shift, 1)[:, : win.crop_width]
                parts.append((weight * low).astype(jnp.bfloat16))
            tables.append(tile_band(band_ref, first_row, win))
        mid = lax.dot_general(
            jnp.concatenate(tables, axis=0),
            jnp.concatenate(parts, axis=0),
            (((0,), (0,)), ((), ())),
            preferred_element_type=jnp.float32,
        )
        store(mid.astype(jnp.bfloat16).reshape(shape))


def forward_kernel(meta_ref, pupil_ref, band_ref, *refs, base, win, halves):
    low_refs, out_refs = refs[: 2 * halves], refs[2 * halves :]
    lows = [low_refs[2 * half : 2 * half + 2] for half in range(halves)]

    def image(index):
        def store(value):
            for number, out_ref in enumerate(out_refs):

                @pl.when(index == number)
                def _():
                    out_ref[...] = value

        image_band(meta_ref, base + index, lows, pupil_ref, band_ref, win, store)

    pl.loop(0, len(out_refs))(image)


def forward_grid_kernel(meta_ref, pupil_ref, band_ref, real_ref, imag_ref, out_ref, *, win):
    def store(value):
        out_ref[0] = value

    lows = [(real_ref, imag_ref)]
    image_band(meta_ref, pl.program_id(0), lows, pupil_ref, band_ref, win, store)


def subtract_image(meta_ref, slot, back_ref, pupil_ref, band_ref, out_ref, win):
    first_row, left = meta_ref[0, slot], meta_ref[meta_ref.shape[0] - 1, slot]
    tile_rows, crop_width = win.tile_rows, win.crop_width

    @pl.when(win.active(first_row))
    def _():
        col_start = win.column(left)
        weight = tile_weight(pupil_ref, first_row, win) * step_size
        table = tile_band(band_ref, first_row, win)
        back = back_ref[...].reshape(table.shape[1], crop_width)
        grad = jnp.dot(table, back, preferred_element_type=jnp.float32)
        columns = pl.ds(col_start, win.columns)
        pad = jnp.zeros((tile_rows, win.columns - crop_width), jnp.float32)
        for part in range(2):
            piece = grad[part * tile_rows : (part + 1) * tile_rows] * weight
            piece = pltpu.roll(jnp.concatenate([piece, pad], axis=1), left - col_start, 1)
            out_ref[part, :, columns] = out_ref[part, :, columns] - piece


def backward_kernel(meta_ref, pupil_ref, band_ref, spec_ref, *refs, slots, win):
    back_refs, out_ref = refs[:-1], refs[-1]
    out_ref[...] = spec_ref[...]
    for slot, back_ref in zip(slots, back_refs):
        subtract_image(meta_ref, slot, back_ref, pupil_ref, band_ref, out_ref, win)


def backward_grid_kernel(meta_ref, pupil_ref, band_ref, spec_ref, back_ref, out_ref, *, win):
    step = pl.program_id(0)

    @pl.when(step == 0)
    def _():
        out_ref[...] = spec_ref[...]

    subtract_image(meta_ref, step, back_ref, pupil_ref, band_ref, out_ref, win)


def middle_kernel(*refs, terms):
    term_refs, (image_ref, cos_ref, sin_ref, out_ref, mid_ref, resid_ref) = refs[:terms], refs[terms:]
    _, band, crop_width = term_refs[0].shape
    block = min(512, crop_width)
    total = sum(ref[...].astype(jnp.float32) for ref in term_refs)
    mid_ref[...] = total.astype(jnp.bfloat16).reshape(2 * band, crop_width)
    dot = functools.partial(jnp.dot, preferred_element_type=jnp.float32)
    for start in range(0, crop_width, block):
        columns = slice(start, start + block)
        by_cos = dot(mid_ref[...], cos_ref[:, columns])
        by_sin = dot(mid_ref[...], sin_ref[:, columns])
        field_real = by_cos[:band] - by_sin[band:]
        field_imag = by_sin[:band] + by_cos[band:]
        power = field_real * field_real + field_imag * field_imag
        measured = image_ref[0, :, columns].astype(jnp.float32)
        keeping = 1.0 - measured * lax.rsqrt(jnp.maximum(power, 1.0))
        resid_ref[:band, columns] = (field_real * keeping).astype(jnp.bfloat16)
        resid_ref[band:, columns] = (field_imag * keeping).astype(jnp.bfloat16)
    for start in range(0, crop_width, block):
        columns = slice(start, start + block)
        by_cos = dot(resid_ref[...], cos_ref[:, columns])
        by_sin = dot(resid_ref[...], sin_ref[:, columns])
        out_ref[0, :, columns] = (by_cos[:band] + by_sin[band:]).astype(jnp.bfloat16)
        out_ref[1, :, columns] = (by_cos[band:] - by_sin[:band]).astype(jnp.bfloat16)


def params():
    return pltpu.CompilerParams(vmem_limit_bytes=vmem_bytes)


def light():
    return pl.CostEstimate(flops=1024, bytes_accessed=1024, transcendentals=0)


vmem = pl.BlockSpec(memory_space=pltpu.VMEM)
smem = pl.BlockSpec(memory_space=pltpu.SMEM)


def band_type(pupil, band_table, *lead):
    shape = lead + (2, band_table.shape[1] // 2, pupil.shape[1])
    return jax.ShapeDtypeStruct(shape, jnp.bfloat16)


def forward(meta, lows, pupil, band_table, base, count):
    win = Windows(*lows[0][0].shape, pupil.shape[1])
    operands = [meta, pupil, band_table] + [part for low in lows for part in low]
    return pl.pallas_call(
        functools.partial(forward_kernel, base=base, win=win, halves=len(lows)),
        in_specs=[smem] + [vmem] * (len(operands) - 1),
        out_specs=[vmem] * count,
        out_shape=[band_type(pupil, band_table)] * count,
        compiler_params=params(),
        cost_estimate=light(),
        name="forward",
    )(*operands)


def backward(meta, spectrum, pupil, band_table, slots, backs):
    win = Windows(*spectrum.shape[1:], pupil.shape[1])
    return pl.pallas_call(
        functools.partial(backward_kernel, slots=slots, win=win),
        in_specs=[smem] + [vmem] * (3 + len(backs)),
        out_specs=vmem,
        out_shape=jax.ShapeDtypeStruct(spectrum.shape, jnp.float32),
        compiler_params=params(),
        cost_estimate=light(),
        name="backward",
    )(meta, pupil, band_table, spectrum, *backs)


def middle(terms, image, cos_table, sin_table):
    _, band, crop_width = terms[0].shape
    return pl.pallas_call(
        functools.partial(middle_kernel, terms=len(terms)),
        in_specs=[vmem] * (len(terms) + 3),
        out_specs=vmem,
        out_shape=jax.ShapeDtypeStruct((2, band, crop_width), jnp.bfloat16),
        scratch_shapes=[pltpu.VMEM((2 * band, crop_width), jnp.bfloat16)] * 2,
        compiler_params=params(),
        cost_estimate=light(),
        name="middle",
    )(*terms, image, cos_table, sin_table)


def fixed(array):
    return pl.BlockSpec(array.shape, lambda i: (0,) * array.ndim)


def forward_all(meta, low, pupil, band_table):
    win = Windows(*low[0].shape, pupil.shape[1])
    count = meta.shape[1]
    out_type = band_type(pupil, band_table, count)
    return pl.pallas_call(
        functools.partial(forward_grid_kernel, win=win),
        grid=(count,),
        in_specs=[smem] + [fixed(array) for array in (pupil, band_table, *low)],
        out_specs=pl.BlockSpec((1,) + out_type.shape[1:], lambda i: (i, 0, 0, 0)),
        out_shape=out_type,
        compiler_params=params(),
        name="forward_all",
    )(meta, pupil, band_table, *low)


def backward_all(meta, spectrum, pupil, band_table, backs):
    win = Windows(*spectrum.shape[1:], pupil.shape[1])
    return pl.pallas_call(
        functools.partial(backward_grid_kernel, win=win),
        grid=(meta.shape[1],),
        in_specs=[smem]
        + [fixed(array) for array in (pupil, band_table, spectrum)]
        + [pl.BlockSpec((1,) + backs.shape[1:], lambda i: (i, 0, 0, 0))],
        out_specs=fixed(spectrum),
        out_shape=jax.ShapeDtypeStruct(spectrum.shape, jnp.float32),
        compiler_params=params(),
        name="backward_all",
    )(meta, pupil, band_table, spectrum, backs)


def cast_kernel(spec_ref, out_ref):
    out_ref[...] = spec_ref[0].astype(jnp.bfloat16)


def low_part(spectrum, part):
    _, rows, columns = spectrum.shape
    block = columns // 4
    return pl.pallas_call(
        cast_kernel,
        grid=(4,),
        in_specs=[pl.BlockSpec((1, rows, block), lambda i: (part, 0, i))],
        out_specs=pl.BlockSpec((rows, block), lambda i: (0, i)),
        out_shape=jax.ShapeDtypeStruct((rows, columns), jnp.bfloat16),
        compiler_params=params(),
        cost_estimate=light(),
        name="low_part",
    )(spectrum)


def total(*terms):
    return sum(term.astype(jnp.float32) for term in terms).astype(jnp.bfloat16)


def per_device(spectrum, pupil, measured, centre_rows, centre_cols):
    count = lax.axis_size("ty")
    planes = count // 4
    position = lax.axis_index("ty")
    plane = position // 4
    _, tile_rows, slab_columns = spectrum.shape
    crop_width = pupil.shape[0]
    band = measured.shape[1]
    band_start = (crop_width - band) // 2
    cos_table, sin_table = fourier_tables(crop_width)
    chosen_rows = slice(band_start, band_start + band)
    band_table = jnp.asarray(
        np.concatenate([cos_table[:, chosen_rows], sin_table[:, chosen_rows]], axis=1)
    )
    cos_table, sin_table = jnp.asarray(cos_table), jnp.asarray(sin_table)

    half = crop_width // 2

    low = [low_part(spectrum, part) for part in range(2)]

    def image_meta(ids, positions):
        match = ids[:, None] == jnp.arange(count, dtype=jnp.int32)[None, :]
        tops = jnp.sum(jnp.where(match, centre_rows[None, :], 0), axis=1) - half
        lefts = jnp.sum(jnp.where(match, centre_cols[None, :], 0), axis=1) - half
        rows = [place * tile_rows - tops for place in positions]
        return jnp.stack(rows + [lefts]).astype(jnp.int32)

    if planes != 4:
        meta = image_meta(jnp.arange(count, dtype=jnp.int32), [position])
        partial = forward_all(meta, low, pupil, band_table)
        mid = lax.psum_scatter(partial, "ty", scatter_dimension=0, tiled=True)[0]
        back = lax.all_gather(middle([mid], measured, cos_table, sin_table), "ty")
        return backward_all(meta, spectrum, pupil, band_table, back)

    targets = {"far": (3, 3, 0, 0), "next": (2, 2, 1, 1), "beside": (1, 0, 3, 2), "own": (0, 1, 2, 3)}
    own_core = [("far", 2), ("far", 0), ("next", 2), ("next", 0)]
    own_core += [("beside", 2), ("beside", 0), ("own", 2), ("own", 0)]
    slots = {}
    for core in (0, 1):
        for name, y in own_core:
            slots[name, y + core] = len(slots)
    ids = [
        [targets[name][i // 4] * 4 + (i % 4 ^ flip) for (name, flip) in slots]
        for i in range(count)
    ]
    my_ids = lax.dynamic_index_in_dim(jnp.asarray(ids, jnp.int32), position, keepdims=False)
    meta = image_meta(my_ids, [position, position ^ 1])

    def sibling(value):
        return lax.ppermute(value, "ty", [(i, i ^ 1) for i in range(count)])

    def across(value):
        return lax.ppermute(value, "ty", [(i, i ^ 2) for i in range(count)])

    def along(value, plane_pairs):
        pairs = [(4 * a + i, 4 * b + i) for a, b in plane_pairs for i in range(4)]
        return lax.ppermute(value, "ty", pairs)

    inward = [(0, 1), (3, 2)]
    outward = [(1, 0), (2, 3)]
    inner = [(1, 2), (2, 1)]
    together = lax.optimization_barrier

    lows = [low, [sibling(part) for part in low]]
    (far_leaving,) = forward(meta, lows, pupil, band_table, 0, 1)
    far_other = across(far_leaving)
    (
        far_kept,
        next_leaving,
        next_kept,
        beside_leaving,
        beside_kept,
        own_leaving,
        own_kept,
    ) = forward(together((meta, far_leaving))[0], lows, pupil, band_table, 1, 7)
    far_other, far_kept, next_leaving = together((far_other, far_kept, next_leaving))

    from_end = along(total(far_kept, far_other), inward)
    next_other = across(next_leaving)
    from_end, next_other, beside_leaving = together((from_end, next_other, beside_leaving))

    far_inner = along(total(far_kept, far_other, from_end), inner)
    next_inward = along(total(next_kept, next_other), inward)
    beside_other = across(beside_leaving)
    far_inner, next_inward, beside_other, own_leaving = together(
        (far_inner, next_inward, beside_other, own_leaving)
    )

    next_inner = along(total(next_kept, next_other, next_inward), inner)
    beside = along(total(beside_kept, beside_other, far_inner), inward + outward)
    own_other = across(own_leaving)
    terms = [own_kept, own_other, next_inner, beside]
    back = middle(terms, measured, cos_table, sin_table)

    def apply(result, pieces):
        names, values = zip(*pieces)
        return backward(
            meta, result, pupil, band_table, [slots[name] for name in names], list(values)
        )

    from_beside = along(back, inward + outward)
    from_inner = along(back, inner)
    other = across(back)
    twin = sibling(back)
    from_beside, from_inner, other, twin, back = together(
        (from_beside, from_inner, other, twin, back)
    )

    far_inner = along(from_beside, inner)
    next_outward = along(from_inner, outward)
    beside_other = across(from_beside)
    beside_twin, other_twin = sibling(from_beside), sibling(other)
    result = apply(
        spectrum,
        [(("own", 0), back), (("own", 1), twin), (("beside", 0), from_beside), (("own", 2), other)],
    )
    far_inner, next_outward, beside_other, beside_twin, other_twin, result = together(
        (far_inner, next_outward, beside_other, beside_twin, other_twin, result)
    )

    at_ends = (plane == 0) | (plane == 3)
    far_outward = along(far_inner, outward)
    from_next = jnp.where(at_ends, next_outward, from_inner)
    next_other = across(from_next)
    next_twin, beside_other_twin = sibling(from_next), sibling(beside_other)
    result = apply(
        result,
        [
            (("beside", 1), beside_twin),
            (("own", 3), other_twin),
            (("next", 0), from_next),
            (("beside", 2), beside_other),
        ],
    )
    far_outward, next_other, next_twin, beside_other_twin, result = together(
        (far_outward, next_other, next_twin, beside_other_twin, result)
    )

    from_far = jnp.where(at_ends, far_outward, far_inner)
    far_other = across(from_far)
    far_twin, next_other_twin = sibling(from_far), sibling(next_other)
    result = apply(
        result,
        [
            (("next", 1), next_twin),
            (("beside", 3), beside_other_twin),
            (("far", 0), from_far),
            (("next", 2), next_other),
        ],
    )
    far_other, far_twin, next_other_twin, result = together(
        (far_other, far_twin, next_other_twin, result)
    )
    return apply(
        result,
        [
            (("far", 1), far_twin),
            (("next", 3), next_other_twin),
            (("far", 2), far_other),
            (("far", 3), sibling(far_other)),
        ],
    )


def solution(mesh):
    return jax.shard_map(
        per_device,
        mesh=mesh,
        in_specs=(
            P(None, ("groups", "ty"), None),
            P(),
            P(("groups", "ty"), None, None),
            P("groups"),
            P("groups"),
        ),
        out_specs=P(None, ("groups", "ty"), None),
        check_vma=False,
    )
```

```python
import functools
import math

import jax
import jax.numpy as jnp
import numpy as np
from jax import lax
from jax.experimental import pallas as pl
from jax.experimental.pallas import tpu as pltpu
from jax.sharding import PartitionSpec as P

step_size = 0.5
lane = 128
row_tile = 16
vmem_bytes = 32 * 1024 * 1024


def fourier_tables(crop_width):
    counter = np.arange(crop_width, dtype=np.int64)
    angle = (counter[:, None] * counter[None, :] % crop_width) * (2.0 * math.pi / crop_width)
    factor = 1.0 / math.sqrt(crop_width)
    cos_table = (np.cos(angle) * factor).astype(np.float32).astype(jnp.bfloat16)
    sin_table = (np.sin(angle) * factor).astype(np.float32).astype(jnp.bfloat16)
    return cos_table, sin_table


def tile_weight(pupil_ref, first_row, win):
    start = win.row(first_row)
    rows = pupil_ref[pl.ds(start, win.rows), :].astype(jnp.float32)
    rows = pltpu.roll(rows, (2 * win.rows + start - first_row) % win.rows, 0)
    shape = (win.tile_rows, win.crop_width)
    row = 2 * (first_row + lax.broadcasted_iota(jnp.int32, shape, 0)) - win.crop_width + 1
    column = 2 * lax.broadcasted_iota(jnp.int32, shape, 1) - win.crop_width + 1
    inside = row * row + column * column <= win.crop_width * win.crop_width
    return jnp.where(inside, rows[: win.tile_rows], 0.0)


def tile_band(band_refs, first_row, win):
    start = win.row(first_row)
    tables = []
    for band_ref in band_refs:
        rows = band_ref[pl.ds(start, win.rows), :].astype(jnp.float32)
        rows = pltpu.roll(rows, (2 * win.rows + start - first_row) % win.rows, 0)
        tables.append(rows[: win.tile_rows].astype(jnp.bfloat16))
    return jnp.concatenate(tables, axis=0)


class Windows:
    def __init__(self, tile_rows, slab_columns, crop_width, main, side):
        self.tile_rows = tile_rows
        self.crop_width = crop_width
        self.rows = tile_rows + row_tile
        self.columns = crop_width + lane
        self.last_row = crop_width - self.rows
        self.main = main
        self.side = side
        self.last_column = slab_columns - self.columns

    def row(self, first_row):
        start = jnp.clip(first_row, 0, self.last_row) // row_tile * row_tile
        return pl.multiple_of(start, row_tile)

    def column(self, left):
        start = jnp.minimum(left // lane * lane, self.last_column)
        return pl.multiple_of(start, lane)

    def active(self, first_row):
        return (first_row > -self.tile_rows) & (first_row < self.crop_width)


def image_band(meta_ref, slot, lows, pupil_ref, band_refs, win, store):
    halves = len(lows)
    left = meta_ref[halves, slot]
    first_rows = [meta_ref[half, slot] for half in range(halves)]
    active = functools.reduce(jnp.logical_or, [win.active(row) for row in first_rows])

    def split(band):
        main = band[: 2 * win.main].reshape(2, win.main, win.crop_width)
        store(main, band[2 * win.main :].reshape(2, win.side, win.crop_width))

    @pl.when(jnp.logical_not(active))
    def _():
        split(jnp.zeros((2 * (win.main + win.side), win.crop_width), jnp.bfloat16))

    @pl.when(active)
    def _():
        col_start = win.column(left)
        shift = (win.columns - (left - col_start)) % win.columns
        parts, tables = [], []
        for first_row, low_refs in zip(first_rows, lows):
            weight = tile_weight(pupil_ref, first_row, win)
            for low_ref in low_refs:
                low = low_ref[:, pl.ds(col_start, win.columns)].astype(jnp.float32)
                low = pltpu.roll(low, shift, 1)[:, : win.crop_width]
                parts.append((weight * low).astype(jnp.bfloat16))
            tables.append(tile_band(band_refs, first_row, win))
        mid = lax.dot_general(
            jnp.concatenate(tables, axis=0),
            jnp.concatenate(parts, axis=0),
            (((0,), (0,)), ((), ())),
            preferred_element_type=jnp.float32,
        )
        split(mid.astype(jnp.bfloat16))


def forward_kernel(meta_ref, pupil_ref, plain_ref, turned_ref, *refs, base, count, win, halves):
    low_refs, out_refs = refs[: 2 * halves], refs[-count - 1 :]
    lows = [low_refs[2 * half : 2 * half + 2] for half in range(halves)]
    main_refs, side_ref = out_refs[:-1], out_refs[-1]
    number_row = meta_ref.shape[0] - 1
    if base:
        side_ref[meta_ref[number_row, 0] // 2] = refs[2 * halves][...]

    def image(index):
        def store(main, side):
            for number, main_ref in enumerate(main_refs):

                @pl.when(index == number)
                def _():
                    main_ref[...] = main

            if base:
                side_ref[meta_ref[number_row, base + index] // 2] = side
            else:
                side_ref[...] = side

        bands = (plain_ref, turned_ref)
        image_band(meta_ref, base + index, lows, pupil_ref, bands, win, store)

    pl.loop(0, count)(image)


def forward_grid_kernel(
    meta_ref, pupil_ref, plain_ref, turned_ref, real_ref, imag_ref, main_ref, side_ref, *, win
):
    def store(main, side):
        main_ref[0] = main
        side_ref[0] = side

    lows, bands = [(real_ref, imag_ref)], (plain_ref, turned_ref)
    image_band(meta_ref, pl.program_id(0), lows, pupil_ref, bands, win, store)


def subtract_image(meta_ref, slot, main_ref, side, pupil_ref, band_refs, out_ref, win):
    first_row, left = meta_ref[0, slot], meta_ref[meta_ref.shape[0] - 2, slot]
    tile_rows, crop_width = win.tile_rows, win.crop_width

    @pl.when(win.active(first_row))
    def _():
        col_start = win.column(left)
        weight = tile_weight(pupil_ref, first_row, win) * step_size
        table = tile_band(band_refs, first_row, win)
        dot = functools.partial(jnp.dot, preferred_element_type=jnp.float32)
        terms = []
        if main_ref is not None:
            main = main_ref[...].reshape(2 * win.main, crop_width)
            terms.append(dot(table[:, : 2 * win.main], main))
        if side is not None:
            side_rows = side().reshape(2 * win.side, crop_width)
            terms.append(dot(table[:, 2 * win.main :], side_rows))
        grad = sum(terms)
        columns = pl.ds(col_start, win.columns)
        pad = jnp.zeros((tile_rows, win.columns - crop_width), jnp.float32)
        for part in range(2):
            piece = grad[part * tile_rows : (part + 1) * tile_rows] * weight
            piece = pltpu.roll(jnp.concatenate([piece, pad], axis=1), left - col_start, 1)
            out_ref[part, :, columns] = out_ref[part, :, columns] - piece


def backward_kernel(
    meta_ref, pupil_ref, plain_ref, turned_ref, spec_ref, *refs, slots, side_slots, win
):
    main_refs, out_ref = refs[: len(slots)], refs[-1]
    out_ref[...] = spec_ref[...]
    number_row = meta_ref.shape[0] - 1
    mains = dict(zip(slots, main_refs))
    for slot in list(slots) + [slot for slot in side_slots if slot not in mains]:
        side = None
        if slot in side_slots:
            side = functools.partial(lambda slot: refs[-2][meta_ref[number_row, slot]], slot)
        bands = (plain_ref, turned_ref)
        subtract_image(meta_ref, slot, mains.get(slot), side, pupil_ref, bands, out_ref, win)


def backward_grid_kernel(
    meta_ref, pupil_ref, plain_ref, turned_ref, spec_ref, main_ref, side_ref, out_ref, *, win
):
    step = pl.program_id(0)

    @pl.when(step == 0)
    def _():
        out_ref[...] = spec_ref[...]

    bands = (plain_ref, turned_ref)
    side = functools.partial(lambda: side_ref[0])
    subtract_image(meta_ref, step, main_ref, side, pupil_ref, bands, out_ref, win)


def middle_kernel(*refs, terms):
    main_refs, refs = refs[:terms], refs[terms:]
    side_ref, image_ref, cos_ref, sin_ref, main_out, side_out, mid_ref, resid_ref = refs
    _, main, crop_width = main_refs[0].shape
    band = main + side_ref.shape[1]
    block = min(512, crop_width)
    total = sum(ref[...].astype(jnp.float32) for ref in main_refs).astype(jnp.bfloat16)
    for part in range(2):
        mid_ref[part * band : part * band + main] = total[part]
        mid_ref[part * band + main : (part + 1) * band] = side_ref[part]
    dot = functools.partial(jnp.dot, preferred_element_type=jnp.float32)
    for start in range(0, crop_width, block):
        columns = slice(start, start + block)
        by_cos = dot(mid_ref[...], cos_ref[:, columns])
        by_sin = dot(mid_ref[...], sin_ref[:, columns])
        field_real = by_cos[:band] - by_sin[band:]
        field_imag = by_sin[:band] + by_cos[band:]
        power = field_real * field_real + field_imag * field_imag
        measured = image_ref[0, :, columns].astype(jnp.float32)
        keeping = 1.0 - measured * lax.rsqrt(jnp.maximum(power, 1.0))
        resid_ref[:band, columns] = (field_real * keeping).astype(jnp.bfloat16)
        resid_ref[band:, columns] = (field_imag * keeping).astype(jnp.bfloat16)
    for start in range(0, crop_width, block):
        columns = slice(start, start + block)
        by_cos = dot(resid_ref[...], cos_ref[:, columns])
        by_sin = dot(resid_ref[...], sin_ref[:, columns])
        for part, back in enumerate((by_cos[:band] + by_sin[band:], by_cos[band:] - by_sin[:band])):
            main_out[part, :, columns] = back[:main].astype(jnp.bfloat16)
            side_out[part, :, columns] = back[main:].astype(jnp.bfloat16)


def params():
    return pltpu.CompilerParams(vmem_limit_bytes=vmem_bytes)


def light():
    return pl.CostEstimate(flops=1024, bytes_accessed=1024, transcendentals=0)


vmem = pl.BlockSpec(memory_space=pltpu.VMEM)
smem = pl.BlockSpec(memory_space=pltpu.SMEM)


def side_rows(band):
    return band // 4


def band_type(rows, crop_width, *lead):
    return jax.ShapeDtypeStruct(lead + (2, rows, crop_width), jnp.bfloat16)


def windows(tile_shape, pupil, bands):
    band = bands[0].shape[1] // 2
    side = side_rows(band)
    return Windows(*tile_shape, pupil.shape[1], band - side, side)


def forward(meta, lows, pupil, bands, base, count, first_side=None):
    win = windows(lows[0][0].shape, pupil, bands)
    operands = [meta, pupil, *bands] + [part for low in lows for part in low]
    lead = ()
    if base:
        operands.append(first_side)
        lead = (base + count,)
    return pl.pallas_call(
        functools.partial(forward_kernel, base=base, count=count, win=win, halves=len(lows)),
        in_specs=[smem] + [vmem] * (len(operands) - 1),
        out_specs=[vmem] * (count + 1),
        out_shape=[band_type(win.main, win.crop_width)] * count
        + [band_type(win.side, win.crop_width, *lead)],
        compiler_params=params(),
        cost_estimate=light(),
        name="forward",
    )(*operands)


def backward(meta, spectrum, pupil, bands, slots, backs, side_slots=(), side=None):
    win = windows(spectrum.shape[1:], pupil, bands)
    operands = [meta, pupil, *bands, spectrum, *backs] + [side] * (side is not None)
    return pl.pallas_call(
        functools.partial(backward_kernel, slots=slots, side_slots=side_slots, win=win),
        in_specs=[smem] + [vmem] * (len(operands) - 1),
        out_specs=vmem,
        out_shape=jax.ShapeDtypeStruct(spectrum.shape, jnp.float32),
        compiler_params=params(),
        cost_estimate=light(),
        name="backward",
    )(*operands)


def middle(terms, side, image, cos_table, sin_table):
    _, main, crop_width = terms[0].shape
    band = image.shape[1]
    return pl.pallas_call(
        functools.partial(middle_kernel, terms=len(terms)),
        in_specs=[vmem] * (len(terms) + 4),
        out_specs=[vmem] * 2,
        out_shape=[band_type(main, crop_width), band_type(band - main, crop_width)],
        scratch_shapes=[pltpu.VMEM((2 * band, crop_width), jnp.bfloat16)] * 2,
        compiler_params=params(),
        cost_estimate=light(),
        name="middle",
    )(*terms, side, image, cos_table, sin_table)


def fixed(array):
    return pl.BlockSpec(array.shape, lambda i: (0,) * array.ndim)


def stepped(array):
    return pl.BlockSpec((1,) + array.shape[1:], lambda i: (i, 0, 0, 0))


def forward_all(meta, low, pupil, bands):
    win = windows(low[0].shape, pupil, bands)
    count = meta.shape[1]
    out_types = [band_type(rows, win.crop_width, count) for rows in (win.main, win.side)]
    return pl.pallas_call(
        functools.partial(forward_grid_kernel, win=win),
        grid=(count,),
        in_specs=[smem] + [fixed(array) for array in (pupil, *bands, *low)],
        out_specs=[stepped(out_type) for out_type in out_types],
        out_shape=out_types,
        compiler_params=params(),
        name="forward_all",
    )(meta, pupil, *bands, *low)


def backward_all(meta, spectrum, pupil, bands, backs):
    win = windows(spectrum.shape[1:], pupil, bands)
    main = pl.BlockSpec((None,) + backs[0].shape[1:], lambda i: (i, 0, 0, 0))
    return pl.pallas_call(
        functools.partial(backward_grid_kernel, win=win),
        grid=(meta.shape[1],),
        in_specs=[smem]
        + [fixed(array) for array in (pupil, *bands, spectrum)]
        + [main, stepped(backs[1])],
        out_specs=fixed(spectrum),
        out_shape=jax.ShapeDtypeStruct(spectrum.shape, jnp.float32),
        compiler_params=params(),
        name="backward_all",
    )(meta, pupil, *bands, spectrum, *backs)


def cast_kernel(spec_ref, out_ref):
    out_ref[...] = spec_ref[0].astype(jnp.bfloat16)


def low_part(spectrum, part):
    _, rows, columns = spectrum.shape
    block = columns // 4
    return pl.pallas_call(
        cast_kernel,
        grid=(4,),
        in_specs=[pl.BlockSpec((1, rows, block), lambda i: (part, 0, i))],
        out_specs=pl.BlockSpec((rows, block), lambda i: (0, i)),
        out_shape=jax.ShapeDtypeStruct((rows, columns), jnp.bfloat16),
        compiler_params=params(),
        cost_estimate=light(),
        name="low_part",
    )(spectrum)


def total(*terms):
    return sum(term.astype(jnp.float32) for term in terms).astype(jnp.bfloat16)


def per_device(spectrum, pupil, measured, centre_rows, centre_cols):
    count = lax.axis_size("ty")
    planes = count // 4
    position = lax.axis_index("ty")
    plane = position // 4
    _, tile_rows, slab_columns = spectrum.shape
    crop_width = pupil.shape[0]
    band = measured.shape[1]
    band_start = (crop_width - band) // 2
    cos_table, sin_table = fourier_tables(crop_width)
    split = band_start + band - side_rows(band)
    cuts = [slice(band_start, split), slice(split, band_start + band)]
    plain = [table[:, cut] for cut in cuts for table in (cos_table, sin_table)]
    turned = [table[:, cut] for cut in cuts for table in (-sin_table, cos_table)]
    bands = [jnp.asarray(np.concatenate(columns, axis=1)) for columns in (plain, turned)]
    cos_table, sin_table = jnp.asarray(cos_table), jnp.asarray(sin_table)

    half = crop_width // 2

    low = [low_part(spectrum, part) for part in range(2)]

    def image_meta(ids, positions):
        match = ids[:, None] == jnp.arange(count, dtype=jnp.int32)[None, :]
        tops = jnp.sum(jnp.where(match, centre_rows[None, :], 0), axis=1) - half
        lefts = jnp.sum(jnp.where(match, centre_cols[None, :], 0), axis=1) - half
        rows = [place * tile_rows - tops for place in positions]
        return jnp.stack(rows + [lefts, ids]).astype(jnp.int32)

    if planes != 4:
        meta = image_meta(jnp.arange(count, dtype=jnp.int32), [position])
        parts = forward_all(meta, low, pupil, bands)
        mid = [lax.psum_scatter(part, "ty", scatter_dimension=0, tiled=True)[0] for part in parts]
        backs = middle(mid[:1], mid[1], measured, cos_table, sin_table)
        backs = [lax.all_gather(back, "ty") for back in backs]
        return backward_all(meta, spectrum, pupil, bands, backs)

    targets = {"far": (3, 3, 0, 0), "next": (2, 2, 1, 1), "beside": (1, 0, 3, 2), "own": (0, 1, 2, 3)}
    own_core = [("far", 2), ("far", 0), ("next", 2), ("next", 0)]
    own_core += [("beside", 2), ("beside", 0), ("own", 2), ("own", 0)]
    slots = {}
    for core in (0, 1):
        for name, y in own_core:
            slots[name, y + core] = len(slots)
    ids = [
        [targets[name][i // 4] * 4 + (i % 4 ^ flip) for (name, flip) in slots]
        for i in range(count)
    ]
    my_ids = lax.dynamic_index_in_dim(jnp.asarray(ids, jnp.int32), position, keepdims=False)
    meta = image_meta(my_ids, [position, position ^ 1])

    def sibling(value):
        return lax.ppermute(value, "ty", [(i, i ^ 1) for i in range(count)])

    def across(value):
        return lax.ppermute(value, "ty", [(i, i ^ 2) for i in range(count)])

    def along(value, plane_pairs):
        pairs = [(4 * a + i, 4 * b + i) for a, b in plane_pairs for i in range(4)]
        return lax.ppermute(value, "ty", pairs)

    inward = [(0, 1), (3, 2)]
    outward = [(1, 0), (2, 3)]
    inner = [(1, 2), (2, 1)]
    together = lax.optimization_barrier

    lows = [low, [sibling(part) for part in low]]
    far_leaving, first_side = forward(meta, lows, pupil, bands, 0, 1)
    far_other = across(far_leaving)
    (
        far_kept,
        next_leaving,
        next_kept,
        beside_leaving,
        beside_kept,
        own_leaving,
        own_kept,
        sides,
    ) = forward(together((meta, far_leaving))[0], lows, pupil, bands, 1, 7, first_side)
    same_core = [list(range(core, count, 2)) for core in range(2)]
    side = lax.psum_scatter(
        sides, "ty", scatter_dimension=0, axis_index_groups=same_core, tiled=False
    )
    far_other, far_kept, next_leaving = together((far_other, far_kept, next_leaving))

    from_end = along(total(far_kept, far_other), inward)
    next_other = across(next_leaving)
    from_end, next_other, beside_leaving = together((from_end, next_other, beside_leaving))

    far_inner = along(total(far_kept, far_other, from_end), inner)
    next_inward = along(total(next_kept, next_other), inward)
    beside_other = across(beside_leaving)
    far_inner, next_inward, beside_other, own_leaving, side = together(
        (far_inner, next_inward, beside_other, own_leaving, side)
    )

    next_inner = along(total(next_kept, next_other, next_inward), inner)
    beside = along(total(beside_kept, beside_other, far_inner), inward + outward)
    own_other = across(own_leaving)
    terms = [own_kept, own_other, next_inner, beside]
    back, back_side = middle(terms, side, measured, cos_table, sin_table)
    gathered = lax.all_gather(back_side, "ty")
    all_sides = None

    def apply(result, pieces, more_sides=()):
        names, values = zip(*pieces)
        own_slots = [slots[name] for name in names]
        if all_sides is None:
            return backward(meta, result, pupil, bands, own_slots, values)
        side_slots = own_slots + [slots[name] for name in more_sides]
        return backward(meta, result, pupil, bands, own_slots, values, side_slots, all_sides)

    from_beside = along(back, inward + outward)
    from_inner = along(back, inner)
    other = across(back)
    twin = sibling(back)
    from_beside, from_inner, other, twin, back = together(
        (from_beside, from_inner, other, twin, back)
    )

    far_inner = along(from_beside, inner)
    next_outward = along(from_inner, outward)
    beside_other = across(from_beside)
    beside_twin, other_twin = sibling(from_beside), sibling(other)
    result = apply(
        spectrum,
        [(("own", 0), back), (("own", 1), twin), (("beside", 0), from_beside), (("own", 2), other)],
    )
    far_inner, next_outward, beside_other, beside_twin, other_twin, result, all_sides = together(
        (far_inner, next_outward, beside_other, beside_twin, other_twin, result, gathered)
    )

    at_ends = (plane == 0) | (plane == 3)
    far_outward = along(far_inner, outward)
    from_next = jnp.where(at_ends, next_outward, from_inner)
    next_other = across(from_next)
    next_twin, beside_other_twin = sibling(from_next), sibling(beside_other)
    result = apply(
        result,
        [
            (("beside", 1), beside_twin),
            (("own", 3), other_twin),
            (("next", 0), from_next),
            (("beside", 2), beside_other),
        ],
        [("own", 0), ("own", 1), ("beside", 0), ("own", 2)],
    )
    far_outward, next_other, next_twin, beside_other_twin, result = together(
        (far_outward, next_other, next_twin, beside_other_twin, result)
    )

    from_far = jnp.where(at_ends, far_outward, far_inner)
    far_other = across(from_far)
    far_twin, next_other_twin = sibling(from_far), sibling(next_other)
    result = apply(
        result,
        [
            (("next", 1), next_twin),
            (("beside", 3), beside_other_twin),
            (("far", 0), from_far),
            (("next", 2), next_other),
        ],
    )
    far_other, far_twin, next_other_twin, result = together(
        (far_other, far_twin, next_other_twin, result)
    )
    return apply(
        result,
        [
            (("far", 1), far_twin),
            (("next", 3), next_other_twin),
            (("far", 2), far_other),
            (("far", 3), sibling(far_other)),
        ],
    )


def solution(mesh):
    return jax.shard_map(
        per_device,
        mesh=mesh,
        in_specs=(
            P(None, ("groups", "ty"), None),
            P(),
            P(("groups", "ty"), None, None),
            P("groups"),
            P("groups"),
        ),
        out_specs=P(None, ("groups", "ty"), None),
        check_vma=False,
    )
```

```python
import functools
import math

import jax
import jax.numpy as jnp
import numpy as np
from jax import lax
from jax.experimental import pallas as pl
from jax.experimental.pallas import tpu as pltpu
from jax.sharding import PartitionSpec as P

step_size = 0.5
lane = 128
row_tile = 16
vmem_bytes = 32 * 1024 * 1024


def fourier_tables(crop_width):
    counter = np.arange(crop_width, dtype=np.int64)
    angle = (counter[:, None] * counter[None, :] % crop_width) * (2.0 * math.pi / crop_width)
    factor = 1.0 / math.sqrt(crop_width)
    cos_table = (np.cos(angle) * factor).astype(np.float32).astype(jnp.bfloat16)
    sin_table = (np.sin(angle) * factor).astype(np.float32).astype(jnp.bfloat16)
    return cos_table, sin_table


def tile_weight(pupil_ref, first_row, win):
    start = win.row(first_row)
    rows = pupil_ref[pl.ds(start, win.rows), :].astype(jnp.float32)
    rows = pltpu.roll(rows, (2 * win.rows + start - first_row) % win.rows, 0)
    shape = (win.tile_rows, win.crop_width)
    row = 2 * (first_row + lax.broadcasted_iota(jnp.int32, shape, 0)) - win.crop_width + 1
    column = 2 * lax.broadcasted_iota(jnp.int32, shape, 1) - win.crop_width + 1
    inside = row * row + column * column <= win.crop_width * win.crop_width
    return jnp.where(inside, rows[: win.tile_rows], 0.0)


def tile_band(band_ref, first_row, win):
    start = win.row(first_row)
    rows = band_ref[pl.ds(start, win.rows), :].astype(jnp.float32)
    rows = pltpu.roll(rows, (2 * win.rows + start - first_row) % win.rows, 0)[: win.tile_rows]
    band = rows.shape[1] // 2
    turned = jnp.concatenate([-rows[:, band:], rows[:, :band]], axis=1)
    return jnp.concatenate([rows, turned], axis=0).astype(jnp.bfloat16)


class Windows:
    def __init__(self, tile_rows, slab_columns, crop_width):
        self.tile_rows = tile_rows
        self.crop_width = crop_width
        self.rows = tile_rows + row_tile
        self.columns = crop_width + lane
        self.last_row = crop_width - self.rows
        self.last_column = slab_columns - self.columns

    def row(self, first_row):
        start = jnp.clip(first_row, 0, self.last_row) // row_tile * row_tile
        return pl.multiple_of(start, row_tile)

    def column(self, left):
        start = jnp.minimum(left // lane * lane, self.last_column)
        return pl.multiple_of(start, lane)

    def active(self, first_row):
        return (first_row > -self.tile_rows) & (first_row < self.crop_width)


def image_band(meta_ref, slot, lows, tiles, pupil_ref, band_ref, win, store, came=None):
    left = meta_ref[meta_ref.shape[0] - 1, slot]
    first_rows = [meta_ref[tile, slot] for tile in tiles]
    active = functools.reduce(jnp.logical_or, [win.active(row) for row in first_rows])
    band = band_ref.shape[1] // 2
    shape = (2, band, win.crop_width)

    @pl.when(jnp.logical_not(active))
    def _():
        store(jnp.zeros(shape, jnp.bfloat16) if came is None else came[...])

    @pl.when(active)
    def _():
        col_start = win.column(left)
        shift = (win.columns - (left - col_start)) % win.columns
        parts, tables = [], []
        for first_row, low_refs in zip(first_rows, lows):
            weight = tile_weight(pupil_ref, first_row, win)
            for low_ref in low_refs:
                low = low_ref[:, pl.ds(col_start, win.columns)].astype(jnp.float32)
                low = pltpu.roll(low, shift, 1)[:, : win.crop_width]
                parts.append((weight * low).astype(jnp.bfloat16))
            tables.append(tile_band(band_ref, first_row, win))
        mid = lax.dot_general(
            jnp.concatenate(tables, axis=0),
            jnp.concatenate(parts, axis=0),
            (((0,), (0,)), ((), ())),
            preferred_element_type=jnp.float32,
        )
        if came is not None:
            mid = mid + came[...].reshape(mid.shape).astype(jnp.float32)
        store(mid.astype(jnp.bfloat16).reshape(shape))


def forward_kernel(meta_ref, pupil_ref, band_ref, *refs, base, count, win, tiles):
    out_refs = refs[-count:]
    lows = [refs[2 * half : 2 * half + 2] for half in range(len(tiles))]
    came = refs[2 * len(tiles)] if len(refs) > 2 * len(tiles) + count else None

    def image(index):
        def store(value):
            for number, out_ref in enumerate(out_refs):

                @pl.when(index == number)
                def _():
                    out_ref[...] = value

        image_band(meta_ref, base + index, lows, tiles, pupil_ref, band_ref, win, store, came)

    pl.loop(0, len(out_refs))(image)


def forward_grid_kernel(meta_ref, pupil_ref, band_ref, real_ref, imag_ref, out_ref, *, win):
    def store(value):
        out_ref[0] = value

    lows = [(real_ref, imag_ref)]
    image_band(meta_ref, pl.program_id(0), lows, (0,), pupil_ref, band_ref, win, store)


def subtract_image(meta_ref, slot, back_ref, pupil_ref, band_ref, out_ref, win):
    first_row, left = meta_ref[0, slot], meta_ref[meta_ref.shape[0] - 1, slot]
    tile_rows, crop_width = win.tile_rows, win.crop_width

    @pl.when(win.active(first_row))
    def _():
        col_start = win.column(left)
        weight = tile_weight(pupil_ref, first_row, win) * step_size
        table = tile_band(band_ref, first_row, win)
        back = back_ref[...].reshape(table.shape[1], crop_width)
        grad = jnp.dot(table, back, preferred_element_type=jnp.float32)
        columns = pl.ds(col_start, win.columns)
        pad = jnp.zeros((tile_rows, win.columns - crop_width), jnp.float32)
        for part in range(2):
            piece = grad[part * tile_rows : (part + 1) * tile_rows] * weight
            piece = pltpu.roll(jnp.concatenate([piece, pad], axis=1), left - col_start, 1)
            out_ref[part, :, columns] = out_ref[part, :, columns] - piece


def backward_kernel(meta_ref, pupil_ref, band_ref, spec_ref, *refs, slots, win):
    back_refs, out_ref = refs[:-1], refs[-1]
    out_ref[...] = spec_ref[...]
    for slot, back_ref in zip(slots, back_refs):
        subtract_image(meta_ref, slot, back_ref, pupil_ref, band_ref, out_ref, win)


def backward_grid_kernel(meta_ref, pupil_ref, band_ref, spec_ref, back_ref, out_ref, *, win):
    step = pl.program_id(0)

    @pl.when(step == 0)
    def _():
        out_ref[...] = spec_ref[...]

    subtract_image(meta_ref, step, back_ref, pupil_ref, band_ref, out_ref, win)


def middle_kernel(*refs, terms):
    term_refs, (image_ref, cos_ref, sin_ref, out_ref, mid_ref, resid_ref) = refs[:terms], refs[terms:]
    _, band, crop_width = term_refs[0].shape
    block = min(512, crop_width)
    total = sum(ref[...].astype(jnp.float32) for ref in term_refs)
    mid_ref[...] = total.astype(jnp.bfloat16).reshape(2 * band, crop_width)
    dot = functools.partial(jnp.dot, preferred_element_type=jnp.float32)
    for start in range(0, crop_width, block):
        columns = slice(start, start + block)
        by_cos = dot(mid_ref[...], cos_ref[:, columns])
        by_sin = dot(mid_ref[...], sin_ref[:, columns])
        field_real = by_cos[:band] - by_sin[band:]
        field_imag = by_sin[:band] + by_cos[band:]
        power = field_real * field_real + field_imag * field_imag
        measured = image_ref[0, :, columns].astype(jnp.float32)
        keeping = 1.0 - measured * lax.rsqrt(jnp.maximum(power, 1.0))
        resid_ref[:band, columns] = (field_real * keeping).astype(jnp.bfloat16)
        resid_ref[band:, columns] = (field_imag * keeping).astype(jnp.bfloat16)
    for start in range(0, crop_width, block):
        columns = slice(start, start + block)
        by_cos = dot(resid_ref[...], cos_ref[:, columns])
        by_sin = dot(resid_ref[...], sin_ref[:, columns])
        out_ref[0, :, columns] = (by_cos[:band] + by_sin[band:]).astype(jnp.bfloat16)
        out_ref[1, :, columns] = (by_cos[band:] - by_sin[:band]).astype(jnp.bfloat16)


def params():
    return pltpu.CompilerParams(vmem_limit_bytes=vmem_bytes)


def light():
    return pl.CostEstimate(flops=1024, bytes_accessed=1024, transcendentals=0)


vmem = pl.BlockSpec(memory_space=pltpu.VMEM)
smem = pl.BlockSpec(memory_space=pltpu.SMEM)


def band_type(pupil, band_table, *lead):
    shape = lead + (2, band_table.shape[1] // 2, pupil.shape[1])
    return jax.ShapeDtypeStruct(shape, jnp.bfloat16)


def forward(meta, lows, pupil, band_table, base, count, tiles=(0, 1), came=None):
    win = Windows(*lows[0][0].shape, pupil.shape[1])
    operands = [meta, pupil, band_table] + [part for low in lows for part in low]
    operands += [came] * (came is not None)
    return pl.pallas_call(
        functools.partial(forward_kernel, base=base, count=count, win=win, tiles=tiles),
        in_specs=[smem] + [vmem] * (len(operands) - 1),
        out_specs=[vmem] * count,
        out_shape=[band_type(pupil, band_table)] * count,
        compiler_params=params(),
        cost_estimate=light(),
        name="forward",
    )(*operands)


def backward(meta, spectrum, pupil, band_table, slots, backs):
    win = Windows(*spectrum.shape[1:], pupil.shape[1])
    return pl.pallas_call(
        functools.partial(backward_kernel, slots=slots, win=win),
        in_specs=[smem] + [vmem] * (3 + len(backs)),
        out_specs=vmem,
        out_shape=jax.ShapeDtypeStruct(spectrum.shape, jnp.float32),
        compiler_params=params(),
        cost_estimate=light(),
        name="backward",
    )(meta, pupil, band_table, spectrum, *backs)


def middle(terms, image, cos_table, sin_table):
    _, band, crop_width = terms[0].shape
    return pl.pallas_call(
        functools.partial(middle_kernel, terms=len(terms)),
        in_specs=[vmem] * (len(terms) + 3),
        out_specs=vmem,
        out_shape=jax.ShapeDtypeStruct((2, band, crop_width), jnp.bfloat16),
        scratch_shapes=[pltpu.VMEM((2 * band, crop_width), jnp.bfloat16)] * 2,
        compiler_params=params(),
        cost_estimate=light(),
        name="middle",
    )(*terms, image, cos_table, sin_table)


def fixed(array):
    return pl.BlockSpec(array.shape, lambda i: (0,) * array.ndim)


def forward_all(meta, low, pupil, band_table):
    win = Windows(*low[0].shape, pupil.shape[1])
    count = meta.shape[1]
    out_type = band_type(pupil, band_table, count)
    return pl.pallas_call(
        functools.partial(forward_grid_kernel, win=win),
        grid=(count,),
        in_specs=[smem] + [fixed(array) for array in (pupil, band_table, *low)],
        out_specs=pl.BlockSpec((1,) + out_type.shape[1:], lambda i: (i, 0, 0, 0)),
        out_shape=out_type,
        compiler_params=params(),
        name="forward_all",
    )(meta, pupil, band_table, *low)


def backward_all(meta, spectrum, pupil, band_table, backs):
    win = Windows(*spectrum.shape[1:], pupil.shape[1])
    return pl.pallas_call(
        functools.partial(backward_grid_kernel, win=win),
        grid=(meta.shape[1],),
        in_specs=[smem]
        + [fixed(array) for array in (pupil, band_table, spectrum)]
        + [pl.BlockSpec((1,) + backs.shape[1:], lambda i: (i, 0, 0, 0))],
        out_specs=fixed(spectrum),
        out_shape=jax.ShapeDtypeStruct(spectrum.shape, jnp.float32),
        compiler_params=params(),
        name="backward_all",
    )(meta, pupil, band_table, spectrum, backs)


def cast_kernel(spec_ref, out_ref, held, sems, *, part):
    blocks, _, width = held.shape
    columns = [pl.ds(block * width, width) for block in range(blocks)]
    copies = [
        pltpu.make_async_copy(spec_ref.at[part, :, columns[i]], held.at[i], sems.at[i])
        for i in range(blocks)
    ]
    for copy in copies:
        copy.start()
    for i, copy in enumerate(copies):
        copy.wait()
        out_ref[:, columns[i]] = held[i].astype(jnp.bfloat16)


def low_part(spectrum, part):
    _, rows, columns = spectrum.shape
    return pl.pallas_call(
        functools.partial(cast_kernel, part=part),
        in_specs=[pl.BlockSpec(memory_space=pltpu.HBM)],
        out_specs=vmem,
        out_shape=jax.ShapeDtypeStruct((rows, columns), jnp.bfloat16),
        scratch_shapes=[
            pltpu.VMEM((4, rows, columns // 4), jnp.float32),
            pltpu.SemaphoreType.DMA((4,)),
        ],
        compiler_params=params(),
        cost_estimate=light(),
        name="low_part",
    )(spectrum)


def total(*terms):
    return sum(term.astype(jnp.float32) for term in terms).astype(jnp.bfloat16)


def per_device(spectrum, pupil, measured, centre_rows, centre_cols):
    count = lax.axis_size("ty")
    planes = count // 4
    position = lax.axis_index("ty")
    plane = position // 4
    _, tile_rows, slab_columns = spectrum.shape
    crop_width = pupil.shape[0]
    band = measured.shape[1]
    band_start = (crop_width - band) // 2
    cos_table, sin_table = fourier_tables(crop_width)
    chosen_rows = slice(band_start, band_start + band)
    band_table = jnp.asarray(
        np.concatenate([cos_table[:, chosen_rows], sin_table[:, chosen_rows]], axis=1)
    )
    cos_table, sin_table = jnp.asarray(cos_table), jnp.asarray(sin_table)

    half = crop_width // 2

    low = [low_part(spectrum, part) for part in range(2)]

    def image_meta(ids, positions):
        match = ids[:, None] == jnp.arange(count, dtype=jnp.int32)[None, :]
        tops = jnp.sum(jnp.where(match, centre_rows[None, :], 0), axis=1) - half
        lefts = jnp.sum(jnp.where(match, centre_cols[None, :], 0), axis=1) - half
        rows = [place * tile_rows - tops for place in positions]
        return jnp.stack(rows + [lefts]).astype(jnp.int32)

    if planes != 4:
        meta = image_meta(jnp.arange(count, dtype=jnp.int32), [position])
        partial = forward_all(meta, low, pupil, band_table)
        mid = lax.psum_scatter(partial, "ty", scatter_dimension=0, tiled=True)[0]
        back = lax.all_gather(middle([mid], measured, cos_table, sin_table), "ty")
        return backward_all(meta, spectrum, pupil, band_table, back)

    targets = {"far": (3, 3, 0, 0), "next": (2, 2, 1, 1), "beside": (1, 0, 3, 2), "own": (0, 1, 2, 3)}
    own_core = [("far", 2), ("far", 0), ("next", 2), ("next", 0)]
    own_core += [("beside", 2), ("beside", 0), ("own", 2), ("own", 0)]
    slots = {}
    for core in (0, 1):
        for name, y in own_core:
            slots[name, y + core] = len(slots)
    ids = [
        [targets[name][i // 4] * 4 + (i % 4 ^ flip) for (name, flip) in slots]
        for i in range(count)
    ]
    my_ids = lax.dynamic_index_in_dim(jnp.asarray(ids, jnp.int32), position, keepdims=False)
    meta = image_meta(my_ids, [position, position ^ 1])

    def sibling(value):
        return lax.ppermute(value, "ty", [(i, i ^ 1) for i in range(count)])

    def across(value):
        return lax.ppermute(value, "ty", [(i, i ^ 2) for i in range(count)])

    def along(value, plane_pairs):
        pairs = [(4 * a + i, 4 * b + i) for a, b in plane_pairs for i in range(4)]
        return lax.ppermute(value, "ty", pairs)

    inward = [(0, 1), (3, 2)]
    outward = [(1, 0), (2, 3)]
    inner = [(1, 2), (2, 1)]
    together = lax.optimization_barrier

    lows = [low, [sibling(part) for part in low]]
    (far_leaving,) = forward(meta, lows[:1], pupil, band_table, 0, 1, (0,))
    (far_leaving,) = forward(meta, lows[1:], pupil, band_table, 0, 1, (1,), far_leaving)
    far_other = across(far_leaving)
    (
        far_kept,
        next_leaving,
        next_kept,
        beside_leaving,
        beside_kept,
        own_leaving,
        own_kept,
    ) = forward(together((meta, far_leaving))[0], lows, pupil, band_table, 1, 7)
    far_other, far_kept, next_leaving = together((far_other, far_kept, next_leaving))

    from_end = along(total(far_kept, far_other), inward)
    next_other = across(next_leaving)
    from_end, next_other, beside_leaving = together((from_end, next_other, beside_leaving))

    far_inner = along(total(far_kept, far_other, from_end), inner)
    next_inward = along(total(next_kept, next_other), inward)
    beside_other = across(beside_leaving)
    far_inner, next_inward, beside_other, own_leaving = together(
        (far_inner, next_inward, beside_other, own_leaving)
    )

    next_inner = along(total(next_kept, next_other, next_inward), inner)
    beside = along(total(beside_kept, beside_other, far_inner), inward + outward)
    own_other = across(own_leaving)
    terms = [own_kept, own_other, next_inner, beside]
    back = middle(terms, measured, cos_table, sin_table)

    def apply(result, pieces):
        names, values = zip(*pieces)
        return backward(
            meta, result, pupil, band_table, [slots[name] for name in names], list(values)
        )

    other = across(back)
    from_inner = along(back, inner)
    from_beside = along(back, inward + outward)
    other, from_inner, from_beside, back = together((other, from_inner, from_beside, back))

    twin, beside_twin = sibling(back), sibling(from_beside)
    beside_other = across(from_beside)
    far_inner = along(from_beside, inner)
    next_outward = along(from_inner, outward)
    result = apply(
        spectrum, [(("own", 0), back), (("beside", 0), from_beside), (("own", 2), other)]
    )
    twin, beside_twin, beside_other, far_inner, next_outward, other, result = together(
        (twin, beside_twin, beside_other, far_inner, next_outward, other, result)
    )

    at_ends = (plane == 0) | (plane == 3)
    from_next = jnp.where(at_ends, next_outward, from_inner)
    other_twin, next_twin = sibling(other), sibling(from_next)
    next_other = across(from_next)
    far_outward = along(far_inner, outward)
    result = apply(
        result,
        [
            (("own", 1), twin),
            (("beside", 1), beside_twin),
            (("next", 0), from_next),
            (("beside", 2), beside_other),
        ],
    )
    other_twin, next_twin, next_other, far_outward, beside_other, result = together(
        (other_twin, next_twin, next_other, far_outward, beside_other, result)
    )

    from_far = jnp.where(at_ends, far_outward, far_inner)
    beside_other_twin, far_twin = sibling(beside_other), sibling(from_far)
    next_other_twin = sibling(next_other)
    far_other = across(from_far)
    result = apply(
        result,
        [
            (("own", 3), other_twin),
            (("next", 1), next_twin),
            (("far", 0), from_far),
            (("next", 2), next_other),
        ],
    )
    result = apply(
        result,
        [
            (("beside", 3), beside_other_twin),
            (("far", 1), far_twin),
            (("next", 3), next_other_twin),
        ],
    )
    far_other, result = together((far_other, result))
    return apply(result, [(("far", 2), far_other), (("far", 3), sibling(far_other))])


def solution(mesh):
    return jax.shard_map(
        per_device,
        mesh=mesh,
        in_specs=(
            P(None, ("groups", "ty"), None),
            P(),
            P(("groups", "ty"), None, None),
            P("groups"),
            P("groups"),
        ),
        out_specs=P(None, ("groups", "ty"), None),
        check_vma=False,
    )
```

```python
import functools
import math

import jax
import jax.numpy as jnp
import numpy as np
from jax import lax
from jax.experimental import pallas as pl
from jax.experimental.pallas import tpu as pltpu
from jax.sharding import PartitionSpec as P

step_size = 0.5
lane = 128
row_tile = 16
vmem_bytes = 32 * 1024 * 1024


def fourier_tables(crop_width):
    counter = np.arange(crop_width, dtype=np.int64)
    angle = (counter[:, None] * counter[None, :] % crop_width) * (2.0 * math.pi / crop_width)
    factor = 1.0 / math.sqrt(crop_width)
    cos_table = (np.cos(angle) * factor).astype(np.float32).astype(jnp.bfloat16)
    sin_table = (np.sin(angle) * factor).astype(np.float32).astype(jnp.bfloat16)
    return cos_table, sin_table


def tile_weight(pupil_ref, first_row, win):
    start = win.row(first_row)
    rows = pupil_ref[pl.ds(start, win.rows), :].astype(jnp.float32)
    rows = pltpu.roll(rows, (2 * win.rows + start - first_row) % win.rows, 0)
    shape = (win.tile_rows, win.crop_width)
    row = 2 * (first_row + lax.broadcasted_iota(jnp.int32, shape, 0)) - win.crop_width + 1
    column = 2 * lax.broadcasted_iota(jnp.int32, shape, 1) - win.crop_width + 1
    inside = row * row + column * column <= win.crop_width * win.crop_width
    return jnp.where(inside, rows[: win.tile_rows], 0.0)


def tile_band(band_ref, first_row, win):
    start = win.row(first_row)
    rows = band_ref[pl.ds(start, win.rows), :].astype(jnp.float32)
    rows = pltpu.roll(rows, (2 * win.rows + start - first_row) % win.rows, 0)[: win.tile_rows]
    band = rows.shape[1] // 2
    turned = jnp.concatenate([-rows[:, band:], rows[:, :band]], axis=1)
    return jnp.concatenate([rows, turned], axis=0).astype(jnp.bfloat16)


class Windows:
    def __init__(self, tile_rows, slab_columns, crop_width):
        self.tile_rows = tile_rows
        self.crop_width = crop_width
        self.rows = tile_rows + row_tile
        self.columns = crop_width + lane
        self.last_row = crop_width - self.rows
        self.last_column = slab_columns - self.columns

    def row(self, first_row):
        start = jnp.clip(first_row, 0, self.last_row) // row_tile * row_tile
        return pl.multiple_of(start, row_tile)

    def column(self, left):
        start = jnp.minimum(left // lane * lane, self.last_column)
        return pl.multiple_of(start, lane)

    def active(self, first_row):
        return (first_row > -self.tile_rows) & (first_row < self.crop_width)


def image_band(meta_ref, slot, lows, tiles, pupil_ref, band_ref, win, store, came=None):
    left = meta_ref[meta_ref.shape[0] - 1, slot]
    first_rows = [meta_ref[tile, slot] for tile in tiles]
    active = functools.reduce(jnp.logical_or, [win.active(row) for row in first_rows])
    band = band_ref.shape[1] // 2
    shape = (2, band, win.crop_width)

    @pl.when(jnp.logical_not(active))
    def _():
        store(jnp.zeros(shape, jnp.bfloat16) if came is None else came[...])

    @pl.when(active)
    def _():
        col_start = win.column(left)
        shift = (win.columns - (left - col_start)) % win.columns
        parts, tables = [], []
        for first_row, low_refs in zip(first_rows, lows):
            weight = tile_weight(pupil_ref, first_row, win)
            for low_ref in low_refs:
                low = low_ref[:, pl.ds(col_start, win.columns)].astype(jnp.float32)
                low = pltpu.roll(low, shift, 1)[:, : win.crop_width]
                parts.append((weight * low).astype(jnp.bfloat16))
            tables.append(tile_band(band_ref, first_row, win))
        mid = lax.dot_general(
            jnp.concatenate(tables, axis=0),
            jnp.concatenate(parts, axis=0),
            (((0,), (0,)), ((), ())),
            preferred_element_type=jnp.float32,
        )
        if came is not None:
            mid = mid + came[...].reshape(mid.shape).astype(jnp.float32)
        store(mid.astype(jnp.bfloat16).reshape(shape))


def forward_kernel(meta_ref, pupil_ref, band_ref, *refs, base, images, count, win, tiles):
    out_refs = refs[-count:]
    lows = [refs[2 * half : 2 * half + 2] for half in range(len(tiles))]
    came = refs[2 * len(tiles)] if len(refs) > 2 * len(tiles) + count else None
    streams = count // images

    def image(index):
        def store(value):
            for number in range(images):

                @pl.when(index == number)
                def _():
                    for stream in range(streams):
                        out_ref = out_refs[number * streams + stream]
                        rows = out_ref.shape[1]
                        out_ref[...] = value[:, stream * rows : (stream + 1) * rows]

        image_band(meta_ref, base + index, lows, tiles, pupil_ref, band_ref, win, store, came)

    pl.loop(0, images)(image)


def forward_grid_kernel(meta_ref, pupil_ref, band_ref, real_ref, imag_ref, out_ref, *, win):
    def store(value):
        out_ref[0] = value

    lows = [(real_ref, imag_ref)]
    image_band(meta_ref, pl.program_id(0), lows, (0,), pupil_ref, band_ref, win, store)


def subtract_image(meta_ref, slot, back_ref, pupil_ref, band_ref, out_ref, win):
    first_row, left = meta_ref[0, slot], meta_ref[meta_ref.shape[0] - 1, slot]
    tile_rows, crop_width = win.tile_rows, win.crop_width

    @pl.when(win.active(first_row))
    def _():
        col_start = win.column(left)
        weight = tile_weight(pupil_ref, first_row, win) * step_size
        table = tile_band(band_ref, first_row, win)
        back = back_ref[...].reshape(table.shape[1], crop_width)
        grad = jnp.dot(table, back, preferred_element_type=jnp.float32)
        columns = pl.ds(col_start, win.columns)
        pad = jnp.zeros((tile_rows, win.columns - crop_width), jnp.float32)
        for part in range(2):
            piece = grad[part * tile_rows : (part + 1) * tile_rows] * weight
            piece = pltpu.roll(jnp.concatenate([piece, pad], axis=1), left - col_start, 1)
            out_ref[part, :, columns] = out_ref[part, :, columns] - piece


def backward_kernel(meta_ref, pupil_ref, band_ref, spec_ref, *refs, slots, win):
    back_refs, out_ref = refs[:-1], refs[-1]
    out_ref[...] = spec_ref[...]
    for slot, back_ref in zip(slots, back_refs):
        subtract_image(meta_ref, slot, back_ref, pupil_ref, band_ref, out_ref, win)


def backward_grid_kernel(meta_ref, pupil_ref, band_ref, spec_ref, back_ref, out_ref, *, win):
    step = pl.program_id(0)

    @pl.when(step == 0)
    def _():
        out_ref[...] = spec_ref[...]

    subtract_image(meta_ref, step, back_ref, pupil_ref, band_ref, out_ref, win)


def middle_kernel(*refs, terms, streams):
    term_refs, refs = refs[: terms * streams], refs[terms * streams :]
    image_ref, cos_ref, sin_ref, out_ref, mid_ref, resid_ref = refs
    _, rows, crop_width = term_refs[0].shape
    band = rows * streams
    block = min(512, crop_width)
    for stream in range(streams):
        of_stream = term_refs[stream * terms : (stream + 1) * terms]
        total = sum(ref[...].astype(jnp.float32) for ref in of_stream).astype(jnp.bfloat16)
        for part in range(2):
            start = part * band + stream * rows
            mid_ref[start : start + rows] = total[part]
    dot = functools.partial(jnp.dot, preferred_element_type=jnp.float32)
    for start in range(0, crop_width, block):
        columns = slice(start, start + block)
        by_cos = dot(mid_ref[...], cos_ref[:, columns])
        by_sin = dot(mid_ref[...], sin_ref[:, columns])
        field_real = by_cos[:band] - by_sin[band:]
        field_imag = by_sin[:band] + by_cos[band:]
        power = field_real * field_real + field_imag * field_imag
        measured = image_ref[0, :, columns].astype(jnp.float32)
        keeping = 1.0 - measured * lax.rsqrt(jnp.maximum(power, 1.0))
        resid_ref[:band, columns] = (field_real * keeping).astype(jnp.bfloat16)
        resid_ref[band:, columns] = (field_imag * keeping).astype(jnp.bfloat16)
    for start in range(0, crop_width, block):
        columns = slice(start, start + block)
        by_cos = dot(resid_ref[...], cos_ref[:, columns])
        by_sin = dot(resid_ref[...], sin_ref[:, columns])
        out_ref[0, :, columns] = (by_cos[:band] + by_sin[band:]).astype(jnp.bfloat16)
        out_ref[1, :, columns] = (by_cos[band:] - by_sin[:band]).astype(jnp.bfloat16)


def params():
    return pltpu.CompilerParams(vmem_limit_bytes=vmem_bytes)


def light():
    return pl.CostEstimate(flops=1024, bytes_accessed=1024, transcendentals=0)


vmem = pl.BlockSpec(memory_space=pltpu.VMEM)
smem = pl.BlockSpec(memory_space=pltpu.SMEM)


def band_type(pupil, band_table, *lead):
    shape = lead + (2, band_table.shape[1] // 2, pupil.shape[1])
    return jax.ShapeDtypeStruct(shape, jnp.bfloat16)


def forward(meta, lows, pupil, band_table, base, images, tiles=(0, 1), came=None, streams=1):
    win = Windows(*lows[0][0].shape, pupil.shape[1])
    operands = [meta, pupil, band_table] + [part for low in lows for part in low]
    operands += [came] * (came is not None)
    count = images * streams
    _, rows, columns = band_type(pupil, band_table).shape
    return pl.pallas_call(
        functools.partial(
            forward_kernel, base=base, images=images, count=count, win=win, tiles=tiles
        ),
        in_specs=[smem] + [vmem] * (len(operands) - 1),
        out_specs=[vmem] * count,
        out_shape=[jax.ShapeDtypeStruct((2, rows // streams, columns), jnp.bfloat16)] * count,
        compiler_params=params(),
        cost_estimate=light(),
        name="forward",
    )(*operands)


def backward(meta, spectrum, pupil, band_table, slots, backs):
    win = Windows(*spectrum.shape[1:], pupil.shape[1])
    return pl.pallas_call(
        functools.partial(backward_kernel, slots=slots, win=win),
        in_specs=[smem] + [vmem] * (3 + len(backs)),
        out_specs=vmem,
        out_shape=jax.ShapeDtypeStruct(spectrum.shape, jnp.float32),
        compiler_params=params(),
        cost_estimate=light(),
        name="backward",
    )(meta, pupil, band_table, spectrum, *backs)


def middle(streams, image, cos_table, sin_table):
    _, rows, crop_width = streams[0][0].shape
    band = rows * len(streams)
    terms = [term for stream in streams for term in stream]
    return pl.pallas_call(
        functools.partial(
            middle_kernel, terms=len(streams[0]), streams=len(streams)
        ),
        in_specs=[vmem] * (len(terms) + 3),
        out_specs=vmem,
        out_shape=jax.ShapeDtypeStruct((2, band, crop_width), jnp.bfloat16),
        scratch_shapes=[pltpu.VMEM((2 * band, crop_width), jnp.bfloat16)] * 2,
        compiler_params=params(),
        cost_estimate=light(),
        name="middle",
    )(*terms, image, cos_table, sin_table)


def fixed(array):
    return pl.BlockSpec(array.shape, lambda i: (0,) * array.ndim)


def forward_all(meta, low, pupil, band_table):
    win = Windows(*low[0].shape, pupil.shape[1])
    count = meta.shape[1]
    out_type = band_type(pupil, band_table, count)
    return pl.pallas_call(
        functools.partial(forward_grid_kernel, win=win),
        grid=(count,),
        in_specs=[smem] + [fixed(array) for array in (pupil, band_table, *low)],
        out_specs=pl.BlockSpec((1,) + out_type.shape[1:], lambda i: (i, 0, 0, 0)),
        out_shape=out_type,
        compiler_params=params(),
        name="forward_all",
    )(meta, pupil, band_table, *low)


def backward_all(meta, spectrum, pupil, band_table, backs):
    win = Windows(*spectrum.shape[1:], pupil.shape[1])
    return pl.pallas_call(
        functools.partial(backward_grid_kernel, win=win),
        grid=(meta.shape[1],),
        in_specs=[smem]
        + [fixed(array) for array in (pupil, band_table, spectrum)]
        + [pl.BlockSpec((1,) + backs.shape[1:], lambda i: (i, 0, 0, 0))],
        out_specs=fixed(spectrum),
        out_shape=jax.ShapeDtypeStruct(spectrum.shape, jnp.float32),
        compiler_params=params(),
        name="backward_all",
    )(meta, pupil, band_table, spectrum, backs)


def cast_kernel(spec_ref, out_ref, held, sems, *, part):
    blocks, _, width = held.shape
    columns = [pl.ds(block * width, width) for block in range(blocks)]
    copies = [
        pltpu.make_async_copy(spec_ref.at[part, :, columns[i]], held.at[i], sems.at[i])
        for i in range(blocks)
    ]
    for copy in copies:
        copy.start()
    for i, copy in enumerate(copies):
        copy.wait()
        out_ref[:, columns[i]] = held[i].astype(jnp.bfloat16)


def low_part(spectrum, part):
    _, rows, columns = spectrum.shape
    return pl.pallas_call(
        functools.partial(cast_kernel, part=part),
        in_specs=[pl.BlockSpec(memory_space=pltpu.HBM)],
        out_specs=vmem,
        out_shape=jax.ShapeDtypeStruct((rows, columns), jnp.bfloat16),
        scratch_shapes=[
            pltpu.VMEM((4, rows, columns // 4), jnp.float32),
            pltpu.SemaphoreType.DMA((4,)),
        ],
        compiler_params=params(),
        cost_estimate=light(),
        name="low_part",
    )(spectrum)


def total(*terms):
    return sum(term.astype(jnp.float32) for term in terms).astype(jnp.bfloat16)


def per_device(spectrum, pupil, measured, centre_rows, centre_cols):
    count = lax.axis_size("ty")
    planes = count // 4
    position = lax.axis_index("ty")
    plane = position // 4
    _, tile_rows, slab_columns = spectrum.shape
    crop_width = pupil.shape[0]
    band = measured.shape[1]
    band_start = (crop_width - band) // 2
    cos_table, sin_table = fourier_tables(crop_width)
    chosen_rows = slice(band_start, band_start + band)
    band_table = jnp.asarray(
        np.concatenate([cos_table[:, chosen_rows], sin_table[:, chosen_rows]], axis=1)
    )
    cos_table, sin_table = jnp.asarray(cos_table), jnp.asarray(sin_table)

    half = crop_width // 2

    low = [low_part(spectrum, part) for part in range(2)]

    def image_meta(ids, positions):
        match = ids[:, None] == jnp.arange(count, dtype=jnp.int32)[None, :]
        tops = jnp.sum(jnp.where(match, centre_rows[None, :], 0), axis=1) - half
        lefts = jnp.sum(jnp.where(match, centre_cols[None, :], 0), axis=1) - half
        rows = [place * tile_rows - tops for place in positions]
        return jnp.stack(rows + [lefts]).astype(jnp.int32)

    if planes != 4:
        meta = image_meta(jnp.arange(count, dtype=jnp.int32), [position])
        partial = forward_all(meta, low, pupil, band_table)
        mid = lax.psum_scatter(partial, "ty", scatter_dimension=0, tiled=True)[0]
        back = lax.all_gather(middle([[mid]], measured, cos_table, sin_table), "ty")
        return backward_all(meta, spectrum, pupil, band_table, back)

    targets = {"far": (3, 3, 0, 0), "next": (2, 2, 1, 1), "beside": (1, 0, 3, 2), "own": (0, 1, 2, 3)}
    own_core = [("far", 2), ("far", 0), ("next", 2), ("next", 0)]
    own_core += [("beside", 2), ("beside", 0), ("own", 2), ("own", 0)]
    slots = {}
    for core in (0, 1):
        for name, y in own_core:
            slots[name, y + core] = len(slots)
    ids = [
        [targets[name][i // 4] * 4 + (i % 4 ^ flip) for (name, flip) in slots]
        for i in range(count)
    ]
    my_ids = lax.dynamic_index_in_dim(jnp.asarray(ids, jnp.int32), position, keepdims=False)
    meta = image_meta(my_ids, [position, position ^ 1])

    def sibling(value):
        return lax.ppermute(value, "ty", [(i, i ^ 1) for i in range(count)])

    def across(value):
        return lax.ppermute(value, "ty", [(i, i ^ 2) for i in range(count)])

    def along(value, plane_pairs):
        pairs = [(4 * a + i, 4 * b + i) for a, b in plane_pairs for i in range(4)]
        return lax.ppermute(value, "ty", pairs)

    inward = [(0, 1), (3, 2)]
    outward = [(1, 0), (2, 3)]
    inner = [(1, 2), (2, 1)]
    together = lax.optimization_barrier

    lows = [low, [sibling(part) for part in low]]
    streams = 2
    (own_rows,) = forward(meta, lows[:1], pupil, band_table, 0, 1, (0,))
    far_leaving = forward(
        meta, lows[1:], pupil, band_table, 0, 1, (1,), own_rows, streams=streams
    )
    far_other = [across(value) for value in far_leaving]
    made = forward(
        together((meta, far_leaving[0]))[0], lows, pupil, band_table, 1, 7, streams=streams
    )
    summed, held = [], None
    for stream in reversed(range(streams)):
        (
            far_kept,
            next_leaving,
            next_kept,
            beside_leaving,
            beside_kept,
            own_leaving,
            own_kept,
        ) = made[stream::streams]
        far, far_kept, next_leaving = together((far_other[stream], far_kept, next_leaving))

        next_other = across(next_leaving)
        from_end = along(total(far_kept, far), inward)
        from_end, next_other, beside_leaving = together((from_end, next_other, beside_leaving))

        beside_other = across(beside_leaving)
        next_inward = along(total(next_kept, next_other), inward)
        far_inner = along(total(far_kept, far, from_end), inner)
        far_inner, next_inward, beside_other, own_leaving = together(
            (far_inner, next_inward, beside_other, own_leaving)
        )

        own_other = across(own_leaving)
        next_inner = along(total(next_kept, next_other, next_inward), inner)
        beside = along(total(beside_kept, beside_other, far_inner), inward + outward)
        terms = [own_kept, own_other, next_inner, beside]
        if stream > 0:
            terms = [total(*terms)]
            held = terms[0]
        else:
            terms[0] = together((terms[0], held))[0]
            terms = [total(*terms)]
        summed.insert(0, terms)
    back = middle(summed, measured, cos_table, sin_table)

    def apply(result, pieces):
        names, values = zip(*pieces)
        return backward(
            meta, result, pupil, band_table, [slots[name] for name in names], list(values)
        )

    other = across(back)
    from_inner = along(back, inner)
    from_beside = along(back, inward + outward)
    other, from_inner, from_beside, back = together((other, from_inner, from_beside, back))

    beside_twin, other_twin = sibling(from_beside), sibling(other)
    beside_other = across(from_beside)
    far_inner = along(from_beside, inner)
    next_outward = along(from_inner, outward)
    result = apply(
        spectrum, [(("own", 0), back), (("beside", 0), from_beside), (("own", 2), other)]
    )
    beside_twin, other_twin, beside_other, far_inner, next_outward, back, result = together(
        (beside_twin, other_twin, beside_other, far_inner, next_outward, back, result)
    )

    at_ends = (plane == 0) | (plane == 3)
    from_next = jnp.where(at_ends, next_outward, from_inner)
    twin, next_twin = sibling(back), sibling(from_next)
    next_other = across(from_next)
    far_outward = along(far_inner, outward)
    result = apply(
        result,
        [
            (("own", 3), other_twin),
            (("beside", 1), beside_twin),
            (("next", 0), from_next),
            (("beside", 2), beside_other),
        ],
    )
    twin, next_twin, next_other, far_outward, beside_other, result = together(
        (twin, next_twin, next_other, far_outward, beside_other, result)
    )

    from_far = jnp.where(at_ends, far_outward, far_inner)
    beside_other_twin, far_twin = sibling(beside_other), sibling(from_far)
    next_other_twin = sibling(next_other)
    far_other = across(from_far)
    result = apply(
        result,
        [
            (("own", 1), twin),
            (("next", 1), next_twin),
            (("far", 0), from_far),
            (("next", 2), next_other),
        ],
    )
    result = apply(
        result,
        [
            (("beside", 3), beside_other_twin),
            (("far", 1), far_twin),
            (("next", 3), next_other_twin),
        ],
    )
    far_other, result = together((far_other, result))
    return apply(result, [(("far", 2), far_other), (("far", 3), sibling(far_other))])


def solution(mesh):
    return jax.shard_map(
        per_device,
        mesh=mesh,
        in_specs=(
            P(None, ("groups", "ty"), None),
            P(),
            P(("groups", "ty"), None, None),
            P("groups"),
            P("groups"),
        ),
        out_specs=P(None, ("groups", "ty"), None),
        check_vma=False,
    )
```

```python
import functools
import math

import jax
import jax.numpy as jnp
import numpy as np
from jax import lax
from jax.experimental import pallas as pl
from jax.experimental.pallas import tpu as pltpu
from jax.sharding import PartitionSpec as P

step_size = 0.5
lane = 128
row_tile = 16
vmem_bytes = 32 * 1024 * 1024
backward_bytes = 40 * 1024 * 1024


def fourier_tables(crop_width):
    counter = np.arange(crop_width, dtype=np.int64)
    angle = (counter[:, None] * counter[None, :] % crop_width) * (2.0 * math.pi / crop_width)
    factor = 1.0 / math.sqrt(crop_width)
    cos_table = (np.cos(angle) * factor).astype(np.float32).astype(jnp.bfloat16)
    sin_table = (np.sin(angle) * factor).astype(np.float32).astype(jnp.bfloat16)
    return cos_table, sin_table


def tile_weight(pupil_ref, first_row, win):
    start = win.row(first_row)
    rows = pupil_ref[pl.ds(start, win.rows), :].astype(jnp.float32)
    rows = pltpu.roll(rows, (2 * win.rows + start - first_row) % win.rows, 0)
    shape = (win.tile_rows, win.crop_width)
    row = 2 * (first_row + lax.broadcasted_iota(jnp.int32, shape, 0)) - win.crop_width + 1
    column = 2 * lax.broadcasted_iota(jnp.int32, shape, 1) - win.crop_width + 1
    inside = row * row + column * column <= win.crop_width * win.crop_width
    return jnp.where(inside, rows[: win.tile_rows], 0.0)


def tile_band(band_ref, first_row, win):
    start = win.row(first_row)
    rows = band_ref[pl.ds(start, win.rows), :].astype(jnp.float32)
    rows = pltpu.roll(rows, (2 * win.rows + start - first_row) % win.rows, 0)[: win.tile_rows]
    band = rows.shape[1] // 2
    turned = jnp.concatenate([-rows[:, band:], rows[:, :band]], axis=1)
    return jnp.concatenate([rows, turned], axis=0).astype(jnp.bfloat16)


class Windows:
    def __init__(self, tile_rows, slab_columns, crop_width):
        self.tile_rows = tile_rows
        self.crop_width = crop_width
        self.rows = tile_rows + row_tile
        self.columns = crop_width + lane
        self.last_row = crop_width - self.rows
        self.last_column = slab_columns - self.columns

    def row(self, first_row):
        start = jnp.clip(first_row, 0, self.last_row) // row_tile * row_tile
        return pl.multiple_of(start, row_tile)

    def column(self, left):
        start = jnp.minimum(left // lane * lane, self.last_column)
        return pl.multiple_of(start, lane)

    def active(self, first_row):
        return (first_row > -self.tile_rows) & (first_row < self.crop_width)


def image_band(meta_ref, slot, lows, tiles, pupil_ref, band_ref, win, store, came=None):
    left = meta_ref[meta_ref.shape[0] - 1, slot]
    first_rows = [meta_ref[tile, slot] for tile in tiles]
    active = functools.reduce(jnp.logical_or, [win.active(row) for row in first_rows])
    band = band_ref.shape[1] // 2
    shape = (2, band, win.crop_width)

    @pl.when(jnp.logical_not(active))
    def _():
        store(jnp.zeros(shape, jnp.bfloat16) if came is None else came[...])

    @pl.when(active)
    def _():
        col_start = win.column(left)
        shift = (win.columns - (left - col_start)) % win.columns
        parts, tables = [], []
        for first_row, low_refs in zip(first_rows, lows):
            weight = tile_weight(pupil_ref, first_row, win)
            for low_ref in low_refs:
                low = low_ref[:, pl.ds(col_start, win.columns)].astype(jnp.float32)
                low = pltpu.roll(low, shift, 1)[:, : win.crop_width]
                parts.append((weight * low).astype(jnp.bfloat16))
            tables.append(tile_band(band_ref, first_row, win))
        mid = lax.dot_general(
            jnp.concatenate(tables, axis=0),
            jnp.concatenate(parts, axis=0),
            (((0,), (0,)), ((), ())),
            preferred_element_type=jnp.float32,
        )
        if came is not None:
            mid = mid + came[...].reshape(mid.shape).astype(jnp.float32)
        store(mid.astype(jnp.bfloat16).reshape(shape))


def forward_kernel(meta_ref, pupil_ref, band_ref, *refs, base, images, count, win, tiles):
    out_refs = refs[-count:]
    lows = [refs[2 * half : 2 * half + 2] for half in range(len(tiles))]
    came = refs[2 * len(tiles)] if len(refs) > 2 * len(tiles) + count else None
    streams = count // images

    def image(index):
        def store(value):
            for number in range(images):

                @pl.when(index == number)
                def _():
                    for stream in range(streams):
                        out_ref = out_refs[number * streams + stream]
                        rows = out_ref.shape[1]
                        out_ref[...] = value[:, stream * rows : (stream + 1) * rows]

        image_band(meta_ref, base + index, lows, tiles, pupil_ref, band_ref, win, store, came)

    pl.loop(0, images)(image)


def forward_grid_kernel(meta_ref, pupil_ref, band_ref, real_ref, imag_ref, out_ref, *, win):
    def store(value):
        out_ref[0] = value

    lows = [(real_ref, imag_ref)]
    image_band(meta_ref, pl.program_id(0), lows, (0,), pupil_ref, band_ref, win, store)


def subtract_image(meta_ref, slot, back_refs, pupil_ref, band_ref, out_ref, win, tile=0):
    first_row, left = meta_ref[tile, slot], meta_ref[meta_ref.shape[0] - 1, slot]
    tile_rows, crop_width = win.tile_rows, win.crop_width

    @pl.when(win.active(first_row))
    def _():
        col_start = win.column(left)
        weight = tile_weight(pupil_ref, first_row, win) * step_size
        table = tile_band(band_ref, first_row, win)
        band = table.shape[1] // 2
        rows = band // len(back_refs)
        held = [number for number, ref in enumerate(back_refs) if ref is not None]
        if len(held) < len(back_refs):
            starts = [part * band + number * rows for part in range(2) for number in held]
            table = jnp.concatenate([table[:, start : start + rows] for start in starts], axis=1)
        back = [back_refs[number][part] for part in range(2) for number in held]
        back = jnp.concatenate(back, axis=0)
        grad = jnp.dot(table, back, preferred_element_type=jnp.float32)
        columns = pl.ds(col_start, win.columns)
        pad = jnp.zeros((tile_rows, win.columns - crop_width), jnp.float32)
        for part in range(2):
            piece = grad[part * tile_rows : (part + 1) * tile_rows] * weight
            piece = pltpu.roll(jnp.concatenate([piece, pad], axis=1), left - col_start, 1)
            out_ref[part, :, columns] = out_ref[part, :, columns] - piece


def backward_kernel(meta_ref, pupil_ref, band_ref, *refs, slots, held, parts, win):
    part_refs, back_refs, out_ref = refs[:parts], iter(refs[parts:-1]), refs[-1]
    for number in range(parts - 1):
        chunk = part_refs[number + 1][...].astype(jnp.float32)
        width = chunk.shape[2]
        columns = slice(number * width, (number + 1) * width)
        out_ref[:, :, columns] = part_refs[0][:, :, columns] + chunk
    if parts == 1:
        out_ref[...] = part_refs[0][...]
    for slot, groups in zip(slots, held):
        of_image = [next(back_refs) if there else None for there in groups]
        subtract_image(meta_ref, slot, of_image, pupil_ref, band_ref, out_ref, win)


def sibling_kernel(meta_ref, pupil_ref, band_ref, *refs, slots, held, parts, win):
    backs = sum(map(sum, held))
    part_refs, back_refs, total_ref = refs[:parts], iter(refs[parts : parts + backs]), refs[-1]
    out_refs = refs[parts + backs : -1]
    if parts:
        total_ref[...] = part_refs[0][...].astype(jnp.float32)
    else:
        total_ref[...] = jnp.zeros_like(total_ref)
    for slot, groups in zip(slots, held):
        of_image = [next(back_refs) if there else None for there in groups]
        subtract_image(meta_ref, slot, of_image, pupil_ref, band_ref, total_ref, win, 1)
    width = out_refs[0].shape[2]
    for number, out_ref in enumerate(out_refs):
        out_ref[...] = total_ref[:, :, number * width : (number + 1) * width].astype(jnp.bfloat16)


def backward_grid_kernel(meta_ref, pupil_ref, band_ref, spec_ref, back_ref, out_ref, *, win):
    step = pl.program_id(0)

    @pl.when(step == 0)
    def _():
        out_ref[...] = spec_ref[...]

    subtract_image(meta_ref, step, [back_ref.at[0]], pupil_ref, band_ref, out_ref, win)


def middle_kernel(*refs, terms, streams):
    term_refs, refs = refs[: terms * streams], refs[terms * streams :]
    (image_ref, cos_ref, sin_ref), refs = refs[:3], refs[3:]
    out_refs, (mid_ref, resid_ref) = refs[:streams], refs[streams:]
    _, rows, crop_width = term_refs[0].shape
    band = rows * streams
    block = min(512, crop_width)
    for stream in range(streams):
        of_stream = term_refs[stream * terms : (stream + 1) * terms]
        total = sum(ref[...].astype(jnp.float32) for ref in of_stream).astype(jnp.bfloat16)
        for part in range(2):
            start = part * band + stream * rows
            mid_ref[start : start + rows] = total[part]
    dot = functools.partial(jnp.dot, preferred_element_type=jnp.float32)
    for start in range(0, crop_width, block):
        columns = slice(start, start + block)
        by_cos = dot(mid_ref[...], cos_ref[:, columns])
        by_sin = dot(mid_ref[...], sin_ref[:, columns])
        field_real = by_cos[:band] - by_sin[band:]
        field_imag = by_sin[:band] + by_cos[band:]
        power = field_real * field_real + field_imag * field_imag
        measured = image_ref[0, :, columns].astype(jnp.float32)
        keeping = 1.0 - measured * lax.rsqrt(jnp.maximum(power, 1.0))
        resid_ref[:band, columns] = (field_real * keeping).astype(jnp.bfloat16)
        resid_ref[band:, columns] = (field_imag * keeping).astype(jnp.bfloat16)
    for start in range(0, crop_width, block):
        columns = slice(start, start + block)
        by_cos = dot(resid_ref[...], cos_ref[:, columns])
        by_sin = dot(resid_ref[...], sin_ref[:, columns])
        for part, back in enumerate((by_cos[:band] + by_sin[band:], by_cos[band:] - by_sin[:band])):
            for stream, out_ref in enumerate(out_refs):
                of_stream = back[stream * rows : (stream + 1) * rows]
                out_ref[part, :, columns] = of_stream.astype(jnp.bfloat16)


def params():
    return pltpu.CompilerParams(vmem_limit_bytes=vmem_bytes)


def light():
    return pl.CostEstimate(flops=1024, bytes_accessed=1024, transcendentals=0)


vmem = pl.BlockSpec(memory_space=pltpu.VMEM)
smem = pl.BlockSpec(memory_space=pltpu.SMEM)


def band_type(pupil, band_table, *lead):
    shape = lead + (2, band_table.shape[1] // 2, pupil.shape[1])
    return jax.ShapeDtypeStruct(shape, jnp.bfloat16)


def forward(meta, lows, pupil, band_table, base, images, tiles=(0, 1), came=None, streams=1):
    win = Windows(*lows[0][0].shape, pupil.shape[1])
    operands = [meta, pupil, band_table] + [part for low in lows for part in low]
    operands += [came] * (came is not None)
    count = images * streams
    _, rows, columns = band_type(pupil, band_table).shape
    return pl.pallas_call(
        functools.partial(
            forward_kernel, base=base, images=images, count=count, win=win, tiles=tiles
        ),
        in_specs=[smem] + [vmem] * (len(operands) - 1),
        out_specs=[vmem] * count,
        out_shape=[jax.ShapeDtypeStruct((2, rows // streams, columns), jnp.bfloat16)] * count,
        compiler_params=params(),
        cost_estimate=light(),
        name="forward",
    )(*operands)


def backward(meta, shape, pupil, band_table, parts, slots, backs, chunks=0):
    win = Windows(*shape[1:], pupil.shape[1])
    held = [[back is not None for back in groups] for groups in backs]
    operands = list(parts) + [back for groups in backs for back in groups if back is not None]
    kernel = sibling_kernel if chunks else backward_kernel
    out_shape = jax.ShapeDtypeStruct(shape, jnp.float32)
    if chunks:
        chunk = shape[:2] + (shape[2] // chunks,)
        out_shape = [jax.ShapeDtypeStruct(chunk, jnp.bfloat16)] * chunks
    return pl.pallas_call(
        functools.partial(kernel, slots=slots, held=held, parts=len(parts), win=win),
        in_specs=[smem] + [vmem] * (2 + len(operands)),
        out_specs=[vmem] * chunks if chunks else vmem,
        out_shape=out_shape,
        scratch_shapes=[pltpu.VMEM(shape, jnp.float32)] * (chunks > 0),
        compiler_params=pltpu.CompilerParams(vmem_limit_bytes=backward_bytes),
        cost_estimate=light(),
        name="backward",
    )(meta, pupil, band_table, *operands)


def middle(streams, image, cos_table, sin_table):
    _, rows, crop_width = streams[0][0].shape
    band = rows * len(streams)
    terms = [term for stream in streams for term in stream]
    return pl.pallas_call(
        functools.partial(
            middle_kernel, terms=len(streams[0]), streams=len(streams)
        ),
        in_specs=[vmem] * (len(terms) + 3),
        out_specs=[vmem] * len(streams),
        out_shape=[jax.ShapeDtypeStruct((2, rows, crop_width), jnp.bfloat16)] * len(streams),
        scratch_shapes=[pltpu.VMEM((2 * band, crop_width), jnp.bfloat16)] * 2,
        compiler_params=params(),
        cost_estimate=light(),
        name="middle",
    )(*terms, image, cos_table, sin_table)


def fixed(array):
    return pl.BlockSpec(array.shape, lambda i: (0,) * array.ndim)


def forward_all(meta, low, pupil, band_table):
    win = Windows(*low[0].shape, pupil.shape[1])
    count = meta.shape[1]
    out_type = band_type(pupil, band_table, count)
    return pl.pallas_call(
        functools.partial(forward_grid_kernel, win=win),
        grid=(count,),
        in_specs=[smem] + [fixed(array) for array in (pupil, band_table, *low)],
        out_specs=pl.BlockSpec((1,) + out_type.shape[1:], lambda i: (i, 0, 0, 0)),
        out_shape=out_type,
        compiler_params=params(),
        name="forward_all",
    )(meta, pupil, band_table, *low)


def backward_all(meta, spectrum, pupil, band_table, backs):
    win = Windows(*spectrum.shape[1:], pupil.shape[1])
    return pl.pallas_call(
        functools.partial(backward_grid_kernel, win=win),
        grid=(meta.shape[1],),
        in_specs=[smem]
        + [fixed(array) for array in (pupil, band_table, spectrum)]
        + [pl.BlockSpec((1,) + backs.shape[1:], lambda i: (i, 0, 0, 0))],
        out_specs=fixed(spectrum),
        out_shape=jax.ShapeDtypeStruct(spectrum.shape, jnp.float32),
        compiler_params=params(),
        name="backward_all",
    )(meta, pupil, band_table, spectrum, backs)


def cast_kernel(spec_ref, out_ref, held, sems, *, part):
    blocks, _, width = held.shape
    columns = [pl.ds(block * width, width) for block in range(blocks)]
    copies = [
        pltpu.make_async_copy(spec_ref.at[part, :, columns[i]], held.at[i], sems.at[i])
        for i in range(blocks)
    ]
    for copy in copies:
        copy.start()
    for i, copy in enumerate(copies):
        copy.wait()
        out_ref[:, columns[i]] = held[i].astype(jnp.bfloat16)


def low_part(spectrum, part):
    _, rows, columns = spectrum.shape
    return pl.pallas_call(
        functools.partial(cast_kernel, part=part),
        in_specs=[pl.BlockSpec(memory_space=pltpu.HBM)],
        out_specs=vmem,
        out_shape=jax.ShapeDtypeStruct((rows, columns), jnp.bfloat16),
        scratch_shapes=[
            pltpu.VMEM((4, rows, columns // 4), jnp.float32),
            pltpu.SemaphoreType.DMA((4,)),
        ],
        compiler_params=params(),
        cost_estimate=light(),
        name="low_part",
    )(spectrum)


def total(*terms):
    return sum(term.astype(jnp.float32) for term in terms).astype(jnp.bfloat16)


def per_device(spectrum, pupil, measured, centre_rows, centre_cols):
    count = lax.axis_size("ty")
    planes = count // 4
    position = lax.axis_index("ty")
    plane = position // 4
    _, tile_rows, slab_columns = spectrum.shape
    crop_width = pupil.shape[0]
    band = measured.shape[1]
    band_start = (crop_width - band) // 2
    cos_table, sin_table = fourier_tables(crop_width)
    chosen_rows = slice(band_start, band_start + band)
    band_table = jnp.asarray(
        np.concatenate([cos_table[:, chosen_rows], sin_table[:, chosen_rows]], axis=1)
    )
    cos_table, sin_table = jnp.asarray(cos_table), jnp.asarray(sin_table)

    half = crop_width // 2

    low = [low_part(spectrum, part) for part in range(2)]

    def image_meta(ids, positions):
        match = ids[:, None] == jnp.arange(count, dtype=jnp.int32)[None, :]
        tops = jnp.sum(jnp.where(match, centre_rows[None, :], 0), axis=1) - half
        lefts = jnp.sum(jnp.where(match, centre_cols[None, :], 0), axis=1) - half
        rows = [place * tile_rows - tops for place in positions]
        return jnp.stack(rows + [lefts]).astype(jnp.int32)

    if planes != 4:
        meta = image_meta(jnp.arange(count, dtype=jnp.int32), [position])
        partial = forward_all(meta, low, pupil, band_table)
        mid = lax.psum_scatter(partial, "ty", scatter_dimension=0, tiled=True)[0]
        back = lax.all_gather(middle([[mid]], measured, cos_table, sin_table)[0], "ty")
        return backward_all(meta, spectrum, pupil, band_table, back)

    targets = {"far": (3, 3, 0, 0), "next": (2, 2, 1, 1), "beside": (1, 0, 3, 2), "own": (0, 1, 2, 3)}
    own_core = [("far", 2), ("far", 0), ("next", 2), ("next", 0)]
    own_core += [("beside", 2), ("beside", 0), ("own", 2), ("own", 0)]
    slots = {}
    for core in (0, 1):
        for name, y in own_core:
            slots[name, y + core] = len(slots)
    ids = [
        [targets[name][i // 4] * 4 + (i % 4 ^ flip) for (name, flip) in slots]
        for i in range(count)
    ]
    my_ids = lax.dynamic_index_in_dim(jnp.asarray(ids, jnp.int32), position, keepdims=False)
    meta = image_meta(my_ids, [position, position ^ 1])

    def sibling(value):
        return lax.ppermute(value, "ty", [(i, i ^ 1) for i in range(count)])

    def across(value):
        return lax.ppermute(value, "ty", [(i, i ^ 2) for i in range(count)])

    def along(value, plane_pairs):
        pairs = [(4 * a + i, 4 * b + i) for a, b in plane_pairs for i in range(4)]
        return lax.ppermute(value, "ty", pairs)

    inward = [(0, 1), (3, 2)]
    outward = [(1, 0), (2, 3)]
    inner = [(1, 2), (2, 1)]
    together = lax.optimization_barrier

    lows = [low, [sibling(part) for part in low]]
    streams = 2
    (own_rows,) = forward(meta, lows[:1], pupil, band_table, 0, 1, (0,))
    far_leaving = forward(
        meta, lows[1:], pupil, band_table, 0, 1, (1,), own_rows, streams=streams
    )
    far_other = [across(value) for value in far_leaving]
    made = forward(
        together((meta, far_leaving[0]))[0], lows, pupil, band_table, 1, 7, streams=streams
    )
    summed, held = [], None
    for stream in reversed(range(streams)):
        (
            far_kept,
            next_leaving,
            next_kept,
            beside_leaving,
            beside_kept,
            own_leaving,
            own_kept,
        ) = made[stream::streams]
        far, far_kept, next_leaving = together((far_other[stream], far_kept, next_leaving))

        next_other = across(next_leaving)
        from_end = along(total(far_kept, far), inward)
        from_end, next_other, beside_leaving = together((from_end, next_other, beside_leaving))

        beside_other = across(beside_leaving)
        next_inward = along(total(next_kept, next_other), inward)
        far_inner = along(total(far_kept, far, from_end), inner)
        far_inner, next_inward, beside_other, own_leaving = together(
            (far_inner, next_inward, beside_other, own_leaving)
        )

        own_other = across(own_leaving)
        next_inner = along(total(next_kept, next_other, next_inward), inner)
        beside = along(total(beside_kept, beside_other, far_inner), inward + outward)
        terms = [own_kept, own_other, next_inner, beside]
        if stream > 0:
            terms = [total(*terms)]
            held = terms[0]
        else:
            terms[0] = together((terms[0], held))[0]
            terms = [total(*terms)]
        summed.insert(0, terms)
    backs = middle(summed, measured, cos_table, sin_table)

    at_ends = (plane == 0) | (plane == 3)
    lead, last = streams - 1, 0
    pieces = {}

    def apply(parts, names, chunks=0):
        taken = [[pieces.get((name, stream)) for stream in range(streams)] for name in names]
        own_slots = [slots[name] for name in names]
        shape = spectrum.shape
        return backward(meta, shape, pupil, band_table, parts, own_slots, taken, chunks)

    def close(stream, *names):
        closed = together(tuple(pieces[name, stream] for name in names))
        for name, value in zip(names, closed):
            pieces[name, stream] = value

    for stream in (lead, last):
        back = pieces[("own", 0), stream] = backs[stream]
        pieces[("own", 2), stream] = across(back)
        pieces["inner", stream] = along(back, inner)
        pieces[("beside", 0), stream] = along(back, inward + outward)
        close(stream, ("own", 2), "inner", ("beside", 0))
    early, later, late = (
        [("own", 0), ("beside", 0), ("own", 2)],
        [("next", 0), ("beside", 2)],
        [("far", 0), ("next", 2)],
    )
    for stream in (lead, last):
        pieces[("beside", 2), stream] = across(pieces[("beside", 0), stream])
        pieces["far inner", stream] = along(pieces[("beside", 0), stream], inner)
        pieces["outward", stream] = along(pieces["inner", stream], outward)
        if stream == last:
            pieces["result", stream] = apply([spectrum], early)
            close(stream, ("beside", 2), "far inner", "outward", "result")
        else:
            close(stream, ("beside", 2), "far inner", "outward")
    for stream in (lead, last):
        from_next = jnp.where(at_ends, pieces["outward", stream], pieces["inner", stream])
        pieces[("next", 0), stream] = from_next
        pieces[("next", 2), stream] = across(from_next)
        pieces["far outward", stream] = along(pieces["far inner", stream], outward)
        if stream == lead:
            pieces["slab", stream] = apply([], early, 1)[0]
        else:
            pieces["slab", stream] = apply([pieces["slab", lead]], later, 1)[0]
        close(stream, ("next", 2), "far outward", "slab")
    for stream in (lead, last):
        from_far = jnp.where(at_ends, pieces["far outward", stream], pieces["far inner", stream])
        pieces[("far", 0), stream] = from_far
        pieces[("far", 2), stream] = across(from_far)
    slab, pieces[("far", 2), lead] = together((pieces["slab", last], pieces[("far", 2), lead]))
    slab = [sibling(chunk) for chunk in apply([slab], late, 2)]
    result = apply([pieces["result", last]], later + late)
    for stream in (lead, last):
        if stream == last:
            arriving, result, twin = together(
                (pieces[("far", 2), stream], result, pieces[("far", 3), lead])
            )
            pieces[("far", 2), stream], pieces[("far", 3), lead] = arriving, twin
        pieces[("far", 3), stream] = sibling(pieces[("far", 2), stream])
    return apply([result] + slab, [("far", 2), ("far", 3)])


def solution(mesh):
    return jax.shard_map(
        per_device,
        mesh=mesh,
        in_specs=(
            P(None, ("groups", "ty"), None),
            P(),
            P(("groups", "ty"), None, None),
            P("groups"),
            P("groups"),
        ),
        out_specs=P(None, ("groups", "ty"), None),
        check_vma=False,
    )
```

```python
import functools
import math

import jax
import jax.numpy as jnp
import numpy as np
from jax import lax
from jax.experimental import pallas as pl
from jax.experimental.pallas import tpu as pltpu
from jax.sharding import PartitionSpec as P

step_size = 0.5
lane = 128
row_tile = 16
vmem_bytes = 32 * 1024 * 1024
backward_bytes = 40 * 1024 * 1024


def fourier_tables(crop_width):
    counter = np.arange(crop_width, dtype=np.int64)
    angle = (counter[:, None] * counter[None, :] % crop_width) * (2.0 * math.pi / crop_width)
    factor = 1.0 / math.sqrt(crop_width)
    cos_table = (np.cos(angle) * factor).astype(np.float32).astype(jnp.bfloat16)
    sin_table = (np.sin(angle) * factor).astype(np.float32).astype(jnp.bfloat16)
    return cos_table, sin_table


def tile_weight(pupil_ref, first_row, win):
    start = win.row(first_row)
    rows = pupil_ref[pl.ds(start, win.rows), :].astype(jnp.float32)
    rows = pltpu.roll(rows, (2 * win.rows + start - first_row) % win.rows, 0)
    shape = (win.tile_rows, win.crop_width)
    row = 2 * (first_row + lax.broadcasted_iota(jnp.int32, shape, 0)) - win.crop_width + 1
    column = 2 * lax.broadcasted_iota(jnp.int32, shape, 1) - win.crop_width + 1
    inside = row * row + column * column <= win.crop_width * win.crop_width
    return jnp.where(inside, rows[: win.tile_rows], 0.0)


def tile_band(band_ref, first_row, win):
    start = win.row(first_row)
    rows = band_ref[pl.ds(start, win.rows), :].astype(jnp.float32)
    rows = pltpu.roll(rows, (2 * win.rows + start - first_row) % win.rows, 0)[: win.tile_rows]
    band = rows.shape[1] // 2
    turned = jnp.concatenate([-rows[:, band:], rows[:, :band]], axis=1)
    return jnp.concatenate([rows, turned], axis=0).astype(jnp.bfloat16)


class Windows:
    def __init__(self, tile_rows, slab_columns, crop_width):
        self.tile_rows = tile_rows
        self.crop_width = crop_width
        self.rows = tile_rows + row_tile
        self.columns = crop_width + lane
        self.last_row = crop_width - self.rows
        self.last_column = slab_columns - self.columns

    def row(self, first_row):
        start = jnp.clip(first_row, 0, self.last_row) // row_tile * row_tile
        return pl.multiple_of(start, row_tile)

    def column(self, left):
        start = jnp.minimum(left // lane * lane, self.last_column)
        return pl.multiple_of(start, lane)

    def active(self, first_row):
        return (first_row > -self.tile_rows) & (first_row < self.crop_width)


def image_band(meta_ref, slot, lows, tiles, pupil_ref, band_ref, win, store, came=None):
    left = meta_ref[meta_ref.shape[0] - 1, slot]
    first_rows = [meta_ref[tile, slot] for tile in tiles]
    active = functools.reduce(jnp.logical_or, [win.active(row) for row in first_rows])
    band = band_ref.shape[1] // 2
    shape = (2, band, win.crop_width)

    @pl.when(jnp.logical_not(active))
    def _():
        store(jnp.zeros(shape, jnp.bfloat16) if came is None else came[...])

    @pl.when(active)
    def _():
        col_start = win.column(left)
        shift = (win.columns - (left - col_start)) % win.columns
        parts, tables = [], []
        for first_row, low_refs in zip(first_rows, lows):
            weight = tile_weight(pupil_ref, first_row, win)
            for low_ref in low_refs:
                low = low_ref[:, pl.ds(col_start, win.columns)].astype(jnp.float32)
                low = pltpu.roll(low, shift, 1)[:, : win.crop_width]
                parts.append((weight * low).astype(jnp.bfloat16))
            tables.append(tile_band(band_ref, first_row, win))
        mid = lax.dot_general(
            jnp.concatenate(tables, axis=0),
            jnp.concatenate(parts, axis=0),
            (((0,), (0,)), ((), ())),
            preferred_element_type=jnp.float32,
        )
        if came is not None:
            mid = mid + came[...].reshape(mid.shape).astype(jnp.float32)
        store(mid.astype(jnp.bfloat16).reshape(shape))


def forward_kernel(meta_ref, pupil_ref, band_ref, *refs, base, images, count, win, tiles):
    out_refs = refs[-count:]
    lows = [refs[2 * half : 2 * half + 2] for half in range(len(tiles))]
    came = refs[2 * len(tiles)] if len(refs) > 2 * len(tiles) + count else None
    streams = count // images

    def image(index):
        def store(value):
            for number in range(images):

                @pl.when(index == number)
                def _():
                    for stream in range(streams):
                        out_ref = out_refs[number * streams + stream]
                        rows = out_ref.shape[1]
                        out_ref[...] = value[:, stream * rows : (stream + 1) * rows]

        image_band(meta_ref, base + index, lows, tiles, pupil_ref, band_ref, win, store, came)

    pl.loop(0, images)(image)


def forward_grid_kernel(meta_ref, pupil_ref, band_ref, real_ref, imag_ref, out_ref, *, win):
    def store(value):
        out_ref[0] = value

    lows = [(real_ref, imag_ref)]
    image_band(meta_ref, pl.program_id(0), lows, (0,), pupil_ref, band_ref, win, store)


def subtract_image(meta_ref, slot, back_refs, pupil_ref, band_ref, out_ref, win, tile=0):
    first_row, left = meta_ref[tile, slot], meta_ref[meta_ref.shape[0] - 1, slot]
    tile_rows, crop_width = win.tile_rows, win.crop_width

    @pl.when(win.active(first_row))
    def _():
        col_start = win.column(left)
        weight = tile_weight(pupil_ref, first_row, win) * step_size
        table = tile_band(band_ref, first_row, win)
        band = table.shape[1] // 2
        rows = band // len(back_refs)
        held = [number for number, ref in enumerate(back_refs) if ref is not None]
        if len(held) < len(back_refs):
            starts = [part * band + number * rows for part in range(2) for number in held]
            table = jnp.concatenate([table[:, start : start + rows] for start in starts], axis=1)
        back = [back_refs[number][part] for part in range(2) for number in held]
        back = jnp.concatenate(back, axis=0)
        grad = jnp.dot(table, back, preferred_element_type=jnp.float32)
        columns = pl.ds(col_start, win.columns)
        pad = jnp.zeros((tile_rows, win.columns - crop_width), jnp.float32)
        for part in range(2):
            piece = grad[part * tile_rows : (part + 1) * tile_rows] * weight
            piece = pltpu.roll(jnp.concatenate([piece, pad], axis=1), left - col_start, 1)
            out_ref[part, :, columns] = out_ref[part, :, columns] - piece


def backward_kernel(meta_ref, pupil_ref, band_ref, *refs, slots, held, parts, win):
    part_refs, back_refs, out_ref = refs[:parts], iter(refs[parts:-1]), refs[-1]
    start = 0
    for chunk_ref in part_refs[1:]:
        columns = slice(start, start + chunk_ref.shape[2])
        out_ref[:, :, columns] = part_refs[0][:, :, columns] + chunk_ref[...].astype(jnp.float32)
        start = columns.stop
    if parts == 1:
        out_ref[...] = part_refs[0][...]
    for slot, groups in zip(slots, held):
        of_image = [next(back_refs) if there else None for there in groups]
        subtract_image(meta_ref, slot, of_image, pupil_ref, band_ref, out_ref, win)


def sibling_kernel(meta_ref, pupil_ref, band_ref, *refs, slots, held, parts, win):
    backs = sum(map(sum, held))
    part_refs, back_refs, total_ref = refs[:parts], iter(refs[parts : parts + backs]), refs[-1]
    out_refs = refs[parts + backs : -1]
    if parts:
        total_ref[...] = part_refs[0][...].astype(jnp.float32)
    else:
        total_ref[...] = jnp.zeros_like(total_ref)
    for slot, groups in zip(slots, held):
        of_image = [next(back_refs) if there else None for there in groups]
        subtract_image(meta_ref, slot, of_image, pupil_ref, band_ref, total_ref, win, 1)
    start = 0
    for out_ref in out_refs:
        end = start + out_ref.shape[2]
        out_ref[...] = total_ref[:, :, start:end].astype(jnp.bfloat16)
        start = end


def backward_grid_kernel(meta_ref, pupil_ref, band_ref, spec_ref, back_ref, out_ref, *, win):
    step = pl.program_id(0)

    @pl.when(step == 0)
    def _():
        out_ref[...] = spec_ref[...]

    subtract_image(meta_ref, step, [back_ref.at[0]], pupil_ref, band_ref, out_ref, win)


def middle_kernel(*refs, terms, streams):
    term_refs, refs = refs[: terms * streams], refs[terms * streams :]
    (image_ref, cos_ref, sin_ref), refs = refs[:3], refs[3:]
    out_refs, (mid_ref, resid_ref) = refs[:streams], refs[streams:]
    _, rows, crop_width = term_refs[0].shape
    band = rows * streams
    block = min(512, crop_width)
    for stream in range(streams):
        of_stream = term_refs[stream * terms : (stream + 1) * terms]
        total = sum(ref[...].astype(jnp.float32) for ref in of_stream).astype(jnp.bfloat16)
        for part in range(2):
            start = part * band + stream * rows
            mid_ref[start : start + rows] = total[part]
    dot = functools.partial(jnp.dot, preferred_element_type=jnp.float32)
    for start in range(0, crop_width, block):
        columns = slice(start, start + block)
        by_cos = dot(mid_ref[...], cos_ref[:, columns])
        by_sin = dot(mid_ref[...], sin_ref[:, columns])
        field_real = by_cos[:band] - by_sin[band:]
        field_imag = by_sin[:band] + by_cos[band:]
        power = field_real * field_real + field_imag * field_imag
        measured = image_ref[0, :, columns].astype(jnp.float32)
        keeping = 1.0 - measured * lax.rsqrt(jnp.maximum(power, 1.0))
        resid_ref[:band, columns] = (field_real * keeping).astype(jnp.bfloat16)
        resid_ref[band:, columns] = (field_imag * keeping).astype(jnp.bfloat16)
    for start in range(0, crop_width, block):
        columns = slice(start, start + block)
        by_cos = dot(resid_ref[...], cos_ref[:, columns])
        by_sin = dot(resid_ref[...], sin_ref[:, columns])
        for part, back in enumerate((by_cos[:band] + by_sin[band:], by_cos[band:] - by_sin[:band])):
            for stream, out_ref in enumerate(out_refs):
                of_stream = back[stream * rows : (stream + 1) * rows]
                out_ref[part, :, columns] = of_stream.astype(jnp.bfloat16)


def params():
    return pltpu.CompilerParams(vmem_limit_bytes=vmem_bytes)


def light():
    return pl.CostEstimate(flops=1024, bytes_accessed=1024, transcendentals=0)


vmem = pl.BlockSpec(memory_space=pltpu.VMEM)
smem = pl.BlockSpec(memory_space=pltpu.SMEM)


def band_type(pupil, band_table, *lead):
    shape = lead + (2, band_table.shape[1] // 2, pupil.shape[1])
    return jax.ShapeDtypeStruct(shape, jnp.bfloat16)


def forward(meta, lows, pupil, band_table, base, images, tiles=(0, 1), came=None, streams=1):
    win = Windows(*lows[0][0].shape, pupil.shape[1])
    operands = [meta, pupil, band_table] + [part for low in lows for part in low]
    operands += [came] * (came is not None)
    count = images * streams
    _, rows, columns = band_type(pupil, band_table).shape
    return pl.pallas_call(
        functools.partial(
            forward_kernel, base=base, images=images, count=count, win=win, tiles=tiles
        ),
        in_specs=[smem] + [vmem] * (len(operands) - 1),
        out_specs=[vmem] * count,
        out_shape=[jax.ShapeDtypeStruct((2, rows // streams, columns), jnp.bfloat16)] * count,
        compiler_params=params(),
        cost_estimate=light(),
        name="forward",
    )(*operands)


def backward(meta, shape, pupil, band_table, parts, slots, backs, chunks=0):
    win = Windows(*shape[1:], pupil.shape[1])
    held = [[back is not None for back in groups] for groups in backs]
    operands = list(parts) + [back for groups in backs for back in groups if back is not None]
    kernel = sibling_kernel if chunks else backward_kernel
    out_shape = jax.ShapeDtypeStruct(shape, jnp.float32)
    if chunks:
        cuts = [shape[2] // lane * number // chunks * lane for number in range(chunks + 1)]
        out_shape = [
            jax.ShapeDtypeStruct(shape[:2] + (end - start,), jnp.bfloat16)
            for start, end in zip(cuts, cuts[1:])
        ]
    return pl.pallas_call(
        functools.partial(kernel, slots=slots, held=held, parts=len(parts), win=win),
        in_specs=[smem] + [vmem] * (2 + len(operands)),
        out_specs=[vmem] * chunks if chunks else vmem,
        out_shape=out_shape,
        scratch_shapes=[pltpu.VMEM(shape, jnp.float32)] * (chunks > 0),
        compiler_params=pltpu.CompilerParams(vmem_limit_bytes=backward_bytes),
        cost_estimate=light(),
        name="backward",
    )(meta, pupil, band_table, *operands)


def middle(streams, image, cos_table, sin_table):
    _, rows, crop_width = streams[0][0].shape
    band = rows * len(streams)
    terms = [term for stream in streams for term in stream]
    return pl.pallas_call(
        functools.partial(
            middle_kernel, terms=len(streams[0]), streams=len(streams)
        ),
        in_specs=[vmem] * (len(terms) + 3),
        out_specs=[vmem] * len(streams),
        out_shape=[jax.ShapeDtypeStruct((2, rows, crop_width), jnp.bfloat16)] * len(streams),
        scratch_shapes=[pltpu.VMEM((2 * band, crop_width), jnp.bfloat16)] * 2,
        compiler_params=params(),
        cost_estimate=light(),
        name="middle",
    )(*terms, image, cos_table, sin_table)


def fixed(array):
    return pl.BlockSpec(array.shape, lambda i: (0,) * array.ndim)


def forward_all(meta, low, pupil, band_table):
    win = Windows(*low[0].shape, pupil.shape[1])
    count = meta.shape[1]
    out_type = band_type(pupil, band_table, count)
    return pl.pallas_call(
        functools.partial(forward_grid_kernel, win=win),
        grid=(count,),
        in_specs=[smem] + [fixed(array) for array in (pupil, band_table, *low)],
        out_specs=pl.BlockSpec((1,) + out_type.shape[1:], lambda i: (i, 0, 0, 0)),
        out_shape=out_type,
        compiler_params=params(),
        name="forward_all",
    )(meta, pupil, band_table, *low)


def backward_all(meta, spectrum, pupil, band_table, backs):
    win = Windows(*spectrum.shape[1:], pupil.shape[1])
    return pl.pallas_call(
        functools.partial(backward_grid_kernel, win=win),
        grid=(meta.shape[1],),
        in_specs=[smem]
        + [fixed(array) for array in (pupil, band_table, spectrum)]
        + [pl.BlockSpec((1,) + backs.shape[1:], lambda i: (i, 0, 0, 0))],
        out_specs=fixed(spectrum),
        out_shape=jax.ShapeDtypeStruct(spectrum.shape, jnp.float32),
        compiler_params=params(),
        name="backward_all",
    )(meta, pupil, band_table, spectrum, backs)


def cast_kernel(spec_ref, out_ref, held, sems, *, part):
    blocks, _, width = held.shape
    columns = [pl.ds(block * width, width) for block in range(blocks)]
    copies = [
        pltpu.make_async_copy(spec_ref.at[part, :, columns[i]], held.at[i], sems.at[i])
        for i in range(blocks)
    ]
    for copy in copies:
        copy.start()
    for i, copy in enumerate(copies):
        copy.wait()
        out_ref[:, columns[i]] = held[i].astype(jnp.bfloat16)


def low_part(spectrum, part):
    _, rows, columns = spectrum.shape
    return pl.pallas_call(
        functools.partial(cast_kernel, part=part),
        in_specs=[pl.BlockSpec(memory_space=pltpu.HBM)],
        out_specs=vmem,
        out_shape=jax.ShapeDtypeStruct((rows, columns), jnp.bfloat16),
        scratch_shapes=[
            pltpu.VMEM((4, rows, columns // 4), jnp.float32),
            pltpu.SemaphoreType.DMA((4,)),
        ],
        compiler_params=params(),
        cost_estimate=light(),
        name="low_part",
    )(spectrum)


def total(*terms):
    return sum(term.astype(jnp.float32) for term in terms).astype(jnp.bfloat16)


def per_device(spectrum, pupil, measured, centre_rows, centre_cols):
    count = lax.axis_size("ty")
    planes = count // 4
    position = lax.axis_index("ty")
    plane = position // 4
    _, tile_rows, slab_columns = spectrum.shape
    crop_width = pupil.shape[0]
    band = measured.shape[1]
    band_start = (crop_width - band) // 2
    cos_table, sin_table = fourier_tables(crop_width)
    chosen_rows = slice(band_start, band_start + band)
    band_table = jnp.asarray(
        np.concatenate([cos_table[:, chosen_rows], sin_table[:, chosen_rows]], axis=1)
    )
    cos_table, sin_table = jnp.asarray(cos_table), jnp.asarray(sin_table)

    half = crop_width // 2

    low = [low_part(spectrum, part) for part in range(2)]

    def image_meta(ids, positions):
        match = ids[:, None] == jnp.arange(count, dtype=jnp.int32)[None, :]
        tops = jnp.sum(jnp.where(match, centre_rows[None, :], 0), axis=1) - half
        lefts = jnp.sum(jnp.where(match, centre_cols[None, :], 0), axis=1) - half
        rows = [place * tile_rows - tops for place in positions]
        return jnp.stack(rows + [lefts]).astype(jnp.int32)

    if planes != 4:
        meta = image_meta(jnp.arange(count, dtype=jnp.int32), [position])
        partial = forward_all(meta, low, pupil, band_table)
        mid = lax.psum_scatter(partial, "ty", scatter_dimension=0, tiled=True)[0]
        back = lax.all_gather(middle([[mid]], measured, cos_table, sin_table)[0], "ty")
        return backward_all(meta, spectrum, pupil, band_table, back)

    targets = {"far": (3, 3, 0, 0), "next": (2, 2, 1, 1), "beside": (1, 0, 3, 2), "own": (0, 1, 2, 3)}
    own_core = [("far", 2), ("far", 0), ("next", 2), ("next", 0)]
    own_core += [("beside", 2), ("beside", 0), ("own", 2), ("own", 0)]
    slots = {}
    for core in (0, 1):
        for name, y in own_core:
            slots[name, y + core] = len(slots)
    ids = [
        [targets[name][i // 4] * 4 + (i % 4 ^ flip) for (name, flip) in slots]
        for i in range(count)
    ]
    my_ids = lax.dynamic_index_in_dim(jnp.asarray(ids, jnp.int32), position, keepdims=False)
    meta = image_meta(my_ids, [position, position ^ 1])

    def sibling(value):
        return lax.ppermute(value, "ty", [(i, i ^ 1) for i in range(count)])

    def across(value):
        return lax.ppermute(value, "ty", [(i, i ^ 2) for i in range(count)])

    def along(value, plane_pairs):
        pairs = [(4 * a + i, 4 * b + i) for a, b in plane_pairs for i in range(4)]
        return lax.ppermute(value, "ty", pairs)

    inward = [(0, 1), (3, 2)]
    outward = [(1, 0), (2, 3)]
    inner = [(1, 2), (2, 1)]
    together = lax.optimization_barrier

    lows = [low, [sibling(part) for part in low]]
    streams = 2
    (own_rows,) = forward(meta, lows[:1], pupil, band_table, 0, 1, (0,))
    far_leaving = forward(
        meta, lows[1:], pupil, band_table, 0, 1, (1,), own_rows, streams=streams
    )
    far_other = [across(value) for value in far_leaving]
    made = forward(
        together((meta, far_leaving[0]))[0], lows, pupil, band_table, 1, 7, streams=streams
    )
    summed, held = [], None
    for stream in reversed(range(streams)):
        (
            far_kept,
            next_leaving,
            next_kept,
            beside_leaving,
            beside_kept,
            own_leaving,
            own_kept,
        ) = made[stream::streams]
        far, far_kept, next_leaving = together((far_other[stream], far_kept, next_leaving))

        next_other = across(next_leaving)
        from_end = along(total(far_kept, far), inward)
        from_end, next_other, beside_leaving = together((from_end, next_other, beside_leaving))

        beside_other = across(beside_leaving)
        next_inward = along(total(next_kept, next_other), inward)
        far_inner = along(total(far_kept, far, from_end), inner)
        far_inner, next_inward, beside_other, own_leaving = together(
            (far_inner, next_inward, beside_other, own_leaving)
        )

        own_other = across(own_leaving)
        next_inner = along(total(next_kept, next_other, next_inward), inner)
        beside = along(total(beside_kept, beside_other, far_inner), inward + outward)
        terms = [own_kept, own_other, next_inner, beside]
        if stream > 0:
            terms = [total(*terms)]
            held = terms[0]
        else:
            terms[0] = together((terms[0], held))[0]
            terms = [total(*terms)]
        summed.insert(0, terms)
    backs = middle(summed, measured, cos_table, sin_table)

    at_ends = (plane == 0) | (plane == 3)
    lead, last = streams - 1, 0
    pieces = {}

    def apply(parts, names, chunks=0):
        taken = [[pieces.get((name, stream)) for stream in range(streams)] for name in names]
        own_slots = [slots[name] for name in names]
        shape = spectrum.shape
        return backward(meta, shape, pupil, band_table, parts, own_slots, taken, chunks)

    def close(stream, *names):
        closed = together(tuple(pieces[name, stream] for name in names))
        for name, value in zip(names, closed):
            pieces[name, stream] = value

    early, later, late = (
        [("beside", 0), ("own", 2)],
        [("next", 0), ("beside", 2)],
        [("far", 0), ("next", 2)],
    )
    for stream in (lead, last):
        back = pieces[("own", 0), stream] = backs[stream]
        pieces[("own", 2), stream] = across(back)
        pieces["inner", stream] = along(back, inner)
        pieces[("beside", 0), stream] = along(back, inward + outward)
        close(stream, ("own", 2), "inner", ("beside", 0))
    result = apply([spectrum], [("own", 0)])
    pieces["inner", last], result = together((pieces["inner", last], result))
    for stream in (lead, last):
        pieces[("beside", 2), stream] = across(pieces[("beside", 0), stream])
        pieces["far inner", stream] = along(pieces[("beside", 0), stream], inner)
        pieces["outward", stream] = along(pieces["inner", stream], outward)
        if stream == lead:
            pieces["sum", stream] = apply([], [("own", 0)] + early, 1)[0]
        else:
            pieces["sum", stream] = apply([result], early)
        close(stream, ("beside", 2), "far inner", "outward", "sum")
    slab, result = pieces["sum", lead], pieces["sum", last]
    for stream in (lead, last):
        from_next = jnp.where(at_ends, pieces["outward", stream], pieces["inner", stream])
        pieces[("next", 0), stream] = from_next
        pieces[("next", 2), stream] = across(from_next)
        pieces["far outward", stream] = along(pieces["far inner", stream], outward)
        if stream == last:
            pieces["slab", stream] = apply([slab], later, 1)[0]
            pieces["sum", stream] = apply([result], later)
            close(stream, ("next", 2), "far outward", "slab", "sum")
        else:
            close(stream, ("next", 2), "far outward")
    slab, result = pieces["slab", last], pieces["sum", last]
    for stream in (lead, last):
        from_far = jnp.where(at_ends, pieces["far outward", stream], pieces["far inner", stream])
        pieces[("far", 0), stream] = from_far
        pieces[("far", 2), stream] = across(from_far)
    far_other = pieces[("far", 2), lead]
    slab, far_other = together((slab, far_other))
    chunks = apply([slab], late, 4)
    twin = sibling(far_other)
    slab = [sibling(chunk) for chunk in chunks[:-1]]
    result, twin = together((result, twin))
    result = apply([result], late)
    chunk, result = together((chunks[-1], result))
    slab.append(sibling(chunk))
    arriving, result = together((pieces[("far", 2), last], result))
    pieces[("far", 2), lead], pieces[("far", 3), lead] = far_other, twin
    pieces[("far", 2), last], pieces[("far", 3), last] = arriving, sibling(arriving)
    return apply([result] + slab, [("far", 2), ("far", 3)])


def solution(mesh):
    return jax.shard_map(
        per_device,
        mesh=mesh,
        in_specs=(
            P(None, ("groups", "ty"), None),
            P(),
            P(("groups", "ty"), None, None),
            P("groups"),
            P("groups"),
        ),
        out_specs=P(None, ("groups", "ty"), None),
        check_vma=False,
    )
```

```python
import functools
import math

import jax
import jax.numpy as jnp
import numpy as np
from jax import lax
from jax.experimental import pallas as pl
from jax.experimental.pallas import tpu as pltpu
from jax.sharding import PartitionSpec as P

step_size = 0.5
lane = 128
row_tile = 16
vmem_bytes = 20 * 1024 * 1024
backward_bytes = 20 * 1024 * 1024


def fourier_tables(crop_width):
    counter = np.arange(crop_width, dtype=np.int64)
    angle = (counter[:, None] * counter[None, :] % crop_width) * (2.0 * math.pi / crop_width)
    factor = 1.0 / math.sqrt(crop_width)
    cos_table = (np.cos(angle) * factor).astype(np.float32).astype(jnp.bfloat16)
    sin_table = (np.sin(angle) * factor).astype(np.float32).astype(jnp.bfloat16)
    return cos_table, sin_table


def tile_weight(pupil_ref, first_row, win):
    start = win.row(first_row)
    rows = pupil_ref[pl.ds(start, win.rows), :].astype(jnp.float32)
    rows = pltpu.roll(rows, (2 * win.rows + start - first_row) % win.rows, 0)
    shape = (win.tile_rows, win.crop_width)
    row = 2 * (first_row + lax.broadcasted_iota(jnp.int32, shape, 0)) - win.crop_width + 1
    column = 2 * lax.broadcasted_iota(jnp.int32, shape, 1) - win.crop_width + 1
    inside = row * row + column * column <= win.crop_width * win.crop_width
    return jnp.where(inside, rows[: win.tile_rows], 0.0)


def tile_band(band_ref, first_row, win):
    start = win.row(first_row)
    rows = band_ref[pl.ds(start, win.rows), :].astype(jnp.float32)
    rows = pltpu.roll(rows, (2 * win.rows + start - first_row) % win.rows, 0)[: win.tile_rows]
    band = rows.shape[1] // 2
    turned = jnp.concatenate([-rows[:, band:], rows[:, :band]], axis=1)
    return jnp.concatenate([rows, turned], axis=0).astype(jnp.bfloat16)


class Windows:
    def __init__(self, tile_rows, slab_columns, crop_width):
        self.tile_rows = tile_rows
        self.crop_width = crop_width
        self.rows = tile_rows + row_tile
        self.columns = crop_width + lane
        self.last_row = crop_width - self.rows
        self.last_column = slab_columns - self.columns

    def row(self, first_row):
        start = jnp.clip(first_row, 0, self.last_row) // row_tile * row_tile
        return pl.multiple_of(start, row_tile)

    def column(self, left):
        start = jnp.minimum(left // lane * lane, self.last_column)
        return pl.multiple_of(start, lane)

    def active(self, first_row):
        return (first_row > -self.tile_rows) & (first_row < self.crop_width)


def image_band(meta_ref, slot, lows, tiles, pupil_ref, band_ref, win, store, came=None):
    left = meta_ref[meta_ref.shape[0] - 1, slot]
    first_rows = [meta_ref[tile, slot] for tile in tiles]
    active = functools.reduce(jnp.logical_or, [win.active(row) for row in first_rows])
    band = band_ref.shape[1] // 2
    shape = (2, band, win.crop_width)

    @pl.when(jnp.logical_not(active))
    def _():
        store(jnp.zeros(shape, jnp.bfloat16) if came is None else came[...])

    @pl.when(active)
    def _():
        col_start = win.column(left)
        shift = (win.columns - (left - col_start)) % win.columns
        parts, tables = [], []
        for first_row, low_refs in zip(first_rows, lows):
            weight = tile_weight(pupil_ref, first_row, win)
            for low_ref in low_refs:
                low = low_ref[:, pl.ds(col_start, win.columns)].astype(jnp.float32)
                low = pltpu.roll(low, shift, 1)[:, : win.crop_width]
                parts.append((weight * low).astype(jnp.bfloat16))
            tables.append(tile_band(band_ref, first_row, win))
        mid = lax.dot_general(
            jnp.concatenate(tables, axis=0),
            jnp.concatenate(parts, axis=0),
            (((0,), (0,)), ((), ())),
            preferred_element_type=jnp.float32,
        )
        if came is not None:
            mid = mid + came[...].reshape(mid.shape).astype(jnp.float32)
        store(mid.astype(jnp.bfloat16).reshape(shape))


def forward_kernel(meta_ref, pupil_ref, band_ref, *refs, base, images, count, win, tiles):
    out_refs = refs[-count:]
    lows = [refs[2 * half : 2 * half + 2] for half in range(len(tiles))]
    came = refs[2 * len(tiles)] if len(refs) > 2 * len(tiles) + count else None
    streams = count // images

    def image(index):
        def store(value):
            for number in range(images):

                @pl.when(index == number)
                def _():
                    for stream in range(streams):
                        out_ref = out_refs[number * streams + stream]
                        rows = out_ref.shape[1]
                        out_ref[...] = value[:, stream * rows : (stream + 1) * rows]

        image_band(meta_ref, base + index, lows, tiles, pupil_ref, band_ref, win, store, came)

    pl.loop(0, images)(image)


def forward_grid_kernel(meta_ref, pupil_ref, band_ref, real_ref, imag_ref, out_ref, *, win):
    def store(value):
        out_ref[0] = value

    lows = [(real_ref, imag_ref)]
    image_band(meta_ref, pl.program_id(0), lows, (0,), pupil_ref, band_ref, win, store)


def subtract_image(meta_ref, slot, back_refs, pupil_ref, band_ref, out_ref, win, tile=0):
    first_row, left = meta_ref[tile, slot], meta_ref[meta_ref.shape[0] - 1, slot]
    tile_rows, crop_width = win.tile_rows, win.crop_width

    @pl.when(win.active(first_row))
    def _():
        col_start = win.column(left)
        weight = tile_weight(pupil_ref, first_row, win) * step_size
        table = tile_band(band_ref, first_row, win)
        band = table.shape[1] // 2
        rows = band // len(back_refs)
        held = [number for number, ref in enumerate(back_refs) if ref is not None]
        if len(held) < len(back_refs):
            starts = [part * band + number * rows for part in range(2) for number in held]
            table = jnp.concatenate([table[:, start : start + rows] for start in starts], axis=1)
        back = [back_refs[number][part] for part in range(2) for number in held]
        back = jnp.concatenate(back, axis=0)
        grad = jnp.dot(table, back, preferred_element_type=jnp.float32)
        columns = pl.ds(col_start, win.columns)
        pad = jnp.zeros((tile_rows, win.columns - crop_width), jnp.float32)
        for part in range(2):
            piece = grad[part * tile_rows : (part + 1) * tile_rows] * weight
            piece = pltpu.roll(jnp.concatenate([piece, pad], axis=1), left - col_start, 1)
            out_ref[part, :, columns] = out_ref[part, :, columns] - piece


def backward_kernel(meta_ref, pupil_ref, band_ref, *refs, slots, held, parts, win):
    part_refs, back_refs, out_ref = refs[:parts], iter(refs[parts:-1]), refs[-1]
    start = 0
    for chunk_ref in part_refs[1:]:
        columns = slice(start, start + chunk_ref.shape[2])
        out_ref[:, :, columns] = part_refs[0][:, :, columns] + chunk_ref[...].astype(jnp.float32)
        start = columns.stop
    if parts == 1:
        out_ref[...] = part_refs[0][...]
    for slot, groups in zip(slots, held):
        of_image = [next(back_refs) if there else None for there in groups]
        subtract_image(meta_ref, slot, of_image, pupil_ref, band_ref, out_ref, win)


def sibling_kernel(meta_ref, pupil_ref, band_ref, *refs, slots, held, parts, win):
    backs = sum(map(sum, held))
    part_refs, back_refs, total_ref = refs[:parts], iter(refs[parts : parts + backs]), refs[-1]
    out_refs = refs[parts + backs : -1]
    if parts:
        total_ref[...] = part_refs[0][...].astype(jnp.float32)
    else:
        total_ref[...] = jnp.zeros_like(total_ref)
    for slot, groups in zip(slots, held):
        of_image = [next(back_refs) if there else None for there in groups]
        subtract_image(meta_ref, slot, of_image, pupil_ref, band_ref, total_ref, win, 1)
    start = 0
    for out_ref in out_refs:
        end = start + out_ref.shape[2]
        out_ref[...] = total_ref[:, :, start:end].astype(jnp.bfloat16)
        start = end


def backward_grid_kernel(meta_ref, pupil_ref, band_ref, spec_ref, back_ref, out_ref, *, win):
    step = pl.program_id(0)

    @pl.when(step == 0)
    def _():
        out_ref[...] = spec_ref[...]

    subtract_image(meta_ref, step, [back_ref.at[0]], pupil_ref, band_ref, out_ref, win)


def middle_kernel(*refs, terms, streams):
    term_refs, refs = refs[: terms * streams], refs[terms * streams :]
    (image_ref, cos_ref, sin_ref), refs = refs[:3], refs[3:]
    out_refs, (mid_ref, resid_ref) = refs[:streams], refs[streams:]
    _, rows, crop_width = term_refs[0].shape
    band = rows * streams
    block = min(512, crop_width)
    for stream in range(streams):
        of_stream = term_refs[stream * terms : (stream + 1) * terms]
        total = sum(ref[...].astype(jnp.float32) for ref in of_stream).astype(jnp.bfloat16)
        for part in range(2):
            start = part * band + stream * rows
            mid_ref[start : start + rows] = total[part]
    dot = functools.partial(jnp.dot, preferred_element_type=jnp.float32)
    for start in range(0, crop_width, block):
        columns = slice(start, start + block)
        by_cos = dot(mid_ref[...], cos_ref[:, columns])
        by_sin = dot(mid_ref[...], sin_ref[:, columns])
        field_real = by_cos[:band] - by_sin[band:]
        field_imag = by_sin[:band] + by_cos[band:]
        power = field_real * field_real + field_imag * field_imag
        measured = image_ref[0, :, columns].astype(jnp.float32)
        keeping = 1.0 - measured * lax.rsqrt(jnp.maximum(power, 1.0))
        resid_ref[:band, columns] = (field_real * keeping).astype(jnp.bfloat16)
        resid_ref[band:, columns] = (field_imag * keeping).astype(jnp.bfloat16)
    for start in range(0, crop_width, block):
        columns = slice(start, start + block)
        by_cos = dot(resid_ref[...], cos_ref[:, columns])
        by_sin = dot(resid_ref[...], sin_ref[:, columns])
        for part, back in enumerate((by_cos[:band] + by_sin[band:], by_cos[band:] - by_sin[:band])):
            for stream, out_ref in enumerate(out_refs):
                of_stream = back[stream * rows : (stream + 1) * rows]
                out_ref[part, :, columns] = of_stream.astype(jnp.bfloat16)


def params():
    return pltpu.CompilerParams(vmem_limit_bytes=vmem_bytes)


def light():
    return pl.CostEstimate(flops=1024, bytes_accessed=1024, transcendentals=0)


vmem = pl.BlockSpec(memory_space=pltpu.VMEM)
smem = pl.BlockSpec(memory_space=pltpu.SMEM)


def band_type(pupil, band_table, *lead):
    shape = lead + (2, band_table.shape[1] // 2, pupil.shape[1])
    return jax.ShapeDtypeStruct(shape, jnp.bfloat16)


def forward(meta, lows, pupil, band_table, base, images, tiles=(0, 1), came=None, streams=1):
    win = Windows(*lows[0][0].shape, pupil.shape[1])
    operands = [meta, pupil, band_table] + [part for low in lows for part in low]
    operands += [came] * (came is not None)
    count = images * streams
    _, rows, columns = band_type(pupil, band_table).shape
    return pl.pallas_call(
        functools.partial(
            forward_kernel, base=base, images=images, count=count, win=win, tiles=tiles
        ),
        in_specs=[smem] + [vmem] * (len(operands) - 1),
        out_specs=[vmem] * count,
        out_shape=[jax.ShapeDtypeStruct((2, rows // streams, columns), jnp.bfloat16)] * count,
        compiler_params=params(),
        cost_estimate=light(),
        name="forward",
    )(*operands)


def backward(meta, shape, pupil, band_table, parts, slots, backs, chunks=0):
    win = Windows(*shape[1:], pupil.shape[1])
    held = [[back is not None for back in groups] for groups in backs]
    operands = list(parts) + [back for groups in backs for back in groups if back is not None]
    kernel = sibling_kernel if chunks else backward_kernel
    out_shape = jax.ShapeDtypeStruct(shape, jnp.float32)
    if chunks:
        cuts = [shape[2] // lane * number // chunks * lane for number in range(chunks + 1)]
        out_shape = [
            jax.ShapeDtypeStruct(shape[:2] + (end - start,), jnp.bfloat16)
            for start, end in zip(cuts, cuts[1:])
        ]
    return pl.pallas_call(
        functools.partial(kernel, slots=slots, held=held, parts=len(parts), win=win),
        in_specs=[smem] + [vmem] * (2 + len(operands)),
        out_specs=[vmem] * chunks if chunks else vmem,
        out_shape=out_shape,
        scratch_shapes=[pltpu.VMEM(shape, jnp.float32)] * (chunks > 0),
        compiler_params=pltpu.CompilerParams(vmem_limit_bytes=backward_bytes),
        cost_estimate=light(),
        name="backward",
    )(meta, pupil, band_table, *operands)


def middle(streams, image, cos_table, sin_table):
    _, rows, crop_width = streams[0][0].shape
    band = rows * len(streams)
    terms = [term for stream in streams for term in stream]
    return pl.pallas_call(
        functools.partial(
            middle_kernel, terms=len(streams[0]), streams=len(streams)
        ),
        in_specs=[vmem] * (len(terms) + 3),
        out_specs=[vmem] * len(streams),
        out_shape=[jax.ShapeDtypeStruct((2, rows, crop_width), jnp.bfloat16)] * len(streams),
        scratch_shapes=[pltpu.VMEM((2 * band, crop_width), jnp.bfloat16)] * 2,
        compiler_params=params(),
        cost_estimate=light(),
        name="middle",
    )(*terms, image, cos_table, sin_table)


def fixed(array):
    return pl.BlockSpec(array.shape, lambda i: (0,) * array.ndim)


def forward_all(meta, low, pupil, band_table):
    win = Windows(*low[0].shape, pupil.shape[1])
    count = meta.shape[1]
    out_type = band_type(pupil, band_table, count)
    return pl.pallas_call(
        functools.partial(forward_grid_kernel, win=win),
        grid=(count,),
        in_specs=[smem] + [fixed(array) for array in (pupil, band_table, *low)],
        out_specs=pl.BlockSpec((1,) + out_type.shape[1:], lambda i: (i, 0, 0, 0)),
        out_shape=out_type,
        compiler_params=params(),
        name="forward_all",
    )(meta, pupil, band_table, *low)


def backward_all(meta, spectrum, pupil, band_table, backs):
    win = Windows(*spectrum.shape[1:], pupil.shape[1])
    return pl.pallas_call(
        functools.partial(backward_grid_kernel, win=win),
        grid=(meta.shape[1],),
        in_specs=[smem]
        + [fixed(array) for array in (pupil, band_table, spectrum)]
        + [pl.BlockSpec((1,) + backs.shape[1:], lambda i: (i, 0, 0, 0))],
        out_specs=fixed(spectrum),
        out_shape=jax.ShapeDtypeStruct(spectrum.shape, jnp.float32),
        compiler_params=params(),
        name="backward_all",
    )(meta, pupil, band_table, spectrum, backs)


def cast_kernel(spec_ref, out_ref, held, sems, *, part):
    blocks, _, width = held.shape
    columns = [pl.ds(block * width, width) for block in range(blocks)]
    copies = [
        pltpu.make_async_copy(spec_ref.at[part, :, columns[i]], held.at[i], sems.at[i])
        for i in range(blocks)
    ]
    for copy in copies:
        copy.start()
    for i, copy in enumerate(copies):
        copy.wait()
        out_ref[:, columns[i]] = held[i].astype(jnp.bfloat16)


def low_part(spectrum, part):
    _, rows, columns = spectrum.shape
    return pl.pallas_call(
        functools.partial(cast_kernel, part=part),
        in_specs=[pl.BlockSpec(memory_space=pltpu.HBM)],
        out_specs=vmem,
        out_shape=jax.ShapeDtypeStruct((rows, columns), jnp.bfloat16),
        scratch_shapes=[
            pltpu.VMEM((4, rows, columns // 4), jnp.float32),
            pltpu.SemaphoreType.DMA((4,)),
        ],
        compiler_params=params(),
        cost_estimate=light(),
        name="low_part",
    )(spectrum)


def total(*terms):
    return sum(term.astype(jnp.float32) for term in terms).astype(jnp.bfloat16)


def per_device(spectrum, pupil, measured, centre_rows, centre_cols):
    count = lax.axis_size("ty")
    planes = count // 4
    position = lax.axis_index("ty")
    plane = position // 4
    _, tile_rows, slab_columns = spectrum.shape
    crop_width = pupil.shape[0]
    band = measured.shape[1]
    band_start = (crop_width - band) // 2
    cos_table, sin_table = fourier_tables(crop_width)
    chosen_rows = slice(band_start, band_start + band)
    band_table = jnp.asarray(
        np.concatenate([cos_table[:, chosen_rows], sin_table[:, chosen_rows]], axis=1)
    )
    cos_table, sin_table = jnp.asarray(cos_table), jnp.asarray(sin_table)

    half = crop_width // 2

    low = [low_part(spectrum, part) for part in range(2)]

    def image_meta(ids, positions):
        match = ids[:, None] == jnp.arange(count, dtype=jnp.int32)[None, :]
        tops = jnp.sum(jnp.where(match, centre_rows[None, :], 0), axis=1) - half
        lefts = jnp.sum(jnp.where(match, centre_cols[None, :], 0), axis=1) - half
        rows = [place * tile_rows - tops for place in positions]
        return jnp.stack(rows + [lefts]).astype(jnp.int32)

    if planes != 4:
        meta = image_meta(jnp.arange(count, dtype=jnp.int32), [position])
        partial = forward_all(meta, low, pupil, band_table)
        mid = lax.psum_scatter(partial, "ty", scatter_dimension=0, tiled=True)[0]
        back = lax.all_gather(middle([[mid]], measured, cos_table, sin_table)[0], "ty")
        return backward_all(meta, spectrum, pupil, band_table, back)

    targets = {"far": (3, 3, 0, 0), "next": (2, 2, 1, 1), "beside": (1, 0, 3, 2), "own": (0, 1, 2, 3)}
    own_core = [("far", 2), ("far", 0), ("next", 2), ("next", 0)]
    own_core += [("beside", 2), ("beside", 0), ("own", 2), ("own", 0)]
    slots = {}
    for core in (0, 1):
        for name, y in own_core:
            slots[name, y + core] = len(slots)
    ids = [
        [targets[name][i // 4] * 4 + (i % 4 ^ flip) for (name, flip) in slots]
        for i in range(count)
    ]
    my_ids = lax.dynamic_index_in_dim(jnp.asarray(ids, jnp.int32), position, keepdims=False)
    meta = image_meta(my_ids, [position, position ^ 1])

    def sibling(value):
        return lax.ppermute(value, "ty", [(i, i ^ 1) for i in range(count)])

    def across(value):
        return lax.ppermute(value, "ty", [(i, i ^ 2) for i in range(count)])

    def along(value, plane_pairs):
        pairs = [(4 * a + i, 4 * b + i) for a, b in plane_pairs for i in range(4)]
        return lax.ppermute(value, "ty", pairs)

    inward = [(0, 1), (3, 2)]
    outward = [(1, 0), (2, 3)]
    inner = [(1, 2), (2, 1)]
    together = lax.optimization_barrier

    lows = [low, [sibling(part) for part in low]]
    streams = 2
    (own_rows,) = forward(meta, lows[:1], pupil, band_table, 0, 1, (0,))
    far_leaving = forward(
        meta, lows[1:], pupil, band_table, 0, 1, (1,), own_rows, streams=streams
    )
    far_other = [across(value) for value in far_leaving]
    made = forward(
        together((meta, far_leaving[0]))[0], lows, pupil, band_table, 1, 7, streams=streams
    )
    summed, held = [], None
    for stream in reversed(range(streams)):
        (
            far_kept,
            next_leaving,
            next_kept,
            beside_leaving,
            beside_kept,
            own_leaving,
            own_kept,
        ) = made[stream::streams]
        far, far_kept, next_leaving = together((far_other[stream], far_kept, next_leaving))

        next_other = across(next_leaving)
        from_end = along(total(far_kept, far), inward)
        from_end, next_other, beside_leaving = together((from_end, next_other, beside_leaving))

        beside_other = across(beside_leaving)
        next_inward = along(total(next_kept, next_other), inward)
        far_inner = along(total(far_kept, far, from_end), inner)
        far_inner, next_inward, beside_other, own_leaving = together(
            (far_inner, next_inward, beside_other, own_leaving)
        )

        own_other = across(own_leaving)
        next_inner = along(total(next_kept, next_other, next_inward), inner)
        beside = along(total(beside_kept, beside_other, far_inner), inward + outward)
        terms = [own_kept, own_other, next_inner, beside]
        if stream > 0:
            terms = [total(*terms)]
            held = terms[0]
        else:
            terms[0] = together((terms[0], held))[0]
            terms = [total(*terms)]
        summed.insert(0, terms)
    backs = middle(summed, measured, cos_table, sin_table)

    at_ends = (plane == 0) | (plane == 3)
    lead, last = streams - 1, 0
    pieces = {}

    def apply(parts, names, chunks=0):
        taken = [[pieces.get((name, stream)) for stream in range(streams)] for name in names]
        own_slots = [slots[name] for name in names]
        shape = spectrum.shape
        return backward(meta, shape, pupil, band_table, parts, own_slots, taken, chunks)

    def close(stream, *names):
        closed = together(tuple(pieces[name, stream] for name in names))
        for name, value in zip(names, closed):
            pieces[name, stream] = value

    early, later, late = (
        [("beside", 0), ("own", 2)],
        [("next", 0), ("beside", 2)],
        [("far", 0), ("next", 2)],
    )
    for stream in (lead, last):
        back = pieces[("own", 0), stream] = backs[stream]
        pieces[("own", 2), stream] = across(back)
        pieces["inner", stream] = along(back, inner)
        pieces[("beside", 0), stream] = along(back, inward + outward)
        close(stream, ("own", 2), "inner", ("beside", 0))
    result = apply([spectrum], [("own", 0)])
    pieces["inner", last], result = together((pieces["inner", last], result))
    for stream in (lead, last):
        pieces[("beside", 2), stream] = across(pieces[("beside", 0), stream])
        pieces["far inner", stream] = along(pieces[("beside", 0), stream], inner)
        pieces["outward", stream] = along(pieces["inner", stream], outward)
        if stream == lead:
            pieces["sum", stream] = apply([], [("own", 0)] + early, 1)[0]
        else:
            pieces["sum", stream] = apply([result], early)
        close(stream, ("beside", 2), "far inner", "outward", "sum")
    slab, result = pieces["sum", lead], pieces["sum", last]
    for stream in (lead, last):
        from_next = jnp.where(at_ends, pieces["outward", stream], pieces["inner", stream])
        pieces[("next", 0), stream] = from_next
        pieces[("next", 2), stream] = across(from_next)
        pieces["far outward", stream] = along(pieces["far inner", stream], outward)
        if stream == last:
            pieces["slab", stream] = apply([slab], later, 1)[0]
            pieces["sum", stream] = apply([result], later)
            close(stream, ("next", 2), "far outward", "slab", "sum")
        else:
            close(stream, ("next", 2), "far outward")
    slab, result = pieces["slab", last], pieces["sum", last]
    for stream in (lead, last):
        from_far = jnp.where(at_ends, pieces["far outward", stream], pieces["far inner", stream])
        pieces[("far", 0), stream] = from_far
        pieces[("far", 2), stream] = across(from_far)
    far_other = pieces[("far", 2), lead]
    slab, far_other = together((slab, far_other))
    chunks = apply([slab], late, 4)
    twin = sibling(far_other)
    slab = [sibling(chunk) for chunk in chunks[:-1]]
    result, twin = together((result, twin))
    result = apply([result], late)
    chunk, result = together((chunks[-1], result))
    slab.append(sibling(chunk))
    arriving, result = together((pieces[("far", 2), last], result))
    pieces[("far", 2), lead], pieces[("far", 3), lead] = far_other, twin
    pieces[("far", 2), last], pieces[("far", 3), last] = arriving, sibling(arriving)
    return apply([result] + slab, [("far", 2), ("far", 3)])


def solution(mesh):
    return jax.shard_map(
        per_device,
        mesh=mesh,
        in_specs=(
            P(None, ("groups", "ty"), None),
            P(),
            P(("groups", "ty"), None, None),
            P("groups"),
            P("groups"),
        ),
        out_specs=P(None, ("groups", "ty"), None),
        check_vma=False,
    )
```

```python
import functools
import math

import jax
import jax.numpy as jnp
import numpy as np
from jax import lax
from jax.experimental import pallas as pl
from jax.experimental.pallas import tpu as pltpu
from jax.sharding import PartitionSpec as P

step_size = 0.5
lane = 128
row_tile = 16
vmem_bytes = 20 * 1024 * 1024
backward_bytes = 20 * 1024 * 1024


def fourier_tables(crop_width):
    counter = np.arange(crop_width, dtype=np.int64)
    angle = (counter[:, None] * counter[None, :] % crop_width) * (2.0 * math.pi / crop_width)
    factor = 1.0 / math.sqrt(crop_width)
    cos_table = (np.cos(angle) * factor).astype(np.float32).astype(jnp.bfloat16)
    sin_table = (np.sin(angle) * factor).astype(np.float32).astype(jnp.bfloat16)
    return cos_table, sin_table


def tile_weight(pupil_ref, first_row, win):
    start = win.row(first_row)
    rows = pupil_ref[pl.ds(start, win.rows), :].astype(jnp.float32)
    rows = pltpu.roll(rows, (2 * win.rows + start - first_row) % win.rows, 0)
    shape = (win.tile_rows, win.crop_width)
    row = 2 * (first_row + lax.broadcasted_iota(jnp.int32, shape, 0)) - win.crop_width + 1
    column = 2 * lax.broadcasted_iota(jnp.int32, shape, 1) - win.crop_width + 1
    inside = row * row + column * column <= win.crop_width * win.crop_width
    return jnp.where(inside, rows[: win.tile_rows], 0.0)


def tile_band(band_ref, first_row, win):
    start = win.row(first_row)
    rows = band_ref[pl.ds(start, win.rows), :].astype(jnp.float32)
    rows = pltpu.roll(rows, (2 * win.rows + start - first_row) % win.rows, 0)[: win.tile_rows]
    band = rows.shape[1] // 2
    turned = jnp.concatenate([-rows[:, band:], rows[:, :band]], axis=1)
    return jnp.concatenate([rows, turned], axis=0).astype(jnp.bfloat16)


class Windows:
    def __init__(self, tile_rows, slab_columns, crop_width):
        self.tile_rows = tile_rows
        self.crop_width = crop_width
        self.rows = tile_rows + row_tile
        self.columns = crop_width + lane
        self.last_row = crop_width - self.rows
        self.last_column = slab_columns - self.columns

    def row(self, first_row):
        start = jnp.clip(first_row, 0, self.last_row) // row_tile * row_tile
        return pl.multiple_of(start, row_tile)

    def column(self, left):
        start = jnp.minimum(left // lane * lane, self.last_column)
        return pl.multiple_of(start, lane)

    def active(self, first_row):
        return (first_row > -self.tile_rows) & (first_row < self.crop_width)


def image_band(meta_ref, slot, lows, tiles, pupil_ref, band_ref, win, store, came=None):
    left = meta_ref[meta_ref.shape[0] - 1, slot]
    first_rows = [meta_ref[tile, slot] for tile in tiles]
    active = functools.reduce(jnp.logical_or, [win.active(row) for row in first_rows])
    band = band_ref.shape[1] // 2
    shape = (2, band, win.crop_width)

    @pl.when(jnp.logical_not(active))
    def _():
        store(jnp.zeros(shape, jnp.bfloat16) if came is None else came[...])

    @pl.when(active)
    def _():
        col_start = win.column(left)
        shift = (win.columns - (left - col_start)) % win.columns
        parts, tables = [], []
        for first_row, low_refs in zip(first_rows, lows):
            weight = tile_weight(pupil_ref, first_row, win)
            for low_ref in low_refs:
                low = low_ref[:, pl.ds(col_start, win.columns)].astype(jnp.float32)
                low = pltpu.roll(low, shift, 1)[:, : win.crop_width]
                parts.append((weight * low).astype(jnp.bfloat16))
            tables.append(tile_band(band_ref, first_row, win))
        mid = lax.dot_general(
            jnp.concatenate(tables, axis=0),
            jnp.concatenate(parts, axis=0),
            (((0,), (0,)), ((), ())),
            preferred_element_type=jnp.float32,
        )
        if came is not None:
            mid = mid + came[...].reshape(mid.shape).astype(jnp.float32)
        store(mid.astype(jnp.bfloat16).reshape(shape))


def forward_kernel(meta_ref, pupil_ref, band_ref, *refs, base, splits, count, win, tiles):
    out_refs = refs[-count:]
    lows = [refs[2 * half : 2 * half + 2] for half in range(len(tiles))]
    came = refs[2 * len(tiles)] if len(refs) > 2 * len(tiles) + count else None

    def image(index):
        def store(value):
            for number, split in enumerate(splits):
                first = sum(splits[:number])

                @pl.when(index == number)
                def _():
                    for stream, out_ref in enumerate(out_refs[first : first + split]):
                        rows = out_ref.shape[1]
                        out_ref[...] = value[:, stream * rows : (stream + 1) * rows]

        image_band(meta_ref, base + index, lows, tiles, pupil_ref, band_ref, win, store, came)

    pl.loop(0, len(splits))(image)


def forward_grid_kernel(meta_ref, pupil_ref, band_ref, real_ref, imag_ref, out_ref, *, win):
    def store(value):
        out_ref[0] = value

    lows = [(real_ref, imag_ref)]
    image_band(meta_ref, pl.program_id(0), lows, (0,), pupil_ref, band_ref, win, store)


def subtract_image(meta_ref, slot, back_refs, pupil_ref, band_ref, out_ref, win, tile=0):
    first_row, left = meta_ref[tile, slot], meta_ref[meta_ref.shape[0] - 1, slot]
    tile_rows, crop_width = win.tile_rows, win.crop_width

    @pl.when(win.active(first_row))
    def _():
        col_start = win.column(left)
        weight = tile_weight(pupil_ref, first_row, win) * step_size
        table = tile_band(band_ref, first_row, win)
        band = table.shape[1] // 2
        rows = band // len(back_refs)
        held = [number for number, ref in enumerate(back_refs) if ref is not None]
        if len(held) < len(back_refs):
            starts = [part * band + number * rows for part in range(2) for number in held]
            table = jnp.concatenate([table[:, start : start + rows] for start in starts], axis=1)
        back = [back_refs[number][part] for part in range(2) for number in held]
        back = jnp.concatenate(back, axis=0)
        grad = jnp.dot(table, back, preferred_element_type=jnp.float32)
        columns = pl.ds(col_start, win.columns)
        pad = jnp.zeros((tile_rows, win.columns - crop_width), jnp.float32)
        for part in range(2):
            piece = grad[part * tile_rows : (part + 1) * tile_rows] * weight
            piece = pltpu.roll(jnp.concatenate([piece, pad], axis=1), left - col_start, 1)
            out_ref[part, :, columns] = out_ref[part, :, columns] - piece


def backward_kernel(meta_ref, pupil_ref, band_ref, *refs, slots, held, parts, win):
    part_refs, back_refs, out_ref = refs[:parts], iter(refs[parts:-1]), refs[-1]
    start = 0
    for chunk_ref in part_refs[1:]:
        columns = slice(start, start + chunk_ref.shape[2])
        out_ref[:, :, columns] = part_refs[0][:, :, columns] + chunk_ref[...].astype(jnp.float32)
        start = columns.stop
    if parts == 1:
        out_ref[...] = part_refs[0][...]
    for slot, groups in zip(slots, held):
        of_image = [next(back_refs) if there else None for there in groups]
        subtract_image(meta_ref, slot, of_image, pupil_ref, band_ref, out_ref, win)


def sibling_kernel(meta_ref, pupil_ref, band_ref, *refs, slots, held, parts, win):
    backs = sum(map(sum, held))
    part_refs, back_refs, total_ref = refs[:parts], iter(refs[parts : parts + backs]), refs[-1]
    out_refs = refs[parts + backs : -1]
    if parts:
        total_ref[...] = part_refs[0][...].astype(jnp.float32)
    else:
        total_ref[...] = jnp.zeros_like(total_ref)
    for slot, groups in zip(slots, held):
        of_image = [next(back_refs) if there else None for there in groups]
        subtract_image(meta_ref, slot, of_image, pupil_ref, band_ref, total_ref, win, 1)
    start = 0
    for out_ref in out_refs:
        end = start + out_ref.shape[2]
        out_ref[...] = total_ref[:, :, start:end].astype(jnp.bfloat16)
        start = end


def backward_grid_kernel(meta_ref, pupil_ref, band_ref, spec_ref, back_ref, out_ref, *, win):
    step = pl.program_id(0)

    @pl.when(step == 0)
    def _():
        out_ref[...] = spec_ref[...]

    subtract_image(meta_ref, step, [back_ref.at[0]], pupil_ref, band_ref, out_ref, win)


def middle_kernel(*refs, whole, terms, streams):
    whole_refs, refs = refs[:whole], refs[whole:]
    term_refs, refs = refs[: terms * streams], refs[terms * streams :]
    (image_ref, cos_ref, sin_ref), refs = refs[:3], refs[3:]
    whole_out, out_refs, (mid_ref, resid_ref) = refs[0], refs[1 : streams + 1], refs[streams + 1 :]
    band, crop_width = image_ref.shape[1:]
    rows = band // streams
    block = min(512, crop_width)
    for stream in range(streams):
        total = sum(
            ref[...].astype(jnp.float32)
            for ref in term_refs[stream * terms : (stream + 1) * terms]
        )
        held = slice(stream * rows, (stream + 1) * rows)
        total = total + sum(ref[:, held].astype(jnp.float32) for ref in whole_refs)
        for part in range(2):
            start = part * band + stream * rows
            mid_ref[start : start + rows] = total[part].astype(jnp.bfloat16)
    dot = functools.partial(jnp.dot, preferred_element_type=jnp.float32)
    for start in range(0, crop_width, block):
        columns = slice(start, start + block)
        by_cos = dot(mid_ref[...], cos_ref[:, columns])
        by_sin = dot(mid_ref[...], sin_ref[:, columns])
        field_real = by_cos[:band] - by_sin[band:]
        field_imag = by_sin[:band] + by_cos[band:]
        power = field_real * field_real + field_imag * field_imag
        measured = image_ref[0, :, columns].astype(jnp.float32)
        keeping = 1.0 - measured * lax.rsqrt(jnp.maximum(power, 1.0))
        resid_ref[:band, columns] = (field_real * keeping).astype(jnp.bfloat16)
        resid_ref[band:, columns] = (field_imag * keeping).astype(jnp.bfloat16)
    for start in range(0, crop_width, block):
        columns = slice(start, start + block)
        by_cos = dot(resid_ref[...], cos_ref[:, columns])
        by_sin = dot(resid_ref[...], sin_ref[:, columns])
        for part, back in enumerate((by_cos[:band] + by_sin[band:], by_cos[band:] - by_sin[:band])):
            back = back.astype(jnp.bfloat16)
            whole_out[part, :, columns] = back
            for stream, out_ref in enumerate(out_refs):
                out_ref[part, :, columns] = back[stream * rows : (stream + 1) * rows]


def params():
    return pltpu.CompilerParams(vmem_limit_bytes=vmem_bytes)


def light():
    return pl.CostEstimate(flops=1024, bytes_accessed=1024, transcendentals=0)


vmem = pl.BlockSpec(memory_space=pltpu.VMEM)
smem = pl.BlockSpec(memory_space=pltpu.SMEM)


def band_type(pupil, band_table, *lead):
    shape = lead + (2, band_table.shape[1] // 2, pupil.shape[1])
    return jax.ShapeDtypeStruct(shape, jnp.bfloat16)


def forward(meta, lows, pupil, band_table, base, splits, tiles=(0, 1), came=None):
    win = Windows(*lows[0][0].shape, pupil.shape[1])
    operands = [meta, pupil, band_table] + [part for low in lows for part in low]
    operands += [came] * (came is not None)
    count = sum(splits)
    _, rows, columns = band_type(pupil, band_table).shape
    return pl.pallas_call(
        functools.partial(
            forward_kernel, base=base, splits=splits, count=count, win=win, tiles=tiles
        ),
        in_specs=[smem] + [vmem] * (len(operands) - 1),
        out_specs=[vmem] * count,
        out_shape=[
            jax.ShapeDtypeStruct((2, rows // split, columns), jnp.bfloat16)
            for split in splits
            for _ in range(split)
        ],
        compiler_params=params(),
        cost_estimate=light(),
        name="forward",
    )(*operands)


def backward(meta, shape, pupil, band_table, parts, slots, backs, chunks=0):
    win = Windows(*shape[1:], pupil.shape[1])
    held = [[back is not None for back in groups] for groups in backs]
    operands = list(parts) + [back for groups in backs for back in groups if back is not None]
    kernel = sibling_kernel if chunks else backward_kernel
    out_shape = jax.ShapeDtypeStruct(shape, jnp.float32)
    if chunks:
        cuts = [shape[2] // lane * number // chunks * lane for number in range(chunks + 1)]
        out_shape = [
            jax.ShapeDtypeStruct(shape[:2] + (end - start,), jnp.bfloat16)
            for start, end in zip(cuts, cuts[1:])
        ]
    return pl.pallas_call(
        functools.partial(kernel, slots=slots, held=held, parts=len(parts), win=win),
        in_specs=[smem] + [vmem] * (2 + len(operands)),
        out_specs=[vmem] * chunks if chunks else vmem,
        out_shape=out_shape,
        scratch_shapes=[pltpu.VMEM(shape, jnp.float32)] * (chunks > 0),
        compiler_params=pltpu.CompilerParams(vmem_limit_bytes=backward_bytes),
        cost_estimate=light(),
        name="backward",
    )(meta, pupil, band_table, *operands)


def middle(whole, streams, image, cos_table, sin_table):
    band, crop_width = image.shape[1:]
    terms = [term for stream in streams for term in stream]
    group = jax.ShapeDtypeStruct((2, band // max(len(streams), 1), crop_width), jnp.bfloat16)
    return pl.pallas_call(
        functools.partial(
            middle_kernel,
            whole=len(whole),
            terms=len(terms) // max(len(streams), 1),
            streams=max(len(streams), 1),
        ),
        in_specs=[vmem] * (len(whole) + len(terms) + 3),
        out_specs=[vmem] * (max(len(streams), 1) + 1),
        out_shape=[jax.ShapeDtypeStruct((2, band, crop_width), jnp.bfloat16)]
        + [group] * max(len(streams), 1),
        scratch_shapes=[pltpu.VMEM((2 * band, crop_width), jnp.bfloat16)] * 2,
        compiler_params=params(),
        cost_estimate=light(),
        name="middle",
    )(*whole, *terms, image, cos_table, sin_table)


def fixed(array):
    return pl.BlockSpec(array.shape, lambda i: (0,) * array.ndim)


def forward_all(meta, low, pupil, band_table):
    win = Windows(*low[0].shape, pupil.shape[1])
    count = meta.shape[1]
    out_type = band_type(pupil, band_table, count)
    return pl.pallas_call(
        functools.partial(forward_grid_kernel, win=win),
        grid=(count,),
        in_specs=[smem] + [fixed(array) for array in (pupil, band_table, *low)],
        out_specs=pl.BlockSpec((1,) + out_type.shape[1:], lambda i: (i, 0, 0, 0)),
        out_shape=out_type,
        compiler_params=params(),
        name="forward_all",
    )(meta, pupil, band_table, *low)


def backward_all(meta, spectrum, pupil, band_table, backs):
    win = Windows(*spectrum.shape[1:], pupil.shape[1])
    return pl.pallas_call(
        functools.partial(backward_grid_kernel, win=win),
        grid=(meta.shape[1],),
        in_specs=[smem]
        + [fixed(array) for array in (pupil, band_table, spectrum)]
        + [pl.BlockSpec((1,) + backs.shape[1:], lambda i: (i, 0, 0, 0))],
        out_specs=fixed(spectrum),
        out_shape=jax.ShapeDtypeStruct(spectrum.shape, jnp.float32),
        compiler_params=params(),
        name="backward_all",
    )(meta, pupil, band_table, spectrum, backs)


def cast_kernel(spec_ref, out_ref, held, sems, *, part):
    blocks, _, width = held.shape
    columns = [pl.ds(block * width, width) for block in range(blocks)]
    copies = [
        pltpu.make_async_copy(spec_ref.at[part, :, columns[i]], held.at[i], sems.at[i])
        for i in range(blocks)
    ]
    for copy in copies:
        copy.start()
    for i, copy in enumerate(copies):
        copy.wait()
        out_ref[:, columns[i]] = held[i].astype(jnp.bfloat16)


def low_part(spectrum, part):
    _, rows, columns = spectrum.shape
    return pl.pallas_call(
        functools.partial(cast_kernel, part=part),
        in_specs=[pl.BlockSpec(memory_space=pltpu.HBM)],
        out_specs=vmem,
        out_shape=jax.ShapeDtypeStruct((rows, columns), jnp.bfloat16),
        scratch_shapes=[
            pltpu.VMEM((4, rows, columns // 4), jnp.float32),
            pltpu.SemaphoreType.DMA((4,)),
        ],
        compiler_params=params(),
        cost_estimate=light(),
        name="low_part",
    )(spectrum)


def total(*terms):
    return sum(term.astype(jnp.float32) for term in terms).astype(jnp.bfloat16)


def per_device(spectrum, pupil, measured, centre_rows, centre_cols):
    count = lax.axis_size("ty")
    planes = count // 4
    position = lax.axis_index("ty")
    plane = position // 4
    _, tile_rows, slab_columns = spectrum.shape
    crop_width = pupil.shape[0]
    band = measured.shape[1]
    band_start = (crop_width - band) // 2
    cos_table, sin_table = fourier_tables(crop_width)
    chosen_rows = slice(band_start, band_start + band)
    band_table = jnp.asarray(
        np.concatenate([cos_table[:, chosen_rows], sin_table[:, chosen_rows]], axis=1)
    )
    cos_table, sin_table = jnp.asarray(cos_table), jnp.asarray(sin_table)

    half = crop_width // 2

    low = [low_part(spectrum, part) for part in range(2)]

    def image_meta(ids, positions):
        match = ids[:, None] == jnp.arange(count, dtype=jnp.int32)[None, :]
        tops = jnp.sum(jnp.where(match, centre_rows[None, :], 0), axis=1) - half
        lefts = jnp.sum(jnp.where(match, centre_cols[None, :], 0), axis=1) - half
        rows = [place * tile_rows - tops for place in positions]
        return jnp.stack(rows + [lefts]).astype(jnp.int32)

    if planes != 4:
        meta = image_meta(jnp.arange(count, dtype=jnp.int32), [position])
        partial = forward_all(meta, low, pupil, band_table)
        mid = lax.psum_scatter(partial, "ty", scatter_dimension=0, tiled=True)[0]
        back = lax.all_gather(middle([mid], [], measured, cos_table, sin_table)[0], "ty")
        return backward_all(meta, spectrum, pupil, band_table, back)

    targets = {"far": (3, 3, 0, 0), "next": (2, 2, 1, 1), "beside": (1, 0, 3, 2), "own": (0, 1, 2, 3)}
    own_core = [("far", 2), ("far", 0), ("next", 2), ("next", 0)]
    own_core += [("beside", 2), ("beside", 0), ("own", 2), ("own", 0)]
    slots = {}
    for core in (0, 1):
        for name, y in own_core:
            slots[name, y + core] = len(slots)
    ids = [
        [targets[name][i // 4] * 4 + (i % 4 ^ flip) for (name, flip) in slots]
        for i in range(count)
    ]
    my_ids = lax.dynamic_index_in_dim(jnp.asarray(ids, jnp.int32), position, keepdims=False)
    meta = image_meta(my_ids, [position, position ^ 1])

    def sibling(value):
        return lax.ppermute(value, "ty", [(i, i ^ 1) for i in range(count)])

    def across(value):
        return lax.ppermute(value, "ty", [(i, i ^ 2) for i in range(count)])

    def along(value, plane_pairs):
        pairs = [(4 * a + i, 4 * b + i) for a, b in plane_pairs for i in range(4)]
        return lax.ppermute(value, "ty", pairs)

    inward = [(0, 1), (3, 2)]
    outward = [(1, 0), (2, 3)]
    inner = [(1, 2), (2, 1)]
    together = lax.optimization_barrier

    lows = [low, [sibling(part) for part in low]]
    streams = 2
    (own_rows,) = forward(meta, lows[:1], pupil, band_table, 0, [1], (0,))
    far_leaving = forward(meta, lows[1:], pupil, band_table, 0, [streams], (1,), own_rows)
    far_other = [across(value) for value in far_leaving]
    splits = [streams] * 7
    made = forward(together((meta, far_leaving[0]))[0], lows, pupil, band_table, 1, splits)
    summed, held = [], None
    for stream in reversed(range(streams)):
        (
            far_kept,
            next_leaving,
            next_kept,
            beside_leaving,
            beside_kept,
            own_leaving,
            own_kept,
        ) = made[stream::streams]
        far, far_kept, next_leaving = together((far_other[stream], far_kept, next_leaving))

        next_other = across(next_leaving)
        from_end = along(total(far_kept, far), inward)
        from_end, next_other, beside_leaving = together((from_end, next_other, beside_leaving))

        beside_other = across(beside_leaving)
        next_inward = along(total(next_kept, next_other), inward)
        far_inner = along(total(far_kept, far, from_end), inner)
        far_inner, next_inward, beside_other, own_leaving = together(
            (far_inner, next_inward, beside_other, own_leaving)
        )

        own_other = across(own_leaving)
        next_inner = along(total(next_kept, next_other, next_inward), inner)
        beside = along(total(beside_kept, beside_other, far_inner), inward + outward)
        terms = [own_kept, own_other, next_inner, beside]
        if stream > 0:
            terms = [total(*terms)]
            held = terms[0]
        else:
            terms[0] = together((terms[0], held))[0]
            terms = [total(*terms)]
        summed.insert(0, terms)
    back, *backs = middle([], summed, measured, cos_table, sin_table)

    at_ends = (plane == 0) | (plane == 3)
    lead, last = streams - 1, 0
    pieces = {}

    def apply(parts, names, chunks=0):
        taken = [
            [pieces[name]]
            if name in pieces
            else [pieces.get((name, stream)) for stream in range(streams)]
            for name in names
        ]
        own_slots = [slots[name] for name in names]
        shape = spectrum.shape
        return backward(meta, shape, pupil, band_table, parts, own_slots, taken, chunks)

    def close(stream, *names):
        closed = together(tuple(pieces[name, stream] for name in names))
        for name, value in zip(names, closed):
            pieces[name, stream] = value

    early, later, late = (
        [("beside", 0), ("own", 2)],
        [("next", 0), ("beside", 2)],
        [("far", 0), ("next", 2)],
    )
    def joined(name):
        return jnp.concatenate([pieces[name, stream] for stream in range(streams)], axis=1)

    pieces["own", 0] = back
    other = across(back)
    for stream in (lead, last):
        pieces["inner", stream] = along(backs[stream], inner)
        pieces["near", stream] = along(backs[stream], inward + outward)
        close(stream, "inner", "near")
    result = apply([spectrum], [("own", 0)])
    pieces["inner", last], result, pieces["own", 2] = together(
        (pieces["inner", last], result, other)
    )
    pieces["beside", 0] = joined("near")
    pieces["other", last] = across(pieces["beside", 0])
    for stream in (lead, last):
        pieces["far inner", stream] = along(pieces["near", stream], inner)
        pieces["outward", stream] = along(pieces["inner", stream], outward)
        if stream == lead:
            pieces["sum", stream] = apply([], [("own", 0)] + early, 1)[0]
            close(stream, "far inner", "outward", "sum")
        else:
            pieces["sum", stream] = apply([result], early)
            close(stream, "far inner", "outward", "sum", "other")
    slab, result = pieces["sum", lead], pieces["sum", last]
    pieces["beside", 2] = pieces["other", last]
    pieces["next", 0] = jnp.where(at_ends, joined("outward"), joined("inner"))
    pieces["other", last] = across(pieces["next", 0])
    for stream in (lead, last):
        pieces["far outward", stream] = along(pieces["far inner", stream], outward)
        if stream == last:
            pieces["slab", stream] = apply([slab], later, 1)[0]
            pieces["sum", stream] = apply([result], later)
            close(stream, "far outward", "slab", "sum", "other")
        else:
            close(stream, "far outward")
    slab, result, pieces["next", 2] = [pieces[name, last] for name in ("slab", "sum", "other")]
    for stream in (lead, last):
        from_far = jnp.where(at_ends, pieces["far outward", stream], pieces["far inner", stream])
        pieces[("far", 0), stream] = from_far
        pieces[("far", 2), stream] = across(from_far)
    far_other = pieces[("far", 2), lead]
    slab, far_other = together((slab, far_other))
    chunks = apply([slab], late, 4)
    twin = sibling(far_other)
    slab = [sibling(chunk) for chunk in chunks[:-1]]
    result, twin = together((result, twin))
    result = apply([result], late)
    chunk, result = together((chunks[-1], result))
    slab.append(sibling(chunk))
    arriving, result = together((pieces[("far", 2), last], result))
    pieces[("far", 2), lead], pieces[("far", 3), lead] = far_other, twin
    pieces[("far", 2), last], pieces[("far", 3), last] = arriving, sibling(arriving)
    return apply([result] + slab, [("far", 2), ("far", 3)])


def solution(mesh):
    return jax.shard_map(
        per_device,
        mesh=mesh,
        in_specs=(
            P(None, ("groups", "ty"), None),
            P(),
            P(("groups", "ty"), None, None),
            P("groups"),
            P("groups"),
        ),
        out_specs=P(None, ("groups", "ty"), None),
        check_vma=False,
    )
```

```python
import functools
import math

import jax
import jax.numpy as jnp
import numpy as np
from jax import lax
from jax.experimental import pallas as pl
from jax.experimental.pallas import tpu as pltpu
from jax.sharding import PartitionSpec as P

step_size = 0.5
lane = 128
row_tile = 16
vmem_bytes = 20 * 1024 * 1024
backward_bytes = 20 * 1024 * 1024


def fourier_tables(crop_width):
    counter = np.arange(crop_width, dtype=np.int64)
    angle = (counter[:, None] * counter[None, :] % crop_width) * (2.0 * math.pi / crop_width)
    factor = 1.0 / math.sqrt(crop_width)
    cos_table = (np.cos(angle) * factor).astype(np.float32).astype(jnp.bfloat16)
    sin_table = (np.sin(angle) * factor).astype(np.float32).astype(jnp.bfloat16)
    return cos_table, sin_table


def tile_weight(pupil_ref, first_row, win):
    start = win.row(first_row)
    rows = pupil_ref[pl.ds(start, win.rows), :].astype(jnp.float32)
    rows = pltpu.roll(rows, (2 * win.rows + start - first_row) % win.rows, 0)
    shape = (win.tile_rows, win.crop_width)
    row = 2 * (first_row + lax.broadcasted_iota(jnp.int32, shape, 0)) - win.crop_width + 1
    column = 2 * lax.broadcasted_iota(jnp.int32, shape, 1) - win.crop_width + 1
    inside = row * row + column * column <= win.crop_width * win.crop_width
    return jnp.where(inside, rows[: win.tile_rows], 0.0)


def tile_band(band_ref, first_row, win):
    start = win.row(first_row)
    rows = band_ref[pl.ds(start, win.rows), :].astype(jnp.float32)
    rows = pltpu.roll(rows, (2 * win.rows + start - first_row) % win.rows, 0)[: win.tile_rows]
    band = rows.shape[1] // 2
    turned = jnp.concatenate([-rows[:, band:], rows[:, :band]], axis=1)
    return jnp.concatenate([rows, turned], axis=0).astype(jnp.bfloat16)


class Windows:
    def __init__(self, tile_rows, slab_columns, crop_width):
        self.tile_rows = tile_rows
        self.crop_width = crop_width
        self.rows = tile_rows + row_tile
        self.columns = crop_width + lane
        self.last_row = crop_width - self.rows
        self.last_column = slab_columns - self.columns

    def row(self, first_row):
        start = jnp.clip(first_row, 0, self.last_row) // row_tile * row_tile
        return pl.multiple_of(start, row_tile)

    def column(self, left):
        start = jnp.minimum(left // lane * lane, self.last_column)
        return pl.multiple_of(start, lane)

    def active(self, first_row):
        return (first_row > -self.tile_rows) & (first_row < self.crop_width)


def image_band(meta_ref, slot, lows, tiles, pupil_ref, band_ref, win, store, came=None):
    left = meta_ref[meta_ref.shape[0] - 1, slot]
    first_rows = [meta_ref[tile, slot] for tile in tiles]
    active = functools.reduce(jnp.logical_or, [win.active(row) for row in first_rows])
    band = band_ref.shape[1] // 2
    shape = (2, band, win.crop_width)

    @pl.when(jnp.logical_not(active))
    def _():
        store(jnp.zeros(shape, jnp.bfloat16) if came is None else came[...])

    @pl.when(active)
    def _():
        col_start = win.column(left)
        shift = (win.columns - (left - col_start)) % win.columns
        parts, tables = [], []
        for first_row, low_refs in zip(first_rows, lows):
            weight = tile_weight(pupil_ref, first_row, win)
            for low_ref in low_refs:
                low = low_ref[:, pl.ds(col_start, win.columns)].astype(jnp.float32)
                low = pltpu.roll(low, shift, 1)[:, : win.crop_width]
                parts.append((weight * low).astype(jnp.bfloat16))
            tables.append(tile_band(band_ref, first_row, win))
        mid = lax.dot_general(
            jnp.concatenate(tables, axis=0),
            jnp.concatenate(parts, axis=0),
            (((0,), (0,)), ((), ())),
            preferred_element_type=jnp.float32,
        )
        if came is not None:
            mid = mid + came[...].reshape(mid.shape).astype(jnp.float32)
        store(mid.astype(jnp.bfloat16).reshape(shape))


def forward_kernel(meta_ref, pupil_ref, band_ref, *refs, base, images, count, win, tiles):
    out_refs = refs[-count:]
    lows = [refs[2 * half : 2 * half + 2] for half in range(len(tiles))]
    came = refs[2 * len(tiles)] if len(refs) > 2 * len(tiles) + count else None
    streams = count // images

    def image(index):
        def store(value):
            for number in range(images):

                @pl.when(index == number)
                def _():
                    for stream in range(streams):
                        out_ref = out_refs[number * streams + stream]
                        rows = out_ref.shape[1]
                        out_ref[...] = value[:, stream * rows : (stream + 1) * rows]

        image_band(meta_ref, base + index, lows, tiles, pupil_ref, band_ref, win, store, came)

    pl.loop(0, images)(image)


def forward_grid_kernel(meta_ref, pupil_ref, band_ref, real_ref, imag_ref, out_ref, *, win):
    def store(value):
        out_ref[0] = value

    lows = [(real_ref, imag_ref)]
    image_band(meta_ref, pl.program_id(0), lows, (0,), pupil_ref, band_ref, win, store)


def subtract_image(meta_ref, slot, back_refs, pupil_ref, band_ref, out_ref, win, tile=0):
    first_row, left = meta_ref[tile, slot], meta_ref[meta_ref.shape[0] - 1, slot]
    tile_rows, crop_width = win.tile_rows, win.crop_width

    @pl.when(win.active(first_row))
    def _():
        col_start = win.column(left)
        weight = tile_weight(pupil_ref, first_row, win) * step_size
        table = tile_band(band_ref, first_row, win)
        band = table.shape[1] // 2
        rows = band // len(back_refs)
        held = [number for number, ref in enumerate(back_refs) if ref is not None]
        if len(held) < len(back_refs):
            starts = [part * band + number * rows for part in range(2) for number in held]
            table = jnp.concatenate([table[:, start : start + rows] for start in starts], axis=1)
        back = [back_refs[number][part] for part in range(2) for number in held]
        back = jnp.concatenate(back, axis=0)
        grad = jnp.dot(table, back, preferred_element_type=jnp.float32)
        columns = pl.ds(col_start, win.columns)
        pad = jnp.zeros((tile_rows, win.columns - crop_width), jnp.float32)
        for part in range(2):
            piece = grad[part * tile_rows : (part + 1) * tile_rows] * weight
            piece = pltpu.roll(jnp.concatenate([piece, pad], axis=1), left - col_start, 1)
            out_ref[part, :, columns] = out_ref[part, :, columns] - piece


def backward_kernel(meta_ref, pupil_ref, band_ref, *refs, slots, held, parts, win):
    part_refs, back_refs, out_ref = refs[:parts], iter(refs[parts:-1]), refs[-1]
    for number in range(parts - 1):
        chunk = part_refs[number + 1][...].astype(jnp.float32)
        width = chunk.shape[2]
        columns = slice(number * width, (number + 1) * width)
        out_ref[:, :, columns] = part_refs[0][:, :, columns] + chunk
    if parts == 1:
        out_ref[...] = part_refs[0][...]
    for slot, groups in zip(slots, held):
        of_image = [next(back_refs) if there else None for there in groups]
        subtract_image(meta_ref, slot, of_image, pupil_ref, band_ref, out_ref, win)


def sibling_kernel(meta_ref, pupil_ref, band_ref, *refs, slots, held, parts, win):
    backs = sum(map(sum, held))
    part_refs, back_refs, total_ref = refs[:parts], iter(refs[parts : parts + backs]), refs[-1]
    out_refs = refs[parts + backs : -1]
    if parts:
        total_ref[...] = part_refs[0][...].astype(jnp.float32)
    else:
        total_ref[...] = jnp.zeros_like(total_ref)
    for slot, groups in zip(slots, held):
        of_image = [next(back_refs) if there else None for there in groups]
        subtract_image(meta_ref, slot, of_image, pupil_ref, band_ref, total_ref, win, 1)
    width = out_refs[0].shape[2]
    for number, out_ref in enumerate(out_refs):
        out_ref[...] = total_ref[:, :, number * width : (number + 1) * width].astype(jnp.bfloat16)


def backward_grid_kernel(meta_ref, pupil_ref, band_ref, spec_ref, back_ref, out_ref, *, win):
    step = pl.program_id(0)

    @pl.when(step == 0)
    def _():
        out_ref[...] = spec_ref[...]

    subtract_image(meta_ref, step, [back_ref.at[0]], pupil_ref, band_ref, out_ref, win)


def middle_kernel(*refs, terms, streams):
    term_refs, refs = refs[: terms * streams], refs[terms * streams :]
    (image_ref, cos_ref, sin_ref), refs = refs[:3], refs[3:]
    out_refs, (mid_ref, resid_ref) = refs[:streams], refs[streams:]
    _, rows, crop_width = term_refs[0].shape
    band = rows * streams
    block = min(512, crop_width)
    for stream in range(streams):
        of_stream = term_refs[stream * terms : (stream + 1) * terms]
        total = sum(ref[...].astype(jnp.float32) for ref in of_stream).astype(jnp.bfloat16)
        for part in range(2):
            start = part * band + stream * rows
            mid_ref[start : start + rows] = total[part]
    dot = functools.partial(jnp.dot, preferred_element_type=jnp.float32)
    for start in range(0, crop_width, block):
        columns = slice(start, start + block)
        by_cos = dot(mid_ref[...], cos_ref[:, columns])
        by_sin = dot(mid_ref[...], sin_ref[:, columns])
        field_real = by_cos[:band] - by_sin[band:]
        field_imag = by_sin[:band] + by_cos[band:]
        power = field_real * field_real + field_imag * field_imag
        measured = image_ref[0, :, columns].astype(jnp.float32)
        keeping = 1.0 - measured * lax.rsqrt(jnp.maximum(power, 1.0))
        resid_ref[:band, columns] = (field_real * keeping).astype(jnp.bfloat16)
        resid_ref[band:, columns] = (field_imag * keeping).astype(jnp.bfloat16)
    for start in range(0, crop_width, block):
        columns = slice(start, start + block)
        by_cos = dot(resid_ref[...], cos_ref[:, columns])
        by_sin = dot(resid_ref[...], sin_ref[:, columns])
        for part, back in enumerate((by_cos[:band] + by_sin[band:], by_cos[band:] - by_sin[:band])):
            for stream, out_ref in enumerate(out_refs):
                of_stream = back[stream * rows : (stream + 1) * rows]
                out_ref[part, :, columns] = of_stream.astype(jnp.bfloat16)


def params():
    return pltpu.CompilerParams(vmem_limit_bytes=vmem_bytes)


def light():
    return pl.CostEstimate(flops=1024, bytes_accessed=1024, transcendentals=0)


vmem = pl.BlockSpec(memory_space=pltpu.VMEM)
smem = pl.BlockSpec(memory_space=pltpu.SMEM)


def band_type(pupil, band_table, *lead):
    shape = lead + (2, band_table.shape[1] // 2, pupil.shape[1])
    return jax.ShapeDtypeStruct(shape, jnp.bfloat16)


def forward(meta, lows, pupil, band_table, base, images, tiles=(0, 1), came=None, streams=1):
    win = Windows(*lows[0][0].shape, pupil.shape[1])
    operands = [meta, pupil, band_table] + [part for low in lows for part in low]
    operands += [came] * (came is not None)
    count = images * streams
    _, rows, columns = band_type(pupil, band_table).shape
    return pl.pallas_call(
        functools.partial(
            forward_kernel, base=base, images=images, count=count, win=win, tiles=tiles
        ),
        in_specs=[smem] + [vmem] * (len(operands) - 1),
        out_specs=[vmem] * count,
        out_shape=[jax.ShapeDtypeStruct((2, rows // streams, columns), jnp.bfloat16)] * count,
        compiler_params=params(),
        cost_estimate=light(),
        name="forward",
    )(*operands)


def backward(meta, shape, pupil, band_table, parts, slots, backs, chunks=0):
    win = Windows(*shape[1:], pupil.shape[1])
    held = [[back is not None for back in groups] for groups in backs]
    operands = list(parts) + [back for groups in backs for back in groups if back is not None]
    kernel = sibling_kernel if chunks else backward_kernel
    out_shape = jax.ShapeDtypeStruct(shape, jnp.float32)
    if chunks:
        chunk = shape[:2] + (shape[2] // chunks,)
        out_shape = [jax.ShapeDtypeStruct(chunk, jnp.bfloat16)] * chunks
    return pl.pallas_call(
        functools.partial(kernel, slots=slots, held=held, parts=len(parts), win=win),
        in_specs=[smem] + [vmem] * (2 + len(operands)),
        out_specs=[vmem] * chunks if chunks else vmem,
        out_shape=out_shape,
        scratch_shapes=[pltpu.VMEM(shape, jnp.float32)] * (chunks > 0),
        compiler_params=pltpu.CompilerParams(vmem_limit_bytes=backward_bytes),
        cost_estimate=light(),
        name="backward",
    )(meta, pupil, band_table, *operands)


def middle(streams, image, cos_table, sin_table):
    _, rows, crop_width = streams[0][0].shape
    band = rows * len(streams)
    terms = [term for stream in streams for term in stream]
    return pl.pallas_call(
        functools.partial(
            middle_kernel, terms=len(streams[0]), streams=len(streams)
        ),
        in_specs=[vmem] * (len(terms) + 3),
        out_specs=[vmem] * len(streams),
        out_shape=[jax.ShapeDtypeStruct((2, rows, crop_width), jnp.bfloat16)] * len(streams),
        scratch_shapes=[pltpu.VMEM((2 * band, crop_width), jnp.bfloat16)] * 2,
        compiler_params=params(),
        cost_estimate=light(),
        name="middle",
    )(*terms, image, cos_table, sin_table)


def fixed(array):
    return pl.BlockSpec(array.shape, lambda i: (0,) * array.ndim)


def forward_all(meta, low, pupil, band_table):
    win = Windows(*low[0].shape, pupil.shape[1])
    count = meta.shape[1]
    out_type = band_type(pupil, band_table, count)
    return pl.pallas_call(
        functools.partial(forward_grid_kernel, win=win),
        grid=(count,),
        in_specs=[smem] + [fixed(array) for array in (pupil, band_table, *low)],
        out_specs=pl.BlockSpec((1,) + out_type.shape[1:], lambda i: (i, 0, 0, 0)),
        out_shape=out_type,
        compiler_params=params(),
        name="forward_all",
    )(meta, pupil, band_table, *low)


def backward_all(meta, spectrum, pupil, band_table, backs):
    win = Windows(*spectrum.shape[1:], pupil.shape[1])
    return pl.pallas_call(
        functools.partial(backward_grid_kernel, win=win),
        grid=(meta.shape[1],),
        in_specs=[smem]
        + [fixed(array) for array in (pupil, band_table, spectrum)]
        + [pl.BlockSpec((1,) + backs.shape[1:], lambda i: (i, 0, 0, 0))],
        out_specs=fixed(spectrum),
        out_shape=jax.ShapeDtypeStruct(spectrum.shape, jnp.float32),
        compiler_params=params(),
        name="backward_all",
    )(meta, pupil, band_table, spectrum, backs)


def cast_kernel(spec_ref, out_ref, held, sems, *, part):
    blocks, _, width = held.shape
    columns = [pl.ds(block * width, width) for block in range(blocks)]
    copies = [
        pltpu.make_async_copy(spec_ref.at[part, :, columns[i]], held.at[i], sems.at[i])
        for i in range(blocks)
    ]
    for copy in copies:
        copy.start()
    for i, copy in enumerate(copies):
        copy.wait()
        out_ref[:, columns[i]] = held[i].astype(jnp.bfloat16)


def low_part(spectrum, part):
    _, rows, columns = spectrum.shape
    return pl.pallas_call(
        functools.partial(cast_kernel, part=part),
        in_specs=[pl.BlockSpec(memory_space=pltpu.HBM)],
        out_specs=vmem,
        out_shape=jax.ShapeDtypeStruct((rows, columns), jnp.bfloat16),
        scratch_shapes=[
            pltpu.VMEM((4, rows, columns // 4), jnp.float32),
            pltpu.SemaphoreType.DMA((4,)),
        ],
        compiler_params=params(),
        cost_estimate=light(),
        name="low_part",
    )(spectrum)


def total(*terms):
    return sum(term.astype(jnp.float32) for term in terms).astype(jnp.bfloat16)


def per_device(spectrum, pupil, measured, centre_rows, centre_cols):
    count = lax.axis_size("ty")
    planes = count // 4
    position = lax.axis_index("ty")
    plane = position // 4
    _, tile_rows, slab_columns = spectrum.shape
    crop_width = pupil.shape[0]
    band = measured.shape[1]
    band_start = (crop_width - band) // 2
    cos_table, sin_table = fourier_tables(crop_width)
    chosen_rows = slice(band_start, band_start + band)
    band_table = jnp.asarray(
        np.concatenate([cos_table[:, chosen_rows], sin_table[:, chosen_rows]], axis=1)
    )
    cos_table, sin_table = jnp.asarray(cos_table), jnp.asarray(sin_table)

    half = crop_width // 2

    low = [low_part(spectrum, part) for part in range(2)]

    def image_meta(ids, positions):
        match = ids[:, None] == jnp.arange(count, dtype=jnp.int32)[None, :]
        tops = jnp.sum(jnp.where(match, centre_rows[None, :], 0), axis=1) - half
        lefts = jnp.sum(jnp.where(match, centre_cols[None, :], 0), axis=1) - half
        rows = [place * tile_rows - tops for place in positions]
        return jnp.stack(rows + [lefts]).astype(jnp.int32)

    if planes != 4:
        meta = image_meta(jnp.arange(count, dtype=jnp.int32), [position])
        partial = forward_all(meta, low, pupil, band_table)
        mid = lax.psum_scatter(partial, "ty", scatter_dimension=0, tiled=True)[0]
        back = lax.all_gather(middle([[mid]], measured, cos_table, sin_table)[0], "ty")
        return backward_all(meta, spectrum, pupil, band_table, back)

    targets = {"far": (3, 3, 0, 0), "next": (2, 2, 1, 1), "beside": (1, 0, 3, 2), "own": (0, 1, 2, 3)}
    own_core = [("far", 2), ("far", 0), ("next", 2), ("next", 0)]
    own_core += [("beside", 2), ("beside", 0), ("own", 2), ("own", 0)]
    slots = {}
    for core in (0, 1):
        for name, y in own_core:
            slots[name, y + core] = len(slots)
    ids = [
        [targets[name][i // 4] * 4 + (i % 4 ^ flip) for (name, flip) in slots]
        for i in range(count)
    ]
    my_ids = lax.dynamic_index_in_dim(jnp.asarray(ids, jnp.int32), position, keepdims=False)
    meta = image_meta(my_ids, [position, position ^ 1])

    def sibling(value):
        return lax.ppermute(value, "ty", [(i, i ^ 1) for i in range(count)])

    def across(value):
        return lax.ppermute(value, "ty", [(i, i ^ 2) for i in range(count)])

    def along(value, plane_pairs):
        pairs = [(4 * a + i, 4 * b + i) for a, b in plane_pairs for i in range(4)]
        return lax.ppermute(value, "ty", pairs)

    inward = [(0, 1), (3, 2)]
    outward = [(1, 0), (2, 3)]
    inner = [(1, 2), (2, 1)]
    together = lax.optimization_barrier

    lows = [low, [sibling(part) for part in low]]
    streams = 2
    (own_rows,) = forward(meta, lows[:1], pupil, band_table, 0, 1, (0,))
    far_leaving = forward(
        meta, lows[1:], pupil, band_table, 0, 1, (1,), own_rows, streams=streams
    )
    far_other = [across(value) for value in far_leaving]
    made = forward(
        together((meta, far_leaving[0]))[0], lows, pupil, band_table, 1, 7, streams=streams
    )
    summed, held = [], None
    for stream in reversed(range(streams)):
        (
            far_kept,
            next_leaving,
            next_kept,
            beside_leaving,
            beside_kept,
            own_leaving,
            own_kept,
        ) = made[stream::streams]
        far, far_kept, next_leaving = together((far_other[stream], far_kept, next_leaving))

        next_other = across(next_leaving)
        from_end = along(total(far_kept, far), inward)
        from_end, next_other, beside_leaving = together((from_end, next_other, beside_leaving))

        beside_other = across(beside_leaving)
        next_inward = along(total(next_kept, next_other), inward)
        far_inner = along(total(far_kept, far, from_end), inner)
        far_inner, next_inward, beside_other, own_leaving = together(
            (far_inner, next_inward, beside_other, own_leaving)
        )

        own_other = across(own_leaving)
        next_inner = along(total(next_kept, next_other, next_inward), inner)
        beside = along(total(beside_kept, beside_other, far_inner), inward + outward)
        terms = [own_kept, own_other, next_inner, beside]
        if stream > 0:
            terms = [total(*terms)]
            held = terms[0]
        else:
            terms[0] = together((terms[0], held))[0]
            terms = [total(*terms)]
        summed.insert(0, terms)
    backs = middle(summed, measured, cos_table, sin_table)

    at_ends = (plane == 0) | (plane == 3)
    lead, last = streams - 1, 0
    pieces = {}

    def apply(parts, names, chunks=0):
        taken = [[pieces.get((name, stream)) for stream in range(streams)] for name in names]
        own_slots = [slots[name] for name in names]
        shape = spectrum.shape
        return backward(meta, shape, pupil, band_table, parts, own_slots, taken, chunks)

    def close(stream, *names):
        closed = together(tuple(pieces[name, stream] for name in names))
        for name, value in zip(names, closed):
            pieces[name, stream] = value

    for stream in (lead, last):
        back = pieces[("own", 0), stream] = backs[stream]
        pieces[("own", 2), stream] = across(back)
        pieces["inner", stream] = along(back, inner)
        pieces[("beside", 0), stream] = along(back, inward + outward)
        close(stream, ("own", 2), "inner", ("beside", 0))
    early, later, late = (
        [("own", 0), ("beside", 0), ("own", 2)],
        [("next", 0), ("beside", 2)],
        [("far", 0), ("next", 2)],
    )
    for stream in (lead, last):
        pieces[("beside", 2), stream] = across(pieces[("beside", 0), stream])
        pieces["far inner", stream] = along(pieces[("beside", 0), stream], inner)
        pieces["outward", stream] = along(pieces["inner", stream], outward)
        if stream == last:
            pieces["result", stream] = apply([spectrum], early)
            close(stream, ("beside", 2), "far inner", "outward", "result")
        else:
            close(stream, ("beside", 2), "far inner", "outward")
    for stream in (lead, last):
        from_next = jnp.where(at_ends, pieces["outward", stream], pieces["inner", stream])
        pieces[("next", 0), stream] = from_next
        pieces[("next", 2), stream] = across(from_next)
        pieces["far outward", stream] = along(pieces["far inner", stream], outward)
        if stream == lead:
            pieces["slab", stream] = apply([], early, 1)[0]
        else:
            pieces["slab", stream] = apply([pieces["slab", lead]], later, 1)[0]
        close(stream, ("next", 2), "far outward", "slab")
    for stream in (lead, last):
        from_far = jnp.where(at_ends, pieces["far outward", stream], pieces["far inner", stream])
        pieces[("far", 0), stream] = from_far
        pieces[("far", 2), stream] = across(from_far)
    slab, pieces[("far", 2), lead] = together((pieces["slab", last], pieces[("far", 2), lead]))
    slab = [sibling(chunk) for chunk in apply([slab], late, 2)]
    result = apply([pieces["result", last]], later + late)
    for stream in (lead, last):
        if stream == last:
            arriving, result, twin = together(
                (pieces[("far", 2), stream], result, pieces[("far", 3), lead])
            )
            pieces[("far", 2), stream], pieces[("far", 3), lead] = arriving, twin
        pieces[("far", 3), stream] = sibling(pieces[("far", 2), stream])
    return apply([result] + slab, [("far", 2), ("far", 3)])


def solution(mesh):
    return jax.shard_map(
        per_device,
        mesh=mesh,
        in_specs=(
            P(None, ("groups", "ty"), None),
            P(),
            P(("groups", "ty"), None, None),
            P("groups"),
            P("groups"),
        ),
        out_specs=P(None, ("groups", "ty"), None),
        check_vma=False,
    )
```

```python
import functools
import math

import jax
import jax.numpy as jnp
import numpy as np
from jax import lax
from jax.experimental import pallas as pl
from jax.experimental.pallas import tpu as pltpu
from jax.sharding import PartitionSpec as P

step_size = 0.5
lane = 128
row_tile = 16
vmem_bytes = 20 * 1024 * 1024
backward_bytes = 20 * 1024 * 1024


def fourier_tables(crop_width):
    counter = np.arange(crop_width, dtype=np.int64)
    angle = (counter[:, None] * counter[None, :] % crop_width) * (2.0 * math.pi / crop_width)
    factor = 1.0 / math.sqrt(crop_width)
    cos_table = (np.cos(angle) * factor).astype(np.float32).astype(jnp.bfloat16)
    sin_table = (np.sin(angle) * factor).astype(np.float32).astype(jnp.bfloat16)
    return cos_table, sin_table


def tile_weight(pupil_ref, first_row, win):
    start = win.row(first_row)
    rows = pupil_ref[pl.ds(start, win.rows), :].astype(jnp.float32)
    rows = pltpu.roll(rows, (2 * win.rows + start - first_row) % win.rows, 0)
    shape = (win.tile_rows, win.crop_width)
    row = 2 * (first_row + lax.broadcasted_iota(jnp.int32, shape, 0)) - win.crop_width + 1
    column = 2 * lax.broadcasted_iota(jnp.int32, shape, 1) - win.crop_width + 1
    inside = row * row + column * column <= win.crop_width * win.crop_width
    return jnp.where(inside, rows[: win.tile_rows], 0.0)


def tile_band(band_ref, first_row, win):
    start = win.row(first_row)
    rows = band_ref[pl.ds(start, win.rows), :].astype(jnp.float32)
    rows = pltpu.roll(rows, (2 * win.rows + start - first_row) % win.rows, 0)[: win.tile_rows]
    band = rows.shape[1] // 2
    turned = jnp.concatenate([-rows[:, band:], rows[:, :band]], axis=1)
    return jnp.concatenate([rows, turned], axis=0).astype(jnp.bfloat16)


class Windows:
    def __init__(self, tile_rows, slab_columns, crop_width):
        self.tile_rows = tile_rows
        self.crop_width = crop_width
        self.rows = tile_rows + row_tile
        self.columns = crop_width + lane
        self.last_row = crop_width - self.rows
        self.last_column = slab_columns - self.columns

    def row(self, first_row):
        start = jnp.clip(first_row, 0, self.last_row) // row_tile * row_tile
        return pl.multiple_of(start, row_tile)

    def column(self, left):
        start = jnp.minimum(left // lane * lane, self.last_column)
        return pl.multiple_of(start, lane)

    def active(self, first_row):
        return (first_row > -self.tile_rows) & (first_row < self.crop_width)


def image_band(meta_ref, slot, lows, tiles, pupil_ref, band_ref, win, store, came=None):
    left = meta_ref[meta_ref.shape[0] - 1, slot]
    first_rows = [meta_ref[tile, slot] for tile in tiles]
    active = functools.reduce(jnp.logical_or, [win.active(row) for row in first_rows])
    band = band_ref.shape[1] // 2
    shape = (2, band, win.crop_width)

    @pl.when(jnp.logical_not(active))
    def _():
        store(jnp.zeros(shape, jnp.bfloat16) if came is None else came[...])

    @pl.when(active)
    def _():
        col_start = win.column(left)
        shift = (win.columns - (left - col_start)) % win.columns
        parts, tables = [], []
        for first_row, low_refs in zip(first_rows, lows):
            weight = tile_weight(pupil_ref, first_row, win)
            for low_ref in low_refs:
                low = low_ref[:, pl.ds(col_start, win.columns)].astype(jnp.float32)
                low = pltpu.roll(low, shift, 1)[:, : win.crop_width]
                parts.append((weight * low).astype(jnp.bfloat16))
            tables.append(tile_band(band_ref, first_row, win))
        mid = lax.dot_general(
            jnp.concatenate(tables, axis=0),
            jnp.concatenate(parts, axis=0),
            (((0,), (0,)), ((), ())),
            preferred_element_type=jnp.float32,
        )
        if came is not None:
            mid = mid + came[...].reshape(mid.shape).astype(jnp.float32)
        store(mid.astype(jnp.bfloat16).reshape(shape))


def forward_kernel(meta_ref, pupil_ref, band_ref, *refs, base, images, count, win, tiles):
    out_refs = refs[-count:]
    lows = [refs[2 * half : 2 * half + 2] for half in range(len(tiles))]
    came = refs[2 * len(tiles)] if len(refs) > 2 * len(tiles) + count else None
    streams = count // images

    def image(index):
        def store(value):
            for number in range(images):

                @pl.when(index == number)
                def _():
                    for stream in range(streams):
                        out_ref = out_refs[number * streams + stream]
                        rows = out_ref.shape[1]
                        out_ref[...] = value[:, stream * rows : (stream + 1) * rows]

        image_band(meta_ref, base + index, lows, tiles, pupil_ref, band_ref, win, store, came)

    pl.loop(0, images)(image)


def forward_grid_kernel(meta_ref, pupil_ref, band_ref, real_ref, imag_ref, out_ref, *, win):
    def store(value):
        out_ref[0] = value

    lows = [(real_ref, imag_ref)]
    image_band(meta_ref, pl.program_id(0), lows, (0,), pupil_ref, band_ref, win, store)


def subtract_image(meta_ref, slot, back_refs, pupil_ref, band_ref, out_ref, win, tile=0):
    first_row, left = meta_ref[tile, slot], meta_ref[meta_ref.shape[0] - 1, slot]
    tile_rows, crop_width = win.tile_rows, win.crop_width

    @pl.when(win.active(first_row))
    def _():
        col_start = win.column(left)
        weight = tile_weight(pupil_ref, first_row, win) * step_size
        table = tile_band(band_ref, first_row, win)
        band = table.shape[1] // 2
        rows = band // len(back_refs)
        held = [number for number, ref in enumerate(back_refs) if ref is not None]
        if len(held) < len(back_refs):
            starts = [part * band + number * rows for part in range(2) for number in held]
            table = jnp.concatenate([table[:, start : start + rows] for start in starts], axis=1)
        back = [back_refs[number][part] for part in range(2) for number in held]
        back = jnp.concatenate(back, axis=0)
        grad = jnp.dot(table, back, preferred_element_type=jnp.float32)
        columns = pl.ds(col_start, win.columns)
        pad = jnp.zeros((tile_rows, win.columns - crop_width), jnp.float32)
        for part in range(2):
            piece = grad[part * tile_rows : (part + 1) * tile_rows] * weight
            piece = pltpu.roll(jnp.concatenate([piece, pad], axis=1), left - col_start, 1)
            out_ref[part, :, columns] = out_ref[part, :, columns] - piece


def backward_kernel(meta_ref, pupil_ref, band_ref, *refs, slots, held, parts, win):
    part_refs, back_refs, out_ref = refs[:parts], iter(refs[parts:-1]), refs[-1]
    for number in range(parts - 1):
        chunk = part_refs[number + 1][...].astype(jnp.float32)
        width = chunk.shape[2]
        columns = slice(number * width, (number + 1) * width)
        out_ref[:, :, columns] = part_refs[0][:, :, columns] + chunk
    if parts == 1:
        out_ref[...] = part_refs[0][...]
    for slot, groups in zip(slots, held):
        of_image = [next(back_refs) if there else None for there in groups]
        subtract_image(meta_ref, slot, of_image, pupil_ref, band_ref, out_ref, win)


def sibling_kernel(meta_ref, pupil_ref, band_ref, *refs, slots, held, parts, win):
    backs = sum(map(sum, held))
    part_refs, back_refs, total_ref = refs[:parts], iter(refs[parts : parts + backs]), refs[-1]
    out_refs = refs[parts + backs : -1]
    if parts:
        total_ref[...] = part_refs[0][...].astype(jnp.float32)
    else:
        total_ref[...] = jnp.zeros_like(total_ref)
    for slot, groups in zip(slots, held):
        of_image = [next(back_refs) if there else None for there in groups]
        subtract_image(meta_ref, slot, of_image, pupil_ref, band_ref, total_ref, win, 1)
    width = out_refs[0].shape[2]
    for number, out_ref in enumerate(out_refs):
        out_ref[...] = total_ref[:, :, number * width : (number + 1) * width].astype(jnp.bfloat16)


def backward_grid_kernel(meta_ref, pupil_ref, band_ref, spec_ref, back_ref, out_ref, *, win):
    step = pl.program_id(0)

    @pl.when(step == 0)
    def _():
        out_ref[...] = spec_ref[...]

    subtract_image(meta_ref, step, [back_ref.at[0]], pupil_ref, band_ref, out_ref, win)


def middle_kernel(*refs, terms, streams):
    term_refs, refs = refs[: terms * streams], refs[terms * streams :]
    (image_ref, cos_ref, sin_ref), refs = refs[:3], refs[3:]
    out_refs, (mid_ref, resid_ref) = refs[:streams], refs[streams:]
    _, rows, crop_width = term_refs[0].shape
    band = rows * streams
    block = min(512, crop_width)
    for stream in range(streams):
        of_stream = term_refs[stream * terms : (stream + 1) * terms]
        total = sum(ref[...].astype(jnp.float32) for ref in of_stream).astype(jnp.bfloat16)
        for part in range(2):
            start = part * band + stream * rows
            mid_ref[start : start + rows] = total[part]
    dot = functools.partial(jnp.dot, preferred_element_type=jnp.float32)
    for start in range(0, crop_width, block):
        columns = slice(start, start + block)
        by_cos = dot(mid_ref[...], cos_ref[:, columns])
        by_sin = dot(mid_ref[...], sin_ref[:, columns])
        field_real = by_cos[:band] - by_sin[band:]
        field_imag = by_sin[:band] + by_cos[band:]
        power = field_real * field_real + field_imag * field_imag
        measured = image_ref[0, :, columns].astype(jnp.float32)
        keeping = 1.0 - measured * lax.rsqrt(jnp.maximum(power, 1.0))
        resid_ref[:band, columns] = (field_real * keeping).astype(jnp.bfloat16)
        resid_ref[band:, columns] = (field_imag * keeping).astype(jnp.bfloat16)
    for start in range(0, crop_width, block):
        columns = slice(start, start + block)
        by_cos = dot(resid_ref[...], cos_ref[:, columns])
        by_sin = dot(resid_ref[...], sin_ref[:, columns])
        for part, back in enumerate((by_cos[:band] + by_sin[band:], by_cos[band:] - by_sin[:band])):
            for stream, out_ref in enumerate(out_refs):
                of_stream = back[stream * rows : (stream + 1) * rows]
                out_ref[part, :, columns] = of_stream.astype(jnp.bfloat16)


def params():
    return pltpu.CompilerParams(vmem_limit_bytes=vmem_bytes)


def light():
    return pl.CostEstimate(flops=1024, bytes_accessed=1024, transcendentals=0)


vmem = pl.BlockSpec(memory_space=pltpu.VMEM)
smem = pl.BlockSpec(memory_space=pltpu.SMEM)


def band_type(pupil, band_table, *lead):
    shape = lead + (2, band_table.shape[1] // 2, pupil.shape[1])
    return jax.ShapeDtypeStruct(shape, jnp.bfloat16)


def forward(meta, lows, pupil, band_table, base, images, tiles=(0, 1), came=None, streams=1):
    win = Windows(*lows[0][0].shape, pupil.shape[1])
    operands = [meta, pupil, band_table] + [part for low in lows for part in low]
    operands += [came] * (came is not None)
    count = images * streams
    _, rows, columns = band_type(pupil, band_table).shape
    return pl.pallas_call(
        functools.partial(
            forward_kernel, base=base, images=images, count=count, win=win, tiles=tiles
        ),
        in_specs=[smem] + [vmem] * (len(operands) - 1),
        out_specs=[vmem] * count,
        out_shape=[jax.ShapeDtypeStruct((2, rows // streams, columns), jnp.bfloat16)] * count,
        compiler_params=params(),
        cost_estimate=light(),
        name="forward",
    )(*operands)


def backward(meta, shape, pupil, band_table, parts, slots, backs, chunks=0):
    win = Windows(*shape[1:], pupil.shape[1])
    held = [[back is not None for back in groups] for groups in backs]
    operands = list(parts) + [back for groups in backs for back in groups if back is not None]
    kernel = sibling_kernel if chunks else backward_kernel
    out_shape = jax.ShapeDtypeStruct(shape, jnp.float32)
    if chunks:
        chunk = shape[:2] + (shape[2] // chunks,)
        out_shape = [jax.ShapeDtypeStruct(chunk, jnp.bfloat16)] * chunks
    return pl.pallas_call(
        functools.partial(kernel, slots=slots, held=held, parts=len(parts), win=win),
        in_specs=[smem] + [vmem] * (2 + len(operands)),
        out_specs=[vmem] * chunks if chunks else vmem,
        out_shape=out_shape,
        scratch_shapes=[pltpu.VMEM(shape, jnp.float32)] * (chunks > 0),
        compiler_params=pltpu.CompilerParams(vmem_limit_bytes=backward_bytes),
        cost_estimate=light(),
        name="backward",
    )(meta, pupil, band_table, *operands)


def middle(streams, image, cos_table, sin_table):
    _, rows, crop_width = streams[0][0].shape
    band = rows * len(streams)
    terms = [term for stream in streams for term in stream]
    return pl.pallas_call(
        functools.partial(
            middle_kernel, terms=len(streams[0]), streams=len(streams)
        ),
        in_specs=[vmem] * (len(terms) + 3),
        out_specs=[vmem] * len(streams),
        out_shape=[jax.ShapeDtypeStruct((2, rows, crop_width), jnp.bfloat16)] * len(streams),
        scratch_shapes=[pltpu.VMEM((2 * band, crop_width), jnp.bfloat16)] * 2,
        compiler_params=params(),
        cost_estimate=light(),
        name="middle",
    )(*terms, image, cos_table, sin_table)


def fixed(array):
    return pl.BlockSpec(array.shape, lambda i: (0,) * array.ndim)


def forward_all(meta, low, pupil, band_table):
    win = Windows(*low[0].shape, pupil.shape[1])
    count = meta.shape[1]
    out_type = band_type(pupil, band_table, count)
    return pl.pallas_call(
        functools.partial(forward_grid_kernel, win=win),
        grid=(count,),
        in_specs=[smem] + [fixed(array) for array in (pupil, band_table, *low)],
        out_specs=pl.BlockSpec((1,) + out_type.shape[1:], lambda i: (i, 0, 0, 0)),
        out_shape=out_type,
        compiler_params=params(),
        name="forward_all",
    )(meta, pupil, band_table, *low)


def backward_all(meta, spectrum, pupil, band_table, backs):
    win = Windows(*spectrum.shape[1:], pupil.shape[1])
    return pl.pallas_call(
        functools.partial(backward_grid_kernel, win=win),
        grid=(meta.shape[1],),
        in_specs=[smem]
        + [fixed(array) for array in (pupil, band_table, spectrum)]
        + [pl.BlockSpec((1,) + backs.shape[1:], lambda i: (i, 0, 0, 0))],
        out_specs=fixed(spectrum),
        out_shape=jax.ShapeDtypeStruct(spectrum.shape, jnp.float32),
        compiler_params=params(),
        name="backward_all",
    )(meta, pupil, band_table, spectrum, backs)


def cast_kernel(spec_ref, out_ref, held, sems, *, part):
    blocks, _, width = held.shape
    columns = [pl.ds(block * width, width) for block in range(blocks)]
    copies = [
        pltpu.make_async_copy(spec_ref.at[part, :, columns[i]], held.at[i], sems.at[i])
        for i in range(blocks)
    ]
    for copy in copies:
        copy.start()
    for i, copy in enumerate(copies):
        copy.wait()
        out_ref[:, columns[i]] = held[i].astype(jnp.bfloat16)


def low_part(spectrum, part):
    _, rows, columns = spectrum.shape
    return pl.pallas_call(
        functools.partial(cast_kernel, part=part),
        in_specs=[pl.BlockSpec(memory_space=pltpu.HBM)],
        out_specs=vmem,
        out_shape=jax.ShapeDtypeStruct((rows, columns), jnp.bfloat16),
        scratch_shapes=[
            pltpu.VMEM((4, rows, columns // 4), jnp.float32),
            pltpu.SemaphoreType.DMA((4,)),
        ],
        compiler_params=params(),
        cost_estimate=light(),
        name="low_part",
    )(spectrum)


def total(*terms):
    return sum(term.astype(jnp.float32) for term in terms).astype(jnp.bfloat16)


def per_device(spectrum, pupil, measured, centre_rows, centre_cols):
    count = lax.axis_size("ty")
    planes = count // 4
    position = lax.axis_index("ty")
    plane = position // 4
    _, tile_rows, slab_columns = spectrum.shape
    crop_width = pupil.shape[0]
    band = measured.shape[1]
    band_start = (crop_width - band) // 2
    cos_table, sin_table = fourier_tables(crop_width)
    chosen_rows = slice(band_start, band_start + band)
    band_table = jnp.asarray(
        np.concatenate([cos_table[:, chosen_rows], sin_table[:, chosen_rows]], axis=1)
    )
    cos_table, sin_table = jnp.asarray(cos_table), jnp.asarray(sin_table)

    half = crop_width // 2

    low = [low_part(spectrum, part) for part in range(2)]

    def image_meta(ids, positions):
        match = ids[:, None] == jnp.arange(count, dtype=jnp.int32)[None, :]
        tops = jnp.sum(jnp.where(match, centre_rows[None, :], 0), axis=1) - half
        lefts = jnp.sum(jnp.where(match, centre_cols[None, :], 0), axis=1) - half
        rows = [place * tile_rows - tops for place in positions]
        return jnp.stack(rows + [lefts]).astype(jnp.int32)

    if planes != 4:
        meta = image_meta(jnp.arange(count, dtype=jnp.int32), [position])
        partial = forward_all(meta, low, pupil, band_table)
        mid = lax.psum_scatter(partial, "ty", scatter_dimension=0, tiled=True)[0]
        back = lax.all_gather(middle([[mid]], measured, cos_table, sin_table)[0], "ty")
        return backward_all(meta, spectrum, pupil, band_table, back)

    targets = {"far": (3, 3, 0, 0), "next": (2, 2, 1, 1), "beside": (1, 0, 3, 2), "own": (0, 1, 2, 3)}
    own_core = [("far", 2), ("far", 0), ("next", 2), ("next", 0)]
    own_core += [("beside", 2), ("beside", 0), ("own", 2), ("own", 0)]
    slots = {}
    for core in (0, 1):
        for name, y in own_core:
            slots[name, y + core] = len(slots)
    ids = [
        [targets[name][i // 4] * 4 + (i % 4 ^ flip) for (name, flip) in slots]
        for i in range(count)
    ]
    my_ids = lax.dynamic_index_in_dim(jnp.asarray(ids, jnp.int32), position, keepdims=False)
    meta = image_meta(my_ids, [position, position ^ 1])

    def sibling(value):
        return lax.ppermute(value, "ty", [(i, i ^ 1) for i in range(count)])

    def across(value):
        return lax.ppermute(value, "ty", [(i, i ^ 2) for i in range(count)])

    def along(value, plane_pairs):
        pairs = [(4 * a + i, 4 * b + i) for a, b in plane_pairs for i in range(4)]
        return lax.ppermute(value, "ty", pairs)

    inward = [(0, 1), (3, 2)]
    outward = [(1, 0), (2, 3)]
    inner = [(1, 2), (2, 1)]
    together = lax.optimization_barrier

    lows = [low, [sibling(part) for part in low]]
    streams = 2
    (own_rows,) = forward(meta, lows[:1], pupil, band_table, 0, 1, (0,))
    far_leaving = forward(
        meta, lows[1:], pupil, band_table, 0, 1, (1,), own_rows, streams=streams
    )
    far_other = [across(value) for value in far_leaving]
    made = forward(
        together((meta, far_leaving[0]))[0], lows, pupil, band_table, 1, 7, streams=streams
    )
    summed, held = [], None
    for stream in reversed(range(streams)):
        (
            far_kept,
            next_leaving,
            next_kept,
            beside_leaving,
            beside_kept,
            own_leaving,
            own_kept,
        ) = made[stream::streams]
        far, far_kept, next_leaving = together((far_other[stream], far_kept, next_leaving))

        next_other = across(next_leaving)
        from_end = along(total(far_kept, far), inward)
        from_end, next_other, beside_leaving = together((from_end, next_other, beside_leaving))

        beside_other = across(beside_leaving)
        next_inward = along(total(next_kept, next_other), inward)
        far_inner = along(total(far_kept, far, from_end), inner)
        far_inner, next_inward, beside_other, own_leaving = together(
            (far_inner, next_inward, beside_other, own_leaving)
        )

        own_other = across(own_leaving)
        next_inner = along(total(next_kept, next_other, next_inward), inner)
        beside = along(total(beside_kept, beside_other, far_inner), inward + outward)
        terms = [own_kept, own_other, next_inner, beside]
        if stream > 0:
            terms = [total(*terms)]
            held = terms[0]
        else:
            terms[0] = together((terms[0], held))[0]
            terms = [total(*terms)]
        summed.insert(0, terms)
    backs = middle(summed, measured, cos_table, sin_table)

    at_ends = (plane == 0) | (plane == 3)
    lead, last = streams - 1, 0
    pieces = {}

    def apply(parts, names, chunks=0):
        taken = [[pieces.get((name, stream)) for stream in range(streams)] for name in names]
        own_slots = [slots[name] for name in names]
        shape = spectrum.shape
        return backward(meta, shape, pupil, band_table, parts, own_slots, taken, chunks)

    def close(stream, *names):
        closed = together(tuple(pieces[name, stream] for name in names))
        for name, value in zip(names, closed):
            pieces[name, stream] = value

    for stream in (lead, last):
        back = pieces[("own", 0), stream] = backs[stream]
        pieces[("own", 2), stream] = across(back)
        pieces["inner", stream] = along(back, inner)
        pieces[("beside", 0), stream] = along(back, inward + outward)
        close(stream, ("own", 2), "inner", ("beside", 0))
    early, later, late = (
        [("own", 0), ("beside", 0), ("own", 2)],
        [("next", 0), ("beside", 2)],
        [("far", 0), ("next", 2)],
    )
    for stream in (lead, last):
        pieces[("beside", 2), stream] = across(pieces[("beside", 0), stream])
        pieces["far inner", stream] = along(pieces[("beside", 0), stream], inner)
        pieces["outward", stream] = along(pieces["inner", stream], outward)
        if stream == last:
            pieces["result", stream] = apply([spectrum], early)
            close(stream, ("beside", 2), "far inner", "outward", "result")
        else:
            pieces["slab", stream] = apply([], early, 1)[0]
            close(stream, ("beside", 2), "far inner", "outward", "slab")
    for stream in (lead, last):
        from_next = jnp.where(at_ends, pieces["outward", stream], pieces["inner", stream])
        pieces[("next", 0), stream] = from_next
        pieces[("next", 2), stream] = across(from_next)
        pieces["far outward", stream] = along(pieces["far inner", stream], outward)
        if stream == last:
            pieces["slab", stream] = apply([pieces["slab", lead]], later, 1)[0]
            close(stream, ("next", 2), "far outward", "slab")
        else:
            close(stream, ("next", 2), "far outward")
    for stream in (lead, last):
        from_far = jnp.where(at_ends, pieces["far outward", stream], pieces["far inner", stream])
        pieces[("far", 0), stream] = from_far
        pieces[("far", 2), stream] = across(from_far)
    slab, pieces[("far", 2), lead] = together((pieces["slab", last], pieces[("far", 2), lead]))
    slab = [sibling(chunk) for chunk in apply([slab], late, 2)]
    result = apply([pieces["result", last]], later + late)
    for stream in (lead, last):
        if stream == last:
            arriving, result, twin = together(
                (pieces[("far", 2), stream], result, pieces[("far", 3), lead])
            )
            pieces[("far", 2), stream], pieces[("far", 3), lead] = arriving, twin
        pieces[("far", 3), stream] = sibling(pieces[("far", 2), stream])
    return apply([result] + slab, [("far", 2), ("far", 3)])


def solution(mesh):
    return jax.shard_map(
        per_device,
        mesh=mesh,
        in_specs=(
            P(None, ("groups", "ty"), None),
            P(),
            P(("groups", "ty"), None, None),
            P("groups"),
            P("groups"),
        ),
        out_specs=P(None, ("groups", "ty"), None),
        check_vma=False,
    )
```

```python
import functools
import math

import jax
import jax.numpy as jnp
import numpy as np
from jax import lax
from jax.experimental import pallas as pl
from jax.experimental.pallas import tpu as pltpu
from jax.sharding import PartitionSpec as P

step_size = 0.5
lane = 128
row_tile = 16
vmem_bytes = 20 * 1024 * 1024
backward_bytes = 20 * 1024 * 1024


def fourier_tables(crop_width):
    counter = np.arange(crop_width, dtype=np.int64)
    angle = (counter[:, None] * counter[None, :] % crop_width) * (2.0 * math.pi / crop_width)
    factor = 1.0 / math.sqrt(crop_width)
    cos_table = (np.cos(angle) * factor).astype(np.float32).astype(jnp.bfloat16)
    sin_table = (np.sin(angle) * factor).astype(np.float32).astype(jnp.bfloat16)
    return cos_table, sin_table


def tile_weight(pupil_ref, first_row, win):
    start = win.row(first_row)
    rows = pupil_ref[pl.ds(start, win.rows), :].astype(jnp.float32)
    rows = pltpu.roll(rows, (2 * win.rows + start - first_row) % win.rows, 0)
    shape = (win.tile_rows, win.crop_width)
    row = 2 * (first_row + lax.broadcasted_iota(jnp.int32, shape, 0)) - win.crop_width + 1
    column = 2 * lax.broadcasted_iota(jnp.int32, shape, 1) - win.crop_width + 1
    inside = row * row + column * column <= win.crop_width * win.crop_width
    return jnp.where(inside, rows[: win.tile_rows], 0.0)


def tile_band(band_ref, first_row, win):
    start = win.row(first_row)
    rows = band_ref[pl.ds(start, win.rows), :].astype(jnp.float32)
    rows = pltpu.roll(rows, (2 * win.rows + start - first_row) % win.rows, 0)[: win.tile_rows]
    band = rows.shape[1] // 2
    turned = jnp.concatenate([-rows[:, band:], rows[:, :band]], axis=1)
    return jnp.concatenate([rows, turned], axis=0).astype(jnp.bfloat16)


class Windows:
    def __init__(self, tile_rows, slab_columns, crop_width):
        self.tile_rows = tile_rows
        self.crop_width = crop_width
        self.rows = tile_rows + row_tile
        self.columns = crop_width + lane
        self.last_row = crop_width - self.rows
        self.last_column = slab_columns - self.columns

    def row(self, first_row):
        start = jnp.clip(first_row, 0, self.last_row) // row_tile * row_tile
        return pl.multiple_of(start, row_tile)

    def column(self, left):
        start = jnp.minimum(left // lane * lane, self.last_column)
        return pl.multiple_of(start, lane)

    def active(self, first_row):
        return (first_row > -self.tile_rows) & (first_row < self.crop_width)


def image_band(meta_ref, slot, lows, tiles, pupil_ref, band_ref, win, store, came=None):
    left = meta_ref[meta_ref.shape[0] - 1, slot]
    first_rows = [meta_ref[tile, slot] for tile in tiles]
    active = functools.reduce(jnp.logical_or, [win.active(row) for row in first_rows])
    band = band_ref.shape[1] // 2
    shape = (2, band, win.crop_width)

    @pl.when(jnp.logical_not(active))
    def _():
        store(jnp.zeros(shape, jnp.bfloat16) if came is None else came[...])

    @pl.when(active)
    def _():
        col_start = win.column(left)
        shift = (win.columns - (left - col_start)) % win.columns
        parts, tables = [], []
        for first_row, low_refs in zip(first_rows, lows):
            weight = tile_weight(pupil_ref, first_row, win)
            for low_ref in low_refs:
                low = low_ref[:, pl.ds(col_start, win.columns)].astype(jnp.float32)
                low = pltpu.roll(low, shift, 1)[:, : win.crop_width]
                parts.append((weight * low).astype(jnp.bfloat16))
            tables.append(tile_band(band_ref, first_row, win))
        mid = lax.dot_general(
            jnp.concatenate(tables, axis=0),
            jnp.concatenate(parts, axis=0),
            (((0,), (0,)), ((), ())),
            preferred_element_type=jnp.float32,
        )
        if came is not None:
            mid = mid + came[...].reshape(mid.shape).astype(jnp.float32)
        store(mid.astype(jnp.bfloat16).reshape(shape))


def forward_kernel(meta_ref, pupil_ref, band_ref, *refs, base, images, count, win, tiles):
    out_refs = refs[-count:]
    lows = [refs[2 * half : 2 * half + 2] for half in range(len(tiles))]
    came = refs[2 * len(tiles)] if len(refs) > 2 * len(tiles) + count else None
    streams = count // images

    def image(index):
        def store(value):
            for number in range(images):

                @pl.when(index == number)
                def _():
                    for stream in range(streams):
                        out_ref = out_refs[number * streams + stream]
                        rows = out_ref.shape[1]
                        out_ref[...] = value[:, stream * rows : (stream + 1) * rows]

        image_band(meta_ref, base + index, lows, tiles, pupil_ref, band_ref, win, store, came)

    pl.loop(0, images)(image)


def forward_grid_kernel(meta_ref, pupil_ref, band_ref, real_ref, imag_ref, out_ref, *, win):
    def store(value):
        out_ref[0] = value

    lows = [(real_ref, imag_ref)]
    image_band(meta_ref, pl.program_id(0), lows, (0,), pupil_ref, band_ref, win, store)


def subtract_image(meta_ref, slot, back_refs, pupil_ref, band_ref, out_ref, win, tile=0):
    first_row, left = meta_ref[tile, slot], meta_ref[meta_ref.shape[0] - 1, slot]
    tile_rows, crop_width = win.tile_rows, win.crop_width

    @pl.when(win.active(first_row))
    def _():
        col_start = win.column(left)
        weight = tile_weight(pupil_ref, first_row, win) * step_size
        table = tile_band(band_ref, first_row, win)
        band = table.shape[1] // 2
        rows = band // len(back_refs)
        held = [number for number, ref in enumerate(back_refs) if ref is not None]
        if len(held) < len(back_refs):
            starts = [part * band + number * rows for part in range(2) for number in held]
            table = jnp.concatenate([table[:, start : start + rows] for start in starts], axis=1)
        back = [back_refs[number][part] for part in range(2) for number in held]
        back = jnp.concatenate(back, axis=0)
        grad = jnp.dot(table, back, preferred_element_type=jnp.float32)
        columns = pl.ds(col_start, win.columns)
        pad = jnp.zeros((tile_rows, win.columns - crop_width), jnp.float32)
        for part in range(2):
            piece = grad[part * tile_rows : (part + 1) * tile_rows] * weight
            piece = pltpu.roll(jnp.concatenate([piece, pad], axis=1), left - col_start, 1)
            out_ref[part, :, columns] = out_ref[part, :, columns] - piece


def backward_kernel(meta_ref, pupil_ref, band_ref, *refs, slots, held, parts, win):
    part_refs, back_refs, out_ref = refs[:parts], iter(refs[parts:-1]), refs[-1]
    for number in range(parts - 1):
        chunk = part_refs[number + 1][...].astype(jnp.float32)
        width = chunk.shape[2]
        columns = slice(number * width, (number + 1) * width)
        out_ref[:, :, columns] = part_refs[0][:, :, columns] + chunk
    if parts == 1:
        out_ref[...] = part_refs[0][...]
    for slot, groups in zip(slots, held):
        of_image = [next(back_refs) if there else None for there in groups]
        subtract_image(meta_ref, slot, of_image, pupil_ref, band_ref, out_ref, win)


def sibling_kernel(meta_ref, pupil_ref, band_ref, *refs, slots, held, parts, win):
    backs = sum(map(sum, held))
    part_refs, back_refs, total_ref = refs[:parts], iter(refs[parts : parts + backs]), refs[-1]
    out_refs = refs[parts + backs : -1]
    if parts:
        total_ref[...] = part_refs[0][...].astype(jnp.float32)
    else:
        total_ref[...] = jnp.zeros_like(total_ref)
    for slot, groups in zip(slots, held):
        of_image = [next(back_refs) if there else None for there in groups]
        subtract_image(meta_ref, slot, of_image, pupil_ref, band_ref, total_ref, win, 1)
    width = out_refs[0].shape[2]
    for number, out_ref in enumerate(out_refs):
        out_ref[...] = total_ref[:, :, number * width : (number + 1) * width].astype(jnp.bfloat16)


def backward_grid_kernel(meta_ref, pupil_ref, band_ref, spec_ref, back_ref, out_ref, *, win):
    step = pl.program_id(0)

    @pl.when(step == 0)
    def _():
        out_ref[...] = spec_ref[...]

    subtract_image(meta_ref, step, [back_ref.at[0]], pupil_ref, band_ref, out_ref, win)


def middle_kernel(*refs, terms, streams):
    term_refs, refs = refs[: terms * streams], refs[terms * streams :]
    (image_ref, cos_ref, sin_ref), refs = refs[:3], refs[3:]
    out_refs, (mid_ref, resid_ref) = refs[:streams], refs[streams:]
    _, rows, crop_width = term_refs[0].shape
    band = rows * streams
    block = min(512, crop_width)
    for stream in range(streams):
        of_stream = term_refs[stream * terms : (stream + 1) * terms]
        total = sum(ref[...].astype(jnp.float32) for ref in of_stream).astype(jnp.bfloat16)
        for part in range(2):
            start = part * band + stream * rows
            mid_ref[start : start + rows] = total[part]
    dot = functools.partial(jnp.dot, preferred_element_type=jnp.float32)
    for start in range(0, crop_width, block):
        columns = slice(start, start + block)
        by_cos = dot(mid_ref[...], cos_ref[:, columns])
        by_sin = dot(mid_ref[...], sin_ref[:, columns])
        field_real = by_cos[:band] - by_sin[band:]
        field_imag = by_sin[:band] + by_cos[band:]
        power = field_real * field_real + field_imag * field_imag
        measured = image_ref[0, :, columns].astype(jnp.float32)
        keeping = 1.0 - measured * lax.rsqrt(jnp.maximum(power, 1.0))
        resid_ref[:band, columns] = (field_real * keeping).astype(jnp.bfloat16)
        resid_ref[band:, columns] = (field_imag * keeping).astype(jnp.bfloat16)
    for start in range(0, crop_width, block):
        columns = slice(start, start + block)
        by_cos = dot(resid_ref[...], cos_ref[:, columns])
        by_sin = dot(resid_ref[...], sin_ref[:, columns])
        for part, back in enumerate((by_cos[:band] + by_sin[band:], by_cos[band:] - by_sin[:band])):
            for stream, out_ref in enumerate(out_refs):
                of_stream = back[stream * rows : (stream + 1) * rows]
                out_ref[part, :, columns] = of_stream.astype(jnp.bfloat16)


def params():
    return pltpu.CompilerParams(vmem_limit_bytes=vmem_bytes)


def light():
    return pl.CostEstimate(flops=1024, bytes_accessed=1024, transcendentals=0)


vmem = pl.BlockSpec(memory_space=pltpu.VMEM)
smem = pl.BlockSpec(memory_space=pltpu.SMEM)


def band_type(pupil, band_table, *lead):
    shape = lead + (2, band_table.shape[1] // 2, pupil.shape[1])
    return jax.ShapeDtypeStruct(shape, jnp.bfloat16)


def forward(meta, lows, pupil, band_table, base, images, tiles=(0, 1), came=None, streams=1):
    win = Windows(*lows[0][0].shape, pupil.shape[1])
    operands = [meta, pupil, band_table] + [part for low in lows for part in low]
    operands += [came] * (came is not None)
    count = images * streams
    _, rows, columns = band_type(pupil, band_table).shape
    return pl.pallas_call(
        functools.partial(
            forward_kernel, base=base, images=images, count=count, win=win, tiles=tiles
        ),
        in_specs=[smem] + [vmem] * (len(operands) - 1),
        out_specs=[vmem] * count,
        out_shape=[jax.ShapeDtypeStruct((2, rows // streams, columns), jnp.bfloat16)] * count,
        compiler_params=params(),
        cost_estimate=light(),
        name="forward",
    )(*operands)


def backward(meta, shape, pupil, band_table, parts, slots, backs, chunks=0):
    win = Windows(*shape[1:], pupil.shape[1])
    held = [[back is not None for back in groups] for groups in backs]
    operands = list(parts) + [back for groups in backs for back in groups if back is not None]
    kernel = sibling_kernel if chunks else backward_kernel
    out_shape = jax.ShapeDtypeStruct(shape, jnp.float32)
    if chunks:
        chunk = shape[:2] + (shape[2] // chunks,)
        out_shape = [jax.ShapeDtypeStruct(chunk, jnp.bfloat16)] * chunks
    return pl.pallas_call(
        functools.partial(kernel, slots=slots, held=held, parts=len(parts), win=win),
        in_specs=[smem] + [vmem] * (2 + len(operands)),
        out_specs=[vmem] * chunks if chunks else vmem,
        out_shape=out_shape,
        scratch_shapes=[pltpu.VMEM(shape, jnp.float32)] * (chunks > 0),
        compiler_params=pltpu.CompilerParams(vmem_limit_bytes=backward_bytes),
        cost_estimate=light(),
        name="backward",
    )(meta, pupil, band_table, *operands)


def middle(streams, image, cos_table, sin_table):
    _, rows, crop_width = streams[0][0].shape
    band = rows * len(streams)
    terms = [term for stream in streams for term in stream]
    return pl.pallas_call(
        functools.partial(
            middle_kernel, terms=len(streams[0]), streams=len(streams)
        ),
        in_specs=[vmem] * (len(terms) + 3),
        out_specs=[vmem] * len(streams),
        out_shape=[jax.ShapeDtypeStruct((2, rows, crop_width), jnp.bfloat16)] * len(streams),
        scratch_shapes=[pltpu.VMEM((2 * band, crop_width), jnp.bfloat16)] * 2,
        compiler_params=params(),
        cost_estimate=light(),
        name="middle",
    )(*terms, image, cos_table, sin_table)


def fixed(array):
    return pl.BlockSpec(array.shape, lambda i: (0,) * array.ndim)


def forward_all(meta, low, pupil, band_table):
    win = Windows(*low[0].shape, pupil.shape[1])
    count = meta.shape[1]
    out_type = band_type(pupil, band_table, count)
    return pl.pallas_call(
        functools.partial(forward_grid_kernel, win=win),
        grid=(count,),
        in_specs=[smem] + [fixed(array) for array in (pupil, band_table, *low)],
        out_specs=pl.BlockSpec((1,) + out_type.shape[1:], lambda i: (i, 0, 0, 0)),
        out_shape=out_type,
        compiler_params=params(),
        name="forward_all",
    )(meta, pupil, band_table, *low)


def backward_all(meta, spectrum, pupil, band_table, backs):
    win = Windows(*spectrum.shape[1:], pupil.shape[1])
    return pl.pallas_call(
        functools.partial(backward_grid_kernel, win=win),
        grid=(meta.shape[1],),
        in_specs=[smem]
        + [fixed(array) for array in (pupil, band_table, spectrum)]
        + [pl.BlockSpec((1,) + backs.shape[1:], lambda i: (i, 0, 0, 0))],
        out_specs=fixed(spectrum),
        out_shape=jax.ShapeDtypeStruct(spectrum.shape, jnp.float32),
        compiler_params=params(),
        name="backward_all",
    )(meta, pupil, band_table, spectrum, backs)


def cast_kernel(spec_ref, out_ref, held, sems, *, part):
    blocks, _, width = held.shape
    columns = [pl.ds(block * width, width) for block in range(blocks)]
    copies = [
        pltpu.make_async_copy(spec_ref.at[part, :, columns[i]], held.at[i], sems.at[i])
        for i in range(blocks)
    ]
    for copy in copies:
        copy.start()
    for i, copy in enumerate(copies):
        copy.wait()
        out_ref[:, columns[i]] = held[i].astype(jnp.bfloat16)


def low_part(spectrum, part):
    _, rows, columns = spectrum.shape
    return pl.pallas_call(
        functools.partial(cast_kernel, part=part),
        in_specs=[pl.BlockSpec(memory_space=pltpu.HBM)],
        out_specs=vmem,
        out_shape=jax.ShapeDtypeStruct((rows, columns), jnp.bfloat16),
        scratch_shapes=[
            pltpu.VMEM((4, rows, columns // 4), jnp.float32),
            pltpu.SemaphoreType.DMA((4,)),
        ],
        compiler_params=params(),
        cost_estimate=light(),
        name="low_part",
    )(spectrum)


def total(*terms):
    return sum(term.astype(jnp.float32) for term in terms).astype(jnp.bfloat16)


def per_device(spectrum, pupil, measured, centre_rows, centre_cols):
    count = lax.axis_size("ty")
    planes = count // 4
    position = lax.axis_index("ty")
    plane = position // 4
    _, tile_rows, slab_columns = spectrum.shape
    crop_width = pupil.shape[0]
    band = measured.shape[1]
    band_start = (crop_width - band) // 2
    cos_table, sin_table = fourier_tables(crop_width)
    chosen_rows = slice(band_start, band_start + band)
    band_table = jnp.asarray(
        np.concatenate([cos_table[:, chosen_rows], sin_table[:, chosen_rows]], axis=1)
    )
    cos_table, sin_table = jnp.asarray(cos_table), jnp.asarray(sin_table)

    half = crop_width // 2

    low = [low_part(spectrum, part) for part in range(2)]

    def image_meta(ids, positions):
        match = ids[:, None] == jnp.arange(count, dtype=jnp.int32)[None, :]
        tops = jnp.sum(jnp.where(match, centre_rows[None, :], 0), axis=1) - half
        lefts = jnp.sum(jnp.where(match, centre_cols[None, :], 0), axis=1) - half
        rows = [place * tile_rows - tops for place in positions]
        return jnp.stack(rows + [lefts]).astype(jnp.int32)

    if planes != 4:
        meta = image_meta(jnp.arange(count, dtype=jnp.int32), [position])
        partial = forward_all(meta, low, pupil, band_table)
        mid = lax.psum_scatter(partial, "ty", scatter_dimension=0, tiled=True)[0]
        back = lax.all_gather(middle([[mid]], measured, cos_table, sin_table)[0], "ty")
        return backward_all(meta, spectrum, pupil, band_table, back)

    targets = {"far": (3, 3, 0, 0), "next": (2, 2, 1, 1), "beside": (1, 0, 3, 2), "own": (0, 1, 2, 3)}
    own_core = [("far", 2), ("far", 0), ("next", 2), ("next", 0)]
    own_core += [("beside", 2), ("beside", 0), ("own", 2), ("own", 0)]
    slots = {}
    for core in (0, 1):
        for name, y in own_core:
            slots[name, y + core] = len(slots)
    ids = [
        [targets[name][i // 4] * 4 + (i % 4 ^ flip) for (name, flip) in slots]
        for i in range(count)
    ]
    my_ids = lax.dynamic_index_in_dim(jnp.asarray(ids, jnp.int32), position, keepdims=False)
    meta = image_meta(my_ids, [position, position ^ 1])

    def sibling(value):
        return lax.ppermute(value, "ty", [(i, i ^ 1) for i in range(count)])

    def across(value):
        return lax.ppermute(value, "ty", [(i, i ^ 2) for i in range(count)])

    def along(value, plane_pairs):
        pairs = [(4 * a + i, 4 * b + i) for a, b in plane_pairs for i in range(4)]
        return lax.ppermute(value, "ty", pairs)

    inward = [(0, 1), (3, 2)]
    outward = [(1, 0), (2, 3)]
    inner = [(1, 2), (2, 1)]
    together = lax.optimization_barrier

    lows = [low, [sibling(part) for part in low]]
    streams = 2
    (own_rows,) = forward(meta, lows[:1], pupil, band_table, 0, 1, (0,))
    far_leaving = forward(
        meta, lows[1:], pupil, band_table, 0, 1, (1,), own_rows, streams=streams
    )
    far_other = [across(value) for value in far_leaving]
    made = forward(
        together((meta, far_leaving[0]))[0], lows, pupil, band_table, 1, 7, streams=streams
    )
    summed, held = [], None
    for stream in reversed(range(streams)):
        (
            far_kept,
            next_leaving,
            next_kept,
            beside_leaving,
            beside_kept,
            own_leaving,
            own_kept,
        ) = made[stream::streams]
        far, far_kept, next_leaving = together((far_other[stream], far_kept, next_leaving))

        next_other = across(next_leaving)
        from_end = along(total(far_kept, far), inward)
        from_end, next_other, beside_leaving = together((from_end, next_other, beside_leaving))

        beside_other = across(beside_leaving)
        next_inward = along(total(next_kept, next_other), inward)
        far_inner = along(total(far_kept, far, from_end), inner)
        far_inner, next_inward, beside_other, own_leaving = together(
            (far_inner, next_inward, beside_other, own_leaving)
        )

        own_other = across(own_leaving)
        next_inner = along(total(next_kept, next_other, next_inward), inner)
        beside = along(total(beside_kept, beside_other, far_inner), inward + outward)
        terms = [own_kept, own_other, next_inner, beside]
        if stream > 0:
            terms = [total(*terms)]
            held = terms[0]
        else:
            terms[0] = together((terms[0], held))[0]
            terms = [total(*terms)]
        summed.insert(0, terms)
    backs = middle(summed, measured, cos_table, sin_table)

    at_ends = (plane == 0) | (plane == 3)
    lead, last = streams - 1, 0
    pieces = {}

    def apply(parts, names, chunks=0):
        taken = [[pieces.get((name, stream)) for stream in range(streams)] for name in names]
        own_slots = [slots[name] for name in names]
        shape = spectrum.shape
        return backward(meta, shape, pupil, band_table, parts, own_slots, taken, chunks)

    def close(stream, *names):
        closed = together(tuple(pieces[name, stream] for name in names))
        for name, value in zip(names, closed):
            pieces[name, stream] = value

    for stream in (lead, last):
        back = pieces[("own", 0), stream] = backs[stream]
        pieces[("own", 2), stream] = across(back)
        pieces["inner", stream] = along(back, inner)
        pieces[("beside", 0), stream] = along(back, inward + outward)
        close(stream, ("own", 2), "inner", ("beside", 0))
    early, later, late = (
        [("own", 0), ("beside", 0), ("own", 2)],
        [("next", 0), ("beside", 2)],
        [("far", 0), ("next", 2)],
    )
    for stream in (lead, last):
        pieces[("beside", 2), stream] = across(pieces[("beside", 0), stream])
        pieces["far inner", stream] = along(pieces[("beside", 0), stream], inner)
        pieces["outward", stream] = along(pieces["inner", stream], outward)
        if stream == last:
            pieces["result", stream] = apply([spectrum], early)
            close(stream, ("beside", 2), "far inner", "outward", "result")
        else:
            pieces["slab", stream] = apply([], early, 1)[0]
            close(stream, ("beside", 2), "far inner", "outward", "slab")
    for stream in (lead, last):
        from_next = jnp.where(at_ends, pieces["outward", stream], pieces["inner", stream])
        pieces[("next", 0), stream] = from_next
        pieces[("next", 2), stream] = across(from_next)
        pieces["far outward", stream] = along(pieces["far inner", stream], outward)
        if stream == last:
            pieces["slab", stream] = apply([pieces["slab", lead]], later, 1)[0]
            close(stream, ("next", 2), "far outward", "slab")
        else:
            close(stream, ("next", 2), "far outward")
    for stream in (lead, last):
        from_far = jnp.where(at_ends, pieces["far outward", stream], pieces["far inner", stream])
        pieces[("far", 0), stream] = from_far
        pieces[("far", 2), stream] = across(from_far)
    chunks = apply([pieces["slab", last]], late, 4)
    slab = [sibling(chunk) for chunk in chunks]
    result = apply([pieces["result", last]], later + late)
    arriving, result, slab[0], slab[1] = together(
        (pieces[("far", 2), last], result, slab[0], slab[1])
    )
    pieces[("far", 2), last] = arriving
    for stream in (lead, last):
        pieces[("far", 3), stream] = sibling(pieces[("far", 2), stream])
    return apply([result] + slab, [("far", 2), ("far", 3)])


def solution(mesh):
    return jax.shard_map(
        per_device,
        mesh=mesh,
        in_specs=(
            P(None, ("groups", "ty"), None),
            P(),
            P(("groups", "ty"), None, None),
            P("groups"),
            P("groups"),
        ),
        out_specs=P(None, ("groups", "ty"), None),
        check_vma=False,
    )
```

```python
import functools
import math

import jax
import jax.numpy as jnp
import numpy as np
from jax import lax
from jax.experimental import pallas as pl
from jax.experimental.pallas import tpu as pltpu
from jax.sharding import PartitionSpec as P

step_size = 0.5
lane = 128
row_tile = 16
vmem_bytes = 20 * 1024 * 1024
backward_bytes = 20 * 1024 * 1024


def fourier_tables(crop_width):
    counter = np.arange(crop_width, dtype=np.int64)
    angle = (counter[:, None] * counter[None, :] % crop_width) * (2.0 * math.pi / crop_width)
    factor = 1.0 / math.sqrt(crop_width)
    cos_table = (np.cos(angle) * factor).astype(np.float32).astype(jnp.bfloat16)
    sin_table = (np.sin(angle) * factor).astype(np.float32).astype(jnp.bfloat16)
    return cos_table, sin_table


def tile_weight(pupil_ref, first_row, win):
    start = win.row(first_row)
    rows = pupil_ref[pl.ds(start, win.rows), :].astype(jnp.float32)
    rows = pltpu.roll(rows, (2 * win.rows + start - first_row) % win.rows, 0)
    shape = (win.tile_rows, win.crop_width)
    row = 2 * (first_row + lax.broadcasted_iota(jnp.int32, shape, 0)) - win.crop_width + 1
    column = 2 * lax.broadcasted_iota(jnp.int32, shape, 1) - win.crop_width + 1
    inside = row * row + column * column <= win.crop_width * win.crop_width
    return jnp.where(inside, rows[: win.tile_rows], 0.0)


def tile_band(band_ref, first_row, win):
    start = win.row(first_row)
    rows = band_ref[pl.ds(start, win.rows), :].astype(jnp.float32)
    rows = pltpu.roll(rows, (2 * win.rows + start - first_row) % win.rows, 0)[: win.tile_rows]
    band = rows.shape[1] // 2
    turned = jnp.concatenate([-rows[:, band:], rows[:, :band]], axis=1)
    return jnp.concatenate([rows, turned], axis=0).astype(jnp.bfloat16)


class Windows:
    def __init__(self, tile_rows, slab_columns, crop_width):
        self.tile_rows = tile_rows
        self.crop_width = crop_width
        self.rows = tile_rows + row_tile
        self.columns = crop_width + lane
        self.last_row = crop_width - self.rows
        self.last_column = slab_columns - self.columns

    def row(self, first_row):
        start = jnp.clip(first_row, 0, self.last_row) // row_tile * row_tile
        return pl.multiple_of(start, row_tile)

    def column(self, left):
        start = jnp.minimum(left // lane * lane, self.last_column)
        return pl.multiple_of(start, lane)

    def active(self, first_row):
        return (first_row > -self.tile_rows) & (first_row < self.crop_width)


def image_band(meta_ref, slot, lows, tiles, pupil_ref, band_ref, win, store, came=None):
    left = meta_ref[meta_ref.shape[0] - 1, slot]
    first_rows = [meta_ref[tile, slot] for tile in tiles]
    active = functools.reduce(jnp.logical_or, [win.active(row) for row in first_rows])
    band = band_ref.shape[1] // 2
    shape = (2, band, win.crop_width)

    @pl.when(jnp.logical_not(active))
    def _():
        store(jnp.zeros(shape, jnp.bfloat16) if came is None else came[...])

    @pl.when(active)
    def _():
        col_start = win.column(left)
        shift = (win.columns - (left - col_start)) % win.columns
        parts, tables = [], []
        for first_row, low_refs in zip(first_rows, lows):
            weight = tile_weight(pupil_ref, first_row, win)
            for low_ref in low_refs:
                low = low_ref[:, pl.ds(col_start, win.columns)].astype(jnp.float32)
                low = pltpu.roll(low, shift, 1)[:, : win.crop_width]
                parts.append((weight * low).astype(jnp.bfloat16))
            tables.append(tile_band(band_ref, first_row, win))
        mid = lax.dot_general(
            jnp.concatenate(tables, axis=0),
            jnp.concatenate(parts, axis=0),
            (((0,), (0,)), ((), ())),
            preferred_element_type=jnp.float32,
        )
        if came is not None:
            mid = mid + came[...].reshape(mid.shape).astype(jnp.float32)
        store(mid.astype(jnp.bfloat16).reshape(shape))


def forward_kernel(meta_ref, pupil_ref, band_ref, *refs, base, images, count, win, tiles):
    out_refs = refs[-count:]
    lows = [refs[2 * half : 2 * half + 2] for half in range(len(tiles))]
    came = refs[2 * len(tiles)] if len(refs) > 2 * len(tiles) + count else None
    streams = count // images

    def image(index):
        def store(value):
            for number in range(images):

                @pl.when(index == number)
                def _():
                    for stream in range(streams):
                        out_ref = out_refs[number * streams + stream]
                        rows = out_ref.shape[1]
                        out_ref[...] = value[:, stream * rows : (stream + 1) * rows]

        image_band(meta_ref, base + index, lows, tiles, pupil_ref, band_ref, win, store, came)

    pl.loop(0, images)(image)


def forward_grid_kernel(meta_ref, pupil_ref, band_ref, real_ref, imag_ref, out_ref, *, win):
    def store(value):
        out_ref[0] = value

    lows = [(real_ref, imag_ref)]
    image_band(meta_ref, pl.program_id(0), lows, (0,), pupil_ref, band_ref, win, store)


def subtract_image(meta_ref, slot, back_refs, pupil_ref, band_ref, out_ref, win, tile=0):
    first_row, left = meta_ref[tile, slot], meta_ref[meta_ref.shape[0] - 1, slot]
    tile_rows, crop_width = win.tile_rows, win.crop_width

    @pl.when(win.active(first_row))
    def _():
        col_start = win.column(left)
        weight = tile_weight(pupil_ref, first_row, win) * step_size
        table = tile_band(band_ref, first_row, win)
        band = table.shape[1] // 2
        rows = band // len(back_refs)
        held = [number for number, ref in enumerate(back_refs) if ref is not None]
        if len(held) < len(back_refs):
            starts = [part * band + number * rows for part in range(2) for number in held]
            table = jnp.concatenate([table[:, start : start + rows] for start in starts], axis=1)
        back = [back_refs[number][part] for part in range(2) for number in held]
        back = jnp.concatenate(back, axis=0)
        grad = jnp.dot(table, back, preferred_element_type=jnp.float32)
        columns = pl.ds(col_start, win.columns)
        pad = jnp.zeros((tile_rows, win.columns - crop_width), jnp.float32)
        for part in range(2):
            piece = grad[part * tile_rows : (part + 1) * tile_rows] * weight
            piece = pltpu.roll(jnp.concatenate([piece, pad], axis=1), left - col_start, 1)
            out_ref[part, :, columns] = out_ref[part, :, columns] - piece


def backward_kernel(meta_ref, pupil_ref, band_ref, *refs, slots, held, parts, win):
    part_refs, back_refs, out_ref = refs[:parts], iter(refs[parts:-1]), refs[-1]
    for number in range(parts - 1):
        chunk = part_refs[number + 1][...].astype(jnp.float32)
        width = chunk.shape[2]
        columns = slice(number * width, (number + 1) * width)
        out_ref[:, :, columns] = part_refs[0][:, :, columns] + chunk
    if parts == 1:
        out_ref[...] = part_refs[0][...]
    for slot, groups in zip(slots, held):
        of_image = [next(back_refs) if there else None for there in groups]
        subtract_image(meta_ref, slot, of_image, pupil_ref, band_ref, out_ref, win)


def sibling_kernel(meta_ref, pupil_ref, band_ref, *refs, slots, held, parts, win):
    backs = sum(map(sum, held))
    part_refs, back_refs, total_ref = refs[:parts], iter(refs[parts : parts + backs]), refs[-1]
    out_refs = refs[parts + backs : -1]
    if parts:
        total_ref[...] = part_refs[0][...].astype(jnp.float32)
    else:
        total_ref[...] = jnp.zeros_like(total_ref)
    for slot, groups in zip(slots, held):
        of_image = [next(back_refs) if there else None for there in groups]
        subtract_image(meta_ref, slot, of_image, pupil_ref, band_ref, total_ref, win, 1)
    width = out_refs[0].shape[2]
    for number, out_ref in enumerate(out_refs):
        out_ref[...] = total_ref[:, :, number * width : (number + 1) * width].astype(jnp.bfloat16)


def backward_grid_kernel(meta_ref, pupil_ref, band_ref, spec_ref, back_ref, out_ref, *, win):
    step = pl.program_id(0)

    @pl.when(step == 0)
    def _():
        out_ref[...] = spec_ref[...]

    subtract_image(meta_ref, step, [back_ref.at[0]], pupil_ref, band_ref, out_ref, win)


def middle_kernel(*refs, terms, streams):
    term_refs, refs = refs[: terms * streams], refs[terms * streams :]
    (image_ref, cos_ref, sin_ref), refs = refs[:3], refs[3:]
    out_refs, (mid_ref, resid_ref) = refs[:streams], refs[streams:]
    _, rows, crop_width = term_refs[0].shape
    band = rows * streams
    block = min(512, crop_width)
    for stream in range(streams):
        of_stream = term_refs[stream * terms : (stream + 1) * terms]
        total = sum(ref[...].astype(jnp.float32) for ref in of_stream).astype(jnp.bfloat16)
        for part in range(2):
            start = part * band + stream * rows
            mid_ref[start : start + rows] = total[part]
    dot = functools.partial(jnp.dot, preferred_element_type=jnp.float32)
    for start in range(0, crop_width, block):
        columns = slice(start, start + block)
        by_cos = dot(mid_ref[...], cos_ref[:, columns])
        by_sin = dot(mid_ref[...], sin_ref[:, columns])
        field_real = by_cos[:band] - by_sin[band:]
        field_imag = by_sin[:band] + by_cos[band:]
        power = field_real * field_real + field_imag * field_imag
        measured = image_ref[0, :, columns].astype(jnp.float32)
        keeping = 1.0 - measured * lax.rsqrt(jnp.maximum(power, 1.0))
        resid_ref[:band, columns] = (field_real * keeping).astype(jnp.bfloat16)
        resid_ref[band:, columns] = (field_imag * keeping).astype(jnp.bfloat16)
    for start in range(0, crop_width, block):
        columns = slice(start, start + block)
        by_cos = dot(resid_ref[...], cos_ref[:, columns])
        by_sin = dot(resid_ref[...], sin_ref[:, columns])
        for part, back in enumerate((by_cos[:band] + by_sin[band:], by_cos[band:] - by_sin[:band])):
            for stream, out_ref in enumerate(out_refs):
                of_stream = back[stream * rows : (stream + 1) * rows]
                out_ref[part, :, columns] = of_stream.astype(jnp.bfloat16)


def params():
    return pltpu.CompilerParams(vmem_limit_bytes=vmem_bytes)


def light():
    return pl.CostEstimate(flops=1024, bytes_accessed=1024, transcendentals=0)


vmem = pl.BlockSpec(memory_space=pltpu.VMEM)
smem = pl.BlockSpec(memory_space=pltpu.SMEM)


def band_type(pupil, band_table, *lead):
    shape = lead + (2, band_table.shape[1] // 2, pupil.shape[1])
    return jax.ShapeDtypeStruct(shape, jnp.bfloat16)


def forward(meta, lows, pupil, band_table, base, images, tiles=(0, 1), came=None, streams=1):
    win = Windows(*lows[0][0].shape, pupil.shape[1])
    operands = [meta, pupil, band_table] + [part for low in lows for part in low]
    operands += [came] * (came is not None)
    count = images * streams
    _, rows, columns = band_type(pupil, band_table).shape
    return pl.pallas_call(
        functools.partial(
            forward_kernel, base=base, images=images, count=count, win=win, tiles=tiles
        ),
        in_specs=[smem] + [vmem] * (len(operands) - 1),
        out_specs=[vmem] * count,
        out_shape=[jax.ShapeDtypeStruct((2, rows // streams, columns), jnp.bfloat16)] * count,
        compiler_params=params(),
        cost_estimate=light(),
        name="forward",
    )(*operands)


def backward(meta, shape, pupil, band_table, parts, slots, backs, chunks=0):
    win = Windows(*shape[1:], pupil.shape[1])
    held = [[back is not None for back in groups] for groups in backs]
    operands = list(parts) + [back for groups in backs for back in groups if back is not None]
    kernel = sibling_kernel if chunks else backward_kernel
    out_shape = jax.ShapeDtypeStruct(shape, jnp.float32)
    if chunks:
        chunk = shape[:2] + (shape[2] // chunks,)
        out_shape = [jax.ShapeDtypeStruct(chunk, jnp.bfloat16)] * chunks
    return pl.pallas_call(
        functools.partial(kernel, slots=slots, held=held, parts=len(parts), win=win),
        in_specs=[smem] + [vmem] * (2 + len(operands)),
        out_specs=[vmem] * chunks if chunks else vmem,
        out_shape=out_shape,
        scratch_shapes=[pltpu.VMEM(shape, jnp.float32)] * (chunks > 0),
        compiler_params=pltpu.CompilerParams(vmem_limit_bytes=backward_bytes),
        cost_estimate=light(),
        name="backward",
    )(meta, pupil, band_table, *operands)


def middle(streams, image, cos_table, sin_table):
    _, rows, crop_width = streams[0][0].shape
    band = rows * len(streams)
    terms = [term for stream in streams for term in stream]
    return pl.pallas_call(
        functools.partial(
            middle_kernel, terms=len(streams[0]), streams=len(streams)
        ),
        in_specs=[vmem] * (len(terms) + 3),
        out_specs=[vmem] * len(streams),
        out_shape=[jax.ShapeDtypeStruct((2, rows, crop_width), jnp.bfloat16)] * len(streams),
        scratch_shapes=[pltpu.VMEM((2 * band, crop_width), jnp.bfloat16)] * 2,
        compiler_params=params(),
        cost_estimate=light(),
        name="middle",
    )(*terms, image, cos_table, sin_table)


def fixed(array):
    return pl.BlockSpec(array.shape, lambda i: (0,) * array.ndim)


def forward_all(meta, low, pupil, band_table):
    win = Windows(*low[0].shape, pupil.shape[1])
    count = meta.shape[1]
    out_type = band_type(pupil, band_table, count)
    return pl.pallas_call(
        functools.partial(forward_grid_kernel, win=win),
        grid=(count,),
        in_specs=[smem] + [fixed(array) for array in (pupil, band_table, *low)],
        out_specs=pl.BlockSpec((1,) + out_type.shape[1:], lambda i: (i, 0, 0, 0)),
        out_shape=out_type,
        compiler_params=params(),
        name="forward_all",
    )(meta, pupil, band_table, *low)


def backward_all(meta, spectrum, pupil, band_table, backs):
    win = Windows(*spectrum.shape[1:], pupil.shape[1])
    return pl.pallas_call(
        functools.partial(backward_grid_kernel, win=win),
        grid=(meta.shape[1],),
        in_specs=[smem]
        + [fixed(array) for array in (pupil, band_table, spectrum)]
        + [pl.BlockSpec((1,) + backs.shape[1:], lambda i: (i, 0, 0, 0))],
        out_specs=fixed(spectrum),
        out_shape=jax.ShapeDtypeStruct(spectrum.shape, jnp.float32),
        compiler_params=params(),
        name="backward_all",
    )(meta, pupil, band_table, spectrum, backs)


def cast_kernel(spec_ref, out_ref, held, sems, *, part):
    blocks, _, width = held.shape
    columns = [pl.ds(block * width, width) for block in range(blocks)]
    copies = [
        pltpu.make_async_copy(spec_ref.at[part, :, columns[i]], held.at[i], sems.at[i])
        for i in range(blocks)
    ]
    for copy in copies:
        copy.start()
    for i, copy in enumerate(copies):
        copy.wait()
        out_ref[:, columns[i]] = held[i].astype(jnp.bfloat16)


def low_part(spectrum, part):
    _, rows, columns = spectrum.shape
    return pl.pallas_call(
        functools.partial(cast_kernel, part=part),
        in_specs=[pl.BlockSpec(memory_space=pltpu.HBM)],
        out_specs=vmem,
        out_shape=jax.ShapeDtypeStruct((rows, columns), jnp.bfloat16),
        scratch_shapes=[
            pltpu.VMEM((4, rows, columns // 4), jnp.float32),
            pltpu.SemaphoreType.DMA((4,)),
        ],
        compiler_params=params(),
        cost_estimate=light(),
        name="low_part",
    )(spectrum)


def total(*terms):
    return sum(term.astype(jnp.float32) for term in terms).astype(jnp.bfloat16)


def per_device(spectrum, pupil, measured, centre_rows, centre_cols):
    count = lax.axis_size("ty")
    planes = count // 4
    position = lax.axis_index("ty")
    plane = position // 4
    _, tile_rows, slab_columns = spectrum.shape
    crop_width = pupil.shape[0]
    band = measured.shape[1]
    band_start = (crop_width - band) // 2
    cos_table, sin_table = fourier_tables(crop_width)
    chosen_rows = slice(band_start, band_start + band)
    band_table = jnp.asarray(
        np.concatenate([cos_table[:, chosen_rows], sin_table[:, chosen_rows]], axis=1)
    )
    cos_table, sin_table = jnp.asarray(cos_table), jnp.asarray(sin_table)

    half = crop_width // 2

    low = [low_part(spectrum, part) for part in range(2)]

    def image_meta(ids, positions):
        match = ids[:, None] == jnp.arange(count, dtype=jnp.int32)[None, :]
        tops = jnp.sum(jnp.where(match, centre_rows[None, :], 0), axis=1) - half
        lefts = jnp.sum(jnp.where(match, centre_cols[None, :], 0), axis=1) - half
        rows = [place * tile_rows - tops for place in positions]
        return jnp.stack(rows + [lefts]).astype(jnp.int32)

    if planes != 4:
        meta = image_meta(jnp.arange(count, dtype=jnp.int32), [position])
        partial = forward_all(meta, low, pupil, band_table)
        mid = lax.psum_scatter(partial, "ty", scatter_dimension=0, tiled=True)[0]
        back = lax.all_gather(middle([[mid]], measured, cos_table, sin_table)[0], "ty")
        return backward_all(meta, spectrum, pupil, band_table, back)

    targets = {"far": (3, 3, 0, 0), "next": (2, 2, 1, 1), "beside": (1, 0, 3, 2), "own": (0, 1, 2, 3)}
    own_core = [("far", 2), ("far", 0), ("next", 2), ("next", 0)]
    own_core += [("beside", 2), ("beside", 0), ("own", 2), ("own", 0)]
    slots = {}
    for core in (0, 1):
        for name, y in own_core:
            slots[name, y + core] = len(slots)
    ids = [
        [targets[name][i // 4] * 4 + (i % 4 ^ flip) for (name, flip) in slots]
        for i in range(count)
    ]
    my_ids = lax.dynamic_index_in_dim(jnp.asarray(ids, jnp.int32), position, keepdims=False)
    meta = image_meta(my_ids, [position, position ^ 1])

    def sibling(value):
        return lax.ppermute(value, "ty", [(i, i ^ 1) for i in range(count)])

    def across(value):
        return lax.ppermute(value, "ty", [(i, i ^ 2) for i in range(count)])

    def along(value, plane_pairs):
        pairs = [(4 * a + i, 4 * b + i) for a, b in plane_pairs for i in range(4)]
        return lax.ppermute(value, "ty", pairs)

    inward = [(0, 1), (3, 2)]
    outward = [(1, 0), (2, 3)]
    inner = [(1, 2), (2, 1)]
    together = lax.optimization_barrier

    lows = [low, [sibling(part) for part in low]]
    streams = 2
    (own_rows,) = forward(meta, lows[:1], pupil, band_table, 0, 1, (0,))
    far_leaving = forward(
        meta, lows[1:], pupil, band_table, 0, 1, (1,), own_rows, streams=streams
    )
    far_other = [across(value) for value in far_leaving]
    made = forward(
        together((meta, far_leaving[0]))[0], lows, pupil, band_table, 1, 7, streams=streams
    )
    summed, held = [], None
    for stream in reversed(range(streams)):
        (
            far_kept,
            next_leaving,
            next_kept,
            beside_leaving,
            beside_kept,
            own_leaving,
            own_kept,
        ) = made[stream::streams]
        far, far_kept, next_leaving = together((far_other[stream], far_kept, next_leaving))

        next_other = across(next_leaving)
        from_end = along(total(far_kept, far), inward)
        from_end, next_other, beside_leaving = together((from_end, next_other, beside_leaving))

        beside_other = across(beside_leaving)
        next_inward = along(total(next_kept, next_other), inward)
        far_inner = along(total(far_kept, far, from_end), inner)
        far_inner, next_inward, beside_other, own_leaving = together(
            (far_inner, next_inward, beside_other, own_leaving)
        )

        own_other = across(own_leaving)
        next_inner = along(total(next_kept, next_other, next_inward), inner)
        beside = along(total(beside_kept, beside_other, far_inner), inward + outward)
        terms = [own_kept, own_other, next_inner, beside]
        if stream > 0:
            terms = [total(*terms)]
            held = terms[0]
        else:
            terms[0] = together((terms[0], held))[0]
            terms = [total(*terms)]
        summed.insert(0, terms)
    backs = middle(summed, measured, cos_table, sin_table)

    at_ends = (plane == 0) | (plane == 3)
    lead, last = streams - 1, 0
    pieces = {}

    def apply(parts, names, chunks=0):
        taken = [[pieces.get((name, stream)) for stream in range(streams)] for name in names]
        own_slots = [slots[name] for name in names]
        shape = spectrum.shape
        return backward(meta, shape, pupil, band_table, parts, own_slots, taken, chunks)

    def close(stream, *names):
        closed = together(tuple(pieces[name, stream] for name in names))
        for name, value in zip(names, closed):
            pieces[name, stream] = value

    for stream in (lead, last):
        back = pieces[("own", 0), stream] = backs[stream]
        pieces[("own", 2), stream] = across(back)
        pieces["inner", stream] = along(back, inner)
        pieces[("beside", 0), stream] = along(back, inward + outward)
        close(stream, ("own", 2), "inner", ("beside", 0))
    early, later, late = (
        [("own", 0), ("beside", 0), ("own", 2)],
        [("next", 0), ("beside", 2)],
        [("far", 0), ("next", 2)],
    )
    for stream in (lead, last):
        pieces[("beside", 2), stream] = across(pieces[("beside", 0), stream])
        pieces["far inner", stream] = along(pieces[("beside", 0), stream], inner)
        pieces["outward", stream] = along(pieces["inner", stream], outward)
        if stream == last:
            pieces["result", stream] = apply([spectrum], early)
            close(stream, ("beside", 2), "far inner", "outward", "result")
        else:
            pieces["slab", stream] = apply([], early, 1)[0]
            close(stream, ("beside", 2), "far inner", "outward", "slab")
    for stream in (lead, last):
        from_next = jnp.where(at_ends, pieces["outward", stream], pieces["inner", stream])
        pieces[("next", 0), stream] = from_next
        pieces[("next", 2), stream] = across(from_next)
        pieces["far outward", stream] = along(pieces["far inner", stream], outward)
        if stream == last:
            pieces["slab", stream] = apply([pieces["slab", lead]], later, 1)[0]
            close(stream, ("next", 2), "far outward", "slab")
        else:
            close(stream, ("next", 2), "far outward")
    for stream in (lead, last):
        from_far = jnp.where(at_ends, pieces["far outward", stream], pieces["far inner", stream])
        pieces[("far", 0), stream] = from_far
        pieces[("far", 2), stream] = across(from_far)
    slab = [sibling(chunk) for chunk in apply([pieces["slab", last]], late, 4)]
    result = apply([pieces["result", last]], later + late)
    pieces[("far", 2), lead], result = together((pieces[("far", 2), lead], result))
    pieces[("far", 3), lead] = sibling(pieces[("far", 2), lead])
    pieces[("far", 2), last], pieces[("far", 3), lead] = together(
        (pieces[("far", 2), last], pieces[("far", 3), lead])
    )
    pieces[("far", 3), last] = sibling(pieces[("far", 2), last])
    return apply([result] + slab, [("far", 2), ("far", 3)])


def solution(mesh):
    return jax.shard_map(
        per_device,
        mesh=mesh,
        in_specs=(
            P(None, ("groups", "ty"), None),
            P(),
            P(("groups", "ty"), None, None),
            P("groups"),
            P("groups"),
        ),
        out_specs=P(None, ("groups", "ty"), None),
        check_vma=False,
    )
```

```python
import functools
import math

import jax
import jax.numpy as jnp
import numpy as np
from jax import lax
from jax.experimental import pallas as pl
from jax.experimental.pallas import tpu as pltpu
from jax.sharding import PartitionSpec as P

step_size = 0.5
lane = 128
row_tile = 16
vmem_bytes = 20 * 1024 * 1024
backward_bytes = 20 * 1024 * 1024


def fourier_tables(crop_width):
    counter = np.arange(crop_width, dtype=np.int64)
    angle = (counter[:, None] * counter[None, :] % crop_width) * (2.0 * math.pi / crop_width)
    factor = 1.0 / math.sqrt(crop_width)
    cos_table = (np.cos(angle) * factor).astype(np.float32).astype(jnp.bfloat16)
    sin_table = (np.sin(angle) * factor).astype(np.float32).astype(jnp.bfloat16)
    return cos_table, sin_table


def tile_weight(pupil_ref, first_row, win):
    start = win.row(first_row)
    rows = pupil_ref[pl.ds(start, win.rows), :].astype(jnp.float32)
    rows = pltpu.roll(rows, (2 * win.rows + start - first_row) % win.rows, 0)
    shape = (win.tile_rows, win.crop_width)
    row = 2 * (first_row + lax.broadcasted_iota(jnp.int32, shape, 0)) - win.crop_width + 1
    column = 2 * lax.broadcasted_iota(jnp.int32, shape, 1) - win.crop_width + 1
    inside = row * row + column * column <= win.crop_width * win.crop_width
    return jnp.where(inside, rows[: win.tile_rows], 0.0)


def tile_band(band_ref, first_row, win):
    start = win.row(first_row)
    rows = band_ref[pl.ds(start, win.rows), :].astype(jnp.float32)
    rows = pltpu.roll(rows, (2 * win.rows + start - first_row) % win.rows, 0)[: win.tile_rows]
    band = rows.shape[1] // 2
    turned = jnp.concatenate([-rows[:, band:], rows[:, :band]], axis=1)
    return jnp.concatenate([rows, turned], axis=0).astype(jnp.bfloat16)


class Windows:
    def __init__(self, tile_rows, slab_columns, crop_width):
        self.tile_rows = tile_rows
        self.crop_width = crop_width
        self.rows = tile_rows + row_tile
        self.columns = crop_width + lane
        self.last_row = crop_width - self.rows
        self.last_column = slab_columns - self.columns

    def row(self, first_row):
        start = jnp.clip(first_row, 0, self.last_row) // row_tile * row_tile
        return pl.multiple_of(start, row_tile)

    def column(self, left):
        start = jnp.minimum(left // lane * lane, self.last_column)
        return pl.multiple_of(start, lane)

    def active(self, first_row):
        return (first_row > -self.tile_rows) & (first_row < self.crop_width)


def image_band(meta_ref, slot, lows, tiles, pupil_ref, band_ref, win, store, came=None):
    left = meta_ref[meta_ref.shape[0] - 1, slot]
    first_rows = [meta_ref[tile, slot] for tile in tiles]
    active = functools.reduce(jnp.logical_or, [win.active(row) for row in first_rows])
    band = band_ref.shape[1] // 2
    shape = (2, band, win.crop_width)

    @pl.when(jnp.logical_not(active))
    def _():
        store(jnp.zeros(shape, jnp.bfloat16) if came is None else came[...])

    @pl.when(active)
    def _():
        col_start = win.column(left)
        shift = (win.columns - (left - col_start)) % win.columns
        parts, tables = [], []
        for first_row, low_refs in zip(first_rows, lows):
            weight = tile_weight(pupil_ref, first_row, win)
            for low_ref in low_refs:
                low = low_ref[:, pl.ds(col_start, win.columns)].astype(jnp.float32)
                low = pltpu.roll(low, shift, 1)[:, : win.crop_width]
                parts.append((weight * low).astype(jnp.bfloat16))
            tables.append(tile_band(band_ref, first_row, win))
        mid = lax.dot_general(
            jnp.concatenate(tables, axis=0),
            jnp.concatenate(parts, axis=0),
            (((0,), (0,)), ((), ())),
            preferred_element_type=jnp.float32,
        )
        if came is not None:
            mid = mid + came[...].reshape(mid.shape).astype(jnp.float32)
        store(mid.astype(jnp.bfloat16).reshape(shape))


def forward_kernel(meta_ref, pupil_ref, band_ref, *refs, base, images, count, win, tiles):
    out_refs = refs[-count:]
    lows = [refs[2 * half : 2 * half + 2] for half in range(len(tiles))]
    came = refs[2 * len(tiles)] if len(refs) > 2 * len(tiles) + count else None
    streams = count // images

    def image(index):
        def store(value):
            for number in range(images):

                @pl.when(index == number)
                def _():
                    for stream in range(streams):
                        out_ref = out_refs[number * streams + stream]
                        rows = out_ref.shape[1]
                        out_ref[...] = value[:, stream * rows : (stream + 1) * rows]

        image_band(meta_ref, base + index, lows, tiles, pupil_ref, band_ref, win, store, came)

    pl.loop(0, images)(image)


def forward_grid_kernel(meta_ref, pupil_ref, band_ref, real_ref, imag_ref, out_ref, *, win):
    def store(value):
        out_ref[0] = value

    lows = [(real_ref, imag_ref)]
    image_band(meta_ref, pl.program_id(0), lows, (0,), pupil_ref, band_ref, win, store)


def subtract_image(meta_ref, slot, back_refs, pupil_ref, band_ref, out_ref, win, tile=0):
    first_row, left = meta_ref[tile, slot], meta_ref[meta_ref.shape[0] - 1, slot]
    tile_rows, crop_width = win.tile_rows, win.crop_width

    @pl.when(win.active(first_row))
    def _():
        col_start = win.column(left)
        weight = tile_weight(pupil_ref, first_row, win) * step_size
        table = tile_band(band_ref, first_row, win)
        band = table.shape[1] // 2
        rows = band // len(back_refs)
        held = [number for number, ref in enumerate(back_refs) if ref is not None]
        if len(held) < len(back_refs):
            starts = [part * band + number * rows for part in range(2) for number in held]
            table = jnp.concatenate([table[:, start : start + rows] for start in starts], axis=1)
        back = [back_refs[number][part] for part in range(2) for number in held]
        back = jnp.concatenate(back, axis=0)
        grad = jnp.dot(table, back, preferred_element_type=jnp.float32)
        columns = pl.ds(col_start, win.columns)
        pad = jnp.zeros((tile_rows, win.columns - crop_width), jnp.float32)
        for part in range(2):
            piece = grad[part * tile_rows : (part + 1) * tile_rows] * weight
            piece = pltpu.roll(jnp.concatenate([piece, pad], axis=1), left - col_start, 1)
            out_ref[part, :, columns] = out_ref[part, :, columns] - piece


def backward_kernel(meta_ref, pupil_ref, band_ref, *refs, slots, held, parts, win):
    part_refs, back_refs, out_ref = refs[:parts], iter(refs[parts:-1]), refs[-1]
    for number in range(parts - 1):
        chunk = part_refs[number + 1][...].astype(jnp.float32)
        width = chunk.shape[2]
        columns = slice(number * width, (number + 1) * width)
        out_ref[:, :, columns] = part_refs[0][:, :, columns] + chunk
    if parts == 1:
        out_ref[...] = part_refs[0][...]
    for slot, groups in zip(slots, held):
        of_image = [next(back_refs) if there else None for there in groups]
        subtract_image(meta_ref, slot, of_image, pupil_ref, band_ref, out_ref, win)


def sibling_kernel(meta_ref, pupil_ref, band_ref, *refs, slots, held, parts, win):
    backs = sum(map(sum, held))
    part_refs, back_refs, total_ref = refs[:parts], iter(refs[parts : parts + backs]), refs[-1]
    out_refs = refs[parts + backs : -1]
    if parts:
        total_ref[...] = part_refs[0][...].astype(jnp.float32)
    else:
        total_ref[...] = jnp.zeros_like(total_ref)
    for slot, groups in zip(slots, held):
        of_image = [next(back_refs) if there else None for there in groups]
        subtract_image(meta_ref, slot, of_image, pupil_ref, band_ref, total_ref, win, 1)
    width = out_refs[0].shape[2]
    for number, out_ref in enumerate(out_refs):
        out_ref[...] = total_ref[:, :, number * width : (number + 1) * width].astype(jnp.bfloat16)


def backward_grid_kernel(meta_ref, pupil_ref, band_ref, spec_ref, back_ref, out_ref, *, win):
    step = pl.program_id(0)

    @pl.when(step == 0)
    def _():
        out_ref[...] = spec_ref[...]

    subtract_image(meta_ref, step, [back_ref.at[0]], pupil_ref, band_ref, out_ref, win)


def middle_kernel(*refs, terms, streams):
    term_refs, refs = refs[: terms * streams], refs[terms * streams :]
    (image_ref, cos_ref, sin_ref), refs = refs[:3], refs[3:]
    out_refs, (mid_ref, resid_ref) = refs[:streams], refs[streams:]
    _, rows, crop_width = term_refs[0].shape
    band = rows * streams
    block = min(512, crop_width)
    for stream in range(streams):
        of_stream = term_refs[stream * terms : (stream + 1) * terms]
        total = sum(ref[...].astype(jnp.float32) for ref in of_stream).astype(jnp.bfloat16)
        for part in range(2):
            start = part * band + stream * rows
            mid_ref[start : start + rows] = total[part]
    dot = functools.partial(jnp.dot, preferred_element_type=jnp.float32)
    for start in range(0, crop_width, block):
        columns = slice(start, start + block)
        by_cos = dot(mid_ref[...], cos_ref[:, columns])
        by_sin = dot(mid_ref[...], sin_ref[:, columns])
        field_real = by_cos[:band] - by_sin[band:]
        field_imag = by_sin[:band] + by_cos[band:]
        power = field_real * field_real + field_imag * field_imag
        measured = image_ref[0, :, columns].astype(jnp.float32)
        keeping = 1.0 - measured * lax.rsqrt(jnp.maximum(power, 1.0))
        resid_ref[:band, columns] = (field_real * keeping).astype(jnp.bfloat16)
        resid_ref[band:, columns] = (field_imag * keeping).astype(jnp.bfloat16)
    for start in range(0, crop_width, block):
        columns = slice(start, start + block)
        by_cos = dot(resid_ref[...], cos_ref[:, columns])
        by_sin = dot(resid_ref[...], sin_ref[:, columns])
        for part, back in enumerate((by_cos[:band] + by_sin[band:], by_cos[band:] - by_sin[:band])):
            for stream, out_ref in enumerate(out_refs):
                of_stream = back[stream * rows : (stream + 1) * rows]
                out_ref[part, :, columns] = of_stream.astype(jnp.bfloat16)


def params():
    return pltpu.CompilerParams(vmem_limit_bytes=vmem_bytes)


def light():
    return pl.CostEstimate(flops=1024, bytes_accessed=1024, transcendentals=0)


vmem = pl.BlockSpec(memory_space=pltpu.VMEM)
smem = pl.BlockSpec(memory_space=pltpu.SMEM)


def band_type(pupil, band_table, *lead):
    shape = lead + (2, band_table.shape[1] // 2, pupil.shape[1])
    return jax.ShapeDtypeStruct(shape, jnp.bfloat16)


def forward(meta, lows, pupil, band_table, base, images, tiles=(0, 1), came=None, streams=1):
    win = Windows(*lows[0][0].shape, pupil.shape[1])
    operands = [meta, pupil, band_table] + [part for low in lows for part in low]
    operands += [came] * (came is not None)
    count = images * streams
    _, rows, columns = band_type(pupil, band_table).shape
    return pl.pallas_call(
        functools.partial(
            forward_kernel, base=base, images=images, count=count, win=win, tiles=tiles
        ),
        in_specs=[smem] + [vmem] * (len(operands) - 1),
        out_specs=[vmem] * count,
        out_shape=[jax.ShapeDtypeStruct((2, rows // streams, columns), jnp.bfloat16)] * count,
        compiler_params=params(),
        cost_estimate=light(),
        name="forward",
    )(*operands)


def backward(meta, shape, pupil, band_table, parts, slots, backs, chunks=0):
    win = Windows(*shape[1:], pupil.shape[1])
    held = [[back is not None for back in groups] for groups in backs]
    operands = list(parts) + [back for groups in backs for back in groups if back is not None]
    kernel = sibling_kernel if chunks else backward_kernel
    out_shape = jax.ShapeDtypeStruct(shape, jnp.float32)
    if chunks:
        chunk = shape[:2] + (shape[2] // chunks,)
        out_shape = [jax.ShapeDtypeStruct(chunk, jnp.bfloat16)] * chunks
    return pl.pallas_call(
        functools.partial(kernel, slots=slots, held=held, parts=len(parts), win=win),
        in_specs=[smem] + [vmem] * (2 + len(operands)),
        out_specs=[vmem] * chunks if chunks else vmem,
        out_shape=out_shape,
        scratch_shapes=[pltpu.VMEM(shape, jnp.float32)] * (chunks > 0),
        compiler_params=pltpu.CompilerParams(vmem_limit_bytes=backward_bytes),
        cost_estimate=light(),
        name="backward",
    )(meta, pupil, band_table, *operands)


def middle(streams, image, cos_table, sin_table):
    _, rows, crop_width = streams[0][0].shape
    band = rows * len(streams)
    terms = [term for stream in streams for term in stream]
    return pl.pallas_call(
        functools.partial(
            middle_kernel, terms=len(streams[0]), streams=len(streams)
        ),
        in_specs=[vmem] * (len(terms) + 3),
        out_specs=[vmem] * len(streams),
        out_shape=[jax.ShapeDtypeStruct((2, rows, crop_width), jnp.bfloat16)] * len(streams),
        scratch_shapes=[pltpu.VMEM((2 * band, crop_width), jnp.bfloat16)] * 2,
        compiler_params=params(),
        cost_estimate=light(),
        name="middle",
    )(*terms, image, cos_table, sin_table)


def fixed(array):
    return pl.BlockSpec(array.shape, lambda i: (0,) * array.ndim)


def forward_all(meta, low, pupil, band_table):
    win = Windows(*low[0].shape, pupil.shape[1])
    count = meta.shape[1]
    out_type = band_type(pupil, band_table, count)
    return pl.pallas_call(
        functools.partial(forward_grid_kernel, win=win),
        grid=(count,),
        in_specs=[smem] + [fixed(array) for array in (pupil, band_table, *low)],
        out_specs=pl.BlockSpec((1,) + out_type.shape[1:], lambda i: (i, 0, 0, 0)),
        out_shape=out_type,
        compiler_params=params(),
        name="forward_all",
    )(meta, pupil, band_table, *low)


def backward_all(meta, spectrum, pupil, band_table, backs):
    win = Windows(*spectrum.shape[1:], pupil.shape[1])
    return pl.pallas_call(
        functools.partial(backward_grid_kernel, win=win),
        grid=(meta.shape[1],),
        in_specs=[smem]
        + [fixed(array) for array in (pupil, band_table, spectrum)]
        + [pl.BlockSpec((1,) + backs.shape[1:], lambda i: (i, 0, 0, 0))],
        out_specs=fixed(spectrum),
        out_shape=jax.ShapeDtypeStruct(spectrum.shape, jnp.float32),
        compiler_params=params(),
        name="backward_all",
    )(meta, pupil, band_table, spectrum, backs)


def cast_kernel(spec_ref, out_ref, held, sems, *, part):
    blocks, _, width = held.shape
    columns = [pl.ds(block * width, width) for block in range(blocks)]
    copies = [
        pltpu.make_async_copy(spec_ref.at[part, :, columns[i]], held.at[i], sems.at[i])
        for i in range(blocks)
    ]
    for copy in copies:
        copy.start()
    for i, copy in enumerate(copies):
        copy.wait()
        out_ref[:, columns[i]] = held[i].astype(jnp.bfloat16)


def low_part(spectrum, part):
    _, rows, columns = spectrum.shape
    return pl.pallas_call(
        functools.partial(cast_kernel, part=part),
        in_specs=[pl.BlockSpec(memory_space=pltpu.HBM)],
        out_specs=vmem,
        out_shape=jax.ShapeDtypeStruct((rows, columns), jnp.bfloat16),
        scratch_shapes=[
            pltpu.VMEM((4, rows, columns // 4), jnp.float32),
            pltpu.SemaphoreType.DMA((4,)),
        ],
        compiler_params=params(),
        cost_estimate=light(),
        name="low_part",
    )(spectrum)


def total(*terms):
    return sum(term.astype(jnp.float32) for term in terms).astype(jnp.bfloat16)


def per_device(spectrum, pupil, measured, centre_rows, centre_cols):
    count = lax.axis_size("ty")
    planes = count // 4
    position = lax.axis_index("ty")
    plane = position // 4
    _, tile_rows, slab_columns = spectrum.shape
    crop_width = pupil.shape[0]
    band = measured.shape[1]
    band_start = (crop_width - band) // 2
    cos_table, sin_table = fourier_tables(crop_width)
    chosen_rows = slice(band_start, band_start + band)
    band_table = jnp.asarray(
        np.concatenate([cos_table[:, chosen_rows], sin_table[:, chosen_rows]], axis=1)
    )
    cos_table, sin_table = jnp.asarray(cos_table), jnp.asarray(sin_table)

    half = crop_width // 2

    low = [low_part(spectrum, part) for part in range(2)]

    def image_meta(ids, positions):
        match = ids[:, None] == jnp.arange(count, dtype=jnp.int32)[None, :]
        tops = jnp.sum(jnp.where(match, centre_rows[None, :], 0), axis=1) - half
        lefts = jnp.sum(jnp.where(match, centre_cols[None, :], 0), axis=1) - half
        rows = [place * tile_rows - tops for place in positions]
        return jnp.stack(rows + [lefts]).astype(jnp.int32)

    if planes != 4:
        meta = image_meta(jnp.arange(count, dtype=jnp.int32), [position])
        partial = forward_all(meta, low, pupil, band_table)
        mid = lax.psum_scatter(partial, "ty", scatter_dimension=0, tiled=True)[0]
        back = lax.all_gather(middle([[mid]], measured, cos_table, sin_table)[0], "ty")
        return backward_all(meta, spectrum, pupil, band_table, back)

    targets = {"far": (3, 3, 0, 0), "next": (2, 2, 1, 1), "beside": (1, 0, 3, 2), "own": (0, 1, 2, 3)}
    own_core = [("far", 2), ("far", 0), ("next", 2), ("next", 0)]
    own_core += [("beside", 2), ("beside", 0), ("own", 2), ("own", 0)]
    slots = {}
    for core in (0, 1):
        for name, y in own_core:
            slots[name, y + core] = len(slots)
    ids = [
        [targets[name][i // 4] * 4 + (i % 4 ^ flip) for (name, flip) in slots]
        for i in range(count)
    ]
    my_ids = lax.dynamic_index_in_dim(jnp.asarray(ids, jnp.int32), position, keepdims=False)
    meta = image_meta(my_ids, [position, position ^ 1])

    def sibling(value):
        return lax.ppermute(value, "ty", [(i, i ^ 1) for i in range(count)])

    def across(value):
        return lax.ppermute(value, "ty", [(i, i ^ 2) for i in range(count)])

    def along(value, plane_pairs):
        pairs = [(4 * a + i, 4 * b + i) for a, b in plane_pairs for i in range(4)]
        return lax.ppermute(value, "ty", pairs)

    inward = [(0, 1), (3, 2)]
    outward = [(1, 0), (2, 3)]
    inner = [(1, 2), (2, 1)]
    together = lax.optimization_barrier

    lows = [low, [sibling(part) for part in low]]
    streams = 2
    (own_rows,) = forward(meta, lows[:1], pupil, band_table, 0, 1, (0,))
    far_leaving = forward(
        meta, lows[1:], pupil, band_table, 0, 1, (1,), own_rows, streams=streams
    )
    far_other = [across(value) for value in far_leaving]
    made = forward(
        together((meta, far_leaving[0]))[0], lows, pupil, band_table, 1, 7, streams=streams
    )
    summed, held = [], None
    for stream in reversed(range(streams)):
        (
            far_kept,
            next_leaving,
            next_kept,
            beside_leaving,
            beside_kept,
            own_leaving,
            own_kept,
        ) = made[stream::streams]
        far, far_kept, next_leaving = together((far_other[stream], far_kept, next_leaving))

        next_other = across(next_leaving)
        from_end = along(total(far_kept, far), inward)
        from_end, next_other, beside_leaving = together((from_end, next_other, beside_leaving))

        beside_other = across(beside_leaving)
        next_inward = along(total(next_kept, next_other), inward)
        far_inner = along(total(far_kept, far, from_end), inner)
        far_inner, next_inward, beside_other, own_leaving = together(
            (far_inner, next_inward, beside_other, own_leaving)
        )

        own_other = across(own_leaving)
        next_inner = along(total(next_kept, next_other, next_inward), inner)
        beside = along(total(beside_kept, beside_other, far_inner), inward + outward)
        terms = [own_kept, own_other, next_inner, beside]
        if stream > 0:
            terms = [total(*terms)]
            held = terms[0]
        else:
            terms[0] = together((terms[0], held))[0]
            terms = [total(*terms)]
        summed.insert(0, terms)
    backs = middle(summed, measured, cos_table, sin_table)

    at_ends = (plane == 0) | (plane == 3)
    lead, last = streams - 1, 0
    pieces = {}

    def apply(parts, names, chunks=0):
        taken = [[pieces.get((name, stream)) for stream in range(streams)] for name in names]
        own_slots = [slots[name] for name in names]
        shape = spectrum.shape
        return backward(meta, shape, pupil, band_table, parts, own_slots, taken, chunks)

    def close(stream, *names):
        closed = together(tuple(pieces[name, stream] for name in names))
        for name, value in zip(names, closed):
            pieces[name, stream] = value

    for stream in (lead, last):
        back = pieces[("own", 0), stream] = backs[stream]
        pieces[("own", 2), stream] = across(back)
        pieces["inner", stream] = along(back, inner)
        pieces[("beside", 0), stream] = along(back, inward + outward)
        close(stream, ("own", 2), "inner", ("beside", 0))
    early, later, late = (
        [("own", 0), ("beside", 0), ("own", 2)],
        [("next", 0), ("beside", 2)],
        [("far", 0), ("next", 2)],
    )
    for stream in (lead, last):
        pieces[("beside", 2), stream] = across(pieces[("beside", 0), stream])
        pieces["far inner", stream] = along(pieces[("beside", 0), stream], inner)
        pieces["outward", stream] = along(pieces["inner", stream], outward)
        if stream == last:
            pieces["result", stream] = apply([spectrum], early)
            close(stream, ("beside", 2), "far inner", "outward", "result")
        else:
            pieces["slab", stream] = apply([], early, 1)[0]
            close(stream, ("beside", 2), "far inner", "outward", "slab")
    for stream in (lead, last):
        from_next = jnp.where(at_ends, pieces["outward", stream], pieces["inner", stream])
        pieces[("next", 0), stream] = from_next
        pieces[("next", 2), stream] = across(from_next)
        pieces["far outward", stream] = along(pieces["far inner", stream], outward)
        if stream == last:
            pieces["slab", stream] = apply([pieces["slab", lead]], later, 1)[0]
            close(stream, ("next", 2), "far outward", "slab")
        else:
            close(stream, ("next", 2), "far outward")
    for stream in (lead, last):
        from_far = jnp.where(at_ends, pieces["far outward", stream], pieces["far inner", stream])
        pieces[("far", 0), stream] = from_far
        pieces[("far", 2), stream] = across(from_far)
    far_other = pieces[("far", 2), lead]
    slab, far_other = together((pieces["slab", last], far_other))
    chunks = apply([slab], late, 4)
    twin = sibling(far_other)
    slab = [sibling(chunk) for chunk in chunks[:-1]]
    result, twin = together((pieces["result", last], twin))
    result = apply([result], later + late)
    chunk, result = together((chunks[-1], result))
    slab.append(sibling(chunk))
    arriving, result = together((pieces[("far", 2), last], result))
    pieces[("far", 2), lead], pieces[("far", 3), lead] = far_other, twin
    pieces[("far", 2), last], pieces[("far", 3), last] = arriving, sibling(arriving)
    return apply([result] + slab, [("far", 2), ("far", 3)])


def solution(mesh):
    return jax.shard_map(
        per_device,
        mesh=mesh,
        in_specs=(
            P(None, ("groups", "ty"), None),
            P(),
            P(("groups", "ty"), None, None),
            P("groups"),
            P("groups"),
        ),
        out_specs=P(None, ("groups", "ty"), None),
        check_vma=False,
    )
```

```python
import functools
import math

import jax
import jax.numpy as jnp
import numpy as np
from jax import lax
from jax.experimental import pallas as pl
from jax.experimental.pallas import tpu as pltpu
from jax.sharding import PartitionSpec as P

step_size = 0.5
lane = 128
row_tile = 16
vmem_bytes = 20 * 1024 * 1024
backward_bytes = 20 * 1024 * 1024


def fourier_tables(crop_width):
    counter = np.arange(crop_width, dtype=np.int64)
    angle = (counter[:, None] * counter[None, :] % crop_width) * (2.0 * math.pi / crop_width)
    factor = 1.0 / math.sqrt(crop_width)
    cos_table = (np.cos(angle) * factor).astype(np.float32).astype(jnp.bfloat16)
    sin_table = (np.sin(angle) * factor).astype(np.float32).astype(jnp.bfloat16)
    return cos_table, sin_table


def tile_weight(pupil_ref, first_row, win):
    start = win.row(first_row)
    rows = pupil_ref[pl.ds(start, win.rows), :].astype(jnp.float32)
    rows = pltpu.roll(rows, (2 * win.rows + start - first_row) % win.rows, 0)
    shape = (win.tile_rows, win.crop_width)
    row = 2 * (first_row + lax.broadcasted_iota(jnp.int32, shape, 0)) - win.crop_width + 1
    column = 2 * lax.broadcasted_iota(jnp.int32, shape, 1) - win.crop_width + 1
    inside = row * row + column * column <= win.crop_width * win.crop_width
    return jnp.where(inside, rows[: win.tile_rows], 0.0)


def tile_band(band_ref, first_row, win):
    start = win.row(first_row)
    rows = band_ref[pl.ds(start, win.rows), :].astype(jnp.float32)
    rows = pltpu.roll(rows, (2 * win.rows + start - first_row) % win.rows, 0)[: win.tile_rows]
    band = rows.shape[1] // 2
    turned = jnp.concatenate([-rows[:, band:], rows[:, :band]], axis=1)
    return jnp.concatenate([rows, turned], axis=0).astype(jnp.bfloat16)


class Windows:
    def __init__(self, tile_rows, slab_columns, crop_width):
        self.tile_rows = tile_rows
        self.crop_width = crop_width
        self.rows = tile_rows + row_tile
        self.columns = crop_width + lane
        self.last_row = crop_width - self.rows
        self.last_column = slab_columns - self.columns

    def row(self, first_row):
        start = jnp.clip(first_row, 0, self.last_row) // row_tile * row_tile
        return pl.multiple_of(start, row_tile)

    def column(self, left):
        start = jnp.minimum(left // lane * lane, self.last_column)
        return pl.multiple_of(start, lane)

    def active(self, first_row):
        return (first_row > -self.tile_rows) & (first_row < self.crop_width)


def image_band(meta_ref, slot, lows, tiles, pupil_ref, band_ref, win, store, came=None):
    left = meta_ref[meta_ref.shape[0] - 1, slot]
    first_rows = [meta_ref[tile, slot] for tile in tiles]
    active = functools.reduce(jnp.logical_or, [win.active(row) for row in first_rows])
    band = band_ref.shape[1] // 2
    shape = (2, band, win.crop_width)

    @pl.when(jnp.logical_not(active))
    def _():
        store(jnp.zeros(shape, jnp.bfloat16) if came is None else came[...])

    @pl.when(active)
    def _():
        col_start = win.column(left)
        shift = (win.columns - (left - col_start)) % win.columns
        parts, tables = [], []
        for first_row, low_refs in zip(first_rows, lows):
            weight = tile_weight(pupil_ref, first_row, win)
            for low_ref in low_refs:
                low = low_ref[:, pl.ds(col_start, win.columns)].astype(jnp.float32)
                low = pltpu.roll(low, shift, 1)[:, : win.crop_width]
                parts.append((weight * low).astype(jnp.bfloat16))
            tables.append(tile_band(band_ref, first_row, win))
        mid = lax.dot_general(
            jnp.concatenate(tables, axis=0),
            jnp.concatenate(parts, axis=0),
            (((0,), (0,)), ((), ())),
            preferred_element_type=jnp.float32,
        )
        if came is not None:
            mid = mid + came[...].reshape(mid.shape).astype(jnp.float32)
        store(mid.astype(jnp.bfloat16).reshape(shape))


def forward_kernel(meta_ref, pupil_ref, band_ref, *refs, base, images, count, win, tiles):
    out_refs = refs[-count:]
    lows = [refs[2 * half : 2 * half + 2] for half in range(len(tiles))]
    came = refs[2 * len(tiles)] if len(refs) > 2 * len(tiles) + count else None
    streams = count // images

    def image(index):
        def store(value):
            for number in range(images):

                @pl.when(index == number)
                def _():
                    for stream in range(streams):
                        out_ref = out_refs[number * streams + stream]
                        rows = out_ref.shape[1]
                        out_ref[...] = value[:, stream * rows : (stream + 1) * rows]

        image_band(meta_ref, base + index, lows, tiles, pupil_ref, band_ref, win, store, came)

    pl.loop(0, images)(image)


def forward_grid_kernel(meta_ref, pupil_ref, band_ref, real_ref, imag_ref, out_ref, *, win):
    def store(value):
        out_ref[0] = value

    lows = [(real_ref, imag_ref)]
    image_band(meta_ref, pl.program_id(0), lows, (0,), pupil_ref, band_ref, win, store)


def subtract_image(meta_ref, slot, back_refs, pupil_ref, band_ref, out_ref, win, tile=0):
    first_row, left = meta_ref[tile, slot], meta_ref[meta_ref.shape[0] - 1, slot]
    tile_rows, crop_width = win.tile_rows, win.crop_width

    @pl.when(win.active(first_row))
    def _():
        col_start = win.column(left)
        weight = tile_weight(pupil_ref, first_row, win) * step_size
        table = tile_band(band_ref, first_row, win)
        band = table.shape[1] // 2
        rows = band // len(back_refs)
        held = [number for number, ref in enumerate(back_refs) if ref is not None]
        if len(held) < len(back_refs):
            starts = [part * band + number * rows for part in range(2) for number in held]
            table = jnp.concatenate([table[:, start : start + rows] for start in starts], axis=1)
        back = [back_refs[number][part] for part in range(2) for number in held]
        back = jnp.concatenate(back, axis=0)
        grad = jnp.dot(table, back, preferred_element_type=jnp.float32)
        columns = pl.ds(col_start, win.columns)
        pad = jnp.zeros((tile_rows, win.columns - crop_width), jnp.float32)
        for part in range(2):
            piece = grad[part * tile_rows : (part + 1) * tile_rows] * weight
            piece = pltpu.roll(jnp.concatenate([piece, pad], axis=1), left - col_start, 1)
            out_ref[part, :, columns] = out_ref[part, :, columns] - piece


def backward_kernel(meta_ref, pupil_ref, band_ref, *refs, slots, held, parts, win):
    part_refs, back_refs, out_ref = refs[:parts], iter(refs[parts:-1]), refs[-1]
    for number in range(parts - 1):
        chunk = part_refs[number + 1][...].astype(jnp.float32)
        width = chunk.shape[2]
        columns = slice(number * width, (number + 1) * width)
        out_ref[:, :, columns] = part_refs[0][:, :, columns] + chunk
    if parts == 1:
        out_ref[...] = part_refs[0][...]
    for slot, groups in zip(slots, held):
        of_image = [next(back_refs) if there else None for there in groups]
        subtract_image(meta_ref, slot, of_image, pupil_ref, band_ref, out_ref, win)


def sibling_kernel(meta_ref, pupil_ref, band_ref, *refs, slots, held, parts, win):
    backs = sum(map(sum, held))
    part_refs, back_refs, total_ref = refs[:parts], iter(refs[parts : parts + backs]), refs[-1]
    out_refs = refs[parts + backs : -1]
    if parts:
        total_ref[...] = part_refs[0][...].astype(jnp.float32)
    else:
        total_ref[...] = jnp.zeros_like(total_ref)
    for slot, groups in zip(slots, held):
        of_image = [next(back_refs) if there else None for there in groups]
        subtract_image(meta_ref, slot, of_image, pupil_ref, band_ref, total_ref, win, 1)
    width = out_refs[0].shape[2]
    for number, out_ref in enumerate(out_refs):
        out_ref[...] = total_ref[:, :, number * width : (number + 1) * width].astype(jnp.bfloat16)


def backward_grid_kernel(meta_ref, pupil_ref, band_ref, spec_ref, back_ref, out_ref, *, win):
    step = pl.program_id(0)

    @pl.when(step == 0)
    def _():
        out_ref[...] = spec_ref[...]

    subtract_image(meta_ref, step, [back_ref.at[0]], pupil_ref, band_ref, out_ref, win)


def middle_kernel(*refs, terms, streams):
    term_refs, refs = refs[: terms * streams], refs[terms * streams :]
    (image_ref, cos_ref, sin_ref), refs = refs[:3], refs[3:]
    out_refs, (mid_ref, resid_ref) = refs[:streams], refs[streams:]
    _, rows, crop_width = term_refs[0].shape
    band = rows * streams
    block = min(512, crop_width)
    for stream in range(streams):
        of_stream = term_refs[stream * terms : (stream + 1) * terms]
        total = sum(ref[...].astype(jnp.float32) for ref in of_stream).astype(jnp.bfloat16)
        for part in range(2):
            start = part * band + stream * rows
            mid_ref[start : start + rows] = total[part]
    dot = functools.partial(jnp.dot, preferred_element_type=jnp.float32)
    for start in range(0, crop_width, block):
        columns = slice(start, start + block)
        by_cos = dot(mid_ref[...], cos_ref[:, columns])
        by_sin = dot(mid_ref[...], sin_ref[:, columns])
        field_real = by_cos[:band] - by_sin[band:]
        field_imag = by_sin[:band] + by_cos[band:]
        power = field_real * field_real + field_imag * field_imag
        measured = image_ref[0, :, columns].astype(jnp.float32)
        keeping = 1.0 - measured * lax.rsqrt(jnp.maximum(power, 1.0))
        resid_ref[:band, columns] = (field_real * keeping).astype(jnp.bfloat16)
        resid_ref[band:, columns] = (field_imag * keeping).astype(jnp.bfloat16)
    for start in range(0, crop_width, block):
        columns = slice(start, start + block)
        by_cos = dot(resid_ref[...], cos_ref[:, columns])
        by_sin = dot(resid_ref[...], sin_ref[:, columns])
        for part, back in enumerate((by_cos[:band] + by_sin[band:], by_cos[band:] - by_sin[:band])):
            for stream, out_ref in enumerate(out_refs):
                of_stream = back[stream * rows : (stream + 1) * rows]
                out_ref[part, :, columns] = of_stream.astype(jnp.bfloat16)


def params():
    return pltpu.CompilerParams(vmem_limit_bytes=vmem_bytes)


def light():
    return pl.CostEstimate(flops=1024, bytes_accessed=1024, transcendentals=0)


vmem = pl.BlockSpec(memory_space=pltpu.VMEM)
smem = pl.BlockSpec(memory_space=pltpu.SMEM)


def band_type(pupil, band_table, *lead):
    shape = lead + (2, band_table.shape[1] // 2, pupil.shape[1])
    return jax.ShapeDtypeStruct(shape, jnp.bfloat16)


def forward(meta, lows, pupil, band_table, base, images, tiles=(0, 1), came=None, streams=1):
    win = Windows(*lows[0][0].shape, pupil.shape[1])
    operands = [meta, pupil, band_table] + [part for low in lows for part in low]
    operands += [came] * (came is not None)
    count = images * streams
    _, rows, columns = band_type(pupil, band_table).shape
    return pl.pallas_call(
        functools.partial(
            forward_kernel, base=base, images=images, count=count, win=win, tiles=tiles
        ),
        in_specs=[smem] + [vmem] * (len(operands) - 1),
        out_specs=[vmem] * count,
        out_shape=[jax.ShapeDtypeStruct((2, rows // streams, columns), jnp.bfloat16)] * count,
        compiler_params=params(),
        cost_estimate=light(),
        name="forward",
    )(*operands)


def backward(meta, shape, pupil, band_table, parts, slots, backs, chunks=0):
    win = Windows(*shape[1:], pupil.shape[1])
    held = [[back is not None for back in groups] for groups in backs]
    operands = list(parts) + [back for groups in backs for back in groups if back is not None]
    kernel = sibling_kernel if chunks else backward_kernel
    out_shape = jax.ShapeDtypeStruct(shape, jnp.float32)
    if chunks:
        chunk = shape[:2] + (shape[2] // chunks,)
        out_shape = [jax.ShapeDtypeStruct(chunk, jnp.bfloat16)] * chunks
    return pl.pallas_call(
        functools.partial(kernel, slots=slots, held=held, parts=len(parts), win=win),
        in_specs=[smem] + [vmem] * (2 + len(operands)),
        out_specs=[vmem] * chunks if chunks else vmem,
        out_shape=out_shape,
        scratch_shapes=[pltpu.VMEM(shape, jnp.float32)] * (chunks > 0),
        compiler_params=pltpu.CompilerParams(vmem_limit_bytes=backward_bytes),
        cost_estimate=light(),
        name="backward",
    )(meta, pupil, band_table, *operands)


def middle(streams, image, cos_table, sin_table):
    _, rows, crop_width = streams[0][0].shape
    band = rows * len(streams)
    terms = [term for stream in streams for term in stream]
    return pl.pallas_call(
        functools.partial(
            middle_kernel, terms=len(streams[0]), streams=len(streams)
        ),
        in_specs=[vmem] * (len(terms) + 3),
        out_specs=[vmem] * len(streams),
        out_shape=[jax.ShapeDtypeStruct((2, rows, crop_width), jnp.bfloat16)] * len(streams),
        scratch_shapes=[pltpu.VMEM((2 * band, crop_width), jnp.bfloat16)] * 2,
        compiler_params=params(),
        cost_estimate=light(),
        name="middle",
    )(*terms, image, cos_table, sin_table)


def fixed(array):
    return pl.BlockSpec(array.shape, lambda i: (0,) * array.ndim)


def forward_all(meta, low, pupil, band_table):
    win = Windows(*low[0].shape, pupil.shape[1])
    count = meta.shape[1]
    out_type = band_type(pupil, band_table, count)
    return pl.pallas_call(
        functools.partial(forward_grid_kernel, win=win),
        grid=(count,),
        in_specs=[smem] + [fixed(array) for array in (pupil, band_table, *low)],
        out_specs=pl.BlockSpec((1,) + out_type.shape[1:], lambda i: (i, 0, 0, 0)),
        out_shape=out_type,
        compiler_params=params(),
        name="forward_all",
    )(meta, pupil, band_table, *low)


def backward_all(meta, spectrum, pupil, band_table, backs):
    win = Windows(*spectrum.shape[1:], pupil.shape[1])
    return pl.pallas_call(
        functools.partial(backward_grid_kernel, win=win),
        grid=(meta.shape[1],),
        in_specs=[smem]
        + [fixed(array) for array in (pupil, band_table, spectrum)]
        + [pl.BlockSpec((1,) + backs.shape[1:], lambda i: (i, 0, 0, 0))],
        out_specs=fixed(spectrum),
        out_shape=jax.ShapeDtypeStruct(spectrum.shape, jnp.float32),
        compiler_params=params(),
        name="backward_all",
    )(meta, pupil, band_table, spectrum, backs)


def cast_kernel(spec_ref, out_ref, held, sems, *, part):
    blocks, _, width = held.shape
    columns = [pl.ds(block * width, width) for block in range(blocks)]
    copies = [
        pltpu.make_async_copy(spec_ref.at[part, :, columns[i]], held.at[i], sems.at[i])
        for i in range(blocks)
    ]
    for copy in copies:
        copy.start()
    for i, copy in enumerate(copies):
        copy.wait()
        out_ref[:, columns[i]] = held[i].astype(jnp.bfloat16)


def low_part(spectrum, part):
    _, rows, columns = spectrum.shape
    return pl.pallas_call(
        functools.partial(cast_kernel, part=part),
        in_specs=[pl.BlockSpec(memory_space=pltpu.HBM)],
        out_specs=vmem,
        out_shape=jax.ShapeDtypeStruct((rows, columns), jnp.bfloat16),
        scratch_shapes=[
            pltpu.VMEM((4, rows, columns // 4), jnp.float32),
            pltpu.SemaphoreType.DMA((4,)),
        ],
        compiler_params=params(),
        cost_estimate=light(),
        name="low_part",
    )(spectrum)


def total(*terms):
    return sum(term.astype(jnp.float32) for term in terms).astype(jnp.bfloat16)


def per_device(spectrum, pupil, measured, centre_rows, centre_cols):
    count = lax.axis_size("ty")
    planes = count // 4
    position = lax.axis_index("ty")
    plane = position // 4
    _, tile_rows, slab_columns = spectrum.shape
    crop_width = pupil.shape[0]
    band = measured.shape[1]
    band_start = (crop_width - band) // 2
    cos_table, sin_table = fourier_tables(crop_width)
    chosen_rows = slice(band_start, band_start + band)
    band_table = jnp.asarray(
        np.concatenate([cos_table[:, chosen_rows], sin_table[:, chosen_rows]], axis=1)
    )
    cos_table, sin_table = jnp.asarray(cos_table), jnp.asarray(sin_table)

    half = crop_width // 2

    low = [low_part(spectrum, part) for part in range(2)]

    def image_meta(ids, positions):
        match = ids[:, None] == jnp.arange(count, dtype=jnp.int32)[None, :]
        tops = jnp.sum(jnp.where(match, centre_rows[None, :], 0), axis=1) - half
        lefts = jnp.sum(jnp.where(match, centre_cols[None, :], 0), axis=1) - half
        rows = [place * tile_rows - tops for place in positions]
        return jnp.stack(rows + [lefts]).astype(jnp.int32)

    if planes != 4:
        meta = image_meta(jnp.arange(count, dtype=jnp.int32), [position])
        partial = forward_all(meta, low, pupil, band_table)
        mid = lax.psum_scatter(partial, "ty", scatter_dimension=0, tiled=True)[0]
        back = lax.all_gather(middle([[mid]], measured, cos_table, sin_table)[0], "ty")
        return backward_all(meta, spectrum, pupil, band_table, back)

    targets = {"far": (3, 3, 0, 0), "next": (2, 2, 1, 1), "beside": (1, 0, 3, 2), "own": (0, 1, 2, 3)}
    own_core = [("far", 2), ("far", 0), ("next", 2), ("next", 0)]
    own_core += [("beside", 2), ("beside", 0), ("own", 2), ("own", 0)]
    slots = {}
    for core in (0, 1):
        for name, y in own_core:
            slots[name, y + core] = len(slots)
    ids = [
        [targets[name][i // 4] * 4 + (i % 4 ^ flip) for (name, flip) in slots]
        for i in range(count)
    ]
    my_ids = lax.dynamic_index_in_dim(jnp.asarray(ids, jnp.int32), position, keepdims=False)
    meta = image_meta(my_ids, [position, position ^ 1])

    def sibling(value):
        return lax.ppermute(value, "ty", [(i, i ^ 1) for i in range(count)])

    def across(value):
        return lax.ppermute(value, "ty", [(i, i ^ 2) for i in range(count)])

    def along(value, plane_pairs):
        pairs = [(4 * a + i, 4 * b + i) for a, b in plane_pairs for i in range(4)]
        return lax.ppermute(value, "ty", pairs)

    inward = [(0, 1), (3, 2)]
    outward = [(1, 0), (2, 3)]
    inner = [(1, 2), (2, 1)]
    together = lax.optimization_barrier

    lows = [low, [sibling(part) for part in low]]
    streams = 2
    (own_rows,) = forward(meta, lows[:1], pupil, band_table, 0, 1, (0,))
    far_leaving = forward(
        meta, lows[1:], pupil, band_table, 0, 1, (1,), own_rows, streams=streams
    )
    far_other = [across(value) for value in far_leaving]
    made = forward(
        together((meta, far_leaving[0]))[0], lows, pupil, band_table, 1, 7, streams=streams
    )
    summed, held = [], None
    for stream in reversed(range(streams)):
        (
            far_kept,
            next_leaving,
            next_kept,
            beside_leaving,
            beside_kept,
            own_leaving,
            own_kept,
        ) = made[stream::streams]
        far, far_kept, next_leaving = together((far_other[stream], far_kept, next_leaving))

        next_other = across(next_leaving)
        from_end = along(total(far_kept, far), inward)
        from_end, next_other, beside_leaving = together((from_end, next_other, beside_leaving))

        beside_other = across(beside_leaving)
        next_inward = along(total(next_kept, next_other), inward)
        far_inner = along(total(far_kept, far, from_end), inner)
        far_inner, next_inward, beside_other, own_leaving = together(
            (far_inner, next_inward, beside_other, own_leaving)
        )

        own_other = across(own_leaving)
        next_inner = along(total(next_kept, next_other, next_inward), inner)
        beside = along(total(beside_kept, beside_other, far_inner), inward + outward)
        terms = [own_kept, own_other, next_inner, beside]
        if stream > 0:
            terms = [total(*terms)]
            held = terms[0]
        else:
            terms[0] = together((terms[0], held))[0]
            terms = [total(*terms)]
        summed.insert(0, terms)
    backs = middle(summed, measured, cos_table, sin_table)

    at_ends = (plane == 0) | (plane == 3)
    lead, last = streams - 1, 0
    pieces = {}

    def apply(parts, names, chunks=0):
        taken = [[pieces.get((name, stream)) for stream in range(streams)] for name in names]
        own_slots = [slots[name] for name in names]
        shape = spectrum.shape
        return backward(meta, shape, pupil, band_table, parts, own_slots, taken, chunks)

    def close(stream, *names):
        closed = together(tuple(pieces[name, stream] for name in names))
        for name, value in zip(names, closed):
            pieces[name, stream] = value

    for stream in (lead, last):
        back = pieces[("own", 0), stream] = backs[stream]
        pieces[("own", 2), stream] = across(back)
        pieces["inner", stream] = along(back, inner)
        pieces[("beside", 0), stream] = along(back, inward + outward)
        close(stream, ("own", 2), "inner", ("beside", 0))
    early, later, late = (
        [("own", 0), ("beside", 0), ("own", 2)],
        [("next", 0), ("beside", 2)],
        [("far", 0), ("next", 2)],
    )
    for stream in (lead, last):
        pieces[("beside", 2), stream] = across(pieces[("beside", 0), stream])
        pieces["far inner", stream] = along(pieces[("beside", 0), stream], inner)
        pieces["outward", stream] = along(pieces["inner", stream], outward)
        if stream == last:
            pieces["result", stream] = apply([spectrum], early)
            close(stream, ("beside", 2), "far inner", "outward", "result")
        else:
            pieces["slab", stream] = apply([], early, 1)[0]
            close(stream, ("beside", 2), "far inner", "outward", "slab")
    for stream in (lead, last):
        from_next = jnp.where(at_ends, pieces["outward", stream], pieces["inner", stream])
        pieces[("next", 0), stream] = from_next
        pieces[("next", 2), stream] = across(from_next)
        pieces["far outward", stream] = along(pieces["far inner", stream], outward)
        if stream == last:
            pieces["slab", stream] = apply([pieces["slab", lead]], later, 1)[0]
            close(stream, ("next", 2), "far outward", "slab")
        else:
            close(stream, ("next", 2), "far outward")
    for stream in (lead, last):
        from_far = jnp.where(at_ends, pieces["far outward", stream], pieces["far inner", stream])
        pieces[("far", 0), stream] = from_far
        pieces[("far", 2), stream] = across(from_far)
    far_other = pieces[("far", 2), lead]
    slab, far_other = together((pieces["slab", last], far_other))
    chunks = apply([slab], late, 4)
    result = apply([pieces["result", last]], later + late)
    far_other, result = together((far_other, result))
    twin = sibling(far_other)
    slab = [sibling(chunk) for chunk in chunks]
    arriving, result = together((pieces[("far", 2), last], result))
    pieces[("far", 2), lead], pieces[("far", 3), lead] = far_other, twin
    pieces[("far", 2), last], pieces[("far", 3), last] = arriving, sibling(arriving)
    return apply([result] + slab, [("far", 2), ("far", 3)])


def solution(mesh):
    return jax.shard_map(
        per_device,
        mesh=mesh,
        in_specs=(
            P(None, ("groups", "ty"), None),
            P(),
            P(("groups", "ty"), None, None),
            P("groups"),
            P("groups"),
        ),
        out_specs=P(None, ("groups", "ty"), None),
        check_vma=False,
    )
```

```python
import functools
import math

import jax
import jax.numpy as jnp
import numpy as np
from jax import lax
from jax.experimental import pallas as pl
from jax.experimental.pallas import tpu as pltpu
from jax.sharding import PartitionSpec as P

step_size = 0.5
lane = 128
row_tile = 16
vmem_bytes = 20 * 1024 * 1024
backward_bytes = 20 * 1024 * 1024


def fourier_tables(crop_width):
    counter = np.arange(crop_width, dtype=np.int64)
    angle = (counter[:, None] * counter[None, :] % crop_width) * (2.0 * math.pi / crop_width)
    factor = 1.0 / math.sqrt(crop_width)
    cos_table = (np.cos(angle) * factor).astype(np.float32).astype(jnp.bfloat16)
    sin_table = (np.sin(angle) * factor).astype(np.float32).astype(jnp.bfloat16)
    return cos_table, sin_table


def tile_weight(pupil_ref, first_row, win):
    start = win.row(first_row)
    rows = pupil_ref[pl.ds(start, win.rows), :].astype(jnp.float32)
    rows = pltpu.roll(rows, (2 * win.rows + start - first_row) % win.rows, 0)
    shape = (win.tile_rows, win.crop_width)
    row = 2 * (first_row + lax.broadcasted_iota(jnp.int32, shape, 0)) - win.crop_width + 1
    column = 2 * lax.broadcasted_iota(jnp.int32, shape, 1) - win.crop_width + 1
    inside = row * row + column * column <= win.crop_width * win.crop_width
    return jnp.where(inside, rows[: win.tile_rows], 0.0)


def tile_band(band_ref, first_row, win):
    start = win.row(first_row)
    rows = band_ref[pl.ds(start, win.rows), :].astype(jnp.float32)
    rows = pltpu.roll(rows, (2 * win.rows + start - first_row) % win.rows, 0)[: win.tile_rows]
    band = rows.shape[1] // 2
    turned = jnp.concatenate([-rows[:, band:], rows[:, :band]], axis=1)
    return jnp.concatenate([rows, turned], axis=0).astype(jnp.bfloat16)


class Windows:
    def __init__(self, tile_rows, slab_columns, crop_width):
        self.tile_rows = tile_rows
        self.crop_width = crop_width
        self.rows = tile_rows + row_tile
        self.columns = crop_width + lane
        self.last_row = crop_width - self.rows
        self.last_column = slab_columns - self.columns

    def row(self, first_row):
        start = jnp.clip(first_row, 0, self.last_row) // row_tile * row_tile
        return pl.multiple_of(start, row_tile)

    def column(self, left):
        start = jnp.minimum(left // lane * lane, self.last_column)
        return pl.multiple_of(start, lane)

    def active(self, first_row):
        return (first_row > -self.tile_rows) & (first_row < self.crop_width)


def image_band(meta_ref, slot, lows, tiles, pupil_ref, band_ref, win, store, came=None):
    left = meta_ref[meta_ref.shape[0] - 1, slot]
    first_rows = [meta_ref[tile, slot] for tile in tiles]
    active = functools.reduce(jnp.logical_or, [win.active(row) for row in first_rows])
    band = band_ref.shape[1] // 2
    shape = (2, band, win.crop_width)

    @pl.when(jnp.logical_not(active))
    def _():
        store(jnp.zeros(shape, jnp.bfloat16) if came is None else came[...])

    @pl.when(active)
    def _():
        col_start = win.column(left)
        shift = (win.columns - (left - col_start)) % win.columns
        parts, tables = [], []
        for first_row, low_refs in zip(first_rows, lows):
            weight = tile_weight(pupil_ref, first_row, win)
            for low_ref in low_refs:
                low = low_ref[:, pl.ds(col_start, win.columns)].astype(jnp.float32)
                low = pltpu.roll(low, shift, 1)[:, : win.crop_width]
                parts.append((weight * low).astype(jnp.bfloat16))
            tables.append(tile_band(band_ref, first_row, win))
        mid = lax.dot_general(
            jnp.concatenate(tables, axis=0),
            jnp.concatenate(parts, axis=0),
            (((0,), (0,)), ((), ())),
            preferred_element_type=jnp.float32,
        )
        if came is not None:
            mid = mid + came[...].reshape(mid.shape).astype(jnp.float32)
        store(mid.astype(jnp.bfloat16).reshape(shape))


def forward_kernel(meta_ref, pupil_ref, band_ref, *refs, base, images, count, win, tiles):
    out_refs = refs[-count:]
    lows = [refs[2 * half : 2 * half + 2] for half in range(len(tiles))]
    came = refs[2 * len(tiles)] if len(refs) > 2 * len(tiles) + count else None
    streams = count // images

    def image(index):
        def store(value):
            for number in range(images):

                @pl.when(index == number)
                def _():
                    for stream in range(streams):
                        out_ref = out_refs[number * streams + stream]
                        rows = out_ref.shape[1]
                        out_ref[...] = value[:, stream * rows : (stream + 1) * rows]

        image_band(meta_ref, base + index, lows, tiles, pupil_ref, band_ref, win, store, came)

    pl.loop(0, images)(image)


def forward_grid_kernel(meta_ref, pupil_ref, band_ref, real_ref, imag_ref, out_ref, *, win):
    def store(value):
        out_ref[0] = value

    lows = [(real_ref, imag_ref)]
    image_band(meta_ref, pl.program_id(0), lows, (0,), pupil_ref, band_ref, win, store)


def subtract_image(meta_ref, slot, back_refs, pupil_ref, band_ref, out_ref, win, tile=0):
    first_row, left = meta_ref[tile, slot], meta_ref[meta_ref.shape[0] - 1, slot]
    tile_rows, crop_width = win.tile_rows, win.crop_width

    @pl.when(win.active(first_row))
    def _():
        col_start = win.column(left)
        weight = tile_weight(pupil_ref, first_row, win) * step_size
        table = tile_band(band_ref, first_row, win)
        band = table.shape[1] // 2
        rows = band // len(back_refs)
        held = [number for number, ref in enumerate(back_refs) if ref is not None]
        if len(held) < len(back_refs):
            starts = [part * band + number * rows for part in range(2) for number in held]
            table = jnp.concatenate([table[:, start : start + rows] for start in starts], axis=1)
        back = [back_refs[number][part] for part in range(2) for number in held]
        back = jnp.concatenate(back, axis=0)
        grad = jnp.dot(table, back, preferred_element_type=jnp.float32)
        columns = pl.ds(col_start, win.columns)
        pad = jnp.zeros((tile_rows, win.columns - crop_width), jnp.float32)
        for part in range(2):
            piece = grad[part * tile_rows : (part + 1) * tile_rows] * weight
            piece = pltpu.roll(jnp.concatenate([piece, pad], axis=1), left - col_start, 1)
            out_ref[part, :, columns] = out_ref[part, :, columns] - piece


def backward_kernel(meta_ref, pupil_ref, band_ref, *refs, slots, held, parts, win):
    part_refs, back_refs, out_ref = refs[:parts], iter(refs[parts:-1]), refs[-1]
    for number in range(parts - 1):
        chunk = part_refs[number + 1][...].astype(jnp.float32)
        width = chunk.shape[2]
        columns = slice(number * width, (number + 1) * width)
        out_ref[:, :, columns] = part_refs[0][:, :, columns] + chunk
    if parts == 1:
        out_ref[...] = part_refs[0][...]
    if parts == 0:
        out_ref[...] = jnp.zeros_like(out_ref)
    for slot, groups in zip(slots, held):
        of_image = [next(back_refs) if there else None for there in groups]
        subtract_image(meta_ref, slot, of_image, pupil_ref, band_ref, out_ref, win)


def sibling_kernel(meta_ref, pupil_ref, band_ref, *refs, slots, held, parts, win):
    backs = sum(map(sum, held))
    part_refs, back_refs, total_ref = refs[:parts], iter(refs[parts : parts + backs]), refs[-1]
    out_refs = refs[parts + backs : -1]
    if parts:
        total_ref[...] = part_refs[0][...].astype(jnp.float32)
    else:
        total_ref[...] = jnp.zeros_like(total_ref)
    for slot, groups in zip(slots, held):
        of_image = [next(back_refs) if there else None for there in groups]
        subtract_image(meta_ref, slot, of_image, pupil_ref, band_ref, total_ref, win, 1)
    width = out_refs[0].shape[2]
    for number, out_ref in enumerate(out_refs):
        out_ref[...] = total_ref[:, :, number * width : (number + 1) * width].astype(jnp.bfloat16)


def backward_grid_kernel(meta_ref, pupil_ref, band_ref, spec_ref, back_ref, out_ref, *, win):
    step = pl.program_id(0)

    @pl.when(step == 0)
    def _():
        out_ref[...] = spec_ref[...]

    subtract_image(meta_ref, step, [back_ref.at[0]], pupil_ref, band_ref, out_ref, win)


def middle_kernel(*refs, terms, streams):
    term_refs, refs = refs[: terms * streams], refs[terms * streams :]
    (image_ref, cos_ref, sin_ref), refs = refs[:3], refs[3:]
    out_refs, (mid_ref, resid_ref) = refs[:streams], refs[streams:]
    _, rows, crop_width = term_refs[0].shape
    band = rows * streams
    block = min(512, crop_width)
    for stream in range(streams):
        of_stream = term_refs[stream * terms : (stream + 1) * terms]
        total = sum(ref[...].astype(jnp.float32) for ref in of_stream).astype(jnp.bfloat16)
        for part in range(2):
            start = part * band + stream * rows
            mid_ref[start : start + rows] = total[part]
    dot = functools.partial(jnp.dot, preferred_element_type=jnp.float32)
    for start in range(0, crop_width, block):
        columns = slice(start, start + block)
        by_cos = dot(mid_ref[...], cos_ref[:, columns])
        by_sin = dot(mid_ref[...], sin_ref[:, columns])
        field_real = by_cos[:band] - by_sin[band:]
        field_imag = by_sin[:band] + by_cos[band:]
        power = field_real * field_real + field_imag * field_imag
        measured = image_ref[0, :, columns].astype(jnp.float32)
        keeping = 1.0 - measured * lax.rsqrt(jnp.maximum(power, 1.0))
        resid_ref[:band, columns] = (field_real * keeping).astype(jnp.bfloat16)
        resid_ref[band:, columns] = (field_imag * keeping).astype(jnp.bfloat16)
    for start in range(0, crop_width, block):
        columns = slice(start, start + block)
        by_cos = dot(resid_ref[...], cos_ref[:, columns])
        by_sin = dot(resid_ref[...], sin_ref[:, columns])
        for part, back in enumerate((by_cos[:band] + by_sin[band:], by_cos[band:] - by_sin[:band])):
            for stream, out_ref in enumerate(out_refs):
                of_stream = back[stream * rows : (stream + 1) * rows]
                out_ref[part, :, columns] = of_stream.astype(jnp.bfloat16)


def params():
    return pltpu.CompilerParams(vmem_limit_bytes=vmem_bytes)


def light():
    return pl.CostEstimate(flops=1024, bytes_accessed=1024, transcendentals=0)


vmem = pl.BlockSpec(memory_space=pltpu.VMEM)
smem = pl.BlockSpec(memory_space=pltpu.SMEM)


def band_type(pupil, band_table, *lead):
    shape = lead + (2, band_table.shape[1] // 2, pupil.shape[1])
    return jax.ShapeDtypeStruct(shape, jnp.bfloat16)


def forward(meta, lows, pupil, band_table, base, images, tiles=(0, 1), came=None, streams=1):
    win = Windows(*lows[0][0].shape, pupil.shape[1])
    operands = [meta, pupil, band_table] + [part for low in lows for part in low]
    operands += [came] * (came is not None)
    count = images * streams
    _, rows, columns = band_type(pupil, band_table).shape
    return pl.pallas_call(
        functools.partial(
            forward_kernel, base=base, images=images, count=count, win=win, tiles=tiles
        ),
        in_specs=[smem] + [vmem] * (len(operands) - 1),
        out_specs=[vmem] * count,
        out_shape=[jax.ShapeDtypeStruct((2, rows // streams, columns), jnp.bfloat16)] * count,
        compiler_params=params(),
        cost_estimate=light(),
        name="forward",
    )(*operands)


def backward(meta, shape, pupil, band_table, parts, slots, backs, chunks=0):
    win = Windows(*shape[1:], pupil.shape[1])
    held = [[back is not None for back in groups] for groups in backs]
    operands = list(parts) + [back for groups in backs for back in groups if back is not None]
    kernel = sibling_kernel if chunks else backward_kernel
    out_shape = jax.ShapeDtypeStruct(shape, jnp.float32)
    if chunks:
        chunk = shape[:2] + (shape[2] // chunks,)
        out_shape = [jax.ShapeDtypeStruct(chunk, jnp.bfloat16)] * chunks
    return pl.pallas_call(
        functools.partial(kernel, slots=slots, held=held, parts=len(parts), win=win),
        in_specs=[smem] + [vmem] * (2 + len(operands)),
        out_specs=[vmem] * chunks if chunks else vmem,
        out_shape=out_shape,
        scratch_shapes=[pltpu.VMEM(shape, jnp.float32)] * (chunks > 0),
        compiler_params=pltpu.CompilerParams(vmem_limit_bytes=backward_bytes),
        cost_estimate=light(),
        name="backward",
    )(meta, pupil, band_table, *operands)


def middle(streams, image, cos_table, sin_table):
    _, rows, crop_width = streams[0][0].shape
    band = rows * len(streams)
    terms = [term for stream in streams for term in stream]
    return pl.pallas_call(
        functools.partial(
            middle_kernel, terms=len(streams[0]), streams=len(streams)
        ),
        in_specs=[vmem] * (len(terms) + 3),
        out_specs=[vmem] * len(streams),
        out_shape=[jax.ShapeDtypeStruct((2, rows, crop_width), jnp.bfloat16)] * len(streams),
        scratch_shapes=[pltpu.VMEM((2 * band, crop_width), jnp.bfloat16)] * 2,
        compiler_params=params(),
        cost_estimate=light(),
        name="middle",
    )(*terms, image, cos_table, sin_table)


def fixed(array):
    return pl.BlockSpec(array.shape, lambda i: (0,) * array.ndim)


def forward_all(meta, low, pupil, band_table):
    win = Windows(*low[0].shape, pupil.shape[1])
    count = meta.shape[1]
    out_type = band_type(pupil, band_table, count)
    return pl.pallas_call(
        functools.partial(forward_grid_kernel, win=win),
        grid=(count,),
        in_specs=[smem] + [fixed(array) for array in (pupil, band_table, *low)],
        out_specs=pl.BlockSpec((1,) + out_type.shape[1:], lambda i: (i, 0, 0, 0)),
        out_shape=out_type,
        compiler_params=params(),
        name="forward_all",
    )(meta, pupil, band_table, *low)


def backward_all(meta, spectrum, pupil, band_table, backs):
    win = Windows(*spectrum.shape[1:], pupil.shape[1])
    return pl.pallas_call(
        functools.partial(backward_grid_kernel, win=win),
        grid=(meta.shape[1],),
        in_specs=[smem]
        + [fixed(array) for array in (pupil, band_table, spectrum)]
        + [pl.BlockSpec((1,) + backs.shape[1:], lambda i: (i, 0, 0, 0))],
        out_specs=fixed(spectrum),
        out_shape=jax.ShapeDtypeStruct(spectrum.shape, jnp.float32),
        compiler_params=params(),
        name="backward_all",
    )(meta, pupil, band_table, spectrum, backs)


def cast_kernel(spec_ref, out_ref, held, sems, *, part):
    blocks, _, width = held.shape
    columns = [pl.ds(block * width, width) for block in range(blocks)]
    copies = [
        pltpu.make_async_copy(spec_ref.at[part, :, columns[i]], held.at[i], sems.at[i])
        for i in range(blocks)
    ]
    for copy in copies:
        copy.start()
    for i, copy in enumerate(copies):
        copy.wait()
        out_ref[:, columns[i]] = held[i].astype(jnp.bfloat16)


def low_part(spectrum, part):
    _, rows, columns = spectrum.shape
    return pl.pallas_call(
        functools.partial(cast_kernel, part=part),
        in_specs=[pl.BlockSpec(memory_space=pltpu.HBM)],
        out_specs=vmem,
        out_shape=jax.ShapeDtypeStruct((rows, columns), jnp.bfloat16),
        scratch_shapes=[
            pltpu.VMEM((4, rows, columns // 4), jnp.float32),
            pltpu.SemaphoreType.DMA((4,)),
        ],
        compiler_params=params(),
        cost_estimate=light(),
        name="low_part",
    )(spectrum)


def total(*terms):
    return sum(term.astype(jnp.float32) for term in terms).astype(jnp.bfloat16)


def per_device(spectrum, pupil, measured, centre_rows, centre_cols):
    count = lax.axis_size("ty")
    planes = count // 4
    position = lax.axis_index("ty")
    plane = position // 4
    _, tile_rows, slab_columns = spectrum.shape
    crop_width = pupil.shape[0]
    band = measured.shape[1]
    band_start = (crop_width - band) // 2
    cos_table, sin_table = fourier_tables(crop_width)
    chosen_rows = slice(band_start, band_start + band)
    band_table = jnp.asarray(
        np.concatenate([cos_table[:, chosen_rows], sin_table[:, chosen_rows]], axis=1)
    )
    cos_table, sin_table = jnp.asarray(cos_table), jnp.asarray(sin_table)

    half = crop_width // 2

    low = [low_part(spectrum, part) for part in range(2)]

    def image_meta(ids, positions):
        match = ids[:, None] == jnp.arange(count, dtype=jnp.int32)[None, :]
        tops = jnp.sum(jnp.where(match, centre_rows[None, :], 0), axis=1) - half
        lefts = jnp.sum(jnp.where(match, centre_cols[None, :], 0), axis=1) - half
        rows = [place * tile_rows - tops for place in positions]
        return jnp.stack(rows + [lefts]).astype(jnp.int32)

    if planes != 4:
        meta = image_meta(jnp.arange(count, dtype=jnp.int32), [position])
        partial = forward_all(meta, low, pupil, band_table)
        mid = lax.psum_scatter(partial, "ty", scatter_dimension=0, tiled=True)[0]
        back = lax.all_gather(middle([[mid]], measured, cos_table, sin_table)[0], "ty")
        return backward_all(meta, spectrum, pupil, band_table, back)

    targets = {"far": (3, 3, 0, 0), "next": (2, 2, 1, 1), "beside": (1, 0, 3, 2), "own": (0, 1, 2, 3)}
    own_core = [("far", 2), ("far", 0), ("next", 2), ("next", 0)]
    own_core += [("beside", 2), ("beside", 0), ("own", 2), ("own", 0)]
    slots = {}
    for core in (0, 1):
        for name, y in own_core:
            slots[name, y + core] = len(slots)
    ids = [
        [targets[name][i // 4] * 4 + (i % 4 ^ flip) for (name, flip) in slots]
        for i in range(count)
    ]
    my_ids = lax.dynamic_index_in_dim(jnp.asarray(ids, jnp.int32), position, keepdims=False)
    meta = image_meta(my_ids, [position, position ^ 1])

    def sibling(value):
        return lax.ppermute(value, "ty", [(i, i ^ 1) for i in range(count)])

    def across(value):
        return lax.ppermute(value, "ty", [(i, i ^ 2) for i in range(count)])

    def along(value, plane_pairs):
        pairs = [(4 * a + i, 4 * b + i) for a, b in plane_pairs for i in range(4)]
        return lax.ppermute(value, "ty", pairs)

    inward = [(0, 1), (3, 2)]
    outward = [(1, 0), (2, 3)]
    inner = [(1, 2), (2, 1)]
    together = lax.optimization_barrier

    lows = [low, [sibling(part) for part in low]]
    streams = 2
    (own_rows,) = forward(meta, lows[:1], pupil, band_table, 0, 1, (0,))
    far_leaving = forward(
        meta, lows[1:], pupil, band_table, 0, 1, (1,), own_rows, streams=streams
    )
    far_other = [across(value) for value in far_leaving]
    made = forward(
        together((meta, far_leaving[0]))[0], lows, pupil, band_table, 1, 7, streams=streams
    )
    summed, held = [], None
    for stream in reversed(range(streams)):
        (
            far_kept,
            next_leaving,
            next_kept,
            beside_leaving,
            beside_kept,
            own_leaving,
            own_kept,
        ) = made[stream::streams]
        far, far_kept, next_leaving = together((far_other[stream], far_kept, next_leaving))

        next_other = across(next_leaving)
        from_end = along(total(far_kept, far), inward)
        from_end, next_other, beside_leaving = together((from_end, next_other, beside_leaving))

        beside_other = across(beside_leaving)
        next_inward = along(total(next_kept, next_other), inward)
        far_inner = along(total(far_kept, far, from_end), inner)
        far_inner, next_inward, beside_other, own_leaving = together(
            (far_inner, next_inward, beside_other, own_leaving)
        )

        own_other = across(own_leaving)
        next_inner = along(total(next_kept, next_other, next_inward), inner)
        beside = along(total(beside_kept, beside_other, far_inner), inward + outward)
        terms = [own_kept, own_other, next_inner, beside]
        if stream > 0:
            terms = [total(*terms)]
            held = terms[0]
        else:
            terms[0] = together((terms[0], held))[0]
            terms = [total(*terms)]
        summed.insert(0, terms)
    backs = middle(summed, measured, cos_table, sin_table)

    at_ends = (plane == 0) | (plane == 3)
    lead, last = streams - 1, 0
    pieces = {}

    def apply(parts, names, chunks=0):
        taken = [[pieces.get((name, stream)) for stream in range(streams)] for name in names]
        own_slots = [slots[name] for name in names]
        shape = spectrum.shape
        return backward(meta, shape, pupil, band_table, parts, own_slots, taken, chunks)

    def close(stream, *names):
        closed = together(tuple(pieces[name, stream] for name in names))
        for name, value in zip(names, closed):
            pieces[name, stream] = value

    for stream in (lead, last):
        back = pieces[("own", 0), stream] = backs[stream]
        pieces[("own", 2), stream] = across(back)
        pieces["inner", stream] = along(back, inner)
        pieces[("beside", 0), stream] = along(back, inward + outward)
        close(stream, ("own", 2), "inner", ("beside", 0))
    early, later, late = (
        [("own", 0), ("beside", 0), ("own", 2)],
        [("next", 0), ("beside", 2)],
        [("far", 0), ("next", 2)],
    )
    for stream in (lead, last):
        pieces[("beside", 2), stream] = across(pieces[("beside", 0), stream])
        pieces["far inner", stream] = along(pieces[("beside", 0), stream], inner)
        pieces["outward", stream] = along(pieces["inner", stream], outward)
        if stream == last:
            pieces["result", stream] = apply([], early)
            close(stream, ("beside", 2), "far inner", "outward", "result")
        else:
            pieces["slab", stream] = apply([], early, 1)[0]
            close(stream, ("beside", 2), "far inner", "outward", "slab")
    for stream in (lead, last):
        from_next = jnp.where(at_ends, pieces["outward", stream], pieces["inner", stream])
        pieces[("next", 0), stream] = from_next
        pieces[("next", 2), stream] = across(from_next)
        pieces["far outward", stream] = along(pieces["far inner", stream], outward)
        if stream == last:
            pieces["slab", stream] = apply([pieces["slab", lead]], later, 1)[0]
            close(stream, ("next", 2), "far outward", "slab")
        else:
            close(stream, ("next", 2), "far outward")
    for stream in (lead, last):
        from_far = jnp.where(at_ends, pieces["far outward", stream], pieces["far inner", stream])
        pieces[("far", 0), stream] = from_far
        pieces[("far", 2), stream] = across(from_far)
    far_other = pieces[("far", 2), lead]
    slab, far_other = together((pieces["slab", last], far_other))
    chunks = apply([slab], late, 4)
    twin = sibling(far_other)
    slab = [sibling(chunk) for chunk in chunks[:-1]]
    result, twin = together((pieces["result", last], twin))
    result = apply([spectrum, result], later + late)
    chunk, result = together((chunks[-1], result))
    slab.append(sibling(chunk))
    arriving, result = together((pieces[("far", 2), last], result))
    pieces[("far", 2), lead], pieces[("far", 3), lead] = far_other, twin
    pieces[("far", 2), last], pieces[("far", 3), last] = arriving, sibling(arriving)
    return apply([result] + slab, [("far", 2), ("far", 3)])


def solution(mesh):
    return jax.shard_map(
        per_device,
        mesh=mesh,
        in_specs=(
            P(None, ("groups", "ty"), None),
            P(),
            P(("groups", "ty"), None, None),
            P("groups"),
            P("groups"),
        ),
        out_specs=P(None, ("groups", "ty"), None),
        check_vma=False,
    )
```
